32 devices in a mesh: groups: 2 (over y), ta: 4 (over z), gx: 4 (over x, core).
Axes of the slice: x: 2, y: 2, z: 4, core: 2. Of those that a mesh axis runs over, the one named last changes fastest.
Arguments:
- source: bfloat16 [4, 4, 3, 2, 16, 16, 128], P(None, None, None, None, ('groups', 'ta'), 'gx'), parts along dimension 4, may hold values from -6 to 6
- gauge_links: bfloat16 [4, 3, 3, 2, 2, 16, 16, 128], P(None, None, None, None, None, ('groups', 'ta'), 'gx'), parts along dimension 5, may hold values from -2.5 to 2.5
- clover_even: bfloat16 [2, 6, 6, 2, 16, 16, 128], P(None, None, None, None, ('groups', 'ta'), 'gx'), parts along dimension 4, may hold values from -0.5 to 1.5, as said below
- clover_odd_inv: bfloat16 [2, 6, 6, 2, 16, 16, 128], P(None, None, None, None, ('groups', 'ta'), 'gx'), parts along dimension 4, may hold values from -0.5 to 1.5, as said below
Outputs:
- result: bfloat16 [4, 4, 3, 2, 16, 16, 128], P(None, None, None, None, ('groups', 'ta'), 'gx'), parts along dimension 4
The draws below stay inside these ranges and needn't reach their ends.
There are 2 independent parts, one for each index of `groups`. The reference program is written for one: setup_inputs(seed, part) draws one part's arguments, and reference() takes and returns one part's arrays. A program takes and returns all parts, laid end to end along the dimension named above; each array names one. Nothing has to cross between parts.
Inputs may be any that keep to these rules, and one draw needn't show every extreme that they name: `clover_even`: each 6 x 6 block of a site is Hermitian. `clover_odd_inv`: each 6 x 6 block of a site is Hermitian.
All inputs are finite; a program needn't handle non-finite values.
Results may differ from the reference program's by a relative error of at most 0.0055.
Values may be sent and summed in bfloat16 or wider, within the bound.
No kernel may reach another device: no remote copies, remote signals or barrier semaphores. Data moves between devices by JAX's collectives and lax.ppermute only.
A program may use at most 64 MiB of HBM per device.

```python
import jax
import jax.numpy as jnp
from jax import lax

RHS = 4
NZ = 16
NT = 8
NX = 16
PLANE = 128


def hermitian_blocks(key, low_value, high_value, spread):
    first_key, second_key, third_key = jax.random.split(key, 3)
    block_shape = (2, 6, 6, NT, NX, PLANE)
    real_noise = jnp.clip(jax.random.normal(first_key, block_shape, jnp.float32), -3.0, 3.0)
    imag_noise = jnp.clip(jax.random.normal(second_key, block_shape, jnp.float32), -3.0, 3.0)
    real_part = 0.5 * spread * (real_noise + jnp.swapaxes(real_noise, 1, 2))
    imag_part = 0.5 * spread * (imag_noise - jnp.swapaxes(imag_noise, 1, 2))
    diagonal = jax.random.uniform(third_key, (2, 6, 1, NT, NX, PLANE), jnp.float32, low_value, high_value)
    identity = jnp.eye(6, dtype=jnp.float32)[None, :, :, None, None, None]
    real_part = real_part * (1.0 - identity) + identity * diagonal
    return jnp.stack([real_part, imag_part], axis=3).astype(jnp.bfloat16)


def draw_clover_even(key, part):
    key = jax.random.fold_in(key, 11)
    return hermitian_blocks(key, 0.7, 1.3, 0.12)


def draw_clover_odd_inv(key, part):
    key = jax.random.fold_in(key, 23)
    return hermitian_blocks(key, 0.7, 1.3, 0.12)


def shard_levels(own_key, shape, cuts, least, top_value):
    loudness, own = 1.0, jax.random.fold_in(own_key, 6)
    for dim, blocks in cuts:
        draws = jnp.exp(jax.random.uniform(jax.random.fold_in(own, dim), (blocks,), jnp.float32, least / len(cuts), top_value / len(cuts)))
        loudness = loudness * jnp.repeat(draws, shape[dim] // blocks).reshape([-1 if axis == dim else 1 for axis in range(len(shape))])
    return loudness


def scatter_about(stream_key, dims, deviation, bound, shards=(), held_as=jnp.bfloat16):
    level = shard_levels(stream_key, dims, shards, -0.22, 0.18) if shards else 1.0
    result = jax.random.normal(stream_key, dims, jnp.float32) * deviation * level
    return jnp.minimum(jnp.maximum(result, -bound), bound).astype(held_as)


def setup_inputs(seed: int = 0, part: int = 0) -> dict:
    keys = jax.random.split(jax.random.key(seed), 5)
    part_splits = jax.random.split(jax.random.fold_in(keys[4], part), 5)
    source = scatter_about(part_splits[0], (RHS, 4, 3, 2, NT, NX, PLANE), 1.0, 6.0, ((4, 4), (5, 4)))
    gauge_links = scatter_about(part_splits[1], (4, 3, 3, 2, 2, NT, NX, PLANE), 6 ** -0.5, 2.5, ((5, 4), (6, 4)))
    clover_even = draw_clover_even(jax.random.fold_in(jax.random.fold_in(keys[4], part), 71), part)
    clover_odd_inv = draw_clover_odd_inv(jax.random.fold_in(jax.random.fold_in(keys[4], part), 71), part)
    return {"source": source, "gauge_links": gauge_links, "clover_even": clover_even, "clover_odd_inv": clover_odd_inv}


hopping = 0.14
spin_blocks = [[[1, 0], [0, 1]], [[0, -1j], [-1j, 0]], [[0, -1], [1, 0]], [[-1j, 0], [0, 1j]]]
spin_inverses = [[[1, 0], [0, 1]], [[0, 1j], [1j, 0]], [[0, 1], [-1, 0]], [[1j, 0], [0, -1j]]]


def spin_apply(matrix, vector):
    rows_out = []
    for row_index in range(2):
        real_sum = None
        imag_sum = None
        for col_index in range(2):
            factor = complex(matrix[row_index][col_index])
            if factor == 0:
                continue
            real_part = vector[:, col_index, :, 0]
            imag_part = vector[:, col_index, :, 1]
            if factor.real != 0:
                term_real = real_part * factor.real
                term_imag = imag_part * factor.real
            else:
                term_real = imag_part * (-factor.imag)
                term_imag = real_part * factor.imag
            real_sum = term_real if real_sum is None else real_sum + term_real
            imag_sum = term_imag if imag_sum is None else imag_sum + term_imag
        rows_out.append(jnp.stack([real_sum, imag_sum], axis=2))
    return jnp.stack(rows_out, axis=1)


def project(spinor, direction, sign_value):
    upper_half = spinor[:, 0:2].astype(jnp.float32)
    lower_half = spinor[:, 2:4].astype(jnp.float32)
    return (upper_half + sign_value * spin_apply(spin_blocks[direction], lower_half)).astype(jnp.bfloat16)


def rebuild(half_spinor, direction, sign_value):
    lower_half = sign_value * spin_apply(spin_inverses[direction], half_spinor)
    return jnp.concatenate([half_spinor, lower_half], axis=1)


def contract(formula, matrix_part, spinor_part):
    return jnp.einsum(formula, matrix_part.astype(jnp.float32), spinor_part.astype(jnp.float32), precision=lax.Precision.HIGHEST)


def color_apply(matrices, half_spinor, adjoint):
    formula = "batxw,rsbtxw->rsatxw" if adjoint else "abtxw,rsbtxw->rsatxw"
    links_real = matrices[:, :, 0]
    links_imag = matrices[:, :, 1]
    spinor_real = half_spinor[:, :, :, 0]
    spinor_imag = half_spinor[:, :, :, 1]
    if adjoint:
        real_out = contract(formula, links_real, spinor_real) + contract(formula, links_imag, spinor_imag)
        imag_out = contract(formula, links_real, spinor_imag) - contract(formula, links_imag, spinor_real)
    else:
        real_out = contract(formula, links_real, spinor_real) - contract(formula, links_imag, spinor_imag)
        imag_out = contract(formula, links_real, spinor_imag) + contract(formula, links_imag, spinor_real)
    return jnp.stack([real_out, imag_out], axis=3)


def carried(spinor, matrices, direction):
    return color_apply(matrices, project(spinor, direction, 1.0), True).astype(jnp.bfloat16)


def clover_apply(clover, spinor):
    rhs_count = spinor.shape[0]
    blocks = spinor.reshape((rhs_count, 2, 6, 2) + spinor.shape[4:])
    formula = "cijtxw,rcjtxw->rcitxw"
    clover_real = clover[:, :, :, 0]
    clover_imag = clover[:, :, :, 1]
    blocks_real = blocks[:, :, :, 0]
    blocks_imag = blocks[:, :, :, 1]
    real_out = contract(formula, clover_real, blocks_real) - contract(formula, clover_imag, blocks_imag)
    imag_out = contract(formula, clover_real, blocks_imag) + contract(formula, clover_imag, blocks_real)
    return jnp.stack([real_out, imag_out], axis=3).reshape(spinor.shape)


def parity_mask(site_shape, parity):
    half_depth = NZ // 2
    time_index = lax.broadcasted_iota(jnp.int32, site_shape, 0)
    space_index = lax.broadcasted_iota(jnp.int32, site_shape, 1)
    plane_index = lax.broadcasted_iota(jnp.int32, site_shape, 2)
    lattice_y = plane_index // half_depth
    return (time_index + space_index + lattice_y + parity) % 2


def neighbour(values, direction, offset, odd_rows):
    half_depth = NZ // 2
    if direction == 0:
        return jnp.roll(values, -offset, axis=-3)
    if direction == 1:
        return jnp.roll(values, -offset, axis=-2)
    if direction == 2:
        return jnp.roll(values, -offset * half_depth, axis=-1)
    depth_slot = lax.broadcasted_iota(jnp.int32, values.shape[-3:], 2) % half_depth
    if offset == 1:
        shifted = jnp.where(depth_slot == half_depth - 1, jnp.roll(values, half_depth - 1, axis=-1), jnp.roll(values, -1, axis=-1))
        return jnp.where(odd_rows == 1, shifted, values)
    shifted = jnp.where(depth_slot == 0, jnp.roll(values, -(half_depth - 1), axis=-1), jnp.roll(values, 1, axis=-1))
    return jnp.where(odd_rows == 0, shifted, values)


def hop_field(spinor, gauge_links, out_parity):
    in_parity = 1 - out_parity
    odd_rows = parity_mask(spinor.shape[-3:], out_parity)
    summed = jnp.zeros(spinor.shape, jnp.float32)
    for direction in range(4):
        forward_half = neighbour(project(spinor, direction, -1.0), direction, 1, odd_rows)
        summed = summed + rebuild(color_apply(gauge_links[direction, :, :, :, out_parity], forward_half, False), direction, -1.0)
        behind = neighbour(carried(spinor, gauge_links[direction, :, :, :, in_parity], direction), direction, -1, odd_rows)
        summed = summed + rebuild(behind.astype(jnp.float32), direction, 1.0)
    return summed


def schur_step(spinor, gauge_links, clover_even, clover_odd_inv):
    middle = hop_field(spinor, gauge_links, 1).astype(jnp.bfloat16)
    inverted = clover_apply(clover_odd_inv, middle).astype(jnp.bfloat16)
    hopped = hop_field(inverted, gauge_links, 0)
    return (clover_apply(clover_even, spinor) - hopping * hopping * hopped).astype(jnp.bfloat16)


def reference(source, gauge_links, clover_even, clover_odd_inv):
    def twice(single):
        first_pass = schur_step(single[None], gauge_links, clover_even, clover_odd_inv)
        return schur_step(first_pass, gauge_links, clover_even, clover_odd_inv)[0]

    return lax.map(twice, source)
```

```python
import functools

import jax
import jax.numpy as jnp
from jax import lax
from jax.experimental import pallas as pl
from jax.experimental.pallas import tpu as pltpu
from jax.sharding import PartitionSpec as P

HALF_DEPTH = 8
KAPPA2 = 0.14 * 0.14
RHS = 4
F32 = jnp.float32
BF16 = jnp.bfloat16

SPIN = (((0, 0), (1, 0)), ((1, 3), (0, 3)), ((1, 2), (0, 0)), ((0, 3), (1, 1)))
SPIN_INV = (((0, 0), (1, 0)), ((1, 1), (0, 1)), ((1, 0), (0, 2)), ((0, 1), (1, 3)))


def add_power(base, value, power):
    (br, bi), (vr, vi) = base, value
    if power == 0:
        return br + vr, bi + vi
    if power == 1:
        return br - vi, bi + vr
    if power == 2:
        return br - vr, bi - vi
    return br + vi, bi - vr


def project(field, mu, sign):
    shift = 0 if sign > 0 else 2
    half = []
    for row in range(2):
        col, power = SPIN[mu][row]
        for c in range(3):
            half.append(add_power(field[row * 3 + c], field[(2 + col) * 3 + c], (power + shift) % 4))
    return half


def rebuild(acc, half, mu, sign):
    shift = 0 if sign > 0 else 2
    out = list(acc)
    for j in range(6):
        out[j] = add_power(out[j], half[j], 0)
    for row in range(2):
        col, power = SPIN_INV[mu][row]
        for c in range(3):
            j = (2 + row) * 3 + c
            out[j] = add_power(out[j], half[col * 3 + c], (power + shift) % 4)
    return out


def color(links, half, adjoint):
    out = []
    for s in range(2):
        for a in range(3):
            re = im = None
            for b in range(3):
                lr, li = links[b][a] if adjoint else links[a][b]
                vr, vi = half[s * 3 + b]
                if adjoint:
                    tr, ti = lr * vr + li * vi, lr * vi - li * vr
                else:
                    tr, ti = lr * vr - li * vi, lr * vi + li * vr
                re = tr if re is None else re + tr
                im = ti if im is None else im + ti
            out.append((re, im))
    return out


def each(function, half):
    return [(function(re), function(im)) for re, im in half]


def load_pair(ref, index):
    block = ref[index * 16:(index + 1) * 16, :].astype(F32)
    return block[0:8], block[8:16]


def load_links(ref, mu, parity):
    links = []
    for a in range(3):
        row = []
        for b in range(3):
            k = ((mu * 3 + a) * 3 + b) * 2
            row.append((load_pair(ref, k)[parity], load_pair(ref, k + 1)[parity]))
        links.append(row)
    return links


def load_field(ref, r):
    return [load_pair(ref, r * 12 + j) for j in range(12)]


def store_pair(ref, index, pair):
    ref[index * 16:(index + 1) * 16, :] = jnp.concatenate(pair, axis=0).astype(ref.dtype)


def store_field(ref, r, field):
    for j in range(12):
        store_pair(ref, r * 12 + j, field[j])


def site_masks():
    rows = lax.broadcasted_iota(jnp.int32, (8, 128), 0)
    return rows // 4, rows % 4


def roll_rows(value, shift):
    shift %= 8
    return pltpu.roll(value, shift, 0) if shift else value


def select(mask, a, b):
    return jnp.where(mask, a, b)


def send_halos(f_ref, links_ref, parity, outs):
    t_back, t_ahead, x_back, x_ahead, kept = outs
    t_idx, x_idx = site_masks()
    first_t = t_idx == 0
    for mu in range(2):
        links = load_links(links_ref, mu, parity)
        ahead_all, carry_all = [], []
        for r in range(RHS):
            field = load_field(f_ref, r)
            ahead = project(field, mu, -1)
            carry = color(links, project(field, mu, 1), True)
            if mu == 0:
                moved = each(lambda v: roll_rows(v, 4), ahead)
                back = each(lambda v: roll_rows(v, 4), carry)
                for c in range(3):
                    store_pair(t_back, r * 3 + c, [select(first_t, ahead[c + 3][i], moved[c][i]) for i in range(2)])
                    store_pair(t_ahead, r * 3 + c, [select(first_t, back[c][i], carry[c + 3][i]) for i in range(2)])
            else:
                back = each(lambda v: roll_rows(v, 1), carry)
                ahead_all.append(ahead)
                carry_all.append(carry)
                if r % 2 == 1:
                    for c in range(3):
                        front, rear = [], []
                        for i in range(2):
                            group = [h[j][i] for h in ahead_all[-2:] for j in (c, c + 3)]
                            packed = group[0]
                            for k in range(1, 4):
                                packed = select(x_idx == k, roll_rows(group[k], k), packed)
                            front.append(packed)
                            group = [h[j][i] for h in carry_all[-2:] for j in (c, c + 3)]
                            packed = group[0]
                            for k in range(1, 4):
                                packed = select(x_idx == 3 - k, roll_rows(group[k], -k), packed)
                            rear.append(packed)
                        store_pair(x_back, (r // 2) * 3 + c, front)
                        store_pair(x_ahead, (r // 2) * 3 + c, rear)
            for j in range(6):
                store_pair(kept, (mu * RHS + r) * 6 + j, back[j])


def start_kernel(parity, f_ref, links_ref, *outs):
    send_halos(f_ref, links_ref, parity, outs)


def interior_kernel(parity, with_base, *refs):
    if with_base:
        f_ref, links_ref, base_ref, clover_ref, acc_ref = refs
        clover_to(clover_ref, lambda r: load_field(base_ref, r), acc_ref, 1.0)
    else:
        f_ref, links_ref, acc_ref = refs
    out_parity = 1 - parity
    t_idx, x_idx = site_masks()
    lane = lax.broadcasted_iota(jnp.int32, (8, 128), 1)
    odd = (t_idx + x_idx + lane // HALF_DEPTH + out_parity) % 2
    start = lane - lane % HALF_DEPTH
    up = jnp.where(odd == 1, start + (lane + 1) % HALF_DEPTH, lane)
    down = jnp.where(odd == 0, start + (lane + HALF_DEPTH - 1) % HALF_DEPTH, lane)

    def take(value, index):
        return jnp.take_along_axis(value, index, axis=1, mode="promise_in_bounds")

    for mu in (2, 3):
        if mu == 2:
            ahead_of = lambda v: pltpu.roll(v, 128 - HALF_DEPTH, 1)
            behind_of = lambda v: pltpu.roll(v, HALF_DEPTH, 1)
        else:
            ahead_of = lambda v: take(v, up)
            behind_of = lambda v: take(v, down)
        links_out = load_links(links_ref, mu, out_parity)
        links_in = load_links(links_ref, mu, parity)
        for r in range(RHS):
            field = load_field(f_ref, r)
            if mu == 2 and not with_base:
                zero = jnp.zeros((8, 128), F32)
                acc = [(zero, zero)] * 12
            else:
                acc = load_field(acc_ref, r)
            half = color(links_out, each(ahead_of, project(field, mu, -1)), False)
            acc = rebuild(acc, half, mu, -1)
            half = each(behind_of, color(links_in, project(field, mu, 1), True))
            acc = rebuild(acc, half, mu, 1)
            store_field(acc_ref, r, acc)


def clover_to(clover_ref, get_field, out_ref, scale):
    for chi in range(2):
        matrix = {}
        for i in range(6):
            for j in range(i, 6):
                k = (chi * 6 + i) * 6 + j
                block = clover_ref[k * 16:(k + 1) * 16, :].astype(F32)
                re, im = block[0:8], block[8:16]
                if scale != 1.0:
                    re, im = re * scale, im * scale
                matrix[i, j] = (re, im)
        for r in range(RHS):
            field = get_field(r)[chi * 6:chi * 6 + 6]
            for i in range(6):
                re = im = None
                for j in range(6):
                    vr, vi = field[j]
                    mr, mi = matrix[min(i, j), max(i, j)]
                    if i <= j:
                        tr, ti = mr * vr - mi * vi, mr * vi + mi * vr
                    else:
                        tr, ti = mr * vr + mi * vi, mr * vi - mi * vr
                    re = tr if re is None else re + tr
                    im = ti if im is None else im + ti
                store_pair(out_ref, r * 12 + chi * 6 + i, (re, im))


def join_halos(f_ref, links_ref, acc_ref, halos, parity, out_ref):
    from_next_t, from_last_t, from_next_x, from_last_x, kept = halos
    out_parity = 1 - parity
    t_idx, x_idx = site_masks()
    for mu in range(2):
        links = load_links(links_ref, mu, out_parity)
        for r in range(RHS):
            field = load_field(f_ref, r)
            ahead = project(field, mu, -1)
            behind = [load_pair(kept, (mu * RHS + r) * 6 + j) for j in range(6)]
            new_ahead, new_behind = [None] * 6, [None] * 6
            for c in range(3):
                if mu == 0:
                    nxt = load_pair(from_next_t, r * 3 + c)
                    last = load_pair(from_last_t, r * 3 + c)
                    for s in range(2):
                        j = s * 3 + c
                        new_ahead[j] = tuple(
                            select(t_idx == 1, roll_rows(nxt[i], 4 * s), roll_rows(ahead[j][i], 4)) for i in range(2)
                        )
                        new_behind[j] = tuple(
                            select(t_idx == 0, roll_rows(last[i], 4 * s), behind[j][i]) for i in range(2)
                        )
                else:
                    nxt = load_pair(from_next_x, (r // 2) * 3 + c)
                    last = load_pair(from_last_x, (r // 2) * 3 + c)
                    for s in range(2):
                        j = s * 3 + c
                        k = (r % 2) * 2 + s
                        new_ahead[j] = tuple(
                            select(x_idx == 3, roll_rows(nxt[i], 3 - k), roll_rows(ahead[j][i], 7)) for i in range(2)
                        )
                        new_behind[j] = tuple(
                            select(x_idx == 0, roll_rows(last[i], 5 + k), behind[j][i]) for i in range(2)
                        )
            acc = load_field(acc_ref if mu == 0 else out_ref, r)
            acc = rebuild(acc, color(links, new_ahead, False), mu, -1)
            acc = rebuild(acc, new_behind, mu, 1)
            store_field(out_ref, r, acc)


def odd_kernel(f_ref, links_ref, clover_ref, acc_ref, *refs):
    halos, out_ref, outs, summed = refs[:5], refs[5], refs[6:11], refs[11]
    join_halos(f_ref, links_ref, acc_ref, halos, 0, summed)
    clover_to(clover_ref, lambda r: load_field(summed, r), out_ref, -KAPPA2)
    send_halos(out_ref, links_ref, 1, outs)


def even_kernel(f_ref, links_ref, acc_ref, *refs):
    halos, out_ref, outs = refs[:5], refs[5], refs[6:11]
    join_halos(f_ref, links_ref, acc_ref, halos, 1, out_ref)
    send_halos(out_ref, links_ref, 0, outs)


def last_kernel(f_ref, links_ref, acc_ref, *refs):
    halos, out_ref, summed = refs[:5], refs[5], refs[6]
    join_halos(f_ref, links_ref, acc_ref, halos, 1, summed)
    for r in range(RHS):
        store_field(out_ref, r, load_field(summed, r))


ROWS = RHS * 24 * 8


def call(kernel, args, outs, flops, scratch=()):
    return pl.pallas_call(
        kernel,
        out_shape=tuple(jax.ShapeDtypeStruct(shape, dtype) for shape, dtype in outs),
        in_specs=[pl.BlockSpec(memory_space=pltpu.VMEM)] * len(args),
        out_specs=tuple([pl.BlockSpec(memory_space=pltpu.VMEM)] * len(outs)),
        scratch_shapes=list(scratch),
        compiler_params=pltpu.CompilerParams(vmem_limit_bytes=24 * 1024 * 1024),
        cost_estimate=pl.CostEstimate(flops=flops, bytes_accessed=2 * 1024 * 1024, transcendentals=0),
    )(*args)


HALO_OUTS = [((RHS * 3 * 16, 128), BF16)] * 2 + [((RHS * 3 * 8, 128), BF16)] * 2 + [((2 * RHS * 6 * 16, 128), F32)]
FIELD = [((ROWS, 128), F32)]


def exchange(parts):
    t_back, t_ahead, x_back, x_ahead, kept = parts

    def ring(axis, step):
        count = lax.axis_size(axis)
        return [(i, (i + step) % count) for i in range(count)]

    return (
        lax.ppermute(t_back, "ta", ring("ta", -1)),
        lax.ppermute(t_ahead, "ta", ring("ta", 1)),
        lax.ppermute(x_back, "gx", ring("gx", -1)),
        lax.ppermute(x_ahead, "gx", ring("gx", 1)),
        kept,
    )


def per_device(source, gauge_links, clover_even, clover_odd_inv):
    shape = source.shape
    f = source.reshape(-1, 128)
    links = gauge_links.reshape(-1, 128)
    even = clover_even.reshape(-1, 128)
    odd = clover_odd_inv.reshape(-1, 128)
    parts = call(functools.partial(start_kernel, 0), (f, links), HALO_OUTS, 3_000_000)
    field_scratch = [pltpu.VMEM((ROWS, 128), F32)]
    for step in range(2):
        halos = exchange(parts)
        acc, = call(functools.partial(interior_kernel, 0, False), (f, links), FIELD, 4_000_000)
        g, *parts = call(odd_kernel, (f, links, odd, acc, *halos), FIELD + HALO_OUTS, 6_000_000, field_scratch)
        halos = exchange(parts)
        acc, = call(functools.partial(interior_kernel, 1, True), (g, links, f, even), FIELD, 6_000_000)
        if step == 0:
            f, *parts = call(even_kernel, (g, links, acc, *halos), FIELD + HALO_OUTS, 4_000_000)
        else:
            out, = call(last_kernel, (g, links, acc, *halos), [((ROWS, 128), BF16)], 3_000_000, field_scratch)
    return out.reshape(shape)


def solution(mesh):
    field_spec = P(None, None, None, None, ("groups", "ta"), "gx", None)
    link_spec = P(None, None, None, None, None, ("groups", "ta"), "gx", None)
    return jax.shard_map(
        per_device,
        mesh=mesh,
        in_specs=(field_spec, link_spec, field_spec, field_spec),
        out_specs=field_spec,
        check_vma=False,
    )
```

```python
import functools

import jax
import jax.numpy as jnp
from jax import lax
from jax.experimental import pallas as pl
from jax.experimental.pallas import tpu as pltpu
from jax.sharding import PartitionSpec as P

HALF_DEPTH = 8
KAPPA2 = 0.14 * 0.14
RHS = 4
F32 = jnp.float32
BF16 = jnp.bfloat16

SPIN = (((0, 0), (1, 0)), ((1, 3), (0, 3)), ((1, 2), (0, 0)), ((0, 3), (1, 1)))
SPIN_INV = (((0, 0), (1, 0)), ((1, 1), (0, 1)), ((1, 0), (0, 2)), ((0, 1), (1, 3)))


def add_power(base, value, power):
    (br, bi), (vr, vi) = base, value
    if power == 0:
        return br + vr, bi + vi
    if power == 1:
        return br - vi, bi + vr
    if power == 2:
        return br - vr, bi - vi
    return br + vi, bi - vr


def project(field, mu, sign):
    shift = 0 if sign > 0 else 2
    half = []
    for row in range(2):
        col, power = SPIN[mu][row]
        for c in range(3):
            half.append(add_power(field[row * 3 + c], field[(2 + col) * 3 + c], (power + shift) % 4))
    return half


def rebuild(acc, half, mu, sign):
    shift = 0 if sign > 0 else 2
    out = list(acc)
    for j in range(6):
        out[j] = add_power(out[j], half[j], 0)
    for row in range(2):
        col, power = SPIN_INV[mu][row]
        for c in range(3):
            j = (2 + row) * 3 + c
            out[j] = add_power(out[j], half[col * 3 + c], (power + shift) % 4)
    return out


def color(links, half, adjoint):
    out = []
    for s in range(2):
        for a in range(3):
            re = im = None
            for b in range(3):
                lr, li = links[b][a] if adjoint else links[a][b]
                vr, vi = half[s * 3 + b]
                if adjoint:
                    tr, ti = lr * vr + li * vi, lr * vi - li * vr
                else:
                    tr, ti = lr * vr - li * vi, lr * vi + li * vr
                re = tr if re is None else re + tr
                im = ti if im is None else im + ti
            out.append((re, im))
    return out


def each(function, half):
    return [(function(re), function(im)) for re, im in half]


def load_pair(ref, index):
    block = ref[index * 16:(index + 1) * 16, :].astype(F32)
    return block[0:8], block[8:16]


def load_links(ref, mu, parity):
    links = []
    for a in range(3):
        row = []
        for b in range(3):
            k = ((mu * 3 + a) * 3 + b) * 2
            row.append((load_pair(ref, k)[parity], load_pair(ref, k + 1)[parity]))
        links.append(row)
    return links


def load_field(ref, r):
    return [load_pair(ref, r * 12 + j) for j in range(12)]


def store_pair(ref, index, pair):
    ref[index * 16:(index + 1) * 16, :] = jnp.concatenate(pair, axis=0).astype(ref.dtype)


def store_field(ref, r, field):
    for j in range(12):
        store_pair(ref, r * 12 + j, field[j])


def site_masks():
    rows = lax.broadcasted_iota(jnp.int32, (8, 128), 0)
    return rows // 4, rows % 4


def even_device(axis):
    return lax.broadcast(lax.axis_index(axis) % 2, (8, 128)) == 0


def either(even, a, b):
    return [select(even, a[i], b[i]) for i in range(2)]


def roll_rows(value, shift):
    shift %= 8
    return pltpu.roll(value, shift, 0) if shift else value


def select(mask, a, b):
    return jnp.where(mask, a, b)


def send_halos(f_ref, links_ref, parity, outs):
    t_far, t_near, x_far, x_near, kept = outs
    even_t, even_x = even_device("ta"), even_device("gx")
    t_idx, x_idx = site_masks()
    first_t = t_idx == 0
    for mu in range(2):
        links = load_links(links_ref, mu, parity)
        ahead_all, carry_all = [], []
        for r in range(RHS):
            field = load_field(f_ref, r)
            ahead = project(field, mu, -1)
            carry = color(links, project(field, mu, 1), True)
            if mu == 0:
                moved = each(lambda v: roll_rows(v, 4), ahead)
                back = each(lambda v: roll_rows(v, 4), carry)
                for c in range(3):
                    front = [select(first_t, ahead[c + 3][i], moved[c][i]) for i in range(2)]
                    rear = [select(first_t, back[c][i], carry[c + 3][i]) for i in range(2)]
                    store_pair(t_near, r * 3 + c, either(even_t, rear, front))
                    store_pair(t_far, r * 3 + c, either(even_t, front, rear))
            else:
                back = each(lambda v: roll_rows(v, 1), carry)
                ahead_all.append(ahead)
                carry_all.append(carry)
                if r % 2 == 1:
                    for c in range(3):
                        front, rear = [], []
                        for i in range(2):
                            group = [h[j][i] for h in ahead_all[-2:] for j in (c, c + 3)]
                            packed = group[0]
                            for k in range(1, 4):
                                packed = select(x_idx == k, roll_rows(group[k], k), packed)
                            front.append(packed)
                            group = [h[j][i] for h in carry_all[-2:] for j in (c, c + 3)]
                            packed = group[0]
                            for k in range(1, 4):
                                packed = select(x_idx == 3 - k, roll_rows(group[k], -k), packed)
                            rear.append(packed)
                        store_pair(x_near, (r // 2) * 3 + c, either(even_x, rear, front))
                        store_pair(x_far, (r // 2) * 3 + c, either(even_x, front, rear))
            for j in range(6):
                store_pair(kept, (mu * RHS + r) * 6 + j, back[j])


def start_kernel(f_hbm, links_hbm, *refs):
    outs, (f_ref, links_ref, sems) = refs[:5], refs[5:]
    copies = [
        pltpu.make_async_copy(links_hbm.at[pl.ds(0, links_ref.shape[0])], links_ref, sems.at[0]),
        pltpu.make_async_copy(f_hbm, f_ref, sems.at[1]),
    ]
    for copy in copies:
        copy.start()
    for copy in copies:
        copy.wait()
    send_halos(f_ref, links_ref, 0, outs)


def interior_kernel(parity, with_base, *refs):
    if with_base:
        f_ref, links_ref, base_ref, clover_ref, acc_ref = refs
        clover_to(clover_ref, lambda r: load_field(base_ref, r), acc_ref, 1.0)
    else:
        f_ref, links_ref, acc_ref = refs
    out_parity = 1 - parity
    t_idx, x_idx = site_masks()
    lane = lax.broadcasted_iota(jnp.int32, (8, 128), 1)
    odd = (t_idx + x_idx + lane // HALF_DEPTH + out_parity) % 2
    start = lane - lane % HALF_DEPTH
    up = jnp.where(odd == 1, start + (lane + 1) % HALF_DEPTH, lane)
    down = jnp.where(odd == 0, start + (lane + HALF_DEPTH - 1) % HALF_DEPTH, lane)

    def take(value, index):
        return jnp.take_along_axis(value, index, axis=1, mode="promise_in_bounds")

    for mu in (2, 3):
        if mu == 2:
            ahead_of = lambda v: pltpu.roll(v, 128 - HALF_DEPTH, 1)
            behind_of = lambda v: pltpu.roll(v, HALF_DEPTH, 1)
        else:
            ahead_of = lambda v: take(v, up)
            behind_of = lambda v: take(v, down)
        links_out = load_links(links_ref, mu, out_parity)
        links_in = load_links(links_ref, mu, parity)
        for r in range(RHS):
            field = load_field(f_ref, r)
            if mu == 2 and not with_base:
                zero = jnp.zeros((8, 128), F32)
                acc = [(zero, zero)] * 12
            else:
                acc = load_field(acc_ref, r)
            half = color(links_out, each(ahead_of, project(field, mu, -1)), False)
            acc = rebuild(acc, half, mu, -1)
            half = each(behind_of, color(links_in, project(field, mu, 1), True))
            acc = rebuild(acc, half, mu, 1)
            store_field(acc_ref, r, acc)


def clover_to(clover_ref, get_field, out_ref, scale):
    for chi in range(2):
        matrix = {}
        for i in range(6):
            for j in range(i, 6):
                k = (chi * 6 + i) * 6 + j
                block = clover_ref[k * 16:(k + 1) * 16, :].astype(F32)
                re, im = block[0:8], block[8:16]
                if scale != 1.0:
                    re, im = re * scale, im * scale
                matrix[i, j] = (re, im)
        for r in range(RHS):
            field = get_field(r)[chi * 6:chi * 6 + 6]
            for i in range(6):
                re = im = None
                for j in range(6):
                    vr, vi = field[j]
                    mr, mi = matrix[min(i, j), max(i, j)]
                    if i <= j:
                        tr, ti = mr * vr - mi * vi, mr * vi + mi * vr
                    else:
                        tr, ti = mr * vr + mi * vi, mr * vi - mi * vr
                    re = tr if re is None else re + tr
                    im = ti if im is None else im + ti
                store_pair(out_ref, r * 12 + chi * 6 + i, (re, im))


def join_halos(f_ref, links_ref, acc_ref, halos, parity, out_ref):
    t_far, t_near, x_far, x_near, kept = halos
    even_t, even_x = even_device("ta"), even_device("gx")
    out_parity = 1 - parity
    t_idx, x_idx = site_masks()
    for mu in range(2):
        links = load_links(links_ref, mu, out_parity)
        for r in range(RHS):
            field = load_field(f_ref, r)
            ahead = project(field, mu, -1)
            behind = [load_pair(kept, (mu * RHS + r) * 6 + j) for j in range(6)]
            new_ahead, new_behind = [None] * 6, [None] * 6
            for c in range(3):
                if mu == 0:
                    near, far = load_pair(t_near, r * 3 + c), load_pair(t_far, r * 3 + c)
                    nxt, last = either(even_t, near, far), either(even_t, far, near)
                    for s in range(2):
                        j = s * 3 + c
                        new_ahead[j] = tuple(
                            select(t_idx == 1, roll_rows(nxt[i], 4 * s), roll_rows(ahead[j][i], 4)) for i in range(2)
                        )
                        new_behind[j] = tuple(
                            select(t_idx == 0, roll_rows(last[i], 4 * s), behind[j][i]) for i in range(2)
                        )
                else:
                    near, far = load_pair(x_near, (r // 2) * 3 + c), load_pair(x_far, (r // 2) * 3 + c)
                    nxt, last = either(even_x, near, far), either(even_x, far, near)
                    for s in range(2):
                        j = s * 3 + c
                        k = (r % 2) * 2 + s
                        new_ahead[j] = tuple(
                            select(x_idx == 3, roll_rows(nxt[i], 3 - k), roll_rows(ahead[j][i], 7)) for i in range(2)
                        )
                        new_behind[j] = tuple(
                            select(x_idx == 0, roll_rows(last[i], 5 + k), behind[j][i]) for i in range(2)
                        )
            acc = load_field(acc_ref if mu == 0 else out_ref, r)
            acc = rebuild(acc, color(links, new_ahead, False), mu, -1)
            acc = rebuild(acc, new_behind, mu, 1)
            store_field(out_ref, r, acc)


def odd_kernel(f_ref, links_ref, clover_ref, acc_ref, *refs):
    halos, out_ref, outs, summed = refs[:5], refs[5], refs[6:11], refs[11]
    join_halos(f_ref, links_ref, acc_ref, halos, 0, summed)
    clover_to(clover_ref, lambda r: load_field(summed, r), out_ref, -KAPPA2)
    send_halos(out_ref, links_ref, 1, outs)


def even_kernel(f_ref, links_ref, acc_ref, *refs):
    halos, out_ref, outs = refs[:5], refs[5], refs[6:11]
    join_halos(f_ref, links_ref, acc_ref, halos, 1, out_ref)
    send_halos(out_ref, links_ref, 0, outs)


def last_kernel(f_ref, links_ref, acc_ref, *refs):
    halos, out_ref, summed = refs[:5], refs[5], refs[6]
    join_halos(f_ref, links_ref, acc_ref, halos, 1, summed)
    for r in range(RHS):
        store_field(out_ref, r, load_field(summed, r))


ROWS = RHS * 24 * 8


def call(kernel, args, outs, flops, scratch=(), space=pltpu.VMEM):
    return pl.pallas_call(
        kernel,
        out_shape=tuple(jax.ShapeDtypeStruct(shape, dtype) for shape, dtype in outs),
        in_specs=[pl.BlockSpec(memory_space=space)] * len(args),
        out_specs=tuple([pl.BlockSpec(memory_space=pltpu.VMEM)] * len(outs)),
        scratch_shapes=list(scratch),
        compiler_params=pltpu.CompilerParams(vmem_limit_bytes=24 * 1024 * 1024),
        cost_estimate=pl.CostEstimate(flops=flops, bytes_accessed=2 * 1024 * 1024, transcendentals=0),
    )(*args)


HALO_OUTS = [((RHS * 3 * 16, 128), BF16)] * 2 + [((RHS * 3 * 8, 128), BF16)] * 2 + [((2 * RHS * 6 * 16, 128), F32)]
FIELD = [((ROWS, 128), F32)]


def exchange(parts):
    t_far, t_near, x_far, x_near, kept = parts

    def pairs(axis, far):
        count = lax.axis_size(axis)
        assert count % 2 == 0
        return [(i, (i + (1 if (i % 2 == 0) != far else -1)) % count) for i in range(count)]

    return (
        lax.ppermute(t_far, "ta", pairs("ta", True)),
        lax.ppermute(t_near, "ta", pairs("ta", False)),
        lax.ppermute(x_far, "gx", pairs("gx", True)),
        lax.ppermute(x_near, "gx", pairs("gx", False)),
        kept,
    )


def per_device(source, gauge_links, clover_even, clover_odd_inv):
    shape = source.shape
    f = source.reshape(-1, 128)
    links = gauge_links.reshape(-1, 128)
    even = clover_even.reshape(-1, 128)
    odd = clover_odd_inv.reshape(-1, 128)
    start_scratch = [
        pltpu.VMEM((ROWS, 128), BF16),
        pltpu.VMEM((links.shape[0] // 2, 128), BF16),
        pltpu.SemaphoreType.DMA((2,)),
    ]
    held = [pltpu.with_memory_space_constraint(v, pltpu.HBM) for v in (f, links)]
    parts = call(start_kernel, held, HALO_OUTS, 3_000_000, start_scratch, pltpu.HBM)
    field_scratch = [pltpu.VMEM((ROWS, 128), F32)]
    for step in range(2):
        halos = exchange(parts)
        acc, = call(functools.partial(interior_kernel, 0, False), (f, links), FIELD, 4_000_000)
        g, *parts = call(odd_kernel, (f, links, odd, acc, *halos), FIELD + HALO_OUTS, 6_000_000, field_scratch)
        halos = exchange(parts)
        acc, = call(functools.partial(interior_kernel, 1, True), (g, links, f, even), FIELD, 6_000_000)
        if step == 0:
            f, *parts = call(even_kernel, (g, links, acc, *halos), FIELD + HALO_OUTS, 4_000_000)
        else:
            out, = call(last_kernel, (g, links, acc, *halos), [((ROWS, 128), BF16)], 3_000_000, field_scratch)
    return out.reshape(shape)


def solution(mesh):
    field_spec = P(None, None, None, None, ("groups", "ta"), "gx", None)
    link_spec = P(None, None, None, None, None, ("groups", "ta"), "gx", None)
    return jax.shard_map(
        per_device,
        mesh=mesh,
        in_specs=(field_spec, link_spec, field_spec, field_spec),
        out_specs=field_spec,
        check_vma=False,
    )
```

```python
import functools

import jax
import jax.numpy as jnp
from jax import lax
from jax.experimental import pallas as pl
from jax.experimental.pallas import tpu as pltpu
from jax.sharding import PartitionSpec as P

HALF_DEPTH = 8
KAPPA2 = 0.14 * 0.14
RHS = 4
F32 = jnp.float32
BF16 = jnp.bfloat16

SPIN = (((0, 0), (1, 0)), ((1, 3), (0, 3)), ((1, 2), (0, 0)), ((0, 3), (1, 1)))
SPIN_INV = (((0, 0), (1, 0)), ((1, 1), (0, 1)), ((1, 0), (0, 2)), ((0, 1), (1, 3)))


def add_power(base, value, power):
    (br, bi), (vr, vi) = base, value
    if power == 0:
        return br + vr, bi + vi
    if power == 1:
        return br - vi, bi + vr
    if power == 2:
        return br - vr, bi - vi
    return br + vi, bi - vr


def project(field, mu, sign):
    shift = 0 if sign > 0 else 2
    half = []
    for row in range(2):
        col, power = SPIN[mu][row]
        for c in range(3):
            half.append(add_power(field[row * 3 + c], field[(2 + col) * 3 + c], (power + shift) % 4))
    return half


def rebuild(acc, half, mu, sign):
    shift = 0 if sign > 0 else 2
    out = list(acc)
    for j in range(6):
        out[j] = add_power(out[j], half[j], 0)
    for row in range(2):
        col, power = SPIN_INV[mu][row]
        for c in range(3):
            j = (2 + row) * 3 + c
            out[j] = add_power(out[j], half[col * 3 + c], (power + shift) % 4)
    return out


def color(links, half, adjoint):
    out = []
    for s in range(2):
        for a in range(3):
            re = im = None
            for b in range(3):
                lr, li = links[b][a] if adjoint else links[a][b]
                vr, vi = half[s * 3 + b]
                if adjoint:
                    tr, ti = lr * vr + li * vi, lr * vi - li * vr
                else:
                    tr, ti = lr * vr - li * vi, lr * vi + li * vr
                re = tr if re is None else re + tr
                im = ti if im is None else im + ti
            out.append((re, im))
    return out


def each(function, half):
    return [(function(re), function(im)) for re, im in half]


def load_pair(ref, index):
    block = ref[index * 16:(index + 1) * 16, :].astype(F32)
    return block[0:8], block[8:16]


def load_links(ref, mu, parity):
    links = []
    for a in range(3):
        row = []
        for b in range(3):
            k = ((mu * 3 + a) * 3 + b) * 2
            row.append((load_pair(ref, k)[parity], load_pair(ref, k + 1)[parity]))
        links.append(row)
    return links


def load_field(ref, r):
    return [load_pair(ref, r * 12 + j) for j in range(12)]


def store_pair(ref, index, pair):
    ref[index * 16:(index + 1) * 16, :] = jnp.concatenate(pair, axis=0).astype(ref.dtype)


def store_field(ref, r, field):
    for j in range(12):
        store_pair(ref, r * 12 + j, field[j])


def site_masks():
    rows = lax.broadcasted_iota(jnp.int32, (8, 128), 0)
    return rows // 4, rows % 4


def even_device(axis):
    return lax.broadcast(lax.axis_index(axis) % 2, (8, 128)) == 0


def either(even, a, b):
    return [select(even, a[i], b[i]) for i in range(2)]


def roll_rows(value, shift):
    shift %= 8
    return pltpu.roll(value, shift, 0) if shift else value


def select(mask, a, b):
    return jnp.where(mask, a, b)


def send_t(f_ref, links_ref, parity, t_far, t_near, kept, ready=lambda r: None):
    even = even_device("ta")
    t_idx, _ = site_masks()
    first = t_idx == 0
    links = load_links(links_ref, 0, parity)
    for r in range(RHS):
        ready(r)
        field = load_field(f_ref, r)
        ahead = project(field, 0, -1)
        carry = color(links, project(field, 0, 1), True)
        moved = each(lambda v: roll_rows(v, 4), ahead)
        back = each(lambda v: roll_rows(v, 4), carry)
        for c in range(3):
            front = [select(first, ahead[c + 3][i], moved[c][i]) for i in range(2)]
            rear = [select(first, back[c][i], carry[c + 3][i]) for i in range(2)]
            store_pair(t_near, r * 3 + c, either(even, rear, front))
            store_pair(t_far, r * 3 + c, either(even, front, rear))
        for j in range(6):
            store_pair(kept, r * 6 + j, back[j])


def send_x_kernel(parity, f_ref, links_ref, x_far, x_near, kept):
    even = even_device("gx")
    _, x_idx = site_masks()
    links = load_links(links_ref, 1, parity)
    for q in range(RHS // 2):
        fronts, rears = [], []
        for r in (2 * q, 2 * q + 1):
            field = load_field(f_ref, r)
            fronts.append(project(field, 1, -1))
            rears.append(color(links, project(field, 1, 1), True))
            for j in range(6):
                store_pair(kept, r * 6 + j, [roll_rows(v, 1) for v in rears[-1][j]])
        for c in range(3):
            front, rear = [], []
            for i in range(2):
                group = [h[j][i] for h in fronts for j in (c, c + 3)]
                packed = group[0]
                for k in range(1, 4):
                    packed = select(x_idx == k, roll_rows(group[k], k), packed)
                front.append(packed)
                group = [h[j][i] for h in rears for j in (c, c + 3)]
                packed = group[0]
                for k in range(1, 4):
                    packed = select(x_idx == 3 - k, roll_rows(group[k], -k), packed)
                rear.append(packed)
            store_pair(x_near, q * 3 + c, either(even, rear, front))
            store_pair(x_far, q * 3 + c, either(even, front, rear))


def start_kernel(f_hbm, links_hbm, *refs):
    outs, (f_ref, links_ref, sems) = refs[:3], refs[3:]
    part = f_ref.shape[0] // RHS
    copies = [pltpu.make_async_copy(links_hbm.at[pl.ds(0, links_ref.shape[0])], links_ref, sems.at[RHS])]
    for r in range(RHS):
        rows = pl.ds(r * part, part)
        copies.append(pltpu.make_async_copy(f_hbm.at[rows], f_ref.at[rows], sems.at[r]))
    for copy in copies:
        copy.start()
    copies[0].wait()
    send_t(f_ref, links_ref, 0, *outs, ready=lambda r: copies[1 + r].wait())


def interior_kernel(parity, with_base, *refs):
    if with_base:
        f_ref, links_ref, kept_t, kept_x, base_ref, clover_ref, acc_ref = refs
        clover_to(clover_ref, lambda r: load_field(base_ref, r), acc_ref, 1.0)
    else:
        f_ref, links_ref, kept_t, kept_x, acc_ref = refs
    out_parity = 1 - parity
    t_idx, x_idx = site_masks()
    lane = lax.broadcasted_iota(jnp.int32, (8, 128), 1)
    odd = (t_idx + x_idx + lane // HALF_DEPTH + out_parity) % 2
    start = lane - lane % HALF_DEPTH
    up = jnp.where(odd == 1, start + (lane + 1) % HALF_DEPTH, lane)
    down = jnp.where(odd == 0, start + (lane + HALF_DEPTH - 1) % HALF_DEPTH, lane)
    zero = jnp.zeros((8, 128), F32)

    def take(value, index):
        return jnp.take_along_axis(value, index, axis=1, mode="promise_in_bounds")

    for mu in (2, 3, 0, 1):
        if mu == 2:
            ahead_of = lambda v: pltpu.roll(v, 128 - HALF_DEPTH, 1)
            behind_of = lambda v: pltpu.roll(v, HALF_DEPTH, 1)
        elif mu == 3:
            ahead_of = lambda v: take(v, up)
            behind_of = lambda v: take(v, down)
        elif mu == 0:
            ahead_of = lambda v: select(t_idx == 0, roll_rows(v, 4), 0.0)
            behind_of = lambda v: select(t_idx == 1, v, 0.0)
        else:
            ahead_of = lambda v: select(x_idx < 3, roll_rows(v, 7), 0.0)
            behind_of = lambda v: select(x_idx > 0, v, 0.0)
        links_out = load_links(links_ref, mu, out_parity)
        if mu >= 2:
            links_in = load_links(links_ref, mu, parity)
        for r in range(RHS):
            field = load_field(f_ref, r)
            if mu == 2 and not with_base:
                acc = [(zero, zero)] * 12
            else:
                acc = load_field(acc_ref, r)
            half = color(links_out, each(ahead_of, project(field, mu, -1)), False)
            acc = rebuild(acc, half, mu, -1)
            if mu >= 2:
                half = color(links_in, project(field, mu, 1), True)
            else:
                half = [load_pair(kept_t if mu == 0 else kept_x, r * 6 + j) for j in range(6)]
            acc = rebuild(acc, each(behind_of, half), mu, 1)
            store_field(acc_ref, r, acc)


def clover_to(clover_ref, get_field, out_ref, scale):
    for chi in range(2):
        matrix = {}
        for i in range(6):
            for j in range(i, 6):
                k = (chi * 6 + i) * 6 + j
                block = clover_ref[k * 16:(k + 1) * 16, :].astype(F32)
                re, im = block[0:8], block[8:16]
                if scale != 1.0:
                    re, im = re * scale, im * scale
                matrix[i, j] = (re, im)
        for r in range(RHS):
            field = get_field(r)[chi * 6:chi * 6 + 6]
            for i in range(6):
                re = im = None
                for j in range(6):
                    vr, vi = field[j]
                    mr, mi = matrix[min(i, j), max(i, j)]
                    if i <= j:
                        tr, ti = mr * vr - mi * vi, mr * vi + mi * vr
                    else:
                        tr, ti = mr * vr + mi * vi, mr * vi - mi * vr
                    re = tr if re is None else re + tr
                    im = ti if im is None else im + ti
                store_pair(out_ref, r * 12 + chi * 6 + i, (re, im))


def matvec(links, vector):
    out = []
    for a in range(3):
        re = im = None
        for b in range(3):
            (lr, li), (vr, vi) = links[a][b], vector[b]
            tr, ti = lr * vr - li * vi, lr * vi + li * vr
            re = tr if re is None else re + tr
            im = ti if im is None else im + ti
        out.append((re, im))
    return out


def rebuild_signed(acc, half, mu, sign):
    out = list(acc)
    for j in range(6):
        out[j] = add_power(out[j], half[j], 0)
    half = each(lambda v: v * sign, half)
    for row in range(2):
        col, power = SPIN_INV[mu][row]
        for c in range(3):
            j = (2 + row) * 3 + c
            out[j] = add_power(out[j], half[col * 3 + c], power)
    return out


def join_x_kernel(parity, links_ref, acc_ref, x_far, x_near, out_ref):
    even = even_device("gx")
    _, x_idx = site_masks()
    sign = jnp.where(x_idx == 3, -1.0, 1.0).astype(F32)
    links = load_links(links_ref, 1, 1 - parity)

    def edge(value):
        for k in range(3):
            value = select(x_idx == k, roll_rows(value, k - 3), value)
        return value

    links = [each(edge, row) for row in links]
    for q in range(RHS // 2):
        nxt, last = [], []
        for c in range(3):
            near, far = load_pair(x_near, q * 3 + c), load_pair(x_far, q * 3 + c)
            nxt.append(either(even, near, far))
            last.append(either(even, far, near))
        ahead = matvec(links, nxt)
        for r in (2 * q, 2 * q + 1):
            half = [None] * 6
            for s in range(2):
                k = (r % 2) * 2 + s
                for c in range(3):
                    half[s * 3 + c] = tuple(
                        select(
                            x_idx == 3,
                            roll_rows(ahead[c][i], 3 - k),
                            select(x_idx == 0, roll_rows(last[c][i], 5 + k), 0.0),
                        )
                        for i in range(2)
                    )
            store_field(out_ref, r, rebuild_signed(load_field(acc_ref, r), half, 1, sign))


def join_t(links_ref, acc_ref, t_far, t_near, parity, out_ref, done=lambda r: None):
    even = even_device("ta")
    t_idx, _ = site_masks()
    first = t_idx == 0
    sign = jnp.where(first, 1.0, -1.0).astype(F32)
    links = load_links(links_ref, 0, 1 - parity)
    links = [each(lambda v: select(first, roll_rows(v, 4), v), row) for row in links]
    for r in range(RHS):
        nxt, last = [], []
        for c in range(3):
            near, far = load_pair(t_near, r * 3 + c), load_pair(t_far, r * 3 + c)
            nxt.append(either(even, near, far))
            last.append(either(even, far, near))
        ahead = matvec(links, nxt)
        half = [tuple(select(first, last[c][i], ahead[c][i]) for i in range(2)) for c in range(3)]
        half += [
            tuple(roll_rows(select(first, ahead[c][i], last[c][i]), 4) for i in range(2)) for c in range(3)
        ]
        store_field(out_ref, r, rebuild_signed(load_field(acc_ref, r), half, 0, sign))
        done(r)


def odd_kernel(links_ref, clover_ref, acc_ref, t_far, t_near, out_ref, *refs):
    outs, summed = refs[:3], refs[3]
    join_t(links_ref, acc_ref, t_far, t_near, 0, summed)
    clover_to(clover_ref, lambda r: load_field(summed, r), out_ref, -KAPPA2)
    send_t(out_ref, links_ref, 1, *outs)


def even_kernel(links_ref, acc_ref, t_far, t_near, out_ref, *outs):
    join_t(links_ref, acc_ref, t_far, t_near, 1, out_ref)
    send_t(out_ref, links_ref, 0, *outs)


def last_kernel(links_ref, acc_ref, t_far, t_near, out_hbm, held, sems):
    part = held.shape[0] // RHS
    copies = []

    def done(r):
        rows = pl.ds(r * part, part)
        copies.append(pltpu.make_async_copy(held.at[rows], out_hbm.at[rows], sems.at[r]))
        copies[-1].start()

    join_t(links_ref, acc_ref, t_far, t_near, 1, held, done)
    for copy in copies:
        copy.wait()


ROWS = RHS * 24 * 8
FIELD = [((ROWS, 128), F32)]
KEPT = [((RHS * 12 * 8, 128), F32)]
T_HALOS = [((RHS * 3 * 16, 128), BF16)] * 2
X_HALOS = [((RHS * 3 * 8, 128), BF16)] * 2


def call(kernel, args, outs, flops, scratch=(), in_space=pltpu.VMEM, out_space=pltpu.VMEM):
    return pl.pallas_call(
        kernel,
        out_shape=tuple(jax.ShapeDtypeStruct(shape, dtype) for shape, dtype in outs),
        in_specs=[pl.BlockSpec(memory_space=in_space)] * len(args),
        out_specs=tuple([pl.BlockSpec(memory_space=out_space)] * len(outs)),
        scratch_shapes=list(scratch),
        compiler_params=pltpu.CompilerParams(vmem_limit_bytes=24 * 1024 * 1024),
        cost_estimate=pl.CostEstimate(flops=flops, bytes_accessed=2 * 1024 * 1024, transcendentals=0),
    )(*args)


def swap(value, axis, far):
    count = lax.axis_size(axis)
    assert count % 2 == 0
    pairs = [(i, (i + (1 if (i % 2 == 0) != far else -1)) % count) for i in range(count)]
    return lax.ppermute(value, axis, pairs)


def per_device(source, gauge_links, clover_even, clover_odd_inv):
    shape = source.shape
    f = source.reshape(-1, 128)
    links = gauge_links.reshape(-1, 128)
    even = clover_even.reshape(-1, 128)
    odd = clover_odd_inv.reshape(-1, 128)
    held = [pltpu.with_memory_space_constraint(v, pltpu.HBM) for v in (f, links)]
    start_scratch = [
        pltpu.VMEM((ROWS, 128), BF16),
        pltpu.VMEM((links.shape[0] // 4, 128), BF16),
        pltpu.SemaphoreType.DMA((RHS + 1,)),
    ]
    t_far, t_near, kept_t = call(start_kernel, held, T_HALOS + KEPT, 1_500_000, start_scratch, in_space=pltpu.HBM)
    for hop in range(4):
        parity = hop % 2
        t_far, t_near = swap(t_far, "ta", True), swap(t_near, "ta", False)
        x_far, x_near, kept_x = call(
            functools.partial(send_x_kernel, parity), (f, links), X_HALOS + KEPT, 1_500_000
        )
        x_far, x_near = swap(x_far, "gx", True), swap(x_near, "gx", False)
        base = (before, even) if parity else ()
        acc, = call(
            functools.partial(interior_kernel, parity, bool(parity)),
            (f, links, kept_t, kept_x, *base), FIELD, 8_000_000 if parity else 5_000_000,
        )
        acc, = call(functools.partial(join_x_kernel, parity), (links, acc, x_far, x_near), FIELD, 1_000_000)
        before = f
        if parity == 0:
            f, t_far, t_near, kept_t = call(
                odd_kernel, (links, odd, acc, t_far, t_near), FIELD + T_HALOS + KEPT, 4_000_000,
                [pltpu.VMEM((ROWS, 128), F32)],
            )
        elif hop == 1:
            f, t_far, t_near, kept_t = call(
                even_kernel, (links, acc, t_far, t_near), FIELD + T_HALOS + KEPT, 2_000_000
            )
        else:
            out, = call(
                last_kernel, (links, acc, t_far, t_near), [((ROWS, 128), BF16)], 1_000_000,
                [pltpu.VMEM((ROWS, 128), BF16), pltpu.SemaphoreType.DMA((RHS,))], out_space=pltpu.HBM,
            )
    return out.reshape(shape)


def solution(mesh):
    field_spec = P(None, None, None, None, ("groups", "ta"), "gx", None)
    link_spec = P(None, None, None, None, None, ("groups", "ta"), "gx", None)
    return jax.shard_map(
        per_device,
        mesh=mesh,
        in_specs=(field_spec, link_spec, field_spec, field_spec),
        out_specs=field_spec,
        check_vma=False,
    )
```

```python
import functools

import jax
import jax.numpy as jnp
from jax import lax
from jax.experimental import pallas as pl
from jax.experimental.pallas import tpu as pltpu
from jax.sharding import PartitionSpec as P

HALF_DEPTH = 8
KAPPA2 = 0.14 * 0.14
RHS = 4
F32 = jnp.float32
BF16 = jnp.bfloat16

SPIN = (((0, 0), (1, 0)), ((1, 3), (0, 3)), ((1, 2), (0, 0)), ((0, 3), (1, 1)))
SPIN_INV = (((0, 0), (1, 0)), ((1, 1), (0, 1)), ((1, 0), (0, 2)), ((0, 1), (1, 3)))


def add_power(base, value, power):
    (br, bi), (vr, vi) = base, value
    if power == 0:
        return br + vr, bi + vi
    if power == 1:
        return br - vi, bi + vr
    if power == 2:
        return br - vr, bi - vi
    return br + vi, bi - vr


def project(field, mu, sign):
    shift = 0 if sign > 0 else 2
    half = []
    for row in range(2):
        col, power = SPIN[mu][row]
        for c in range(3):
            half.append(add_power(field[row * 3 + c], field[(2 + col) * 3 + c], (power + shift) % 4))
    return half


def rebuild(acc, half, mu, sign):
    shift = 0 if sign > 0 else 2
    out = list(acc)
    for j in range(6):
        out[j] = add_power(out[j], half[j], 0)
    for row in range(2):
        col, power = SPIN_INV[mu][row]
        for c in range(3):
            j = (2 + row) * 3 + c
            out[j] = add_power(out[j], half[col * 3 + c], (power + shift) % 4)
    return out


def color(links, half, adjoint):
    out = []
    for s in range(2):
        for a in range(3):
            re = im = None
            for b in range(3):
                lr, li = links[b][a] if adjoint else links[a][b]
                vr, vi = half[s * 3 + b]
                if adjoint:
                    tr, ti = lr * vr + li * vi, lr * vi - li * vr
                else:
                    tr, ti = lr * vr - li * vi, lr * vi + li * vr
                re = tr if re is None else re + tr
                im = ti if im is None else im + ti
            out.append((re, im))
    return out


def each(function, half):
    return [(function(re), function(im)) for re, im in half]


def load_pair(ref, index):
    block = ref[index * 16:(index + 1) * 16, :].astype(F32)
    return block[0:8], block[8:16]


def load_links(ref, mu, parity):
    links = []
    for a in range(3):
        row = []
        for b in range(3):
            k = ((mu * 3 + a) * 3 + b) * 2
            row.append((load_pair(ref, k)[parity], load_pair(ref, k + 1)[parity]))
        links.append(row)
    return links


def load_field(ref, r):
    return [load_pair(ref, r * 12 + j) for j in range(12)]


def store_pair(ref, index, pair):
    ref[index * 16:(index + 1) * 16, :] = jnp.concatenate(pair, axis=0).astype(ref.dtype)


def store_field(ref, r, field):
    for j in range(12):
        store_pair(ref, r * 12 + j, field[j])


def site_masks():
    rows = lax.broadcasted_iota(jnp.int32, (8, 128), 0)
    return rows // 4, rows % 4


def even_device(axis):
    return lax.broadcast(lax.axis_index(axis) % 2, (8, 128)) == 0


def either(even, a, b):
    if isinstance(even, bool):
        return a if even else b
    return [select(even, a[i], b[i]) for i in range(2)]


def roll_rows(value, shift):
    shift %= 8
    return pltpu.roll(value, shift, 0) if shift else value


def select(mask, a, b):
    return jnp.where(mask, a, b)


def send_t(f_ref, links_ref, parity, even, t_far, t_near, kept, ready=lambda r: None):
    t_idx, _ = site_masks()
    first = t_idx == 0
    links = load_links(links_ref, 0, parity)
    for r in range(RHS):
        ready(r)
        field = load_field(f_ref, r)
        ahead = project(field, 0, -1)
        carry = color(links, project(field, 0, 1), True)
        moved = each(lambda v: roll_rows(v, 4), ahead)
        back = each(lambda v: roll_rows(v, 4), carry)
        for c in range(3):
            front = [select(first, ahead[c + 3][i], moved[c][i]) for i in range(2)]
            rear = [select(first, back[c][i], carry[c + 3][i]) for i in range(2)]
            store_pair(t_near, r * 3 + c, either(even, rear, front))
            store_pair(t_far, r * 3 + c, either(even, front, rear))
        for j in range(6):
            store_pair(kept, r * 6 + j, back[j])


def send_x_kernel(parity, f_ref, links_ref, x_far, x_near, kept):
    even = even_device("gx")
    _, x_idx = site_masks()
    links = load_links(links_ref, 1, parity)
    for q in range(RHS // 2):
        fronts, rears = [], []
        for r in (2 * q, 2 * q + 1):
            field = load_field(f_ref, r)
            fronts.append(project(field, 1, -1))
            rears.append(color(links, project(field, 1, 1), True))
            for j in range(6):
                store_pair(kept, r * 6 + j, [roll_rows(v, 1) for v in rears[-1][j]])
        for c in range(3):
            front, rear = [], []
            for i in range(2):
                group = [h[j][i] for h in fronts for j in (c, c + 3)]
                packed = group[0]
                for k in range(1, 4):
                    packed = select(x_idx == k, roll_rows(group[k], k), packed)
                front.append(packed)
                group = [h[j][i] for h in rears for j in (c, c + 3)]
                packed = group[0]
                for k in range(1, 4):
                    packed = select(x_idx == 3 - k, roll_rows(group[k], -k), packed)
                rear.append(packed)
            store_pair(x_near, q * 3 + c, either(even, rear, front))
            store_pair(x_far, q * 3 + c, either(even, front, rear))


def start_kernel(f_hbm, links_hbm, *refs):
    outs, (f_ref, links_ref, sems) = refs[:3], refs[3:]
    part = f_ref.shape[0] // RHS
    copies = [pltpu.make_async_copy(links_hbm.at[pl.ds(0, links_ref.shape[0])], links_ref, sems.at[RHS])]
    for r in range(RHS):
        rows = pl.ds(r * part, part)
        copies.append(pltpu.make_async_copy(f_hbm.at[rows], f_ref.at[rows], sems.at[r]))
    for copy in copies:
        copy.start()
    copies[0].wait()
    send_t(f_ref, links_ref, 0, even_device("ta"), *outs, ready=lambda r: copies[1 + r].wait())


def interior_kernel(parity, with_base, *refs):
    if with_base:
        f_ref, links_ref, kept_t, kept_x, base_ref, clover_ref, acc_ref = refs
        clover_to(clover_ref, lambda r: load_field(base_ref, r), acc_ref, 1.0)
    else:
        f_ref, links_ref, kept_t, kept_x, acc_ref = refs
    out_parity = 1 - parity
    t_idx, x_idx = site_masks()
    lane = lax.broadcasted_iota(jnp.int32, (8, 128), 1)
    odd = (t_idx + x_idx + lane // HALF_DEPTH + out_parity) % 2
    start = lane - lane % HALF_DEPTH
    up = jnp.where(odd == 1, start + (lane + 1) % HALF_DEPTH, lane)
    down = jnp.where(odd == 0, start + (lane + HALF_DEPTH - 1) % HALF_DEPTH, lane)
    zero = jnp.zeros((8, 128), F32)

    def take(value, index):
        return jnp.take_along_axis(value, index, axis=1, mode="promise_in_bounds")

    for mu in (2, 3, 0, 1):
        if mu == 2:
            ahead_of = lambda v: pltpu.roll(v, 128 - HALF_DEPTH, 1)
            behind_of = lambda v: pltpu.roll(v, HALF_DEPTH, 1)
        elif mu == 3:
            ahead_of = lambda v: take(v, up)
            behind_of = lambda v: take(v, down)
        elif mu == 0:
            ahead_of = lambda v: select(t_idx == 0, roll_rows(v, 4), 0.0)
            behind_of = lambda v: select(t_idx == 1, v, 0.0)
        else:
            ahead_of = lambda v: select(x_idx < 3, roll_rows(v, 7), 0.0)
            behind_of = lambda v: select(x_idx > 0, v, 0.0)
        links_out = load_links(links_ref, mu, out_parity)
        if mu >= 2:
            links_in = load_links(links_ref, mu, parity)
        for r in range(RHS):
            field = load_field(f_ref, r)
            if mu == 2 and not with_base:
                acc = [(zero, zero)] * 12
            else:
                acc = load_field(acc_ref, r)
            half = color(links_out, each(ahead_of, project(field, mu, -1)), False)
            acc = rebuild(acc, half, mu, -1)
            if mu >= 2:
                half = color(links_in, project(field, mu, 1), True)
            else:
                half = [load_pair(kept_t if mu == 0 else kept_x, r * 6 + j) for j in range(6)]
            acc = rebuild(acc, each(behind_of, half), mu, 1)
            store_field(acc_ref, r, acc)


def clover_to(clover_ref, get_field, out_ref, scale):
    for chi in range(2):
        matrix = {}
        for i in range(6):
            for j in range(i, 6):
                k = (chi * 6 + i) * 6 + j
                block = clover_ref[k * 16:(k + 1) * 16, :].astype(F32)
                re, im = block[0:8], block[8:16]
                if scale != 1.0:
                    re, im = re * scale, im * scale
                matrix[i, j] = (re, im)
        for r in range(RHS):
            field = get_field(r)[chi * 6:chi * 6 + 6]
            for i in range(6):
                re = im = None
                for j in range(6):
                    vr, vi = field[j]
                    mr, mi = matrix[min(i, j), max(i, j)]
                    if i <= j:
                        tr, ti = mr * vr - mi * vi, mr * vi + mi * vr
                    else:
                        tr, ti = mr * vr + mi * vi, mr * vi - mi * vr
                    re = tr if re is None else re + tr
                    im = ti if im is None else im + ti
                store_pair(out_ref, r * 12 + chi * 6 + i, (re, im))


def matvec(links, vector):
    out = []
    for a in range(3):
        re = im = None
        for b in range(3):
            (lr, li), (vr, vi) = links[a][b], vector[b]
            tr, ti = lr * vr - li * vi, lr * vi + li * vr
            re = tr if re is None else re + tr
            im = ti if im is None else im + ti
        out.append((re, im))
    return out


def rebuild_signed(acc, half, mu, sign):
    out = list(acc)
    for j in range(6):
        out[j] = add_power(out[j], half[j], 0)
    half = each(lambda v: v * sign, half)
    for row in range(2):
        col, power = SPIN_INV[mu][row]
        for c in range(3):
            j = (2 + row) * 3 + c
            out[j] = add_power(out[j], half[col * 3 + c], power)
    return out


def join_x_kernel(parity, links_ref, acc_ref, x_far, x_near, out_ref):
    even = even_device("gx")
    _, x_idx = site_masks()
    sign = jnp.where(x_idx == 3, -1.0, 1.0).astype(F32)
    links = load_links(links_ref, 1, 1 - parity)

    def edge(value):
        for k in range(3):
            value = select(x_idx == k, roll_rows(value, k - 3), value)
        return value

    links = [each(edge, row) for row in links]
    part = x_near.shape[0] // 2
    x_near = x_near.at[pl.ds(pl.multiple_of((1 - lax.axis_index("gx") % 2) * part, part), part)]
    for q in range(RHS // 2):
        nxt, last = [], []
        for c in range(3):
            near, far = load_pair(x_near, q * 3 + c), load_pair(x_far, q * 3 + c)
            nxt.append(either(even, near, far))
            last.append(either(even, far, near))
        ahead = matvec(links, nxt)
        for r in (2 * q, 2 * q + 1):
            half = [None] * 6
            for s in range(2):
                k = (r % 2) * 2 + s
                for c in range(3):
                    half[s * 3 + c] = tuple(
                        select(
                            x_idx == 3,
                            roll_rows(ahead[c][i], 3 - k),
                            select(x_idx == 0, roll_rows(last[c][i], 5 + k), 0.0),
                        )
                        for i in range(2)
                    )
            store_field(out_ref, r, rebuild_signed(load_field(acc_ref, r), half, 1, sign))


def join_t(links_ref, acc_ref, t_far, t_near, parity, even, out_ref, done=lambda r: None):
    t_idx, _ = site_masks()
    first = t_idx == 0
    sign = jnp.where(first, 1.0, -1.0).astype(F32)
    links = load_links(links_ref, 0, 1 - parity)
    links = [each(lambda v: select(first, roll_rows(v, 4), v), row) for row in links]
    for r in range(RHS):
        nxt, last = [], []
        for c in range(3):
            near, far = load_pair(t_near, r * 3 + c), load_pair(t_far, r * 3 + c)
            nxt.append(either(even, near, far))
            last.append(either(even, far, near))
        ahead = matvec(links, nxt)
        half = [tuple(select(first, last[c][i], ahead[c][i]) for i in range(2)) for c in range(3)]
        half += [
            tuple(roll_rows(select(first, ahead[c][i], last[c][i]), 4) for i in range(2)) for c in range(3)
        ]
        store_field(out_ref, r, rebuild_signed(load_field(acc_ref, r), half, 0, sign))
        done(r)


def for_class(even, body):
    pl.when(lax.axis_index("ta") % 2 == (0 if even else 1))(body)


def odd_kernel(even, links_ref, clover_ref, acc_ref, t_far, t_near, *refs):
    out_ref, kept, far_out, near_out, summed = refs[-5:]

    @functools.partial(for_class, even)
    def body():
        join_t(links_ref, acc_ref, t_far, t_near, 0, even, summed)
        clover_to(clover_ref, lambda r: load_field(summed, r), out_ref, -KAPPA2)
        send_t(out_ref, links_ref, 1, even, far_out, near_out, kept)


def even_kernel(even, links_ref, acc_ref, t_far, t_near, *refs):
    out_ref, kept, far_out, near_out = refs[-4:]

    @functools.partial(for_class, even)
    def body():
        join_t(links_ref, acc_ref, t_far, t_near, 1, even, out_ref)
        send_t(out_ref, links_ref, 0, even, far_out, near_out, kept)


def last_kernel(even, links_ref, acc_ref, t_far, t_near, *refs):
    out_hbm, held, sems = refs[-3:]
    part = held.shape[0] // RHS

    @functools.partial(for_class, even)
    def body():
        copies = []

        def done(r):
            rows = pl.ds(r * part, part)
            copies.append(pltpu.make_async_copy(held.at[rows], out_hbm.at[rows], sems.at[r]))
            copies[-1].start()

        join_t(links_ref, acc_ref, t_far, t_near, 1, even, held, done)
        for copy in copies:
            copy.wait()


ROWS = RHS * 24 * 8
FIELD = [((ROWS, 128), F32)]
KEPT = [((RHS * 12 * 8, 128), F32)]
T_HALOS = [((RHS * 3 * 16, 128), BF16)] * 2
X_HALOS = [((RHS * 3 * 8, 128), BF16)] * 2


def call(kernel, args, outs, flops, scratch=(), in_space=pltpu.VMEM, out_space=pltpu.VMEM, kept=()):
    return pl.pallas_call(
        kernel,
        out_shape=tuple(jax.ShapeDtypeStruct(shape, dtype) for shape, dtype in outs),
        in_specs=[pl.BlockSpec(memory_space=in_space)] * len(args) + [pl.BlockSpec(memory_space=pl.ANY)] * len(kept),
        out_specs=tuple([pl.BlockSpec(memory_space=out_space)] * len(outs)),
        scratch_shapes=list(scratch),
        input_output_aliases={len(args) + i: i for i in range(len(kept))},
        compiler_params=pltpu.CompilerParams(vmem_limit_bytes=24 * 1024 * 1024),
        cost_estimate=pl.CostEstimate(flops=flops, bytes_accessed=flops // 1000, transcendentals=0),
    )(*args, *kept)


def ring_pairs(axis, far):
    count = lax.axis_size(axis)
    assert count % 2 == 0
    return [(i, (i + (1 if (i % 2 == 0) != far else -1)) % count) for i in range(count)]


def swap(value, axis, far):
    return lax.ppermute(value, axis, ring_pairs(axis, far))


def both(value, axis):
    pairs = [[i, i + 1] for i in range(0, lax.axis_size(axis), 2)]
    return lax.all_gather(value, axis, axis_index_groups=pairs, axis=0, tiled=True)


def send(value, axis, far, even):
    return lax.ppermute(value, axis, [p for p in ring_pairs(axis, far) if (p[0] % 2 == 0) == even])


def per_device(source, gauge_links, clover_even, clover_odd_inv):
    shape = source.shape
    f = source.reshape(-1, 128)
    links = gauge_links.reshape(-1, 128)
    even = clover_even.reshape(-1, 128)
    odd = clover_odd_inv.reshape(-1, 128)
    held = [pltpu.with_memory_space_constraint(v, pltpu.HBM) for v in (f, links)]
    start_scratch = [
        pltpu.VMEM((ROWS, 128), BF16),
        pltpu.VMEM((links.shape[0] // 4, 128), BF16),
        pltpu.SemaphoreType.DMA((RHS + 1,)),
    ]
    t_far, t_near, kept_t = call(start_kernel, held, T_HALOS + KEPT, 1_500_000, start_scratch, in_space=pltpu.HBM)
    first = True
    sent = {}
    for who in (first, not first):
        sent[who] = send(t_far, "ta", True, who), send(t_near, "ta", False, who)
    for hop in range(4):
        parity = hop % 2
        x_far, x_near, kept_x = call(
            functools.partial(send_x_kernel, parity), (f, links), X_HALOS + KEPT, 10_000_000_000
        )
        x_far, x_near = swap(x_far, "gx", True), both(x_near, "gx")
        base = (before, even) if parity else ()
        acc, = call(
            functools.partial(interior_kernel, parity, bool(parity)),
            (f, links, kept_t, kept_x, *base), FIELD, 1_000,
        )
        acc, = call(functools.partial(join_x_kernel, parity), (links, acc, x_far, x_near), FIELD, 1_000)
        before = f
        first = not first
        arrived, sent, held = sent, {}, ()
        for who in (first, not first):
            halos = arrived[not who]
            if hop == 3:
                held = call(
                    functools.partial(last_kernel, who), (links, acc, *halos), [((ROWS, 128), BF16)], 1_000_000,
                    [pltpu.VMEM((ROWS, 128), BF16), pltpu.SemaphoreType.DMA((RHS,))], out_space=pltpu.HBM, kept=held,
                )
                continue
            if parity == 0:
                *held, t_far, t_near = call(
                    functools.partial(odd_kernel, who), (links, odd, acc, *halos), FIELD + KEPT + T_HALOS, 10_000_000_000,
                    [pltpu.VMEM((ROWS, 128), F32)], kept=held,
                )
            else:
                *held, t_far, t_near = call(
                    functools.partial(even_kernel, who), (links, acc, *halos), FIELD + KEPT + T_HALOS, 10_000_000_000,
                    kept=held,
                )
            sent[who] = send(t_far, "ta", True, who), send(t_near, "ta", False, who)
        if hop < 3:
            f, kept_t = held
    out, = held
    return out.reshape(shape)


def solution(mesh):
    field_spec = P(None, None, None, None, ("groups", "ta"), "gx", None)
    link_spec = P(None, None, None, None, None, ("groups", "ta"), "gx", None)
    return jax.shard_map(
        per_device,
        mesh=mesh,
        in_specs=(field_spec, link_spec, field_spec, field_spec),
        out_specs=field_spec,
        check_vma=False,
    )
```

```python
import functools

import jax
import jax.numpy as jnp
from jax import lax
from jax.experimental import pallas as pl
from jax.experimental.pallas import tpu as pltpu
from jax.sharding import PartitionSpec as P

HALF_DEPTH = 8
KAPPA2 = 0.14 * 0.14
RHS = 4
F32 = jnp.float32
BF16 = jnp.bfloat16

SPIN = (((0, 0), (1, 0)), ((1, 3), (0, 3)), ((1, 2), (0, 0)), ((0, 3), (1, 1)))
SPIN_INV = (((0, 0), (1, 0)), ((1, 1), (0, 1)), ((1, 0), (0, 2)), ((0, 1), (1, 3)))


def add_power(base, value, power):
    (br, bi), (vr, vi) = base, value
    if power == 0:
        return br + vr, bi + vi
    if power == 1:
        return br - vi, bi + vr
    if power == 2:
        return br - vr, bi - vi
    return br + vi, bi - vr


def project(field, mu, sign):
    shift = 0 if sign > 0 else 2
    half = []
    for row in range(2):
        col, power = SPIN[mu][row]
        for c in range(3):
            half.append(add_power(field[row * 3 + c], field[(2 + col) * 3 + c], (power + shift) % 4))
    return half


def rebuild(acc, half, mu, sign):
    shift = 0 if sign > 0 else 2
    out = list(acc)
    for j in range(6):
        out[j] = add_power(out[j], half[j], 0)
    for row in range(2):
        col, power = SPIN_INV[mu][row]
        for c in range(3):
            j = (2 + row) * 3 + c
            out[j] = add_power(out[j], half[col * 3 + c], (power + shift) % 4)
    return out


def color(links, half, adjoint):
    out = []
    for s in range(2):
        for a in range(3):
            re = im = None
            for b in range(3):
                lr, li = links[b][a] if adjoint else links[a][b]
                vr, vi = half[s * 3 + b]
                if adjoint:
                    tr, ti = lr * vr + li * vi, lr * vi - li * vr
                else:
                    tr, ti = lr * vr - li * vi, lr * vi + li * vr
                re = tr if re is None else re + tr
                im = ti if im is None else im + ti
            out.append((re, im))
    return out


def each(function, half):
    return [(function(re), function(im)) for re, im in half]


def load_pair(ref, index):
    block = ref[index * 16:(index + 1) * 16, :].astype(F32)
    return block[0:8], block[8:16]


def load_links(ref, mu, parity):
    links = []
    for a in range(3):
        row = []
        for b in range(3):
            k = ((mu * 3 + a) * 3 + b) * 2
            row.append((load_pair(ref, k)[parity], load_pair(ref, k + 1)[parity]))
        links.append(row)
    return links


def load_field(ref, r):
    return [load_pair(ref, r * 12 + j) for j in range(12)]


def store_pair(ref, index, pair):
    ref[index * 16:(index + 1) * 16, :] = jnp.concatenate(pair, axis=0).astype(ref.dtype)


def store_field(ref, r, field):
    for j in range(12):
        store_pair(ref, r * 12 + j, field[j])


def site_masks():
    rows = lax.broadcasted_iota(jnp.int32, (8, 128), 0)
    return rows // 4, rows % 4


def even_device(axis):
    return lax.broadcast(lax.axis_index(axis) % 2, (8, 128)) == 0


def either(even, a, b):
    return [select(even, a[i], b[i]) for i in range(2)]


def roll_rows(value, shift):
    shift %= 8
    return pltpu.roll(value, shift, 0) if shift else value


def select(mask, a, b):
    return jnp.where(mask, a, b)


def send_t(f_ref, links_ref, parity, t_near, t_far, kept, ready=lambda r: None):
    even = even_device("ta")
    t_idx, _ = site_masks()
    first = t_idx == 0
    links = load_links(links_ref, 0, parity)
    for r in range(RHS):
        ready(r)
        field = load_field(f_ref, r)
        ahead = project(field, 0, -1)
        carry = color(links, project(field, 0, 1), True)
        moved = each(lambda v: roll_rows(v, 4), ahead)
        back = each(lambda v: roll_rows(v, 4), carry)
        for c in range(3):
            front = [select(first, ahead[c + 3][i], moved[c][i]) for i in range(2)]
            rear = [select(first, back[c][i], carry[c + 3][i]) for i in range(2)]
            store_pair(t_near, r * 3 + c, either(even, rear, front))
            store_pair(t_far, r * 3 + c, either(even, front, rear))
        for j in range(6):
            store_pair(kept, r * 6 + j, back[j])


def send_x_kernel(parity, f_ref, links_ref, x_far, x_near, kept):
    even = even_device("gx")
    _, x_idx = site_masks()
    links = load_links(links_ref, 1, parity)
    for q in range(RHS // 2):
        fronts, rears = [], []
        for r in (2 * q, 2 * q + 1):
            field = load_field(f_ref, r)
            fronts.append(project(field, 1, -1))
            rears.append(color(links, project(field, 1, 1), True))
            for j in range(6):
                store_pair(kept, r * 6 + j, [roll_rows(v, 1) for v in rears[-1][j]])
        for c in range(3):
            front, rear = [], []
            for i in range(2):
                group = [h[j][i] for h in fronts for j in (c, c + 3)]
                packed = group[0]
                for k in range(1, 4):
                    packed = select(x_idx == k, roll_rows(group[k], k), packed)
                front.append(packed)
                group = [h[j][i] for h in rears for j in (c, c + 3)]
                packed = group[0]
                for k in range(1, 4):
                    packed = select(x_idx == 3 - k, roll_rows(group[k], -k), packed)
                rear.append(packed)
            store_pair(x_near, q * 3 + c, either(even, rear, front))
            store_pair(x_far, q * 3 + c, either(even, front, rear))


def start_kernel(f_hbm, links_hbm, *refs):
    outs, (f_ref, links_ref, sems) = refs[:3], refs[3:]
    part = f_ref.shape[0] // RHS
    copies = [pltpu.make_async_copy(links_hbm.at[pl.ds(0, links_ref.shape[0])], links_ref, sems.at[RHS])]
    for r in range(RHS):
        rows = pl.ds(r * part, part)
        copies.append(pltpu.make_async_copy(f_hbm.at[rows], f_ref.at[rows], sems.at[r]))
    for copy in copies:
        copy.start()
    copies[0].wait()
    send_t(f_ref, links_ref, 0, *outs, ready=lambda r: copies[1 + r].wait())


def interior_kernel(parity, with_base, *refs):
    if with_base:
        f_ref, links_ref, kept_t, kept_x, base_ref, clover_ref, acc_ref = refs
        clover_to(clover_ref, lambda r: load_field(base_ref, r), acc_ref, 1.0)
    else:
        f_ref, links_ref, kept_t, kept_x, acc_ref = refs
    out_parity = 1 - parity
    t_idx, x_idx = site_masks()
    lane = lax.broadcasted_iota(jnp.int32, (8, 128), 1)
    odd = (t_idx + x_idx + lane // HALF_DEPTH + out_parity) % 2
    start = lane - lane % HALF_DEPTH
    up = jnp.where(odd == 1, start + (lane + 1) % HALF_DEPTH, lane)
    down = jnp.where(odd == 0, start + (lane + HALF_DEPTH - 1) % HALF_DEPTH, lane)
    zero = jnp.zeros((8, 128), F32)

    def take(value, index):
        return jnp.take_along_axis(value, index, axis=1, mode="promise_in_bounds")

    for mu in (2, 3, 0, 1):
        if mu == 2:
            ahead_of = lambda v: pltpu.roll(v, 128 - HALF_DEPTH, 1)
            behind_of = lambda v: pltpu.roll(v, HALF_DEPTH, 1)
        elif mu == 3:
            ahead_of = lambda v: take(v, up)
            behind_of = lambda v: take(v, down)
        elif mu == 0:
            ahead_of = lambda v: select(t_idx == 0, roll_rows(v, 4), 0.0)
            behind_of = lambda v: select(t_idx == 1, v, 0.0)
        else:
            ahead_of = lambda v: select(x_idx < 3, roll_rows(v, 7), 0.0)
            behind_of = lambda v: select(x_idx > 0, v, 0.0)
        links_out = load_links(links_ref, mu, out_parity)
        if mu >= 2:
            links_in = load_links(links_ref, mu, parity)
        for r in range(RHS):
            field = load_field(f_ref, r)
            if mu == 2 and not with_base:
                acc = [(zero, zero)] * 12
            else:
                acc = load_field(acc_ref, r)
            half = color(links_out, each(ahead_of, project(field, mu, -1)), False)
            acc = rebuild(acc, half, mu, -1)
            if mu >= 2:
                half = color(links_in, project(field, mu, 1), True)
            else:
                half = [load_pair(kept_t if mu == 0 else kept_x, r * 6 + j) for j in range(6)]
            acc = rebuild(acc, each(behind_of, half), mu, 1)
            store_field(acc_ref, r, acc)


def clover_to(clover_ref, get_field, out_ref, scale):
    for chi in range(2):
        matrix = {}
        for i in range(6):
            for j in range(i, 6):
                k = (chi * 6 + i) * 6 + j
                block = clover_ref[k * 16:(k + 1) * 16, :].astype(F32)
                re, im = block[0:8], block[8:16]
                if scale != 1.0:
                    re, im = re * scale, im * scale
                matrix[i, j] = (re, im)
        for r in range(RHS):
            field = get_field(r)[chi * 6:chi * 6 + 6]
            for i in range(6):
                re = im = None
                for j in range(6):
                    vr, vi = field[j]
                    mr, mi = matrix[min(i, j), max(i, j)]
                    if i <= j:
                        tr, ti = mr * vr - mi * vi, mr * vi + mi * vr
                    else:
                        tr, ti = mr * vr + mi * vi, mr * vi - mi * vr
                    re = tr if re is None else re + tr
                    im = ti if im is None else im + ti
                store_pair(out_ref, r * 12 + chi * 6 + i, (re, im))


def matvec(links, vector):
    out = []
    for a in range(3):
        re = im = None
        for b in range(3):
            (lr, li), (vr, vi) = links[a][b], vector[b]
            tr, ti = lr * vr - li * vi, lr * vi + li * vr
            re = tr if re is None else re + tr
            im = ti if im is None else im + ti
        out.append((re, im))
    return out


def rebuild_signed(acc, half, mu, sign):
    out = list(acc)
    for j in range(6):
        out[j] = add_power(out[j], half[j], 0)
    half = each(lambda v: v * sign, half)
    for row in range(2):
        col, power = SPIN_INV[mu][row]
        for c in range(3):
            j = (2 + row) * 3 + c
            out[j] = add_power(out[j], half[col * 3 + c], power)
    return out


def join_x_kernel(parity, links_ref, acc_ref, x_far, x_near, out_ref):
    even = even_device("gx")
    _, x_idx = site_masks()
    sign = jnp.where(x_idx == 3, -1.0, 1.0).astype(F32)
    links = load_links(links_ref, 1, 1 - parity)

    def edge(value):
        for k in range(3):
            value = select(x_idx == k, roll_rows(value, k - 3), value)
        return value

    links = [each(edge, row) for row in links]
    for q in range(RHS // 2):
        nxt, last = [], []
        for c in range(3):
            near, far = load_pair(x_near, q * 3 + c), load_pair(x_far, q * 3 + c)
            nxt.append(either(even, near, far))
            last.append(either(even, far, near))
        ahead = matvec(links, nxt)
        for r in (2 * q, 2 * q + 1):
            half = [None] * 6
            for s in range(2):
                k = (r % 2) * 2 + s
                for c in range(3):
                    half[s * 3 + c] = tuple(
                        select(
                            x_idx == 3,
                            roll_rows(ahead[c][i], 3 - k),
                            select(x_idx == 0, roll_rows(last[c][i], 5 + k), 0.0),
                        )
                        for i in range(2)
                    )
            store_field(out_ref, r, rebuild_signed(load_field(acc_ref, r), half, 1, sign))


def join_t(links_ref, acc_ref, t_near, t_far, parity, out_ref, done=lambda r: None):
    even = even_device("ta")
    t_idx, _ = site_masks()
    first = t_idx == 0
    sign = jnp.where(first, 1.0, -1.0).astype(F32)
    links = load_links(links_ref, 0, 1 - parity)
    links = [each(lambda v: select(first, roll_rows(v, 4), v), row) for row in links]
    for r in range(RHS):
        nxt, last = [], []
        for c in range(3):
            near, far = load_pair(t_near, r * 3 + c), load_pair(t_far, r * 3 + c)
            nxt.append(either(even, near, far))
            last.append(either(even, far, near))
        ahead = matvec(links, nxt)
        half = [tuple(select(first, last[c][i], ahead[c][i]) for i in range(2)) for c in range(3)]
        half += [
            tuple(roll_rows(select(first, ahead[c][i], last[c][i]), 4) for i in range(2)) for c in range(3)
        ]
        store_field(out_ref, r, rebuild_signed(load_field(acc_ref, r), half, 0, sign))
        done(r)


def odd_kernel(links_ref, clover_ref, acc_ref, t_near, t_far, out_ref, *refs):
    outs, summed = refs[:3], refs[3]
    join_t(links_ref, acc_ref, t_near, t_far, 0, summed)
    clover_to(clover_ref, lambda r: load_field(summed, r), out_ref, -KAPPA2)
    send_t(out_ref, links_ref, 1, *outs)


def even_kernel(links_ref, acc_ref, t_near, t_far, out_ref, *outs):
    join_t(links_ref, acc_ref, t_near, t_far, 1, out_ref)
    send_t(out_ref, links_ref, 0, *outs)


def last_kernel(links_ref, acc_ref, t_near, t_far, out_hbm, held, sems):
    part = held.shape[0] // RHS
    copies = []

    def done(r):
        rows = pl.ds(r * part, part)
        copies.append(pltpu.make_async_copy(held.at[rows], out_hbm.at[rows], sems.at[r]))
        copies[-1].start()

    join_t(links_ref, acc_ref, t_near, t_far, 1, held, done)
    for copy in copies:
        copy.wait()


ROWS = RHS * 24 * 8
FIELD = [((ROWS, 128), F32)]
KEPT = [((RHS * 12 * 8, 128), F32)]
T_HALOS = [((RHS * 3 * 16, 128), BF16)] * 2
X_HALOS = [((RHS * 3 * 8, 128), BF16)] * 2


def call(kernel, args, outs, flops, scratch=(), in_space=pltpu.VMEM, out_space=pltpu.VMEM):
    return pl.pallas_call(
        kernel,
        out_shape=tuple(jax.ShapeDtypeStruct(shape, dtype) for shape, dtype in outs),
        in_specs=[pl.BlockSpec(memory_space=in_space)] * len(args),
        out_specs=tuple([pl.BlockSpec(memory_space=out_space)] * len(outs)),
        scratch_shapes=list(scratch),
        compiler_params=pltpu.CompilerParams(vmem_limit_bytes=24 * 1024 * 1024),
        cost_estimate=pl.CostEstimate(flops=flops, bytes_accessed=2 * 1024 * 1024, transcendentals=0),
    )(*args)


def swap(value, axis, far):
    count = lax.axis_size(axis)
    assert count % 2 == 0
    pairs = [(i, (i + (1 if (i % 2 == 0) != far else -1)) % count) for i in range(count)]
    return lax.ppermute(value, axis, pairs)


def per_device(source, gauge_links, clover_even, clover_odd_inv):
    shape = source.shape
    f = source.reshape(-1, 128)
    links = gauge_links.reshape(-1, 128)
    even = clover_even.reshape(-1, 128)
    odd = clover_odd_inv.reshape(-1, 128)
    held = [pltpu.with_memory_space_constraint(v, pltpu.HBM) for v in (f, links)]
    start_scratch = [
        pltpu.VMEM((ROWS, 128), BF16),
        pltpu.VMEM((links.shape[0] // 4, 128), BF16),
        pltpu.SemaphoreType.DMA((RHS + 1,)),
    ]
    t_near, t_far, kept_t = call(start_kernel, held, T_HALOS + KEPT, 1_500_000, start_scratch, in_space=pltpu.HBM)
    for hop in range(4):
        parity = hop % 2
        t_near, t_far = swap(t_near, "ta", False), swap(t_far, "ta", True)
        x_far, x_near, kept_x = call(
            functools.partial(send_x_kernel, parity), (f, links), X_HALOS + KEPT, 1_500_000
        )
        x_far, x_near = swap(x_far, "gx", True), swap(x_near, "gx", False)
        base = (before, even) if parity else ()
        acc, = call(
            functools.partial(interior_kernel, parity, bool(parity)),
            (f, links, kept_t, kept_x, *base), FIELD, 8_000_000 if parity else 5_000_000,
        )
        acc, = call(functools.partial(join_x_kernel, parity), (links, acc, x_far, x_near), FIELD, 1_000_000)
        before = f
        if parity == 0:
            f, t_near, t_far, kept_t = call(
                odd_kernel, (links, odd, acc, t_near, t_far), FIELD + T_HALOS + KEPT, 4_000_000,
                [pltpu.VMEM((ROWS, 128), F32)],
            )
        elif hop == 1:
            f, t_near, t_far, kept_t = call(
                even_kernel, (links, acc, t_near, t_far), FIELD + T_HALOS + KEPT, 2_000_000
            )
        else:
            out, = call(
                last_kernel, (links, acc, t_near, t_far), [((ROWS, 128), BF16)], 1_000_000,
                [pltpu.VMEM((ROWS, 128), BF16), pltpu.SemaphoreType.DMA((RHS,))], out_space=pltpu.HBM,
            )
    return out.reshape(shape)


def solution(mesh):
    field_spec = P(None, None, None, None, ("groups", "ta"), "gx", None)
    link_spec = P(None, None, None, None, None, ("groups", "ta"), "gx", None)
    return jax.shard_map(
        per_device,
        mesh=mesh,
        in_specs=(field_spec, link_spec, field_spec, field_spec),
        out_specs=field_spec,
        check_vma=False,
    )
```

```python
import functools

import jax
import jax.numpy as jnp
from jax import lax
from jax.experimental import pallas as pl
from jax.experimental.pallas import tpu as pltpu
from jax.sharding import PartitionSpec as P

HALF_DEPTH = 8
KAPPA2 = 0.14 * 0.14
RHS = 4
F32 = jnp.float32
BF16 = jnp.bfloat16

SPIN = (((0, 0), (1, 0)), ((1, 3), (0, 3)), ((1, 2), (0, 0)), ((0, 3), (1, 1)))
SPIN_INV = (((0, 0), (1, 0)), ((1, 1), (0, 1)), ((1, 0), (0, 2)), ((0, 1), (1, 3)))


def add_power(base, value, power):
    (br, bi), (vr, vi) = base, value
    if power == 0:
        return br + vr, bi + vi
    if power == 1:
        return br - vi, bi + vr
    if power == 2:
        return br - vr, bi - vi
    return br + vi, bi - vr


def project(field, mu, sign):
    shift = 0 if sign > 0 else 2
    half = []
    for row in range(2):
        col, power = SPIN[mu][row]
        for c in range(3):
            half.append(add_power(field[row * 3 + c], field[(2 + col) * 3 + c], (power + shift) % 4))
    return half


def rebuild(acc, half, mu, sign):
    shift = 0 if sign > 0 else 2
    out = list(acc)
    for j in range(6):
        out[j] = add_power(out[j], half[j], 0)
    for row in range(2):
        col, power = SPIN_INV[mu][row]
        for c in range(3):
            j = (2 + row) * 3 + c
            out[j] = add_power(out[j], half[col * 3 + c], (power + shift) % 4)
    return out


def color(links, half, adjoint):
    out = []
    for s in range(2):
        for a in range(3):
            re = im = None
            for b in range(3):
                lr, li = links[b][a] if adjoint else links[a][b]
                vr, vi = half[s * 3 + b]
                if adjoint:
                    tr, ti = lr * vr + li * vi, lr * vi - li * vr
                else:
                    tr, ti = lr * vr - li * vi, lr * vi + li * vr
                re = tr if re is None else re + tr
                im = ti if im is None else im + ti
            out.append((re, im))
    return out


def each(function, half):
    return [(function(re), function(im)) for re, im in half]


def load_pair(ref, index):
    block = ref[index * 16:(index + 1) * 16, :].astype(F32)
    return block[0:8], block[8:16]


def load_links(ref, mu, parity):
    links = []
    for a in range(3):
        row = []
        for b in range(3):
            k = ((mu * 3 + a) * 3 + b) * 2
            row.append((load_pair(ref, k)[parity], load_pair(ref, k + 1)[parity]))
        links.append(row)
    return links


def load_field(ref, r):
    return [load_pair(ref, r * 12 + j) for j in range(12)]


def store_pair(ref, index, pair):
    ref[index * 16:(index + 1) * 16, :] = jnp.concatenate(pair, axis=0).astype(ref.dtype)


def store_field(ref, r, field):
    for j in range(12):
        store_pair(ref, r * 12 + j, field[j])


def site_masks():
    rows = lax.broadcasted_iota(jnp.int32, (8, 128), 0)
    return rows // 4, rows % 4


def even_device(*axes):
    place = sum(lax.axis_index(axis) for axis in axes)
    return lax.broadcast(place % 2, (8, 128)) == 0


def either(even, a, b):
    return [select(even, a[i], b[i]) for i in range(2)]


def roll_rows(value, shift):
    shift %= 8
    return pltpu.roll(value, shift, 0) if shift else value


def select(mask, a, b):
    return jnp.where(mask, a, b)


def send_t(f_ref, links_ref, parity, t_one, t_two, kept, ready=lambda r: None):
    even = even_device("ta", "gx")
    t_idx, _ = site_masks()
    first = t_idx == 0
    links = load_links(links_ref, 0, parity)
    for r in range(RHS):
        ready(r)
        field = load_field(f_ref, r)
        ahead = project(field, 0, -1)
        carry = color(links, project(field, 0, 1), True)
        moved = each(lambda v: roll_rows(v, 4), ahead)
        back = each(lambda v: roll_rows(v, 4), carry)
        for c in range(3):
            front = [select(first, ahead[c + 3][i], moved[c][i]) for i in range(2)]
            rear = [select(first, back[c][i], carry[c + 3][i]) for i in range(2)]
            store_pair(t_one, r * 3 + c, either(even, rear, front))
            store_pair(t_two, r * 3 + c, either(even, front, rear))
        for j in range(6):
            store_pair(kept, r * 6 + j, back[j])


def send_x_kernel(parity, f_ref, links_ref, x_far, x_near, kept):
    even = even_device("gx")
    _, x_idx = site_masks()
    links = load_links(links_ref, 1, parity)
    for q in range(RHS // 2):
        fronts, rears = [], []
        for r in (2 * q, 2 * q + 1):
            field = load_field(f_ref, r)
            fronts.append(project(field, 1, -1))
            rears.append(color(links, project(field, 1, 1), True))
            for j in range(6):
                store_pair(kept, r * 6 + j, [roll_rows(v, 1) for v in rears[-1][j]])
        for c in range(3):
            front, rear = [], []
            for i in range(2):
                group = [h[j][i] for h in fronts for j in (c, c + 3)]
                packed = group[0]
                for k in range(1, 4):
                    packed = select(x_idx == k, roll_rows(group[k], k), packed)
                front.append(packed)
                group = [h[j][i] for h in rears for j in (c, c + 3)]
                packed = group[0]
                for k in range(1, 4):
                    packed = select(x_idx == 3 - k, roll_rows(group[k], -k), packed)
                rear.append(packed)
            store_pair(x_near, q * 3 + c, either(even, rear, front))
            store_pair(x_far, q * 3 + c, either(even, front, rear))


def start_kernel(f_hbm, links_hbm, *refs):
    outs, (f_ref, links_ref, sems) = refs[:3], refs[3:]
    part = f_ref.shape[0] // RHS
    copies = [pltpu.make_async_copy(links_hbm.at[pl.ds(0, links_ref.shape[0])], links_ref, sems.at[RHS])]
    for r in range(RHS):
        rows = pl.ds(r * part, part)
        copies.append(pltpu.make_async_copy(f_hbm.at[rows], f_ref.at[rows], sems.at[r]))
    for copy in copies:
        copy.start()
    copies[0].wait()
    send_t(f_ref, links_ref, 0, *outs, ready=lambda r: copies[1 + r].wait())


def interior_kernel(parity, with_base, *refs):
    if with_base:
        f_ref, links_ref, kept_t, kept_x, base_ref, clover_ref, acc_ref = refs
        clover_to(clover_ref, lambda r: load_field(base_ref, r), acc_ref, 1.0)
    else:
        f_ref, links_ref, kept_t, kept_x, acc_ref = refs
    out_parity = 1 - parity
    t_idx, x_idx = site_masks()
    lane = lax.broadcasted_iota(jnp.int32, (8, 128), 1)
    odd = (t_idx + x_idx + lane // HALF_DEPTH + out_parity) % 2
    start = lane - lane % HALF_DEPTH
    up = jnp.where(odd == 1, start + (lane + 1) % HALF_DEPTH, lane)
    down = jnp.where(odd == 0, start + (lane + HALF_DEPTH - 1) % HALF_DEPTH, lane)
    zero = jnp.zeros((8, 128), F32)

    def take(value, index):
        return jnp.take_along_axis(value, index, axis=1, mode="promise_in_bounds")

    for mu in (2, 3, 0, 1):
        if mu == 2:
            ahead_of = lambda v: pltpu.roll(v, 128 - HALF_DEPTH, 1)
            behind_of = lambda v: pltpu.roll(v, HALF_DEPTH, 1)
        elif mu == 3:
            ahead_of = lambda v: take(v, up)
            behind_of = lambda v: take(v, down)
        elif mu == 0:
            ahead_of = lambda v: select(t_idx == 0, roll_rows(v, 4), 0.0)
            behind_of = lambda v: select(t_idx == 1, v, 0.0)
        else:
            ahead_of = lambda v: select(x_idx < 3, roll_rows(v, 7), 0.0)
            behind_of = lambda v: select(x_idx > 0, v, 0.0)
        links_out = load_links(links_ref, mu, out_parity)
        if mu >= 2:
            links_in = load_links(links_ref, mu, parity)
        for r in range(RHS):
            field = load_field(f_ref, r)
            if mu == 2 and not with_base:
                acc = [(zero, zero)] * 12
            else:
                acc = load_field(acc_ref, r)
            half = color(links_out, each(ahead_of, project(field, mu, -1)), False)
            acc = rebuild(acc, half, mu, -1)
            if mu >= 2:
                half = color(links_in, project(field, mu, 1), True)
            else:
                half = [load_pair(kept_t if mu == 0 else kept_x, r * 6 + j) for j in range(6)]
            acc = rebuild(acc, each(behind_of, half), mu, 1)
            store_field(acc_ref, r, acc)


def clover_to(clover_ref, get_field, out_ref, scale):
    for chi in range(2):
        matrix = {}
        for i in range(6):
            for j in range(i, 6):
                k = (chi * 6 + i) * 6 + j
                block = clover_ref[k * 16:(k + 1) * 16, :].astype(F32)
                re, im = block[0:8], block[8:16]
                if scale != 1.0:
                    re, im = re * scale, im * scale
                matrix[i, j] = (re, im)
        for r in range(RHS):
            field = get_field(r)[chi * 6:chi * 6 + 6]
            for i in range(6):
                re = im = None
                for j in range(6):
                    vr, vi = field[j]
                    mr, mi = matrix[min(i, j), max(i, j)]
                    if i <= j:
                        tr, ti = mr * vr - mi * vi, mr * vi + mi * vr
                    else:
                        tr, ti = mr * vr + mi * vi, mr * vi - mi * vr
                    re = tr if re is None else re + tr
                    im = ti if im is None else im + ti
                store_pair(out_ref, r * 12 + chi * 6 + i, (re, im))


def matvec(links, vector):
    out = []
    for a in range(3):
        re = im = None
        for b in range(3):
            (lr, li), (vr, vi) = links[a][b], vector[b]
            tr, ti = lr * vr - li * vi, lr * vi + li * vr
            re = tr if re is None else re + tr
            im = ti if im is None else im + ti
        out.append((re, im))
    return out


def rebuild_signed(acc, half, mu, sign):
    out = list(acc)
    for j in range(6):
        out[j] = add_power(out[j], half[j], 0)
    half = each(lambda v: v * sign, half)
    for row in range(2):
        col, power = SPIN_INV[mu][row]
        for c in range(3):
            j = (2 + row) * 3 + c
            out[j] = add_power(out[j], half[col * 3 + c], power)
    return out


def join_x_kernel(parity, links_ref, acc_ref, x_far, x_near, out_ref):
    even = even_device("gx")
    _, x_idx = site_masks()
    sign = jnp.where(x_idx == 3, -1.0, 1.0).astype(F32)
    links = load_links(links_ref, 1, 1 - parity)

    def edge(value):
        for k in range(3):
            value = select(x_idx == k, roll_rows(value, k - 3), value)
        return value

    links = [each(edge, row) for row in links]
    for q in range(RHS // 2):
        nxt, last = [], []
        for c in range(3):
            near, far = load_pair(x_near, q * 3 + c), load_pair(x_far, q * 3 + c)
            nxt.append(either(even, near, far))
            last.append(either(even, far, near))
        ahead = matvec(links, nxt)
        for r in (2 * q, 2 * q + 1):
            half = [None] * 6
            for s in range(2):
                k = (r % 2) * 2 + s
                for c in range(3):
                    half[s * 3 + c] = tuple(
                        select(
                            x_idx == 3,
                            roll_rows(ahead[c][i], 3 - k),
                            select(x_idx == 0, roll_rows(last[c][i], 5 + k), 0.0),
                        )
                        for i in range(2)
                    )
            store_field(out_ref, r, rebuild_signed(load_field(acc_ref, r), half, 1, sign))


def join_t(links_ref, acc_ref, t_one, t_two, parity, out_ref, done=lambda r: None):
    even = even_device("ta", "gx")
    t_idx, _ = site_masks()
    first = t_idx == 0
    sign = jnp.where(first, 1.0, -1.0).astype(F32)
    links = load_links(links_ref, 0, 1 - parity)
    links = [each(lambda v: select(first, roll_rows(v, 4), v), row) for row in links]
    for r in range(RHS):
        nxt, last = [], []
        for c in range(3):
            one, two = load_pair(t_one, r * 3 + c), load_pair(t_two, r * 3 + c)
            nxt.append(either(even, one, two))
            last.append(either(even, two, one))
        ahead = matvec(links, nxt)
        half = [tuple(select(first, last[c][i], ahead[c][i]) for i in range(2)) for c in range(3)]
        half += [
            tuple(roll_rows(select(first, ahead[c][i], last[c][i]), 4) for i in range(2)) for c in range(3)
        ]
        store_field(out_ref, r, rebuild_signed(load_field(acc_ref, r), half, 0, sign))
        done(r)


def odd_kernel(links_ref, clover_ref, acc_ref, t_one, t_two, out_ref, *refs):
    outs, summed = refs[:3], refs[3]
    join_t(links_ref, acc_ref, t_one, t_two, 0, summed)
    clover_to(clover_ref, lambda r: load_field(summed, r), out_ref, -KAPPA2)
    send_t(out_ref, links_ref, 1, *outs)


def even_kernel(links_ref, acc_ref, t_one, t_two, out_ref, *outs):
    join_t(links_ref, acc_ref, t_one, t_two, 1, out_ref)
    send_t(out_ref, links_ref, 0, *outs)


def last_kernel(links_ref, acc_ref, t_one, t_two, out_hbm, held, sems):
    part = held.shape[0] // RHS
    copies = []

    def done(r):
        rows = pl.ds(r * part, part)
        copies.append(pltpu.make_async_copy(held.at[rows], out_hbm.at[rows], sems.at[r]))
        copies[-1].start()

    join_t(links_ref, acc_ref, t_one, t_two, 1, held, done)
    for copy in copies:
        copy.wait()


ROWS = RHS * 24 * 8
FIELD = [((ROWS, 128), F32)]
KEPT = [((RHS * 12 * 8, 128), F32)]
T_HALOS = [((RHS * 3 * 16, 128), BF16)] * 2
X_HALOS = [((RHS * 3 * 8, 128), BF16)] * 2


def call(kernel, args, outs, flops, scratch=(), in_space=pltpu.VMEM, out_space=pltpu.VMEM):
    return pl.pallas_call(
        kernel,
        out_shape=tuple(jax.ShapeDtypeStruct(shape, dtype) for shape, dtype in outs),
        in_specs=[pl.BlockSpec(memory_space=in_space)] * len(args),
        out_specs=tuple([pl.BlockSpec(memory_space=out_space)] * len(outs)),
        scratch_shapes=list(scratch),
        compiler_params=pltpu.CompilerParams(vmem_limit_bytes=24 * 1024 * 1024),
        cost_estimate=pl.CostEstimate(flops=flops, bytes_accessed=2 * 1024 * 1024, transcendentals=0),
    )(*args)


def swap(value, axis, far):
    count = lax.axis_size(axis)
    assert count % 2 == 0
    pairs = [(i, (i + (1 if (i % 2 == 0) != far else -1)) % count) for i in range(count)]
    return lax.ppermute(value, axis, pairs)


def swap_t(value, ahead):
    count, across = lax.axis_size("ta"), lax.axis_size("gx")
    assert count % 2 == 0 and across % 2 == 0
    pairs = []
    for i in range(count):
        for j in range(across):
            step = 1 if ((i + j) % 2 == 0) == ahead else -1
            pairs.append((i * across + j, (i + step) % count * across + j))
    return lax.ppermute(value, ("ta", "gx"), pairs)


def per_device(source, gauge_links, clover_even, clover_odd_inv):
    shape = source.shape
    f = source.reshape(-1, 128)
    links = gauge_links.reshape(-1, 128)
    even = clover_even.reshape(-1, 128)
    odd = clover_odd_inv.reshape(-1, 128)
    held = [pltpu.with_memory_space_constraint(v, pltpu.HBM) for v in (f, links)]
    start_scratch = [
        pltpu.VMEM((ROWS, 128), BF16),
        pltpu.VMEM((links.shape[0] // 4, 128), BF16),
        pltpu.SemaphoreType.DMA((RHS + 1,)),
    ]
    t_one, t_two, kept_t = call(start_kernel, held, T_HALOS + KEPT, 1_500_000, start_scratch, in_space=pltpu.HBM)
    for hop in range(4):
        parity = hop % 2
        t_one, t_two = swap_t(t_one, True), swap_t(t_two, False)
        x_far, x_near, kept_x = call(
            functools.partial(send_x_kernel, parity), (f, links), X_HALOS + KEPT, 1_500_000
        )
        x_far, x_near = swap(x_far, "gx", True), swap(x_near, "gx", False)
        base = (before, even) if parity else ()
        acc, = call(
            functools.partial(interior_kernel, parity, bool(parity)),
            (f, links, kept_t, kept_x, *base), FIELD, 8_000_000 if parity else 5_000_000,
        )
        acc, = call(functools.partial(join_x_kernel, parity), (links, acc, x_far, x_near), FIELD, 1_000_000)
        before = f
        if parity == 0:
            f, t_one, t_two, kept_t = call(
                odd_kernel, (links, odd, acc, t_one, t_two), FIELD + T_HALOS + KEPT, 4_000_000,
                [pltpu.VMEM((ROWS, 128), F32)],
            )
        elif hop == 1:
            f, t_one, t_two, kept_t = call(
                even_kernel, (links, acc, t_one, t_two), FIELD + T_HALOS + KEPT, 2_000_000
            )
        else:
            out, = call(
                last_kernel, (links, acc, t_one, t_two), [((ROWS, 128), BF16)], 1_000_000,
                [pltpu.VMEM((ROWS, 128), BF16), pltpu.SemaphoreType.DMA((RHS,))], out_space=pltpu.HBM,
            )
    return out.reshape(shape)


def solution(mesh):
    field_spec = P(None, None, None, None, ("groups", "ta"), "gx", None)
    link_spec = P(None, None, None, None, None, ("groups", "ta"), "gx", None)
    return jax.shard_map(
        per_device,
        mesh=mesh,
        in_specs=(field_spec, link_spec, field_spec, field_spec),
        out_specs=field_spec,
        check_vma=False,
    )
```

```python
import functools

import jax
import jax.numpy as jnp
from jax import lax
from jax.experimental import pallas as pl
from jax.experimental.pallas import tpu as pltpu
from jax.sharding import PartitionSpec as P

HALF_DEPTH = 8
KAPPA2 = 0.14 * 0.14
RHS = 4
F32 = jnp.float32
BF16 = jnp.bfloat16

SPIN = (((0, 0), (1, 0)), ((1, 3), (0, 3)), ((1, 2), (0, 0)), ((0, 3), (1, 1)))
SPIN_INV = (((0, 0), (1, 0)), ((1, 1), (0, 1)), ((1, 0), (0, 2)), ((0, 1), (1, 3)))


def add_power(base, value, power):
    (br, bi), (vr, vi) = base, value
    if power == 0:
        return br + vr, bi + vi
    if power == 1:
        return br - vi, bi + vr
    if power == 2:
        return br - vr, bi - vi
    return br + vi, bi - vr


def project(field, mu, sign):
    shift = 0 if sign > 0 else 2
    half = []
    for row in range(2):
        col, power = SPIN[mu][row]
        for c in range(3):
            half.append(add_power(field[row * 3 + c], field[(2 + col) * 3 + c], (power + shift) % 4))
    return half


def rebuild(acc, half, mu, sign):
    shift = 0 if sign > 0 else 2
    out = list(acc)
    for j in range(6):
        out[j] = add_power(out[j], half[j], 0)
    for row in range(2):
        col, power = SPIN_INV[mu][row]
        for c in range(3):
            j = (2 + row) * 3 + c
            out[j] = add_power(out[j], half[col * 3 + c], (power + shift) % 4)
    return out


def color(links, half, adjoint):
    out = []
    for s in range(2):
        for a in range(3):
            re = im = None
            for b in range(3):
                lr, li = links[b][a] if adjoint else links[a][b]
                vr, vi = half[s * 3 + b]
                if adjoint:
                    tr, ti = lr * vr + li * vi, lr * vi - li * vr
                else:
                    tr, ti = lr * vr - li * vi, lr * vi + li * vr
                re = tr if re is None else re + tr
                im = ti if im is None else im + ti
            out.append((re, im))
    return out


def each(function, half):
    return [(function(re), function(im)) for re, im in half]


def load_pair(ref, index):
    block = ref[index * 16:(index + 1) * 16, :].astype(F32)
    return block[0:8], block[8:16]


def load_links(ref, mu, parity):
    links = []
    for a in range(3):
        row = []
        for b in range(3):
            k = ((mu * 3 + a) * 3 + b) * 2
            row.append((load_pair(ref, k)[parity], load_pair(ref, k + 1)[parity]))
        links.append(row)
    return links


def load_field(ref, r):
    return [load_pair(ref, r * 12 + j) for j in range(12)]


def store_pair(ref, index, pair):
    ref[index * 16:(index + 1) * 16, :] = jnp.concatenate(pair, axis=0).astype(ref.dtype)


def store_field(ref, r, field):
    for j in range(12):
        store_pair(ref, r * 12 + j, field[j])


def site_masks():
    rows = lax.broadcasted_iota(jnp.int32, (8, 128), 0)
    return rows // 4, rows % 4


def even_device(*axes):
    place = sum(lax.axis_index(axis) for axis in axes)
    return lax.broadcast(place % 2, (8, 128)) == 0


def either(even, a, b):
    return [select(even, a[i], b[i]) for i in range(2)]


def roll_rows(value, shift):
    shift %= 8
    return pltpu.roll(value, shift, 0) if shift else value


def select(mask, a, b):
    return jnp.where(mask, a, b)


def t_edges(links):
    t_idx, _ = site_masks()
    return [each(lambda v: select(t_idx == 0, roll_rows(v, 4), v), row) for row in links]


def x_edges(links):
    _, x_idx = site_masks()

    def edge(value):
        out = value
        for k in range(3):
            out = select(x_idx == k, roll_rows(value, k - 3), out)
        return out

    return [each(edge, row) for row in links]


def send_t(f_ref, links_ref, parity, t_one, t_two, ready=lambda r: None):
    even = even_device("ta", "gx")
    t_idx, _ = site_masks()
    first = t_idx == 0
    links = t_edges(load_links(links_ref, 0, parity))
    for r in range(RHS):
        ready(r)
        field = load_field(f_ref, r)
        ahead, behind = project(field, 0, -1), project(field, 0, 1)
        rears = [
            tuple(select(first, roll_rows(behind[c][i], 4), behind[c + 3][i]) for i in range(2)) for c in range(3)
        ]
        rears = matvec(links, rears, True)
        for c in range(3):
            front = [select(first, ahead[c + 3][i], roll_rows(ahead[c][i], 4)) for i in range(2)]
            store_pair(t_one, r * 3 + c, either(even, rears[c], front))
            store_pair(t_two, r * 3 + c, either(even, front, rears[c]))


def send_x_kernel(parity, f_ref, links_ref, x_far, x_near):
    even = even_device("gx")
    _, x_idx = site_masks()
    links = x_edges(load_links(links_ref, 1, parity))

    def packed(values, row, step):
        out = values[0]
        for k in range(1, 4):
            out = select(x_idx == row + step * k, roll_rows(values[k], step * k), out)
        return out

    for q in range(RHS // 2):
        fields = [load_field(f_ref, r) for r in (2 * q, 2 * q + 1)]
        ahead = [project(field, 1, -1) for field in fields]
        behind = [project(field, 1, 1) for field in fields]
        fronts, rears = [], []
        for c in range(3):
            fronts.append([packed([h[j][i] for h in ahead for j in (c, c + 3)], 0, 1) for i in range(2)])
            rears.append([packed([h[j][i] for h in behind for j in (c, c + 3)], 3, -1) for i in range(2)])
        rears = matvec(links, rears, True)
        for c in range(3):
            store_pair(x_near, q * 3 + c, either(even, rears[c], fronts[c]))
            store_pair(x_far, q * 3 + c, either(even, fronts[c], rears[c]))


def start_kernel(f_hbm, links_hbm, *refs):
    outs, (f_ref, links_ref, sems) = refs[:2], refs[2:]
    part = f_ref.shape[0] // RHS
    copies = [pltpu.make_async_copy(links_hbm.at[pl.ds(0, links_ref.shape[0])], links_ref, sems.at[RHS])]
    for r in range(RHS):
        rows = pl.ds(r * part, part)
        copies.append(pltpu.make_async_copy(f_hbm.at[rows], f_ref.at[rows], sems.at[r]))
    for copy in copies:
        copy.start()
    copies[0].wait()
    send_t(f_ref, links_ref, 0, *outs, ready=lambda r: copies[1 + r].wait())


def interior_kernel(parity, with_base, *refs):
    if with_base:
        f_ref, links_ref, base_ref, clover_ref, acc_ref = refs
        clover_to(clover_ref, lambda r: load_field(base_ref, r), acc_ref, 1.0)
    else:
        f_ref, links_ref, acc_ref = refs
    out_parity = 1 - parity
    t_idx, x_idx = site_masks()
    lane = lax.broadcasted_iota(jnp.int32, (8, 128), 1)
    odd = (t_idx + x_idx + lane // HALF_DEPTH + out_parity) % 2
    start = lane - lane % HALF_DEPTH
    up = jnp.where(odd == 1, start + (lane + 1) % HALF_DEPTH, lane)
    down = jnp.where(odd == 0, start + (lane + HALF_DEPTH - 1) % HALF_DEPTH, lane)
    zero = jnp.zeros((8, 128), F32)

    def take(value, index):
        return jnp.take_along_axis(value, index, axis=1, mode="promise_in_bounds")

    for mu in (2, 3, 0, 1):
        if mu == 2:
            ahead_of = lambda v: pltpu.roll(v, 128 - HALF_DEPTH, 1)
            behind_of = lambda v: pltpu.roll(v, HALF_DEPTH, 1)
        elif mu == 3:
            ahead_of = lambda v: take(v, up)
            behind_of = lambda v: take(v, down)
        elif mu == 0:
            ahead_of = lambda v: select(t_idx == 0, roll_rows(v, 4), 0.0)
            behind_of = lambda v: select(t_idx == 1, roll_rows(v, 4), 0.0)
        else:
            ahead_of = lambda v: select(x_idx < 3, roll_rows(v, 7), 0.0)
            behind_of = lambda v: select(x_idx > 0, roll_rows(v, 1), 0.0)
        links_out = load_links(links_ref, mu, out_parity)
        links_in = load_links(links_ref, mu, parity)
        for r in range(RHS):
            field = load_field(f_ref, r)
            if mu == 2 and not with_base:
                acc = [(zero, zero)] * 12
            else:
                acc = load_field(acc_ref, r)
            half = color(links_out, each(ahead_of, project(field, mu, -1)), False)
            acc = rebuild(acc, half, mu, -1)
            half = color(links_in, project(field, mu, 1), True)
            acc = rebuild(acc, each(behind_of, half), mu, 1)
            store_field(acc_ref, r, acc)


def clover_to(clover_ref, get_field, out_ref, scale):
    for chi in range(2):
        matrix = {}
        for i in range(6):
            for j in range(i, 6):
                k = (chi * 6 + i) * 6 + j
                block = clover_ref[k * 16:(k + 1) * 16, :].astype(F32)
                re, im = block[0:8], block[8:16]
                if scale != 1.0:
                    re, im = re * scale, im * scale
                matrix[i, j] = (re, re + im, im - re)
        for r in range(RHS):
            field = get_field(r)[chi * 6:chi * 6 + 6]
            both = [vr + vi for vr, vi in field]
            for i in range(6):
                one = two = three = None
                for j in range(6):
                    vr, vi = field[j]
                    m, plus, minus = matrix[min(i, j), max(i, j)]
                    t_one = m * both[j]
                    if i <= j:
                        t_two, t_three = -(vi * plus), vr * minus
                    else:
                        t_two, t_three = vi * minus, -(vr * plus)
                    one = t_one if one is None else one + t_one
                    two = t_two if two is None else two + t_two
                    three = t_three if three is None else three + t_three
                store_pair(out_ref, r * 12 + chi * 6 + i, (one + two, one + three))


def matvec(links, vector, adjoint):
    out = []
    for a in range(3):
        re = im = None
        for b in range(3):
            lr, li = links[b][a] if adjoint else links[a][b]
            vr, vi = vector[b]
            if adjoint:
                tr, ti = lr * vr + li * vi, lr * vi - li * vr
            else:
                tr, ti = lr * vr - li * vi, lr * vi + li * vr
            re = tr if re is None else re + tr
            im = ti if im is None else im + ti
        out.append((re, im))
    return out


def rebuild_signed(acc, half, mu, sign):
    out = list(acc)
    for j in range(6):
        out[j] = add_power(out[j], half[j], 0)
    half = each(lambda v: v * sign, half)
    for row in range(2):
        col, power = SPIN_INV[mu][row]
        for c in range(3):
            j = (2 + row) * 3 + c
            out[j] = add_power(out[j], half[col * 3 + c], power)
    return out


def join_x_kernel(parity, links_ref, acc_ref, x_far, x_near, out_ref):
    even = even_device("gx")
    _, x_idx = site_masks()
    sign = jnp.where(x_idx == 3, -1.0, 1.0).astype(F32)
    links = x_edges(load_links(links_ref, 1, 1 - parity))
    for q in range(RHS // 2):
        nxt, last = [], []
        for c in range(3):
            near, far = load_pair(x_near, q * 3 + c), load_pair(x_far, q * 3 + c)
            nxt.append(either(even, near, far))
            last.append(either(even, far, near))
        ahead = matvec(links, nxt, False)
        for r in (2 * q, 2 * q + 1):
            half = [None] * 6
            for s in range(2):
                k = (r % 2) * 2 + s
                for c in range(3):
                    half[s * 3 + c] = tuple(
                        select(
                            x_idx == 3,
                            roll_rows(ahead[c][i], 3 - k),
                            select(x_idx == 0, roll_rows(last[c][i], 5 + k), 0.0),
                        )
                        for i in range(2)
                    )
            store_field(out_ref, r, rebuild_signed(load_field(acc_ref, r), half, 1, sign))


def join_t(links_ref, acc_ref, t_one, t_two, parity, out_ref, done=lambda r: None):
    even = even_device("ta", "gx")
    t_idx, _ = site_masks()
    first = t_idx == 0
    sign = jnp.where(first, 1.0, -1.0).astype(F32)
    links = t_edges(load_links(links_ref, 0, 1 - parity))
    for r in range(RHS):
        nxt, last = [], []
        for c in range(3):
            one, two = load_pair(t_one, r * 3 + c), load_pair(t_two, r * 3 + c)
            nxt.append(either(even, one, two))
            last.append(either(even, two, one))
        ahead = matvec(links, nxt, False)
        half = [tuple(select(first, last[c][i], ahead[c][i]) for i in range(2)) for c in range(3)]
        half += [
            tuple(roll_rows(select(first, ahead[c][i], last[c][i]), 4) for i in range(2)) for c in range(3)
        ]
        store_field(out_ref, r, rebuild_signed(load_field(acc_ref, r), half, 0, sign))
        done(r)


def odd_kernel(links_ref, clover_ref, acc_ref, t_one, t_two, out_ref, *refs):
    outs, summed = refs[:2], refs[2]
    join_t(links_ref, acc_ref, t_one, t_two, 0, summed)
    clover_to(clover_ref, lambda r: load_field(summed, r), out_ref, -KAPPA2)
    send_t(out_ref, links_ref, 1, *outs)


def even_kernel(links_ref, acc_ref, t_one, t_two, out_ref, *outs):
    join_t(links_ref, acc_ref, t_one, t_two, 1, out_ref)
    send_t(out_ref, links_ref, 0, *outs)


def last_kernel(links_ref, acc_ref, t_one, t_two, out_hbm, held, sems):
    part = held.shape[0] // RHS
    copies = []

    def done(r):
        rows = pl.ds(r * part, part)
        copies.append(pltpu.make_async_copy(held.at[rows], out_hbm.at[rows], sems.at[r]))
        copies[-1].start()

    join_t(links_ref, acc_ref, t_one, t_two, 1, held, done)
    for copy in copies:
        copy.wait()


ROWS = RHS * 24 * 8
FIELD = [((ROWS, 128), F32)]
T_HALOS = [((RHS * 3 * 16, 128), BF16)] * 2
X_HALOS = [((RHS * 3 * 8, 128), BF16)] * 2


def call(kernel, args, outs, flops, scratch=(), in_space=pltpu.VMEM, out_space=pltpu.VMEM):
    return pl.pallas_call(
        kernel,
        out_shape=tuple(jax.ShapeDtypeStruct(shape, dtype) for shape, dtype in outs),
        in_specs=[pl.BlockSpec(memory_space=in_space)] * len(args),
        out_specs=tuple([pl.BlockSpec(memory_space=out_space)] * len(outs)),
        scratch_shapes=list(scratch),
        compiler_params=pltpu.CompilerParams(vmem_limit_bytes=24 * 1024 * 1024),
        cost_estimate=pl.CostEstimate(flops=flops, bytes_accessed=2 * 1024 * 1024, transcendentals=0),
    )(*args)


def swap(value, axis, far):
    count = lax.axis_size(axis)
    assert count % 2 == 0
    pairs = [(i, (i + (1 if (i % 2 == 0) != far else -1)) % count) for i in range(count)]
    return lax.ppermute(value, axis, pairs)


def swap_t(value, ahead):
    count, across = lax.axis_size("ta"), lax.axis_size("gx")
    assert count % 2 == 0 and across % 2 == 0
    pairs = []
    for i in range(count):
        for j in range(across):
            step = 1 if ((i + j) % 2 == 0) == ahead else -1
            pairs.append((i * across + j, (i + step) % count * across + j))
    return lax.ppermute(value, ("ta", "gx"), pairs)


def per_device(source, gauge_links, clover_even, clover_odd_inv):
    shape = source.shape
    f = source.reshape(-1, 128)
    links = gauge_links.reshape(-1, 128)
    even = clover_even.reshape(-1, 128)
    odd = clover_odd_inv.reshape(-1, 128)
    held = [pltpu.with_memory_space_constraint(v, pltpu.HBM) for v in (f, links)]
    start_scratch = [
        pltpu.VMEM((ROWS, 128), BF16),
        pltpu.VMEM((links.shape[0] // 4, 128), BF16),
        pltpu.SemaphoreType.DMA((RHS + 1,)),
    ]
    t_one, t_two = call(start_kernel, held, T_HALOS, 1_500_000, start_scratch, in_space=pltpu.HBM)
    for hop in range(4):
        parity = hop % 2
        t_one, t_two = swap_t(t_one, True), swap_t(t_two, False)
        x_far, x_near = call(
            functools.partial(send_x_kernel, parity), (f, links), X_HALOS, 1_500_000
        )
        here, x_far, x_near = lax.optimization_barrier((f, x_far, x_near))
        x_far, x_near = swap(x_far, "gx", True), swap(x_near, "gx", False)
        base = (before, even) if parity else ()
        acc, = call(
            functools.partial(interior_kernel, parity, bool(parity)),
            (here, links, *base), FIELD, 8_000_000 if parity else 5_000_000,
        )
        acc, = call(functools.partial(join_x_kernel, parity), (links, acc, x_far, x_near), FIELD, 1_000_000)
        before = f
        if parity == 0:
            f, t_one, t_two = call(
                odd_kernel, (links, odd, acc, t_one, t_two), FIELD + T_HALOS, 4_000_000,
                [pltpu.VMEM((ROWS, 128), F32)],
            )
        elif hop == 1:
            f, t_one, t_two = call(
                even_kernel, (links, acc, t_one, t_two), FIELD + T_HALOS, 2_000_000
            )
        else:
            out, = call(
                last_kernel, (links, acc, t_one, t_two), [((ROWS, 128), BF16)], 1_000_000,
                [pltpu.VMEM((ROWS, 128), BF16), pltpu.SemaphoreType.DMA((RHS,))], out_space=pltpu.HBM,
            )
    return out.reshape(shape)


def solution(mesh):
    field_spec = P(None, None, None, None, ("groups", "ta"), "gx", None)
    link_spec = P(None, None, None, None, None, ("groups", "ta"), "gx", None)
    return jax.shard_map(
        per_device,
        mesh=mesh,
        in_specs=(field_spec, link_spec, field_spec, field_spec),
        out_specs=field_spec,
        check_vma=False,
    )
```

```python
import functools

import jax
import jax.numpy as jnp
from jax import lax
from jax.experimental import pallas as pl
from jax.experimental.pallas import tpu as pltpu
from jax.sharding import PartitionSpec as P

HALF_DEPTH = 8
KAPPA2 = 0.14 * 0.14
RHS = 4
F32 = jnp.float32
BF16 = jnp.bfloat16

SPIN = (((0, 0), (1, 0)), ((1, 3), (0, 3)), ((1, 2), (0, 0)), ((0, 3), (1, 1)))
SPIN_INV = (((0, 0), (1, 0)), ((1, 1), (0, 1)), ((1, 0), (0, 2)), ((0, 1), (1, 3)))


def add_power(base, value, power):
    (br, bi), (vr, vi) = base, value
    if power == 0:
        return br + vr, bi + vi
    if power == 1:
        return br - vi, bi + vr
    if power == 2:
        return br - vr, bi - vi
    return br + vi, bi - vr


def project(field, mu, sign):
    shift = 0 if sign > 0 else 2
    half = []
    for row in range(2):
        col, power = SPIN[mu][row]
        for c in range(3):
            half.append(add_power(field[row * 3 + c], field[(2 + col) * 3 + c], (power + shift) % 4))
    return half


def rebuild(acc, half, mu, sign):
    shift = 0 if sign > 0 else 2
    out = list(acc)
    for j in range(6):
        out[j] = add_power(out[j], half[j], 0)
    for row in range(2):
        col, power = SPIN_INV[mu][row]
        for c in range(3):
            j = (2 + row) * 3 + c
            out[j] = add_power(out[j], half[col * 3 + c], (power + shift) % 4)
    return out


def color(links, half, adjoint):
    out = []
    for s in range(2):
        for a in range(3):
            re = im = None
            for b in range(3):
                lr, li = links[b][a] if adjoint else links[a][b]
                vr, vi = half[s * 3 + b]
                if adjoint:
                    tr, ti = lr * vr + li * vi, lr * vi - li * vr
                else:
                    tr, ti = lr * vr - li * vi, lr * vi + li * vr
                re = tr if re is None else re + tr
                im = ti if im is None else im + ti
            out.append((re, im))
    return out


def each(function, half):
    return [(function(re), function(im)) for re, im in half]


def load_pair(ref, index):
    block = ref[index * 16:(index + 1) * 16, :].astype(F32)
    return block[0:8], block[8:16]


def load_links(ref, mu, parity):
    links = []
    for a in range(3):
        row = []
        for b in range(3):
            k = ((mu * 3 + a) * 3 + b) * 2
            row.append((load_pair(ref, k)[parity], load_pair(ref, k + 1)[parity]))
        links.append(row)
    return links


def load_field(ref, r):
    return [load_pair(ref, r * 12 + j) for j in range(12)]


def store_pair(ref, index, pair):
    ref[index * 16:(index + 1) * 16, :] = jnp.concatenate(pair, axis=0).astype(ref.dtype)


def store_field(ref, r, field):
    for j in range(12):
        store_pair(ref, r * 12 + j, field[j])


def site_masks():
    rows = lax.broadcasted_iota(jnp.int32, (8, 128), 0)
    return rows // 4, rows % 4


def even_device(*axes):
    place = sum(lax.axis_index(axis) for axis in axes)
    return lax.broadcast(place % 2, (8, 128)) == 0


def either(even, a, b):
    return [select(even, a[i], b[i]) for i in range(2)]


def roll_rows(value, shift):
    shift %= 8
    return pltpu.roll(value, shift, 0) if shift else value


def select(mask, a, b):
    return jnp.where(mask, a, b)


def t_edges(links):
    t_idx, _ = site_masks()
    return [each(lambda v: select(t_idx == 0, roll_rows(v, 4), v), row) for row in links]


def x_edges(links):
    _, x_idx = site_masks()

    def edge(value):
        out = value
        for k in range(3):
            out = select(x_idx == k, roll_rows(value, k - 3), out)
        return out

    return [each(edge, row) for row in links]


def send_t(f_ref, links_ref, parity, t_one, t_two, ready=lambda r: None):
    even = even_device("ta")
    t_idx, _ = site_masks()
    first = t_idx == 0
    links = t_edges(load_links(links_ref, 0, parity))
    for r in range(RHS):
        ready(r)
        field = load_field(f_ref, r)
        ahead, behind = project(field, 0, -1), project(field, 0, 1)
        rears = [
            tuple(select(first, roll_rows(behind[c][i], 4), behind[c + 3][i]) for i in range(2)) for c in range(3)
        ]
        rears = matvec(links, rears, True)
        for c in range(3):
            front = [select(first, ahead[c + 3][i], roll_rows(ahead[c][i], 4)) for i in range(2)]
            store_pair(t_one, r * 3 + c, either(even, rears[c], front))
            store_pair(t_two, r * 3 + c, either(even, front, rears[c]))


def send_x_kernel(parity, f_ref, links_ref, x_far, x_near):
    even = even_device("gx")
    _, x_idx = site_masks()
    links = x_edges(load_links(links_ref, 1, parity))

    def packed(values, row, step):
        out = values[0]
        for k in range(1, 4):
            out = select(x_idx == row + step * k, roll_rows(values[k], step * k), out)
        return out

    for q in range(RHS // 2):
        fields = [load_field(f_ref, r) for r in (2 * q, 2 * q + 1)]
        ahead = [project(field, 1, -1) for field in fields]
        behind = [project(field, 1, 1) for field in fields]
        fronts, rears = [], []
        for c in range(3):
            fronts.append([packed([h[j][i] for h in ahead for j in (c, c + 3)], 0, 1) for i in range(2)])
            rears.append([packed([h[j][i] for h in behind for j in (c, c + 3)], 3, -1) for i in range(2)])
        rears = matvec(links, rears, True)
        for c in range(3):
            store_pair(x_near, q * 3 + c, either(even, rears[c], fronts[c]))
            store_pair(x_far, q * 3 + c, either(even, fronts[c], rears[c]))


def start_kernel(f_hbm, links_hbm, *refs):
    outs, (f_ref, links_ref, sems) = refs[:2], refs[2:]
    part = f_ref.shape[0] // RHS
    copies = [pltpu.make_async_copy(links_hbm.at[pl.ds(0, links_ref.shape[0])], links_ref, sems.at[RHS])]
    for r in range(RHS):
        rows = pl.ds(r * part, part)
        copies.append(pltpu.make_async_copy(f_hbm.at[rows], f_ref.at[rows], sems.at[r]))
    for copy in copies:
        copy.start()
    copies[0].wait()
    send_t(f_ref, links_ref, 0, *outs, ready=lambda r: copies[1 + r].wait())


def interior_kernel(parity, with_base, *refs):
    if with_base:
        f_ref, links_ref, base_ref, clover_ref, acc_ref = refs
        clover_to(clover_ref, lambda r: load_field(base_ref, r), acc_ref, 1.0)
    else:
        f_ref, links_ref, acc_ref = refs
    out_parity = 1 - parity
    t_idx, x_idx = site_masks()
    lane = lax.broadcasted_iota(jnp.int32, (8, 128), 1)
    odd = (t_idx + x_idx + lane // HALF_DEPTH + out_parity) % 2
    start = lane - lane % HALF_DEPTH
    up = jnp.where(odd == 1, start + (lane + 1) % HALF_DEPTH, lane)
    down = jnp.where(odd == 0, start + (lane + HALF_DEPTH - 1) % HALF_DEPTH, lane)
    zero = jnp.zeros((8, 128), F32)

    def take(value, index):
        return jnp.take_along_axis(value, index, axis=1, mode="promise_in_bounds")

    for mu in (2, 3, 0, 1):
        if mu == 2:
            ahead_of = lambda v: pltpu.roll(v, 128 - HALF_DEPTH, 1)
            behind_of = lambda v: pltpu.roll(v, HALF_DEPTH, 1)
        elif mu == 3:
            ahead_of = lambda v: take(v, up)
            behind_of = lambda v: take(v, down)
        elif mu == 0:
            ahead_of = lambda v: select(t_idx == 0, roll_rows(v, 4), 0.0)
            behind_of = lambda v: select(t_idx == 1, roll_rows(v, 4), 0.0)
        else:
            ahead_of = lambda v: select(x_idx < 3, roll_rows(v, 7), 0.0)
            behind_of = lambda v: select(x_idx > 0, roll_rows(v, 1), 0.0)
        links_out = load_links(links_ref, mu, out_parity)
        links_in = load_links(links_ref, mu, parity)
        for r in range(RHS):
            field = load_field(f_ref, r)
            if mu == 2 and not with_base:
                acc = [(zero, zero)] * 12
            else:
                acc = load_field(acc_ref, r)
            half = color(links_out, each(ahead_of, project(field, mu, -1)), False)
            acc = rebuild(acc, half, mu, -1)
            half = color(links_in, project(field, mu, 1), True)
            acc = rebuild(acc, each(behind_of, half), mu, 1)
            store_field(acc_ref, r, acc)


def clover_to(clover_ref, get_field, out_ref, scale):
    for chi in range(2):
        matrix = {}
        for i in range(6):
            for j in range(i, 6):
                k = (chi * 6 + i) * 6 + j
                block = clover_ref[k * 16:(k + 1) * 16, :].astype(F32)
                re, im = block[0:8], block[8:16]
                if scale != 1.0:
                    re, im = re * scale, im * scale
                matrix[i, j] = (re, re + im, im - re)
        for r in range(RHS):
            field = get_field(r)[chi * 6:chi * 6 + 6]
            both = [vr + vi for vr, vi in field]
            for i in range(6):
                one = two = three = None
                for j in range(6):
                    vr, vi = field[j]
                    m, plus, minus = matrix[min(i, j), max(i, j)]
                    t_one = m * both[j]
                    if i <= j:
                        t_two, t_three = -(vi * plus), vr * minus
                    else:
                        t_two, t_three = vi * minus, -(vr * plus)
                    one = t_one if one is None else one + t_one
                    two = t_two if two is None else two + t_two
                    three = t_three if three is None else three + t_three
                store_pair(out_ref, r * 12 + chi * 6 + i, (one + two, one + three))


def matvec(links, vector, adjoint):
    out = []
    for a in range(3):
        re = im = None
        for b in range(3):
            lr, li = links[b][a] if adjoint else links[a][b]
            vr, vi = vector[b]
            if adjoint:
                tr, ti = lr * vr + li * vi, lr * vi - li * vr
            else:
                tr, ti = lr * vr - li * vi, lr * vi + li * vr
            re = tr if re is None else re + tr
            im = ti if im is None else im + ti
        out.append((re, im))
    return out


def rebuild_signed(acc, half, mu, sign):
    out = list(acc)
    for j in range(6):
        out[j] = add_power(out[j], half[j], 0)
    half = each(lambda v: v * sign, half)
    for row in range(2):
        col, power = SPIN_INV[mu][row]
        for c in range(3):
            j = (2 + row) * 3 + c
            out[j] = add_power(out[j], half[col * 3 + c], power)
    return out


def join_x_kernel(parity, links_ref, acc_ref, x_far, x_near, out_ref):
    even = even_device("gx")
    _, x_idx = site_masks()
    sign = jnp.where(x_idx == 3, -1.0, 1.0).astype(F32)
    links = x_edges(load_links(links_ref, 1, 1 - parity))
    for q in range(RHS // 2):
        nxt, last = [], []
        for c in range(3):
            near, far = load_pair(x_near, q * 3 + c), load_pair(x_far, q * 3 + c)
            nxt.append(either(even, near, far))
            last.append(either(even, far, near))
        ahead = matvec(links, nxt, False)
        for r in (2 * q, 2 * q + 1):
            half = [None] * 6
            for s in range(2):
                k = (r % 2) * 2 + s
                for c in range(3):
                    half[s * 3 + c] = tuple(
                        select(
                            x_idx == 3,
                            roll_rows(ahead[c][i], 3 - k),
                            select(x_idx == 0, roll_rows(last[c][i], 5 + k), 0.0),
                        )
                        for i in range(2)
                    )
            store_field(out_ref, r, rebuild_signed(load_field(acc_ref, r), half, 1, sign))


def join_t(links_ref, acc_ref, one_hbm, two_hbm, parity, out_ref, t_one, t_two, sems, done=lambda r: None):
    even = even_device("ta")
    t_idx, _ = site_masks()
    first = t_idx == 0
    part = t_one.shape[0]
    place = lax.axis_index("ta") % 2
    copies = []
    for i, (source, slot, held) in enumerate(((one_hbm, 1 - place, t_one), (two_hbm, place, t_two))):
        rows = pl.ds(pl.multiple_of(slot * part, part), part)
        copies.append(pltpu.make_async_copy(source.at[rows], held, sems.at[i]))
        copies[i].start()
    for copy in copies:
        copy.wait()
    sign = jnp.where(first, 1.0, -1.0).astype(F32)
    links = t_edges(load_links(links_ref, 0, 1 - parity))
    for r in range(RHS):
        nxt, last = [], []
        for c in range(3):
            one, two = load_pair(t_one, r * 3 + c), load_pair(t_two, r * 3 + c)
            nxt.append(either(even, one, two))
            last.append(either(even, two, one))
        ahead = matvec(links, nxt, False)
        half = [tuple(select(first, last[c][i], ahead[c][i]) for i in range(2)) for c in range(3)]
        half += [
            tuple(roll_rows(select(first, ahead[c][i], last[c][i]), 4) for i in range(2)) for c in range(3)
        ]
        store_field(out_ref, r, rebuild_signed(load_field(acc_ref, r), half, 0, sign))
        done(r)


def odd_kernel(links_ref, clover_ref, acc_ref, t_one, t_two, out_ref, *refs):
    outs, summed, held = refs[:2], refs[2], refs[3:]
    join_t(links_ref, acc_ref, t_one, t_two, 0, summed, *held)
    clover_to(clover_ref, lambda r: load_field(summed, r), out_ref, -KAPPA2)
    send_t(out_ref, links_ref, 1, *outs)


def even_kernel(links_ref, acc_ref, t_one, t_two, out_ref, *refs):
    outs, held = refs[:2], refs[2:]
    join_t(links_ref, acc_ref, t_one, t_two, 1, out_ref, *held)
    send_t(out_ref, links_ref, 0, *outs)


def last_kernel(links_ref, acc_ref, t_one, t_two, out_hbm, held, sems, *halos):
    part = held.shape[0] // RHS
    copies = []

    def done(r):
        rows = pl.ds(r * part, part)
        copies.append(pltpu.make_async_copy(held.at[rows], out_hbm.at[rows], sems.at[r]))
        copies[-1].start()

    join_t(links_ref, acc_ref, t_one, t_two, 1, held, *halos, done=done)
    for copy in copies:
        copy.wait()


ROWS = RHS * 24 * 8
FIELD = [((ROWS, 128), F32)]
T_HALOS = [((RHS * 3 * 16, 128), BF16)] * 2
X_HALOS = [((RHS * 3 * 8, 128), BF16)] * 2


HBM_SPEC = pl.BlockSpec(memory_space=pltpu.HBM)
T_HELD = [pltpu.VMEM(T_HALOS[0][0], BF16)] * 2 + [pltpu.SemaphoreType.DMA((2,))]


def call(kernel, args, outs, flops, scratch=(), in_space=pltpu.VMEM, out_space=pltpu.VMEM, in_hbm=0):
    return pl.pallas_call(
        kernel,
        out_shape=tuple(jax.ShapeDtypeStruct(shape, dtype) for shape, dtype in outs),
        in_specs=[pl.BlockSpec(memory_space=in_space)] * (len(args) - in_hbm) + [HBM_SPEC] * in_hbm,
        out_specs=tuple([pl.BlockSpec(memory_space=out_space)] * len(outs)),
        scratch_shapes=list(scratch),
        compiler_params=pltpu.CompilerParams(vmem_limit_bytes=24 * 1024 * 1024),
        cost_estimate=pl.CostEstimate(flops=flops, bytes_accessed=2 * 1024 * 1024, transcendentals=0),
    )(*args)


def swap(value, axis, far):
    count = lax.axis_size(axis)
    assert count % 2 == 0
    pairs = [(i, (i + (1 if (i % 2 == 0) != far else -1)) % count) for i in range(count)]
    return lax.ppermute(value, axis, pairs)


def both(value, axis, far):
    count = lax.axis_size(axis)
    assert count % 2 == 0
    pairs = [[(i + far) % count, (i + far + 1) % count] for i in range(0, count, 2)]
    value = lax.all_gather(value, axis, axis_index_groups=pairs, axis=0, tiled=True)
    return pltpu.with_memory_space_constraint(value, pltpu.HBM)


def per_device(source, gauge_links, clover_even, clover_odd_inv):
    shape = source.shape
    f = source.reshape(-1, 128)
    links = gauge_links.reshape(-1, 128)
    even = clover_even.reshape(-1, 128)
    odd = clover_odd_inv.reshape(-1, 128)
    held = [pltpu.with_memory_space_constraint(v, pltpu.HBM) for v in (f, links)]
    start_scratch = [
        pltpu.VMEM((ROWS, 128), BF16),
        pltpu.VMEM((links.shape[0] // 4, 128), BF16),
        pltpu.SemaphoreType.DMA((RHS + 1,)),
    ]
    t_one, t_two = call(start_kernel, held, T_HALOS, 1_500_000, start_scratch, in_space=pltpu.HBM)
    for hop in range(4):
        parity = hop % 2
        t_one, t_two = both(t_one, "ta", 0), both(t_two, "ta", 1)
        x_far, x_near = call(
            functools.partial(send_x_kernel, parity), (f, links), X_HALOS, 1_500_000
        )
        here, x_far, x_near = lax.optimization_barrier((f, x_far, x_near))
        x_far, x_near = swap(x_far, "gx", True), swap(x_near, "gx", False)
        base = (before, even) if parity else ()
        acc, = call(
            functools.partial(interior_kernel, parity, bool(parity)),
            (here, links, *base), FIELD, 8_000_000 if parity else 5_000_000,
        )
        acc, = call(functools.partial(join_x_kernel, parity), (links, acc, x_far, x_near), FIELD, 1_000_000)
        before = f
        if parity == 0:
            f, t_one, t_two = call(
                odd_kernel, (links, odd, acc, t_one, t_two), FIELD + T_HALOS, 4_000_000,
                [pltpu.VMEM((ROWS, 128), F32)] + T_HELD, in_hbm=2,
            )
        elif hop == 1:
            f, t_one, t_two = call(
                even_kernel, (links, acc, t_one, t_two), FIELD + T_HALOS, 2_000_000, T_HELD, in_hbm=2
            )
        else:
            out, = call(
                last_kernel, (links, acc, t_one, t_two), [((ROWS, 128), BF16)], 1_000_000,
                [pltpu.VMEM((ROWS, 128), BF16), pltpu.SemaphoreType.DMA((RHS,))] + T_HELD, out_space=pltpu.HBM, in_hbm=2,
            )
    return out.reshape(shape)


def solution(mesh):
    field_spec = P(None, None, None, None, ("groups", "ta"), "gx", None)
    link_spec = P(None, None, None, None, None, ("groups", "ta"), "gx", None)
    return jax.shard_map(
        per_device,
        mesh=mesh,
        in_specs=(field_spec, link_spec, field_spec, field_spec),
        out_specs=field_spec,
        check_vma=False,
    )
```

```python
import functools

import jax
import jax.numpy as jnp
from jax import lax
from jax.experimental import pallas as pl
from jax.experimental.pallas import tpu as pltpu
from jax.sharding import PartitionSpec as P

HALF_DEPTH = 8
KAPPA2 = 0.14 * 0.14
RHS = 4
F32 = jnp.float32
BF16 = jnp.bfloat16

SPIN = (((0, 0), (1, 0)), ((1, 3), (0, 3)), ((1, 2), (0, 0)), ((0, 3), (1, 1)))
SPIN_INV = (((0, 0), (1, 0)), ((1, 1), (0, 1)), ((1, 0), (0, 2)), ((0, 1), (1, 3)))


def add_power(base, value, power):
    (br, bi), (vr, vi) = base, value
    if power == 0:
        return br + vr, bi + vi
    if power == 1:
        return br - vi, bi + vr
    if power == 2:
        return br - vr, bi - vi
    return br + vi, bi - vr


def project(field, mu, sign):
    shift = 0 if sign > 0 else 2
    half = []
    for row in range(2):
        col, power = SPIN[mu][row]
        for c in range(3):
            half.append(add_power(field[row * 3 + c], field[(2 + col) * 3 + c], (power + shift) % 4))
    return half


def rebuild(acc, half, mu, sign):
    shift = 0 if sign > 0 else 2
    out = list(acc)
    for j in range(6):
        out[j] = add_power(out[j], half[j], 0)
    for row in range(2):
        col, power = SPIN_INV[mu][row]
        for c in range(3):
            j = (2 + row) * 3 + c
            out[j] = add_power(out[j], half[col * 3 + c], (power + shift) % 4)
    return out


def color(links, half, adjoint):
    out = []
    for s in range(2):
        for a in range(3):
            re = im = None
            for b in range(3):
                lr, li = links[b][a] if adjoint else links[a][b]
                vr, vi = half[s * 3 + b]
                if adjoint:
                    tr, ti = lr * vr + li * vi, lr * vi - li * vr
                else:
                    tr, ti = lr * vr - li * vi, lr * vi + li * vr
                re = tr if re is None else re + tr
                im = ti if im is None else im + ti
            out.append((re, im))
    return out


def each(function, half):
    return [(function(re), function(im)) for re, im in half]


def load_pair(ref, index):
    block = ref[index * 16:(index + 1) * 16, :].astype(F32)
    return block[0:8], block[8:16]


def load_links(ref, mu, parity):
    links = []
    for a in range(3):
        row = []
        for b in range(3):
            k = ((mu * 3 + a) * 3 + b) * 2
            row.append((load_pair(ref, k)[parity], load_pair(ref, k + 1)[parity]))
        links.append(row)
    return links


def load_field(ref, r):
    return [load_pair(ref, r * 12 + j) for j in range(12)]


def store_pair(ref, index, pair):
    ref[index * 16:(index + 1) * 16, :] = jnp.concatenate(pair, axis=0).astype(ref.dtype)


def store_field(ref, r, field):
    for j in range(12):
        store_pair(ref, r * 12 + j, field[j])


def site_masks():
    rows = lax.broadcasted_iota(jnp.int32, (8, 128), 0)
    return rows // 4, rows % 4


def roll_rows(value, shift):
    shift %= 8
    return pltpu.roll(value, shift, 0) if shift else value


def select(mask, a, b):
    return jnp.where(mask, a, b)


def t_edges(links):
    t_idx, _ = site_masks()
    return [each(lambda v: select(t_idx == 0, roll_rows(v, 4), v), row) for row in links]


def x_edges(links):
    _, x_idx = site_masks()

    def edge(value):
        out = value
        for k in range(3):
            out = select(x_idx == k, roll_rows(value, k - 3), out)
        return out

    return [each(edge, row) for row in links]


def slots(ref, axis, count):
    rows = ref.shape[0] // count
    me = lax.axis_index(axis)
    return [pl.multiple_of(lax.rem(me + step, count) * rows, rows) for step in (1, count - 1)]


def store_slot(ref, base, index, pair):
    ref[pl.ds(base + index * 16, 16), :] = jnp.concatenate(pair, axis=0).astype(ref.dtype)


def load_slot(ref, base, index):
    block = ref[pl.ds(base + index * 16, 16), :].astype(F32)
    return block[0:8], block[8:16]


def send_t(f_ref, links_ref, parity, out_ref, count, ready=lambda r: None):
    to_next, to_last = slots(out_ref, "ta", count)
    out_ref[...] = jnp.zeros_like(out_ref)
    t_idx, _ = site_masks()
    first = t_idx == 0
    links = t_edges(load_links(links_ref, 0, parity))
    for r in range(RHS):
        ready(r)
        field = load_field(f_ref, r)
        ahead, behind = project(field, 0, -1), project(field, 0, 1)
        rears = [
            tuple(select(first, roll_rows(behind[c][i], 4), behind[c + 3][i]) for i in range(2)) for c in range(3)
        ]
        rears = matvec(links, rears, True)
        for c in range(3):
            front = [select(first, ahead[c + 3][i], roll_rows(ahead[c][i], 4)) for i in range(2)]
            store_slot(out_ref, to_next, r * 3 + c, rears[c])
            store_slot(out_ref, to_last, r * 3 + c, front)


def send_x_kernel(parity, count, f_ref, links_ref, out_ref):
    to_next, to_last = slots(out_ref, "gx", count)
    out_ref[...] = jnp.zeros_like(out_ref)
    _, x_idx = site_masks()
    links = x_edges(load_links(links_ref, 1, parity))

    def packed(values, row, step):
        out = values[0]
        for k in range(1, 4):
            out = select(x_idx == row + step * k, roll_rows(values[k], step * k), out)
        return out

    for q in range(RHS // 2):
        fields = [load_field(f_ref, r) for r in (2 * q, 2 * q + 1)]
        ahead = [project(field, 1, -1) for field in fields]
        behind = [project(field, 1, 1) for field in fields]
        fronts, rears = [], []
        for c in range(3):
            fronts.append([packed([h[j][i] for h in ahead for j in (c, c + 3)], 0, 1) for i in range(2)])
            rears.append([packed([h[j][i] for h in behind for j in (c, c + 3)], 3, -1) for i in range(2)])
        rears = matvec(links, rears, True)
        for c in range(3):
            store_slot(out_ref, to_next, q * 3 + c, rears[c])
            store_slot(out_ref, to_last, q * 3 + c, fronts[c])


def start_kernel(count, f_hbm, links_hbm, *refs):
    out_ref, f_ref, links_ref, sems = refs
    part = f_ref.shape[0] // RHS
    copies = [pltpu.make_async_copy(links_hbm.at[pl.ds(0, links_ref.shape[0])], links_ref, sems.at[RHS])]
    for r in range(RHS):
        rows = pl.ds(r * part, part)
        copies.append(pltpu.make_async_copy(f_hbm.at[rows], f_ref.at[rows], sems.at[r]))
    for copy in copies:
        copy.start()
    copies[0].wait()
    send_t(f_ref, links_ref, 0, out_ref, count, ready=lambda r: copies[1 + r].wait())


def interior_kernel(parity, with_base, *refs):
    if with_base:
        f_ref, links_ref, base_ref, clover_ref, acc_ref = refs
        clover_to(clover_ref, lambda r: load_field(base_ref, r), acc_ref, 1.0)
    else:
        f_ref, links_ref, acc_ref = refs
    out_parity = 1 - parity
    t_idx, x_idx = site_masks()
    lane = lax.broadcasted_iota(jnp.int32, (8, 128), 1)
    odd = (t_idx + x_idx + lane // HALF_DEPTH + out_parity) % 2
    start = lane - lane % HALF_DEPTH
    up = jnp.where(odd == 1, start + (lane + 1) % HALF_DEPTH, lane)
    down = jnp.where(odd == 0, start + (lane + HALF_DEPTH - 1) % HALF_DEPTH, lane)
    zero = jnp.zeros((8, 128), F32)

    def take(value, index):
        return jnp.take_along_axis(value, index, axis=1, mode="promise_in_bounds")

    for mu in (2, 3, 0, 1):
        if mu == 2:
            ahead_of = lambda v: pltpu.roll(v, 128 - HALF_DEPTH, 1)
            behind_of = lambda v: pltpu.roll(v, HALF_DEPTH, 1)
        elif mu == 3:
            ahead_of = lambda v: take(v, up)
            behind_of = lambda v: take(v, down)
        elif mu == 0:
            ahead_of = lambda v: select(t_idx == 0, roll_rows(v, 4), 0.0)
            behind_of = lambda v: select(t_idx == 1, roll_rows(v, 4), 0.0)
        else:
            ahead_of = lambda v: select(x_idx < 3, roll_rows(v, 7), 0.0)
            behind_of = lambda v: select(x_idx > 0, roll_rows(v, 1), 0.0)
        links_out = load_links(links_ref, mu, out_parity)
        links_in = load_links(links_ref, mu, parity)
        for r in range(RHS):
            field = load_field(f_ref, r)
            if mu == 2 and not with_base:
                acc = [(zero, zero)] * 12
            else:
                acc = load_field(acc_ref, r)
            half = color(links_out, each(ahead_of, project(field, mu, -1)), False)
            acc = rebuild(acc, half, mu, -1)
            half = color(links_in, project(field, mu, 1), True)
            acc = rebuild(acc, each(behind_of, half), mu, 1)
            store_field(acc_ref, r, acc)


def clover_to(clover_ref, get_field, out_ref, scale):
    for chi in range(2):
        matrix = {}
        for i in range(6):
            for j in range(i, 6):
                k = (chi * 6 + i) * 6 + j
                block = clover_ref[k * 16:(k + 1) * 16, :].astype(F32)
                re, im = block[0:8], block[8:16]
                if scale != 1.0:
                    re, im = re * scale, im * scale
                matrix[i, j] = (re, re + im, im - re)
        for r in range(RHS):
            field = get_field(r)[chi * 6:chi * 6 + 6]
            both = [vr + vi for vr, vi in field]
            for i in range(6):
                one = two = three = None
                for j in range(6):
                    vr, vi = field[j]
                    m, plus, minus = matrix[min(i, j), max(i, j)]
                    t_one = m * both[j]
                    if i <= j:
                        t_two, t_three = -(vi * plus), vr * minus
                    else:
                        t_two, t_three = vi * minus, -(vr * plus)
                    one = t_one if one is None else one + t_one
                    two = t_two if two is None else two + t_two
                    three = t_three if three is None else three + t_three
                store_pair(out_ref, r * 12 + chi * 6 + i, (one + two, one + three))


def matvec(links, vector, adjoint):
    out = []
    for a in range(3):
        re = im = None
        for b in range(3):
            lr, li = links[b][a] if adjoint else links[a][b]
            vr, vi = vector[b]
            if adjoint:
                tr, ti = lr * vr + li * vi, lr * vi - li * vr
            else:
                tr, ti = lr * vr - li * vi, lr * vi + li * vr
            re = tr if re is None else re + tr
            im = ti if im is None else im + ti
        out.append((re, im))
    return out


def rebuild_signed(acc, half, mu, sign):
    out = list(acc)
    for j in range(6):
        out[j] = add_power(out[j], half[j], 0)
    half = each(lambda v: v * sign, half)
    for row in range(2):
        col, power = SPIN_INV[mu][row]
        for c in range(3):
            j = (2 + row) * 3 + c
            out[j] = add_power(out[j], half[col * 3 + c], power)
    return out


def join_x_kernel(parity, count, links_ref, acc_ref, x_ref, out_ref):
    from_next, from_last = slots(x_ref, "gx", count)
    _, x_idx = site_masks()
    sign = jnp.where(x_idx == 3, -1.0, 1.0).astype(F32)
    links = x_edges(load_links(links_ref, 1, 1 - parity))
    for q in range(RHS // 2):
        nxt, last = [], []
        for c in range(3):
            nxt.append(load_slot(x_ref, from_next, q * 3 + c))
            last.append(load_slot(x_ref, from_last, q * 3 + c))
        ahead = matvec(links, nxt, False)
        for r in (2 * q, 2 * q + 1):
            half = [None] * 6
            for s in range(2):
                k = (r % 2) * 2 + s
                for c in range(3):
                    half[s * 3 + c] = tuple(
                        select(
                            x_idx == 3,
                            roll_rows(ahead[c][i], 3 - k),
                            select(x_idx == 0, roll_rows(last[c][i], 5 + k), 0.0),
                        )
                        for i in range(2)
                    )
            store_field(out_ref, r, rebuild_signed(load_field(acc_ref, r), half, 1, sign))


def join_t(links_ref, acc_ref, t_ref, parity, out_ref, count, done=lambda r: None):
    from_next, from_last = slots(t_ref, "ta", count)
    t_idx, _ = site_masks()
    first = t_idx == 0
    sign = jnp.where(first, 1.0, -1.0).astype(F32)
    links = t_edges(load_links(links_ref, 0, 1 - parity))
    for r in range(RHS):
        nxt, last = [], []
        for c in range(3):
            nxt.append(load_slot(t_ref, from_next, r * 3 + c))
            last.append(load_slot(t_ref, from_last, r * 3 + c))
        ahead = matvec(links, nxt, False)
        half = [tuple(select(first, last[c][i], ahead[c][i]) for i in range(2)) for c in range(3)]
        half += [
            tuple(roll_rows(select(first, ahead[c][i], last[c][i]), 4) for i in range(2)) for c in range(3)
        ]
        store_field(out_ref, r, rebuild_signed(load_field(acc_ref, r), half, 0, sign))
        done(r)


def odd_kernel(count, links_ref, clover_ref, acc_ref, t_ref, out_ref, halo_ref, summed):
    join_t(links_ref, acc_ref, t_ref, 0, summed, count)
    clover_to(clover_ref, lambda r: load_field(summed, r), out_ref, -KAPPA2)
    send_t(out_ref, links_ref, 1, halo_ref, count)


def even_kernel(count, links_ref, acc_ref, t_ref, out_ref, halo_ref):
    join_t(links_ref, acc_ref, t_ref, 1, out_ref, count)
    send_t(out_ref, links_ref, 0, halo_ref, count)


def last_kernel(count, links_ref, acc_ref, t_ref, out_hbm, held, sems):
    part = held.shape[0] // RHS
    copies = []

    def done(r):
        rows = pl.ds(r * part, part)
        copies.append(pltpu.make_async_copy(held.at[rows], out_hbm.at[rows], sems.at[r]))
        copies[-1].start()

    join_t(links_ref, acc_ref, t_ref, 1, held, count, done)
    for copy in copies:
        copy.wait()


ROWS = RHS * 24 * 8
FIELD = [((ROWS, 128), F32)]
def call(kernel, args, outs, flops, scratch=(), in_space=pltpu.VMEM, out_space=pltpu.VMEM):
    return pl.pallas_call(
        kernel,
        out_shape=tuple(jax.ShapeDtypeStruct(shape, dtype) for shape, dtype in outs),
        in_specs=[pl.BlockSpec(memory_space=in_space)] * len(args),
        out_specs=tuple([pl.BlockSpec(memory_space=out_space)] * len(outs)),
        scratch_shapes=list(scratch),
        compiler_params=pltpu.CompilerParams(vmem_limit_bytes=24 * 1024 * 1024),
        cost_estimate=pl.CostEstimate(flops=flops, bytes_accessed=2 * 1024 * 1024, transcendentals=0),
    )(*args)


def slot_shape(count, rows):
    return [((count * rows, 128), BF16)]


def per_device(source, gauge_links, clover_even, clover_odd_inv):
    shape = source.shape
    across_t, across_x = lax.axis_size("ta"), lax.axis_size("gx")
    t_shape, x_shape = slot_shape(across_t, RHS * 3 * 16), slot_shape(across_x, RHS * 3 * 8)
    f = source.reshape(-1, 128)
    links = gauge_links.reshape(-1, 128)
    even = clover_even.reshape(-1, 128)
    odd = clover_odd_inv.reshape(-1, 128)
    held = [pltpu.with_memory_space_constraint(v, pltpu.HBM) for v in (f, links)]
    start_scratch = [
        pltpu.VMEM((ROWS, 128), BF16),
        pltpu.VMEM((links.shape[0] // 4, 128), BF16),
        pltpu.SemaphoreType.DMA((RHS + 1,)),
    ]
    t_halos, = call(functools.partial(start_kernel, across_t), held, t_shape, 1_500_000, start_scratch, in_space=pltpu.HBM)
    for hop in range(4):
        parity = hop % 2
        t_halos = lax.all_to_all(t_halos, "ta", 0, 0, tiled=True)
        x_halos, = call(functools.partial(send_x_kernel, parity, across_x), (f, links), x_shape, 1_500_000)
        here, x_halos = lax.optimization_barrier((f, x_halos))
        x_halos = lax.all_to_all(x_halos, "gx", 0, 0, tiled=True)
        base = (before, even) if parity else ()
        acc, = call(
            functools.partial(interior_kernel, parity, bool(parity)),
            (here, links, *base), FIELD, 8_000_000 if parity else 5_000_000,
        )
        acc, = call(functools.partial(join_x_kernel, parity, across_x), (links, acc, x_halos), FIELD, 1_000_000)
        before = f
        if parity == 0:
            f, t_halos = call(
                functools.partial(odd_kernel, across_t), (links, odd, acc, t_halos), FIELD + t_shape, 4_000_000,
                [pltpu.VMEM((ROWS, 128), F32)],
            )
        elif hop == 1:
            f, t_halos = call(
                functools.partial(even_kernel, across_t), (links, acc, t_halos), FIELD + t_shape, 2_000_000
            )
        else:
            out, = call(
                functools.partial(last_kernel, across_t), (links, acc, t_halos), [((ROWS, 128), BF16)], 1_000_000,
                [pltpu.VMEM((ROWS, 128), BF16), pltpu.SemaphoreType.DMA((RHS,))], out_space=pltpu.HBM,
            )
    return out.reshape(shape)


def solution(mesh):
    field_spec = P(None, None, None, None, ("groups", "ta"), "gx", None)
    link_spec = P(None, None, None, None, None, ("groups", "ta"), "gx", None)
    return jax.shard_map(
        per_device,
        mesh=mesh,
        in_specs=(field_spec, link_spec, field_spec, field_spec),
        out_specs=field_spec,
        check_vma=False,
    )
```

```python
import functools

import jax
import jax.numpy as jnp
from jax import lax
from jax.experimental import pallas as pl
from jax.experimental.pallas import tpu as pltpu
from jax.sharding import PartitionSpec as P

HALF_DEPTH = 8
KAPPA2 = 0.14 * 0.14
RHS = 4
F32 = jnp.float32
BF16 = jnp.bfloat16

SPIN = (((0, 0), (1, 0)), ((1, 3), (0, 3)), ((1, 2), (0, 0)), ((0, 3), (1, 1)))
SPIN_INV = (((0, 0), (1, 0)), ((1, 1), (0, 1)), ((1, 0), (0, 2)), ((0, 1), (1, 3)))


def add_power(base, value, power):
    (br, bi), (vr, vi) = base, value
    if power == 0:
        return br + vr, bi + vi
    if power == 1:
        return br - vi, bi + vr
    if power == 2:
        return br - vr, bi - vi
    return br + vi, bi - vr


def project(field, mu, sign):
    shift = 0 if sign > 0 else 2
    half = []
    for row in range(2):
        col, power = SPIN[mu][row]
        for c in range(3):
            half.append(add_power(field[row * 3 + c], field[(2 + col) * 3 + c], (power + shift) % 4))
    return half


def rebuild(acc, half, mu, sign):
    shift = 0 if sign > 0 else 2
    out = list(acc)
    for j in range(6):
        out[j] = add_power(out[j], half[j], 0)
    for row in range(2):
        col, power = SPIN_INV[mu][row]
        for c in range(3):
            j = (2 + row) * 3 + c
            out[j] = add_power(out[j], half[col * 3 + c], (power + shift) % 4)
    return out


def color(links, half, adjoint):
    out = []
    for s in range(2):
        for a in range(3):
            re = im = None
            for b in range(3):
                lr, li = links[b][a] if adjoint else links[a][b]
                vr, vi = half[s * 3 + b]
                if adjoint:
                    tr, ti = lr * vr + li * vi, lr * vi - li * vr
                else:
                    tr, ti = lr * vr - li * vi, lr * vi + li * vr
                re = tr if re is None else re + tr
                im = ti if im is None else im + ti
            out.append((re, im))
    return out


def each(function, half):
    return [(function(re), function(im)) for re, im in half]


def block_rows(index):
    if isinstance(index, int):
        return slice(index * 16, (index + 1) * 16)
    return pl.ds(pl.multiple_of(index * 16, 16), 16)


def loop(count, body):
    lax.fori_loop(0, count, lambda i, carry: (body(i), carry)[1], 0)


def load_pair(ref, index):
    block = ref[block_rows(index), :].astype(F32)
    return block[0:8], block[8:16]


def load_links(ref, mu, parity):
    links = []
    for a in range(3):
        row = []
        for b in range(3):
            k = ((mu * 3 + a) * 3 + b) * 2
            row.append((load_pair(ref, k)[parity], load_pair(ref, k + 1)[parity]))
        links.append(row)
    return links


def load_field(ref, r):
    return [load_pair(ref, r * 12 + j) for j in range(12)]


def store_pair(ref, index, pair):
    ref[block_rows(index), :] = jnp.concatenate(pair, axis=0).astype(ref.dtype)


def store_field(ref, r, field):
    for j in range(12):
        store_pair(ref, r * 12 + j, field[j])


def site_masks():
    rows = lax.broadcasted_iota(jnp.int32, (8, 128), 0)
    return rows // 4, rows % 4


def even_device(*axes):
    place = sum(lax.axis_index(axis) for axis in axes)
    return lax.broadcast(place % 2, (8, 128)) == 0


def either(even, a, b):
    return [select(even, a[i], b[i]) for i in range(2)]


def roll_rows(value, shift):
    shift %= 8
    return pltpu.roll(value, shift, 0) if shift else value


def select(mask, a, b):
    return jnp.where(mask, a, b)


def t_edges(links):
    t_idx, _ = site_masks()
    return [each(lambda v: select(t_idx == 0, roll_rows(v, 4), v), row) for row in links]


def x_edges(links):
    _, x_idx = site_masks()

    def edge(value):
        out = value
        for k in range(3):
            out = select(x_idx == k, roll_rows(value, k - 3), out)
        return out

    return [each(edge, row) for row in links]


def send_t(f_ref, links_ref, parity, t_one, t_two, ready=lambda r: None):
    even = even_device("ta", "gx")
    t_idx, _ = site_masks()
    first = t_idx == 0
    links = t_edges(load_links(links_ref, 0, parity))
    @functools.partial(loop, RHS)
    def _(r):
        ready(r)
        field = load_field(f_ref, r)
        ahead, behind = project(field, 0, -1), project(field, 0, 1)
        rears = [
            tuple(select(first, roll_rows(behind[c][i], 4), behind[c + 3][i]) for i in range(2)) for c in range(3)
        ]
        rears = matvec(links, rears, True)
        for c in range(3):
            front = [select(first, ahead[c + 3][i], roll_rows(ahead[c][i], 4)) for i in range(2)]
            store_pair(t_one, r * 3 + c, either(even, rears[c], front))
            store_pair(t_two, r * 3 + c, either(even, front, rears[c]))


def send_x_kernel(parity, f_ref, links_ref, x_far, x_near):
    even = even_device("gx")
    _, x_idx = site_masks()
    links = x_edges(load_links(links_ref, 1, parity))

    def packed(values, row, step):
        out = values[0]
        for k in range(1, 4):
            out = select(x_idx == row + step * k, roll_rows(values[k], step * k), out)
        return out

    @functools.partial(loop, RHS // 2)
    def _(q):
        fields = [load_field(f_ref, r) for r in (2 * q, 2 * q + 1)]
        ahead = [project(field, 1, -1) for field in fields]
        behind = [project(field, 1, 1) for field in fields]
        fronts, rears = [], []
        for c in range(3):
            fronts.append([packed([h[j][i] for h in ahead for j in (c, c + 3)], 0, 1) for i in range(2)])
            rears.append([packed([h[j][i] for h in behind for j in (c, c + 3)], 3, -1) for i in range(2)])
        rears = matvec(links, rears, True)
        for c in range(3):
            store_pair(x_near, q * 3 + c, either(even, rears[c], fronts[c]))
            store_pair(x_far, q * 3 + c, either(even, fronts[c], rears[c]))


def start_kernel(f_hbm, links_hbm, *refs):
    outs, (f_ref, links_ref, sems) = refs[:2], refs[2:]
    part = f_ref.shape[0] // RHS

    def copy_of(r):
        rows = pl.ds(pl.multiple_of(r * part, part), part)
        return pltpu.make_async_copy(f_hbm.at[rows], f_ref.at[rows], sems.at[r])

    link_copy = pltpu.make_async_copy(links_hbm.at[pl.ds(0, links_ref.shape[0])], links_ref, sems.at[RHS])
    link_copy.start()
    for r in range(RHS):
        copy_of(r).start()
    link_copy.wait()
    send_t(f_ref, links_ref, 0, *outs, ready=lambda r: copy_of(r).wait())


def interior_kernel(parity, with_base, *refs):
    if with_base:
        f_ref, links_ref, base_ref, clover_ref, acc_ref = refs
        clover_to(clover_ref, lambda r: load_field(base_ref, r), acc_ref, 1.0)
    else:
        f_ref, links_ref, acc_ref = refs
    out_parity = 1 - parity
    t_idx, x_idx = site_masks()
    lane = lax.broadcasted_iota(jnp.int32, (8, 128), 1)
    odd = (t_idx + x_idx + lane // HALF_DEPTH + out_parity) % 2
    start = lane - lane % HALF_DEPTH
    up = jnp.where(odd == 1, start + (lane + 1) % HALF_DEPTH, lane)
    down = jnp.where(odd == 0, start + (lane + HALF_DEPTH - 1) % HALF_DEPTH, lane)
    zero = jnp.zeros((8, 128), F32)

    def take(value, index):
        return jnp.take_along_axis(value, index, axis=1, mode="promise_in_bounds")

    for mu in (2, 3, 0, 1):
        if mu == 2:
            ahead_of = lambda v: pltpu.roll(v, 128 - HALF_DEPTH, 1)
            behind_of = lambda v: pltpu.roll(v, HALF_DEPTH, 1)
        elif mu == 3:
            ahead_of = lambda v: take(v, up)
            behind_of = lambda v: take(v, down)
        elif mu == 0:
            ahead_of = lambda v: select(t_idx == 0, roll_rows(v, 4), 0.0)
            behind_of = lambda v: select(t_idx == 1, roll_rows(v, 4), 0.0)
        else:
            ahead_of = lambda v: select(x_idx < 3, roll_rows(v, 7), 0.0)
            behind_of = lambda v: select(x_idx > 0, roll_rows(v, 1), 0.0)
        links_out = load_links(links_ref, mu, out_parity)
        links_in = load_links(links_ref, mu, parity)
        @functools.partial(loop, RHS)
        def _(r):
            field = load_field(f_ref, r)
            if mu == 2 and not with_base:
                acc = [(zero, zero)] * 12
            else:
                acc = load_field(acc_ref, r)
            half = color(links_out, each(ahead_of, project(field, mu, -1)), False)
            acc = rebuild(acc, half, mu, -1)
            half = color(links_in, project(field, mu, 1), True)
            acc = rebuild(acc, each(behind_of, half), mu, 1)
            store_field(acc_ref, r, acc)


def clover_to(clover_ref, get_field, out_ref, scale):
    for chi in range(2):
        matrix = {}
        for i in range(6):
            for j in range(i, 6):
                k = (chi * 6 + i) * 6 + j
                block = clover_ref[k * 16:(k + 1) * 16, :].astype(F32)
                re, im = block[0:8], block[8:16]
                if scale != 1.0:
                    re, im = re * scale, im * scale
                matrix[i, j] = (re, re + im, im - re)
        @functools.partial(loop, RHS)
        def _(r):
            field = get_field(r)[chi * 6:chi * 6 + 6]
            both = [vr + vi for vr, vi in field]
            for i in range(6):
                one = two = three = None
                for j in range(6):
                    vr, vi = field[j]
                    m, plus, minus = matrix[min(i, j), max(i, j)]
                    t_one = m * both[j]
                    if i <= j:
                        t_two, t_three = -(vi * plus), vr * minus
                    else:
                        t_two, t_three = vi * minus, -(vr * plus)
                    one = t_one if one is None else one + t_one
                    two = t_two if two is None else two + t_two
                    three = t_three if three is None else three + t_three
                store_pair(out_ref, r * 12 + chi * 6 + i, (one + two, one + three))


def matvec(links, vector, adjoint):
    out = []
    for a in range(3):
        re = im = None
        for b in range(3):
            lr, li = links[b][a] if adjoint else links[a][b]
            vr, vi = vector[b]
            if adjoint:
                tr, ti = lr * vr + li * vi, lr * vi - li * vr
            else:
                tr, ti = lr * vr - li * vi, lr * vi + li * vr
            re = tr if re is None else re + tr
            im = ti if im is None else im + ti
        out.append((re, im))
    return out


def rebuild_signed(acc, half, mu, sign):
    out = list(acc)
    for j in range(6):
        out[j] = add_power(out[j], half[j], 0)
    half = each(lambda v: v * sign, half)
    for row in range(2):
        col, power = SPIN_INV[mu][row]
        for c in range(3):
            j = (2 + row) * 3 + c
            out[j] = add_power(out[j], half[col * 3 + c], power)
    return out


def join_x_kernel(parity, links_ref, acc_ref, x_far, x_near, out_ref):
    even = even_device("gx")
    _, x_idx = site_masks()
    sign = jnp.where(x_idx == 3, -1.0, 1.0).astype(F32)
    links = x_edges(load_links(links_ref, 1, 1 - parity))
    @functools.partial(loop, RHS // 2)
    def _(q):
        nxt, last = [], []
        for c in range(3):
            near, far = load_pair(x_near, q * 3 + c), load_pair(x_far, q * 3 + c)
            nxt.append(either(even, near, far))
            last.append(either(even, far, near))
        ahead = matvec(links, nxt, False)
        for n, r in enumerate((2 * q, 2 * q + 1)):
            half = [None] * 6
            for s in range(2):
                k = n * 2 + s
                for c in range(3):
                    half[s * 3 + c] = tuple(
                        select(
                            x_idx == 3,
                            roll_rows(ahead[c][i], 3 - k),
                            select(x_idx == 0, roll_rows(last[c][i], 5 + k), 0.0),
                        )
                        for i in range(2)
                    )
            store_field(out_ref, r, rebuild_signed(load_field(acc_ref, r), half, 1, sign))


def join_t(links_ref, acc_ref, t_one, t_two, parity, out_ref, done=lambda r: None):
    even = even_device("ta", "gx")
    t_idx, _ = site_masks()
    first = t_idx == 0
    sign = jnp.where(first, 1.0, -1.0).astype(F32)
    links = t_edges(load_links(links_ref, 0, 1 - parity))
    @functools.partial(loop, RHS)
    def _(r):
        nxt, last = [], []
        for c in range(3):
            one, two = load_pair(t_one, r * 3 + c), load_pair(t_two, r * 3 + c)
            nxt.append(either(even, one, two))
            last.append(either(even, two, one))
        ahead = matvec(links, nxt, False)
        half = [tuple(select(first, last[c][i], ahead[c][i]) for i in range(2)) for c in range(3)]
        half += [
            tuple(roll_rows(select(first, ahead[c][i], last[c][i]), 4) for i in range(2)) for c in range(3)
        ]
        store_field(out_ref, r, rebuild_signed(load_field(acc_ref, r), half, 0, sign))
        done(r)


def odd_kernel(links_ref, clover_ref, acc_ref, t_one, t_two, out_ref, *refs):
    outs, summed = refs[:2], refs[2]
    join_t(links_ref, acc_ref, t_one, t_two, 0, summed)
    clover_to(clover_ref, lambda r: load_field(summed, r), out_ref, -KAPPA2)
    send_t(out_ref, links_ref, 1, *outs)


def even_kernel(links_ref, acc_ref, t_one, t_two, out_ref, *outs):
    join_t(links_ref, acc_ref, t_one, t_two, 1, out_ref)
    send_t(out_ref, links_ref, 0, *outs)


def last_kernel(links_ref, acc_ref, t_one, t_two, out_hbm, held, sems):
    part = held.shape[0] // RHS

    def copy_of(r):
        rows = pl.ds(pl.multiple_of(r * part, part), part)
        return pltpu.make_async_copy(held.at[rows], out_hbm.at[rows], sems.at[r])

    join_t(links_ref, acc_ref, t_one, t_two, 1, held, lambda r: copy_of(r).start())
    for r in range(RHS):
        copy_of(r).wait()


ROWS = RHS * 24 * 8
FIELD = [((ROWS, 128), F32)]
T_HALOS = [((RHS * 3 * 16, 128), BF16)] * 2
X_HALOS = [((RHS * 3 * 8, 128), BF16)] * 2


def call(kernel, args, outs, flops, scratch=(), in_space=pltpu.VMEM, out_space=pltpu.VMEM):
    return pl.pallas_call(
        kernel,
        out_shape=tuple(jax.ShapeDtypeStruct(shape, dtype) for shape, dtype in outs),
        in_specs=[pl.BlockSpec(memory_space=in_space)] * len(args),
        out_specs=tuple([pl.BlockSpec(memory_space=out_space)] * len(outs)),
        scratch_shapes=list(scratch),
        compiler_params=pltpu.CompilerParams(vmem_limit_bytes=24 * 1024 * 1024),
        cost_estimate=pl.CostEstimate(flops=flops, bytes_accessed=2 * 1024 * 1024, transcendentals=0),
    )(*args)


def swap(value, axis, far):
    count = lax.axis_size(axis)
    assert count % 2 == 0
    pairs = [(i, (i + (1 if (i % 2 == 0) != far else -1)) % count) for i in range(count)]
    return lax.ppermute(value, axis, pairs)


def swap_t(value, ahead):
    count, across = lax.axis_size("ta"), lax.axis_size("gx")
    assert count % 2 == 0 and across % 2 == 0
    pairs = []
    for i in range(count):
        for j in range(across):
            step = 1 if ((i + j) % 2 == 0) == ahead else -1
            pairs.append((i * across + j, (i + step) % count * across + j))
    return lax.ppermute(value, ("ta", "gx"), pairs)


def per_device(source, gauge_links, clover_even, clover_odd_inv):
    shape = source.shape
    f = source.reshape(-1, 128)
    links = gauge_links.reshape(-1, 128)
    even = clover_even.reshape(-1, 128)
    odd = clover_odd_inv.reshape(-1, 128)
    held = [pltpu.with_memory_space_constraint(v, pltpu.HBM) for v in (f, links)]
    start_scratch = [
        pltpu.VMEM((ROWS, 128), BF16),
        pltpu.VMEM((links.shape[0] // 4, 128), BF16),
        pltpu.SemaphoreType.DMA((RHS + 1,)),
    ]
    t_one, t_two = call(start_kernel, held, T_HALOS, 1_500_000, start_scratch, in_space=pltpu.HBM)
    for hop in range(4):
        parity = hop % 2
        t_one, t_two = swap_t(t_one, True), swap_t(t_two, False)
        x_far, x_near = call(
            functools.partial(send_x_kernel, parity), (f, links), X_HALOS, 1_500_000
        )
        here, x_far, x_near = lax.optimization_barrier((f, x_far, x_near))
        x_far, x_near = swap(x_far, "gx", True), swap(x_near, "gx", False)
        base = (before, even) if parity else ()
        acc, = call(
            functools.partial(interior_kernel, parity, bool(parity)),
            (here, links, *base), FIELD, 8_000_000 if parity else 5_000_000,
        )
        acc, = call(functools.partial(join_x_kernel, parity), (links, acc, x_far, x_near), FIELD, 1_000_000)
        before = f
        if parity == 0:
            f, t_one, t_two = call(
                odd_kernel, (links, odd, acc, t_one, t_two), FIELD + T_HALOS, 4_000_000,
                [pltpu.VMEM((ROWS, 128), F32)],
            )
        elif hop == 1:
            f, t_one, t_two = call(
                even_kernel, (links, acc, t_one, t_two), FIELD + T_HALOS, 2_000_000
            )
        else:
            out, = call(
                last_kernel, (links, acc, t_one, t_two), [((ROWS, 128), BF16)], 1_000_000,
                [pltpu.VMEM((ROWS, 128), BF16), pltpu.SemaphoreType.DMA((RHS,))], out_space=pltpu.HBM,
            )
    return out.reshape(shape)


def solution(mesh):
    field_spec = P(None, None, None, None, ("groups", "ta"), "gx", None)
    link_spec = P(None, None, None, None, None, ("groups", "ta"), "gx", None)
    return jax.shard_map(
        per_device,
        mesh=mesh,
        in_specs=(field_spec, link_spec, field_spec, field_spec),
        out_specs=field_spec,
        check_vma=False,
    )
```

```python
import functools

import jax
import jax.numpy as jnp
from jax import lax
from jax.experimental import pallas as pl
from jax.experimental.pallas import tpu as pltpu
from jax.sharding import PartitionSpec as P

HALF_DEPTH = 8
KAPPA2 = 0.14 * 0.14
RHS = 4
F32 = jnp.float32
BF16 = jnp.bfloat16

SPIN = (((0, 0), (1, 0)), ((1, 3), (0, 3)), ((1, 2), (0, 0)), ((0, 3), (1, 1)))
SPIN_INV = (((0, 0), (1, 0)), ((1, 1), (0, 1)), ((1, 0), (0, 2)), ((0, 1), (1, 3)))


def add_power(base, value, power):
    (br, bi), (vr, vi) = base, value
    if power == 0:
        return br + vr, bi + vi
    if power == 1:
        return br - vi, bi + vr
    if power == 2:
        return br - vr, bi - vi
    return br + vi, bi - vr


def project(field, mu, sign):
    shift = 0 if sign > 0 else 2
    half = []
    for row in range(2):
        col, power = SPIN[mu][row]
        for c in range(3):
            half.append(add_power(field[row * 3 + c], field[(2 + col) * 3 + c], (power + shift) % 4))
    return half


def rebuild(acc, half, mu, sign):
    shift = 0 if sign > 0 else 2
    out = list(acc)
    for j in range(6):
        out[j] = add_power(out[j], half[j], 0)
    for row in range(2):
        col, power = SPIN_INV[mu][row]
        for c in range(3):
            j = (2 + row) * 3 + c
            out[j] = add_power(out[j], half[col * 3 + c], (power + shift) % 4)
    return out


def color(links, half, adjoint):
    out = []
    for s in range(2):
        for a in range(3):
            re = im = None
            for b in range(3):
                lr, li = links[b][a] if adjoint else links[a][b]
                vr, vi = half[s * 3 + b]
                if adjoint:
                    tr, ti = lr * vr + li * vi, lr * vi - li * vr
                else:
                    tr, ti = lr * vr - li * vi, lr * vi + li * vr
                re = tr if re is None else re + tr
                im = ti if im is None else im + ti
            out.append((re, im))
    return out


def each(function, half):
    return [(function(re), function(im)) for re, im in half]


def load_pair(ref, index):
    block = ref[index * 16:(index + 1) * 16, :].astype(F32)
    return block[0:8], block[8:16]


def load_links(ref, mu, parity):
    links = []
    for a in range(3):
        row = []
        for b in range(3):
            k = ((mu * 3 + a) * 3 + b) * 2
            row.append((load_pair(ref, k)[parity], load_pair(ref, k + 1)[parity]))
        links.append(row)
    return links


def load_field(ref, r):
    return [load_pair(ref, r * 12 + j) for j in range(12)]


def store_pair(ref, index, pair):
    ref[index * 16:(index + 1) * 16, :] = jnp.concatenate(pair, axis=0).astype(ref.dtype)


def store_field(ref, r, field):
    for j in range(12):
        store_pair(ref, r * 12 + j, field[j])


def site_masks():
    rows = lax.broadcasted_iota(jnp.int32, (8, 128), 0)
    return rows // 4, rows % 4


def even_device(*axes):
    place = sum(lax.axis_index(axis) for axis in axes)
    return lax.broadcast(place % 2, (8, 128)) == 0


def either(even, a, b):
    return [select(even, a[i], b[i]) for i in range(2)]


def roll_rows(value, shift):
    shift %= 8
    return pltpu.roll(value, shift, 0) if shift else value


def select(mask, a, b):
    return jnp.where(mask, a, b)


def t_edges(links):
    t_idx, _ = site_masks()
    return [each(lambda v: select(t_idx == 0, roll_rows(v, 4), v), row) for row in links]


def x_edges(links):
    _, x_idx = site_masks()

    def edge(value):
        out = value
        for k in range(3):
            out = select(x_idx == k, roll_rows(value, k - 3), out)
        return out

    return [each(edge, row) for row in links]


def send_t(f_ref, links_ref, parity, t_one, t_two, ready=lambda r: None):
    even = even_device("ta", "gx")
    t_idx, _ = site_masks()
    first = t_idx == 0
    links = t_edges(load_links(links_ref, 0, parity))
    for r in range(RHS):
        ready(r)
        field = load_field(f_ref, r)
        ahead, behind = project(field, 0, -1), project(field, 0, 1)
        rears = [
            tuple(select(first, roll_rows(behind[c][i], 4), behind[c + 3][i]) for i in range(2)) for c in range(3)
        ]
        rears = matvec(links, rears, True)
        for c in range(3):
            front = [select(first, ahead[c + 3][i], roll_rows(ahead[c][i], 4)) for i in range(2)]
            store_pair(t_one, r * 3 + c, either(even, rears[c], front))
            store_pair(t_two, r * 3 + c, either(even, front, rears[c]))


def send_x_kernel(parity, f_ref, links_ref, x_far, x_near):
    even = even_device("gx")
    _, x_idx = site_masks()
    links = x_edges(load_links(links_ref, 1, parity))

    def packed(values, row, step):
        out = values[0]
        for k in range(1, 4):
            out = select(x_idx == row + step * k, roll_rows(values[k], step * k), out)
        return out

    for q in range(RHS // 2):
        fields = [load_field(f_ref, r) for r in (2 * q, 2 * q + 1)]
        ahead = [project(field, 1, -1) for field in fields]
        behind = [project(field, 1, 1) for field in fields]
        fronts, rears = [], []
        for c in range(3):
            fronts.append([packed([h[j][i] for h in ahead for j in (c, c + 3)], 0, 1) for i in range(2)])
            rears.append([packed([h[j][i] for h in behind for j in (c, c + 3)], 3, -1) for i in range(2)])
        rears = matvec(links, rears, True)
        for c in range(3):
            store_pair(x_near, q * 3 + c, either(even, rears[c], fronts[c]))
            store_pair(x_far, q * 3 + c, either(even, fronts[c], rears[c]))


def start_kernel(f_hbm, links_hbm, t_one, t_two, f_ref, links_ref, sems):
    part = f_ref.shape[0] // RHS
    t_rows = links_ref.shape[0] // 4

    def copy_rows(source, target, start, size, sem):
        rows = pl.ds(start, size)
        return pltpu.make_async_copy(source.at[rows], target.at[rows], sems.at[sem])

    t_links = copy_rows(links_hbm, links_ref, 0, t_rows, RHS)
    fields = [copy_rows(f_hbm, f_ref, r * part, part, r) for r in range(RHS)]
    others = copy_rows(links_hbm, links_ref, t_rows, links_ref.shape[0] - t_rows, RHS + 1)
    for copy in (t_links, *fields, others):
        copy.start()
    t_links.wait()
    send_t(f_ref, links_ref, 0, t_one, t_two, ready=lambda r: fields[r].wait())
    others.wait()


def interior_kernel(parity, with_base, *refs):
    if with_base:
        f_ref, links_ref, base_ref, clover_ref, acc_ref = refs
        clover_to(clover_ref, lambda r: load_field(base_ref, r), acc_ref, 1.0)
    else:
        f_ref, links_ref, acc_ref = refs
    out_parity = 1 - parity
    t_idx, x_idx = site_masks()
    lane = lax.broadcasted_iota(jnp.int32, (8, 128), 1)
    odd = (t_idx + x_idx + lane // HALF_DEPTH + out_parity) % 2
    start = lane - lane % HALF_DEPTH
    up = jnp.where(odd == 1, start + (lane + 1) % HALF_DEPTH, lane)
    down = jnp.where(odd == 0, start + (lane + HALF_DEPTH - 1) % HALF_DEPTH, lane)
    zero = jnp.zeros((8, 128), F32)

    def take(value, index):
        return jnp.take_along_axis(value, index, axis=1, mode="promise_in_bounds")

    for mu in (2, 3, 0, 1):
        if mu == 2:
            ahead_of = lambda v: pltpu.roll(v, 128 - HALF_DEPTH, 1)
            behind_of = lambda v: pltpu.roll(v, HALF_DEPTH, 1)
        elif mu == 3:
            ahead_of = lambda v: take(v, up)
            behind_of = lambda v: take(v, down)
        elif mu == 0:
            ahead_of = lambda v: select(t_idx == 0, roll_rows(v, 4), 0.0)
            behind_of = lambda v: select(t_idx == 1, roll_rows(v, 4), 0.0)
        else:
            ahead_of = lambda v: select(x_idx < 3, roll_rows(v, 7), 0.0)
            behind_of = lambda v: select(x_idx > 0, roll_rows(v, 1), 0.0)
        links_out = load_links(links_ref, mu, out_parity)
        links_in = load_links(links_ref, mu, parity)
        for r in range(RHS):
            field = load_field(f_ref, r)
            if mu == 2 and not with_base:
                acc = [(zero, zero)] * 12
            else:
                acc = load_field(acc_ref, r)
            half = color(links_out, each(ahead_of, project(field, mu, -1)), False)
            acc = rebuild(acc, half, mu, -1)
            half = color(links_in, project(field, mu, 1), True)
            acc = rebuild(acc, each(behind_of, half), mu, 1)
            store_field(acc_ref, r, acc)


def clover_to(clover_ref, get_field, out_ref, scale):
    for chi in range(2):
        matrix = {}
        for i in range(6):
            for j in range(i, 6):
                k = (chi * 6 + i) * 6 + j
                block = clover_ref[k * 16:(k + 1) * 16, :].astype(F32)
                re, im = block[0:8], block[8:16]
                if scale != 1.0:
                    re, im = re * scale, im * scale
                matrix[i, j] = (re, re + im, im - re)
        for q in range(RHS // 2):
            rhs = (2 * q, 2 * q + 1)
            fields = [get_field(r)[chi * 6:chi * 6 + 6] for r in rhs]
            sums = [[vr + vi for vr, vi in field] for field in fields]
            for i in range(6):
                totals = [None, None]
                for j in range(6):
                    m, plus, minus = matrix[min(i, j), max(i, j)]
                    for n in range(2):
                        vr, vi = fields[n][j]
                        one = m * sums[n][j]
                        if i <= j:
                            two, three = -(vi * plus), vr * minus
                        else:
                            two, three = vi * minus, -(vr * plus)
                        old = totals[n]
                        totals[n] = (one, two, three) if old is None else (old[0] + one, old[1] + two, old[2] + three)
                for n, r in enumerate(rhs):
                    one, two, three = totals[n]
                    store_pair(out_ref, r * 12 + chi * 6 + i, (one + two, one + three))


def matvec(links, vector, adjoint):
    out = []
    for a in range(3):
        re = im = None
        for b in range(3):
            lr, li = links[b][a] if adjoint else links[a][b]
            vr, vi = vector[b]
            if adjoint:
                tr, ti = lr * vr + li * vi, lr * vi - li * vr
            else:
                tr, ti = lr * vr - li * vi, lr * vi + li * vr
            re = tr if re is None else re + tr
            im = ti if im is None else im + ti
        out.append((re, im))
    return out


def rebuild_signed(acc, half, mu, sign):
    out = list(acc)
    for j in range(6):
        out[j] = add_power(out[j], half[j], 0)
    half = each(lambda v: v * sign, half)
    for row in range(2):
        col, power = SPIN_INV[mu][row]
        for c in range(3):
            j = (2 + row) * 3 + c
            out[j] = add_power(out[j], half[col * 3 + c], power)
    return out


def join_x_kernel(parity, links_ref, acc_ref, x_far, x_near, out_ref):
    even = even_device("gx")
    _, x_idx = site_masks()
    sign = jnp.where(x_idx == 3, -1.0, 1.0).astype(F32)
    links = x_edges(load_links(links_ref, 1, 1 - parity))
    for q in range(RHS // 2):
        nxt, last = [], []
        for c in range(3):
            near, far = load_pair(x_near, q * 3 + c), load_pair(x_far, q * 3 + c)
            nxt.append(either(even, near, far))
            last.append(either(even, far, near))
        ahead = matvec(links, nxt, False)
        for r in (2 * q, 2 * q + 1):
            half = [None] * 6
            for s in range(2):
                k = (r % 2) * 2 + s
                for c in range(3):
                    half[s * 3 + c] = tuple(
                        select(
                            x_idx == 3,
                            roll_rows(ahead[c][i], 3 - k),
                            select(x_idx == 0, roll_rows(last[c][i], 5 + k), 0.0),
                        )
                        for i in range(2)
                    )
            store_field(out_ref, r, rebuild_signed(load_field(acc_ref, r), half, 1, sign))


def join_t(links_ref, acc_ref, t_one, t_two, parity, out_ref, done=lambda r: None):
    even = even_device("ta", "gx")
    t_idx, _ = site_masks()
    first = t_idx == 0
    sign = jnp.where(first, 1.0, -1.0).astype(F32)
    links = t_edges(load_links(links_ref, 0, 1 - parity))
    for r in range(RHS):
        nxt, last = [], []
        for c in range(3):
            one, two = load_pair(t_one, r * 3 + c), load_pair(t_two, r * 3 + c)
            nxt.append(either(even, one, two))
            last.append(either(even, two, one))
        ahead = matvec(links, nxt, False)
        half = [tuple(select(first, last[c][i], ahead[c][i]) for i in range(2)) for c in range(3)]
        half += [
            tuple(roll_rows(select(first, ahead[c][i], last[c][i]), 4) for i in range(2)) for c in range(3)
        ]
        store_field(out_ref, r, rebuild_signed(load_field(acc_ref, r), half, 0, sign))
        done(r)


def odd_kernel(links_ref, clover_ref, acc_ref, t_one, t_two, out_ref, *refs):
    outs, summed = refs[:2], refs[2]
    join_t(links_ref, acc_ref, t_one, t_two, 0, summed)
    clover_to(clover_ref, lambda r: load_field(summed, r), out_ref, -KAPPA2)
    send_t(out_ref, links_ref, 1, *outs)


def even_kernel(links_ref, acc_ref, t_one, t_two, out_ref, *outs):
    join_t(links_ref, acc_ref, t_one, t_two, 1, out_ref)
    send_t(out_ref, links_ref, 0, *outs)


def last_kernel(links_ref, acc_ref, t_one, t_two, out_hbm, held, sems):
    part = held.shape[0] // RHS
    copies = []

    def done(r):
        rows = pl.ds(r * part, part)
        copies.append(pltpu.make_async_copy(held.at[rows], out_hbm.at[rows], sems.at[r]))
        copies[-1].start()

    join_t(links_ref, acc_ref, t_one, t_two, 1, held, done)
    for copy in copies:
        copy.wait()


ROWS = RHS * 24 * 8
FIELD = [((ROWS, 128), F32)]
T_HALOS = [((RHS * 3 * 16, 128), BF16)] * 2
X_HALOS = [((RHS * 3 * 8, 128), BF16)] * 2


def call(kernel, args, outs, flops, scratch=(), in_space=pltpu.VMEM, out_space=pltpu.VMEM):
    return pl.pallas_call(
        kernel,
        out_shape=tuple(jax.ShapeDtypeStruct(shape, dtype) for shape, dtype in outs),
        in_specs=[pl.BlockSpec(memory_space=in_space)] * len(args),
        out_specs=tuple([pl.BlockSpec(memory_space=out_space)] * len(outs)),
        scratch_shapes=list(scratch),
        compiler_params=pltpu.CompilerParams(vmem_limit_bytes=24 * 1024 * 1024),
        cost_estimate=pl.CostEstimate(flops=flops, bytes_accessed=2 * 1024 * 1024, transcendentals=0),
    )(*args)


def swap(value, axis, far):
    count = lax.axis_size(axis)
    assert count % 2 == 0
    pairs = [(i, (i + (1 if (i % 2 == 0) != far else -1)) % count) for i in range(count)]
    return lax.ppermute(value, axis, pairs)


def swap_t(value, ahead):
    count, across = lax.axis_size("ta"), lax.axis_size("gx")
    assert count % 2 == 0 and across % 2 == 0
    pairs = []
    for i in range(count):
        for j in range(across):
            step = 1 if ((i + j) % 2 == 0) == ahead else -1
            pairs.append((i * across + j, (i + step) % count * across + j))
    return lax.ppermute(value, ("ta", "gx"), pairs)


def per_device(source, gauge_links, clover_even, clover_odd_inv):
    shape = source.shape
    f = source.reshape(-1, 128)
    links = gauge_links.reshape(-1, 128)
    even = clover_even.reshape(-1, 128)
    odd = clover_odd_inv.reshape(-1, 128)
    held = [pltpu.with_memory_space_constraint(v, pltpu.HBM) for v in (f, links)]
    t_one, t_two, f, links = call(
        start_kernel, held, T_HALOS + [(f.shape, BF16), (links.shape, BF16)], 1_500_000,
        [pltpu.SemaphoreType.DMA((RHS + 2,))], in_space=pltpu.HBM,
    )
    for hop in range(4):
        parity = hop % 2
        t_one, t_two = swap_t(t_one, True), swap_t(t_two, False)
        x_far, x_near = call(
            functools.partial(send_x_kernel, parity), (f, links), X_HALOS, 1_500_000
        )
        here, x_far, x_near = lax.optimization_barrier((f, x_far, x_near))
        x_far, x_near = swap(x_far, "gx", True), swap(x_near, "gx", False)
        base = (before, even) if parity else ()
        acc, = call(
            functools.partial(interior_kernel, parity, bool(parity)),
            (here, links, *base), FIELD, 8_000_000 if parity else 5_000_000,
        )
        acc, = call(functools.partial(join_x_kernel, parity), (links, acc, x_far, x_near), FIELD, 1_000_000)
        before = f
        if parity == 0:
            f, t_one, t_two = call(
                odd_kernel, (links, odd, acc, t_one, t_two), FIELD + T_HALOS, 4_000_000,
                [pltpu.VMEM((ROWS, 128), F32)],
            )
        elif hop == 1:
            f, t_one, t_two = call(
                even_kernel, (links, acc, t_one, t_two), FIELD + T_HALOS, 2_000_000
            )
        else:
            out, = call(
                last_kernel, (links, acc, t_one, t_two), [((ROWS, 128), BF16)], 1_000_000,
                [pltpu.VMEM((ROWS, 128), BF16), pltpu.SemaphoreType.DMA((RHS,))], out_space=pltpu.HBM,
            )
    return out.reshape(shape)


def solution(mesh):
    field_spec = P(None, None, None, None, ("groups", "ta"), "gx", None)
    link_spec = P(None, None, None, None, None, ("groups", "ta"), "gx", None)
    return jax.shard_map(
        per_device,
        mesh=mesh,
        in_specs=(field_spec, link_spec, field_spec, field_spec),
        out_specs=field_spec,
        check_vma=False,
    )
```

```python
import functools

import jax
import jax.numpy as jnp
from jax import lax
from jax.experimental import pallas as pl
from jax.experimental.pallas import tpu as pltpu
from jax.sharding import PartitionSpec as P

HALF_DEPTH = 8
KAPPA2 = 0.14 * 0.14
RHS = 4
F32 = jnp.float32
BF16 = jnp.bfloat16

SPIN = (((0, 0), (1, 0)), ((1, 3), (0, 3)), ((1, 2), (0, 0)), ((0, 3), (1, 1)))
SPIN_INV = (((0, 0), (1, 0)), ((1, 1), (0, 1)), ((1, 0), (0, 2)), ((0, 1), (1, 3)))


def add_power(base, value, power):
    (br, bi), (vr, vi) = base, value
    if power == 0:
        return br + vr, bi + vi
    if power == 1:
        return br - vi, bi + vr
    if power == 2:
        return br - vr, bi - vi
    return br + vi, bi - vr


def project(field, mu, sign):
    shift = 0 if sign > 0 else 2
    half = []
    for row in range(2):
        col, power = SPIN[mu][row]
        for c in range(3):
            half.append(add_power(field[row * 3 + c], field[(2 + col) * 3 + c], (power + shift) % 4))
    return half


def rebuild(acc, half, mu, sign):
    shift = 0 if sign > 0 else 2
    out = list(acc)
    for j in range(6):
        out[j] = add_power(out[j], half[j], 0)
    for row in range(2):
        col, power = SPIN_INV[mu][row]
        for c in range(3):
            j = (2 + row) * 3 + c
            out[j] = add_power(out[j], half[col * 3 + c], (power + shift) % 4)
    return out


def color(links, half, adjoint):
    out = []
    for s in range(2):
        for a in range(3):
            re = im = None
            for b in range(3):
                lr, li = links[b][a] if adjoint else links[a][b]
                vr, vi = half[s * 3 + b]
                if adjoint:
                    tr, ti = lr * vr + li * vi, lr * vi - li * vr
                else:
                    tr, ti = lr * vr - li * vi, lr * vi + li * vr
                re = tr if re is None else re + tr
                im = ti if im is None else im + ti
            out.append((re, im))
    return out


def each(function, half):
    return [(function(re), function(im)) for re, im in half]


def load_pair(ref, index):
    block = ref[index * 16:(index + 1) * 16, :].astype(F32)
    return block[0:8], block[8:16]


def rounded(half):
    out = []
    for pair in half:
        block = jnp.concatenate(pair, axis=0).astype(BF16).astype(F32)
        out.append((block[0:8], block[8:16]))
    return out


def load_links(ref, mu, parity):
    links = []
    for a in range(3):
        row = []
        for b in range(3):
            k = ((mu * 3 + a) * 3 + b) * 2
            row.append((load_pair(ref, k)[parity], load_pair(ref, k + 1)[parity]))
        links.append(row)
    return links


def load_field(ref, r):
    return [load_pair(ref, r * 12 + j) for j in range(12)]


def store_pair(ref, index, pair):
    ref[index * 16:(index + 1) * 16, :] = jnp.concatenate(pair, axis=0).astype(ref.dtype)


def store_field(ref, r, field):
    for j in range(12):
        store_pair(ref, r * 12 + j, field[j])


def site_masks():
    rows = lax.broadcasted_iota(jnp.int32, (8, 128), 0)
    return rows // 4, rows % 4


def even_device(*axes):
    place = sum(lax.axis_index(axis) for axis in axes)
    return lax.broadcast(place % 2, (8, 128)) == 0


def either(even, a, b):
    return [select(even, a[i], b[i]) for i in range(2)]


def roll_rows(value, shift):
    shift %= 8
    return pltpu.roll(value, shift, 0) if shift else value


def select(mask, a, b):
    return jnp.where(mask, a, b)


def t_edges(links):
    t_idx, _ = site_masks()
    return [each(lambda v: select(t_idx == 0, roll_rows(v, 4), v), row) for row in links]


def x_edges(links):
    _, x_idx = site_masks()

    def edge(value):
        out = value
        for k in range(3):
            out = select(x_idx == k, roll_rows(value, k - 3), out)
        return out

    return [each(edge, row) for row in links]


def send_t(f_ref, links_ref, parity, t_one, t_two, ready=lambda r: None):
    even = even_device("ta", "gx")
    t_idx, _ = site_masks()
    first = t_idx == 0
    links = t_edges(load_links(links_ref, 0, parity))
    for r in range(RHS):
        ready(r)
        field = load_field(f_ref, r)
        ahead, behind = project(field, 0, -1), project(field, 0, 1)
        rears = [
            tuple(select(first, roll_rows(behind[c][i], 4), behind[c + 3][i]) for i in range(2)) for c in range(3)
        ]
        rears = matvec(links, rounded(rears), True)
        for c in range(3):
            front = [select(first, ahead[c + 3][i], roll_rows(ahead[c][i], 4)) for i in range(2)]
            store_pair(t_one, r * 3 + c, either(even, rears[c], front))
            store_pair(t_two, r * 3 + c, either(even, front, rears[c]))


def send_x_kernel(parity, f_ref, links_ref, x_far, x_near):
    even = even_device("gx")
    _, x_idx = site_masks()
    links = x_edges(load_links(links_ref, 1, parity))

    def packed(values, row, step):
        out = values[0]
        for k in range(1, 4):
            out = select(x_idx == row + step * k, roll_rows(values[k], step * k), out)
        return out

    for q in range(RHS // 2):
        fields = [load_field(f_ref, r) for r in (2 * q, 2 * q + 1)]
        ahead = [project(field, 1, -1) for field in fields]
        behind = [project(field, 1, 1) for field in fields]
        fronts, rears = [], []
        for c in range(3):
            fronts.append([packed([h[j][i] for h in ahead for j in (c, c + 3)], 0, 1) for i in range(2)])
            rears.append([packed([h[j][i] for h in behind for j in (c, c + 3)], 3, -1) for i in range(2)])
        rears = matvec(links, rounded(rears), True)
        for c in range(3):
            store_pair(x_near, q * 3 + c, either(even, rears[c], fronts[c]))
            store_pair(x_far, q * 3 + c, either(even, fronts[c], rears[c]))


def start_kernel(f_hbm, links_hbm, *refs):
    outs, (f_ref, links_ref, sems) = refs[:2], refs[2:]
    part = f_ref.shape[0] // RHS
    copies = [pltpu.make_async_copy(links_hbm.at[pl.ds(0, links_ref.shape[0])], links_ref, sems.at[RHS])]
    for r in range(RHS):
        rows = pl.ds(r * part, part)
        copies.append(pltpu.make_async_copy(f_hbm.at[rows], f_ref.at[rows], sems.at[r]))
    for copy in copies:
        copy.start()
    copies[0].wait()
    send_t(f_ref, links_ref, 0, *outs, ready=lambda r: copies[1 + r].wait())


def interior_kernel(parity, with_base, *refs):
    if with_base:
        f_ref, links_ref, base_ref, clover_ref, acc_ref = refs
        clover_to(clover_ref, lambda r: load_field(base_ref, r), acc_ref, -1.0 / KAPPA2)
    else:
        f_ref, links_ref, acc_ref = refs
    out_parity = 1 - parity
    t_idx, x_idx = site_masks()
    lane = lax.broadcasted_iota(jnp.int32, (8, 128), 1)
    odd = (t_idx + x_idx + lane // HALF_DEPTH + out_parity) % 2
    start = lane - lane % HALF_DEPTH
    up = jnp.where(odd == 1, start + (lane + 1) % HALF_DEPTH, lane)
    down = jnp.where(odd == 0, start + (lane + HALF_DEPTH - 1) % HALF_DEPTH, lane)
    zero = jnp.zeros((8, 128), F32)

    def take(value, index):
        return jnp.take_along_axis(value, index, axis=1, mode="promise_in_bounds")

    for mu in (2, 3, 0, 1):
        if mu == 2:
            ahead_of = lambda v: pltpu.roll(v, 128 - HALF_DEPTH, 1)
            behind_of = lambda v: pltpu.roll(v, HALF_DEPTH, 1)
        elif mu == 3:
            ahead_of = lambda v: take(v, up)
            behind_of = lambda v: take(v, down)
        elif mu == 0:
            ahead_of = lambda v: select(t_idx == 0, roll_rows(v, 4), 0.0)
            behind_of = lambda v: select(t_idx == 1, roll_rows(v, 4), 0.0)
        else:
            ahead_of = lambda v: select(x_idx < 3, roll_rows(v, 7), 0.0)
            behind_of = lambda v: select(x_idx > 0, roll_rows(v, 1), 0.0)
        links_out = load_links(links_ref, mu, out_parity)
        links_in = load_links(links_ref, mu, parity)
        for r in range(RHS):
            field = load_field(f_ref, r)
            if mu == 2 and not with_base:
                acc = [(zero, zero)] * 12
            else:
                acc = load_field(acc_ref, r)
            half = color(links_out, each(ahead_of, rounded(project(field, mu, -1))), False)
            acc = rebuild(acc, half, mu, -1)
            half = rounded(color(links_in, rounded(project(field, mu, 1)), True))
            acc = rebuild(acc, each(behind_of, half), mu, 1)
            store_field(acc_ref, r, acc)


def clover_to(clover_ref, get_field, out_ref, scale):
    for chi in range(2):
        matrix = {}
        for i in range(6):
            for j in range(i, 6):
                k = (chi * 6 + i) * 6 + j
                block = clover_ref[k * 16:(k + 1) * 16, :].astype(F32)
                re, im = block[0:8], block[8:16]
                if scale != 1.0:
                    re, im = re * scale, im * scale
                matrix[i, j] = (re, re + im, im - re)
        for r in range(RHS):
            field = get_field(r)[chi * 6:chi * 6 + 6]
            both = [vr + vi for vr, vi in field]
            for i in range(6):
                one = two = three = None
                for j in range(6):
                    vr, vi = field[j]
                    m, plus, minus = matrix[min(i, j), max(i, j)]
                    t_one = m * both[j]
                    if i <= j:
                        t_two, t_three = -(vi * plus), vr * minus
                    else:
                        t_two, t_three = vi * minus, -(vr * plus)
                    one = t_one if one is None else one + t_one
                    two = t_two if two is None else two + t_two
                    three = t_three if three is None else three + t_three
                store_pair(out_ref, r * 12 + chi * 6 + i, (one + two, one + three))


def matvec(links, vector, adjoint):
    out = []
    for a in range(3):
        re = im = None
        for b in range(3):
            lr, li = links[b][a] if adjoint else links[a][b]
            vr, vi = vector[b]
            if adjoint:
                tr, ti = lr * vr + li * vi, lr * vi - li * vr
            else:
                tr, ti = lr * vr - li * vi, lr * vi + li * vr
            re = tr if re is None else re + tr
            im = ti if im is None else im + ti
        out.append((re, im))
    return out


def rebuild_signed(acc, half, mu, sign):
    out = list(acc)
    for j in range(6):
        out[j] = add_power(out[j], half[j], 0)
    half = each(lambda v: v * sign, half)
    for row in range(2):
        col, power = SPIN_INV[mu][row]
        for c in range(3):
            j = (2 + row) * 3 + c
            out[j] = add_power(out[j], half[col * 3 + c], power)
    return out


def join_x_kernel(parity, links_ref, acc_ref, x_far, x_near, out_ref):
    even = even_device("gx")
    _, x_idx = site_masks()
    sign = jnp.where(x_idx == 3, -1.0, 1.0).astype(F32)
    links = x_edges(load_links(links_ref, 1, 1 - parity))
    for q in range(RHS // 2):
        nxt, last = [], []
        for c in range(3):
            near, far = load_pair(x_near, q * 3 + c), load_pair(x_far, q * 3 + c)
            nxt.append(either(even, near, far))
            last.append(either(even, far, near))
        ahead = matvec(links, nxt, False)
        for r in (2 * q, 2 * q + 1):
            half = [None] * 6
            for s in range(2):
                k = (r % 2) * 2 + s
                for c in range(3):
                    half[s * 3 + c] = tuple(
                        select(
                            x_idx == 3,
                            roll_rows(ahead[c][i], 3 - k),
                            select(x_idx == 0, roll_rows(last[c][i], 5 + k), 0.0),
                        )
                        for i in range(2)
                    )
            store_field(out_ref, r, rebuild_signed(load_field(acc_ref, r), half, 1, sign))


def join_t(links_ref, acc_ref, t_one, t_two, parity, out_ref, scale=None, done=lambda r: None):
    even = even_device("ta", "gx")
    t_idx, _ = site_masks()
    first = t_idx == 0
    sign = jnp.where(first, 1.0, -1.0).astype(F32)
    links = t_edges(load_links(links_ref, 0, 1 - parity))
    for r in range(RHS):
        nxt, last = [], []
        for c in range(3):
            one, two = load_pair(t_one, r * 3 + c), load_pair(t_two, r * 3 + c)
            nxt.append(either(even, one, two))
            last.append(either(even, two, one))
        ahead = matvec(links, nxt, False)
        half = [tuple(select(first, last[c][i], ahead[c][i]) for i in range(2)) for c in range(3)]
        half += [
            tuple(roll_rows(select(first, ahead[c][i], last[c][i]), 4) for i in range(2)) for c in range(3)
        ]
        field = rebuild_signed(load_field(acc_ref, r), half, 0, sign)
        if scale is not None:
            field = each(lambda v: v * scale, field)
        store_field(out_ref, r, field)
        done(r)


def odd_kernel(links_ref, clover_ref, acc_ref, t_one, t_two, out_ref, *refs):
    outs, summed = refs[:2], refs[2]
    join_t(links_ref, acc_ref, t_one, t_two, 0, summed)
    clover_to(clover_ref, lambda r: load_field(summed, r), out_ref, 1.0)
    send_t(out_ref, links_ref, 1, *outs)


def even_kernel(links_ref, acc_ref, t_one, t_two, out_ref, *outs):
    join_t(links_ref, acc_ref, t_one, t_two, 1, out_ref, -KAPPA2)
    send_t(out_ref, links_ref, 0, *outs)


def last_kernel(links_ref, acc_ref, t_one, t_two, out_hbm, held, sems):
    part = held.shape[0] // RHS
    copies = []

    def done(r):
        rows = pl.ds(r * part, part)
        copies.append(pltpu.make_async_copy(held.at[rows], out_hbm.at[rows], sems.at[r]))
        copies[-1].start()

    join_t(links_ref, acc_ref, t_one, t_two, 1, held, -KAPPA2, done)
    for copy in copies:
        copy.wait()


ROWS = RHS * 24 * 8
FIELD = [((ROWS, 128), BF16)]
SUM = [((ROWS, 128), F32)]
T_HALOS = [((RHS * 3 * 16, 128), BF16)] * 2
X_HALOS = [((RHS * 3 * 8, 128), BF16)] * 2


def call(kernel, args, outs, flops, scratch=(), in_space=pltpu.VMEM, out_space=pltpu.VMEM):
    return pl.pallas_call(
        kernel,
        out_shape=tuple(jax.ShapeDtypeStruct(shape, dtype) for shape, dtype in outs),
        in_specs=[pl.BlockSpec(memory_space=in_space)] * len(args),
        out_specs=tuple([pl.BlockSpec(memory_space=out_space)] * len(outs)),
        scratch_shapes=list(scratch),
        compiler_params=pltpu.CompilerParams(vmem_limit_bytes=24 * 1024 * 1024),
        cost_estimate=pl.CostEstimate(flops=flops, bytes_accessed=2 * 1024 * 1024, transcendentals=0),
    )(*args)


def swap(value, axis, far):
    count = lax.axis_size(axis)
    assert count % 2 == 0
    pairs = [(i, (i + (1 if (i % 2 == 0) != far else -1)) % count) for i in range(count)]
    return lax.ppermute(value, axis, pairs)


def swap_t(value, ahead):
    count, across = lax.axis_size("ta"), lax.axis_size("gx")
    assert count % 2 == 0 and across % 2 == 0
    pairs = []
    for i in range(count):
        for j in range(across):
            step = 1 if ((i + j) % 2 == 0) == ahead else -1
            pairs.append((i * across + j, (i + step) % count * across + j))
    return lax.ppermute(value, ("ta", "gx"), pairs)


def per_device(source, gauge_links, clover_even, clover_odd_inv):
    shape = source.shape
    f = source.reshape(-1, 128)
    links = gauge_links.reshape(-1, 128)
    even = clover_even.reshape(-1, 128)
    odd = clover_odd_inv.reshape(-1, 128)
    held = [pltpu.with_memory_space_constraint(v, pltpu.HBM) for v in (f, links)]
    start_scratch = [
        pltpu.VMEM((ROWS, 128), BF16),
        pltpu.VMEM((links.shape[0] // 4, 128), BF16),
        pltpu.SemaphoreType.DMA((RHS + 1,)),
    ]
    t_one, t_two = call(start_kernel, held, T_HALOS, 1_500_000, start_scratch, in_space=pltpu.HBM)
    for hop in range(4):
        parity = hop % 2
        t_one, t_two = swap_t(t_one, True), swap_t(t_two, False)
        x_far, x_near = call(
            functools.partial(send_x_kernel, parity), (f, links), X_HALOS, 1_500_000
        )
        here, x_far, x_near = lax.optimization_barrier((f, x_far, x_near))
        x_far, x_near = swap(x_far, "gx", True), swap(x_near, "gx", False)
        base = (before, even) if parity else ()
        acc, = call(
            functools.partial(interior_kernel, parity, bool(parity)),
            (here, links, *base), SUM, 8_000_000 if parity else 5_000_000,
        )
        acc, = call(functools.partial(join_x_kernel, parity), (links, acc, x_far, x_near), SUM, 1_000_000)
        before = f
        if parity == 0:
            f, t_one, t_two = call(
                odd_kernel, (links, odd, acc, t_one, t_two), FIELD + T_HALOS, 4_000_000,
                [pltpu.VMEM((ROWS, 128), BF16)],
            )
        elif hop == 1:
            f, t_one, t_two = call(
                even_kernel, (links, acc, t_one, t_two), FIELD + T_HALOS, 2_000_000
            )
        else:
            out, = call(
                last_kernel, (links, acc, t_one, t_two), FIELD, 1_000_000,
                [pltpu.VMEM((ROWS, 128), BF16), pltpu.SemaphoreType.DMA((RHS,))], out_space=pltpu.HBM,
            )
    return out.reshape(shape)


def solution(mesh):
    field_spec = P(None, None, None, None, ("groups", "ta"), "gx", None)
    link_spec = P(None, None, None, None, None, ("groups", "ta"), "gx", None)
    return jax.shard_map(
        per_device,
        mesh=mesh,
        in_specs=(field_spec, link_spec, field_spec, field_spec),
        out_specs=field_spec,
        check_vma=False,
    )
```

```python
import functools

import jax
import jax.numpy as jnp
from jax import lax
from jax.experimental import pallas as pl
from jax.experimental.pallas import tpu as pltpu
from jax.sharding import PartitionSpec as P

HALF_DEPTH = 8
KAPPA2 = 0.14 * 0.14
RHS = 4
F32 = jnp.float32
BF16 = jnp.bfloat16

SPIN = (((0, 0), (1, 0)), ((1, 3), (0, 3)), ((1, 2), (0, 0)), ((0, 3), (1, 1)))
SPIN_INV = (((0, 0), (1, 0)), ((1, 1), (0, 1)), ((1, 0), (0, 2)), ((0, 1), (1, 3)))


def add_power(base, value, power):
    (br, bi), (vr, vi) = base, value
    if power == 0:
        return br + vr, bi + vi
    if power == 1:
        return br - vi, bi + vr
    if power == 2:
        return br - vr, bi - vi
    return br + vi, bi - vr


def project(field, mu, sign):
    shift = 0 if sign > 0 else 2
    half = []
    for row in range(2):
        col, power = SPIN[mu][row]
        for c in range(3):
            half.append(add_power(field[row * 3 + c], field[(2 + col) * 3 + c], (power + shift) % 4))
    return half


def rebuild(acc, half, mu, sign):
    shift = 0 if sign > 0 else 2
    out = list(acc)
    for j in range(6):
        out[j] = add_power(out[j], half[j], 0)
    for row in range(2):
        col, power = SPIN_INV[mu][row]
        for c in range(3):
            j = (2 + row) * 3 + c
            out[j] = add_power(out[j], half[col * 3 + c], (power + shift) % 4)
    return out


def color(links, half, adjoint):
    out = []
    for s in range(2):
        for a in range(3):
            re = im = None
            for b in range(3):
                lr, li = links[b][a] if adjoint else links[a][b]
                vr, vi = half[s * 3 + b]
                if adjoint:
                    tr, ti = lr * vr + li * vi, lr * vi - li * vr
                else:
                    tr, ti = lr * vr - li * vi, lr * vi + li * vr
                re = tr if re is None else re + tr
                im = ti if im is None else im + ti
            out.append((re, im))
    return out


def each(function, half):
    return [(function(re), function(im)) for re, im in half]


def load_pair(ref, index):
    block = ref[index * 16:(index + 1) * 16, :].astype(F32)
    return block[0:8], block[8:16]


def rounded(half):
    out = []
    for pair in half:
        block = jnp.concatenate(pair, axis=0).astype(BF16).astype(F32)
        out.append((block[0:8], block[8:16]))
    return out


def load_links(ref, mu, parity):
    links = []
    for a in range(3):
        row = []
        for b in range(3):
            k = ((mu * 3 + a) * 3 + b) * 2
            row.append((load_pair(ref, k)[parity], load_pair(ref, k + 1)[parity]))
        links.append(row)
    return links


def load_field(ref, r):
    return [load_pair(ref, r * 12 + j) for j in range(12)]


def store_pair(ref, index, pair):
    ref[index * 16:(index + 1) * 16, :] = jnp.concatenate(pair, axis=0).astype(ref.dtype)


def store_field(ref, r, field):
    for j in range(12):
        store_pair(ref, r * 12 + j, field[j])


def site_masks():
    rows = lax.broadcasted_iota(jnp.int32, (8, 128), 0)
    return rows // 4, rows % 4


def even_device(*axes):
    place = sum(lax.axis_index(axis) for axis in axes)
    return lax.broadcast(place % 2, (8, 128)) == 0


def either(even, a, b):
    return [select(even, a[i], b[i]) for i in range(2)]


def roll_rows(value, shift):
    shift %= 8
    return pltpu.roll(value, shift, 0) if shift else value


def select(mask, a, b):
    return jnp.where(mask, a, b)


def t_edges(links):
    t_idx, _ = site_masks()
    return [each(lambda v: select(t_idx == 0, roll_rows(v, 4), v), row) for row in links]


def x_edges(links):
    _, x_idx = site_masks()

    def edge(value):
        out = value
        for k in range(3):
            out = select(x_idx == k, roll_rows(value, k - 3), out)
        return out

    return [each(edge, row) for row in links]


def send_t(f_ref, links_ref, parity, t_one, t_two, ready=lambda r: None):
    even = even_device("ta", "gx")
    t_idx, _ = site_masks()
    first = t_idx == 0
    links = t_edges(load_links(links_ref, 0, parity))
    for r in range(RHS):
        ready(r)
        field = load_field(f_ref, r)
        ahead, behind = project(field, 0, -1), project(field, 0, 1)
        rears = [
            tuple(select(first, roll_rows(behind[c][i], 4), behind[c + 3][i]) for i in range(2)) for c in range(3)
        ]
        rears = matvec(links, rounded(rears), True)
        for c in range(3):
            front = [select(first, ahead[c + 3][i], roll_rows(ahead[c][i], 4)) for i in range(2)]
            store_pair(t_one, r * 3 + c, either(even, rears[c], front))
            store_pair(t_two, r * 3 + c, either(even, front, rears[c]))


def send_x(f_ref, links_ref, parity, x_far, x_near):
    even = even_device("gx")
    _, x_idx = site_masks()
    links = x_edges(load_links(links_ref, 1, parity))

    def packed(values, row, step):
        out = values[0]
        for k in range(1, 4):
            out = select(x_idx == row + step * k, roll_rows(values[k], step * k), out)
        return out

    for q in range(RHS // 2):
        fields = [load_field(f_ref, r) for r in (2 * q, 2 * q + 1)]
        ahead = [project(field, 1, -1) for field in fields]
        behind = [project(field, 1, 1) for field in fields]
        fronts, rears = [], []
        for c in range(3):
            fronts.append([packed([h[j][i] for h in ahead for j in (c, c + 3)], 0, 1) for i in range(2)])
            rears.append([packed([h[j][i] for h in behind for j in (c, c + 3)], 3, -1) for i in range(2)])
        rears = matvec(links, rounded(rears), True)
        for c in range(3):
            store_pair(x_near, q * 3 + c, either(even, rears[c], fronts[c]))
            store_pair(x_far, q * 3 + c, either(even, fronts[c], rears[c]))


def start_kernel(f_hbm, links_hbm, *refs):
    outs, (f_ref, links_ref, sems) = refs[:4], refs[4:]
    part = f_ref.shape[0] // RHS
    copies = [pltpu.make_async_copy(links_hbm.at[pl.ds(0, links_ref.shape[0])], links_ref, sems.at[RHS])]
    for r in range(RHS):
        rows = pl.ds(r * part, part)
        copies.append(pltpu.make_async_copy(f_hbm.at[rows], f_ref.at[rows], sems.at[r]))
    for copy in copies:
        copy.start()
    copies[0].wait()
    send_t(f_ref, links_ref, 0, *outs[:2], ready=lambda r: copies[1 + r].wait())
    send_x(f_ref, links_ref, 0, *outs[2:])


def interior_kernel(parity, with_base, *refs):
    if with_base:
        f_ref, links_ref, base_ref, clover_ref, acc_ref = refs
        clover_to(clover_ref, lambda r: load_field(base_ref, r), acc_ref, -1.0 / KAPPA2)
    else:
        f_ref, links_ref, acc_ref = refs
    out_parity = 1 - parity
    t_idx, x_idx = site_masks()
    lane = lax.broadcasted_iota(jnp.int32, (8, 128), 1)
    odd = (t_idx + x_idx + lane // HALF_DEPTH + out_parity) % 2
    start = lane - lane % HALF_DEPTH
    up = jnp.where(odd == 1, start + (lane + 1) % HALF_DEPTH, lane)
    down = jnp.where(odd == 0, start + (lane + HALF_DEPTH - 1) % HALF_DEPTH, lane)
    zero = jnp.zeros((8, 128), F32)

    def take(value, index):
        return jnp.take_along_axis(value, index, axis=1, mode="promise_in_bounds")

    for mu in (2, 3, 0, 1):
        if mu == 2:
            ahead_of = lambda v: pltpu.roll(v, 128 - HALF_DEPTH, 1)
            behind_of = lambda v: pltpu.roll(v, HALF_DEPTH, 1)
        elif mu == 3:
            ahead_of = lambda v: take(v, up)
            behind_of = lambda v: take(v, down)
        elif mu == 0:
            ahead_of = lambda v: select(t_idx == 0, roll_rows(v, 4), 0.0)
            behind_of = lambda v: select(t_idx == 1, roll_rows(v, 4), 0.0)
        else:
            ahead_of = lambda v: select(x_idx < 3, roll_rows(v, 7), 0.0)
            behind_of = lambda v: select(x_idx > 0, roll_rows(v, 1), 0.0)
        links_out = load_links(links_ref, mu, out_parity)
        links_in = load_links(links_ref, mu, parity)
        for r in range(RHS):
            field = load_field(f_ref, r)
            if mu == 2 and not with_base:
                acc = [(zero, zero)] * 12
            else:
                acc = load_field(acc_ref, r)
            half = color(links_out, each(ahead_of, rounded(project(field, mu, -1))), False)
            acc = rebuild(acc, half, mu, -1)
            half = rounded(color(links_in, rounded(project(field, mu, 1)), True))
            acc = rebuild(acc, each(behind_of, half), mu, 1)
            store_field(acc_ref, r, acc)


def clover_to(clover_ref, get_field, out_ref, scale):
    for chi in range(2):
        matrix = {}
        for i in range(6):
            for j in range(i, 6):
                k = (chi * 6 + i) * 6 + j
                block = clover_ref[k * 16:(k + 1) * 16, :].astype(F32)
                re, im = block[0:8], block[8:16]
                if scale != 1.0:
                    re, im = re * scale, im * scale
                matrix[i, j] = (re, re + im, im - re)
        for r in range(RHS):
            field = get_field(r)[chi * 6:chi * 6 + 6]
            both = [vr + vi for vr, vi in field]
            for i in range(6):
                one = two = three = None
                for j in range(6):
                    vr, vi = field[j]
                    m, plus, minus = matrix[min(i, j), max(i, j)]
                    t_one = m * both[j]
                    if i <= j:
                        t_two, t_three = -(vi * plus), vr * minus
                    else:
                        t_two, t_three = vi * minus, -(vr * plus)
                    one = t_one if one is None else one + t_one
                    two = t_two if two is None else two + t_two
                    three = t_three if three is None else three + t_three
                store_pair(out_ref, r * 12 + chi * 6 + i, (one + two, one + three))


def matvec(links, vector, adjoint):
    out = []
    for a in range(3):
        re = im = None
        for b in range(3):
            lr, li = links[b][a] if adjoint else links[a][b]
            vr, vi = vector[b]
            if adjoint:
                tr, ti = lr * vr + li * vi, lr * vi - li * vr
            else:
                tr, ti = lr * vr - li * vi, lr * vi + li * vr
            re = tr if re is None else re + tr
            im = ti if im is None else im + ti
        out.append((re, im))
    return out


def rebuild_signed(acc, half, mu, sign):
    out = list(acc)
    for j in range(6):
        out[j] = add_power(out[j], half[j], 0)
    half = each(lambda v: v * sign, half)
    for row in range(2):
        col, power = SPIN_INV[mu][row]
        for c in range(3):
            j = (2 + row) * 3 + c
            out[j] = add_power(out[j], half[col * 3 + c], power)
    return out


def join_x_kernel(parity, links_ref, acc_ref, x_far, x_near, out_ref):
    even = even_device("gx")
    _, x_idx = site_masks()
    sign = jnp.where(x_idx == 3, -1.0, 1.0).astype(F32)
    links = x_edges(load_links(links_ref, 1, 1 - parity))
    for q in range(RHS // 2):
        nxt, last = [], []
        for c in range(3):
            near, far = load_pair(x_near, q * 3 + c), load_pair(x_far, q * 3 + c)
            nxt.append(either(even, near, far))
            last.append(either(even, far, near))
        ahead = matvec(links, nxt, False)
        for r in (2 * q, 2 * q + 1):
            half = [None] * 6
            for s in range(2):
                k = (r % 2) * 2 + s
                for c in range(3):
                    half[s * 3 + c] = tuple(
                        select(
                            x_idx == 3,
                            roll_rows(ahead[c][i], 3 - k),
                            select(x_idx == 0, roll_rows(last[c][i], 5 + k), 0.0),
                        )
                        for i in range(2)
                    )
            store_field(out_ref, r, rebuild_signed(load_field(acc_ref, r), half, 1, sign))


def join_t(links_ref, acc_ref, t_one, t_two, parity, out_ref, scale=None, done=lambda r: None):
    even = even_device("ta", "gx")
    t_idx, _ = site_masks()
    first = t_idx == 0
    sign = jnp.where(first, 1.0, -1.0).astype(F32)
    links = t_edges(load_links(links_ref, 0, 1 - parity))
    for r in range(RHS):
        nxt, last = [], []
        for c in range(3):
            one, two = load_pair(t_one, r * 3 + c), load_pair(t_two, r * 3 + c)
            nxt.append(either(even, one, two))
            last.append(either(even, two, one))
        ahead = matvec(links, nxt, False)
        half = [tuple(select(first, last[c][i], ahead[c][i]) for i in range(2)) for c in range(3)]
        half += [
            tuple(roll_rows(select(first, ahead[c][i], last[c][i]), 4) for i in range(2)) for c in range(3)
        ]
        field = rebuild_signed(load_field(acc_ref, r), half, 0, sign)
        if scale is not None:
            field = each(lambda v: v * scale, field)
        store_field(out_ref, r, field)
        done(r)


def odd_kernel(links_ref, clover_ref, acc_ref, t_one, t_two, out_ref, *refs):
    outs, summed = refs[:4], refs[4]
    join_t(links_ref, acc_ref, t_one, t_two, 0, summed)
    clover_to(clover_ref, lambda r: load_field(summed, r), out_ref, 1.0)
    send_t(out_ref, links_ref, 1, *outs[:2])
    send_x(out_ref, links_ref, 1, *outs[2:])


def even_kernel(links_ref, acc_ref, t_one, t_two, out_ref, *outs):
    join_t(links_ref, acc_ref, t_one, t_two, 1, out_ref, -KAPPA2)
    send_t(out_ref, links_ref, 0, *outs[:2])
    send_x(out_ref, links_ref, 0, *outs[2:])


def last_kernel(links_ref, acc_ref, t_one, t_two, out_hbm, held, sems):
    part = held.shape[0] // RHS
    copies = []

    def done(r):
        rows = pl.ds(r * part, part)
        copies.append(pltpu.make_async_copy(held.at[rows], out_hbm.at[rows], sems.at[r]))
        copies[-1].start()

    join_t(links_ref, acc_ref, t_one, t_two, 1, held, -KAPPA2, done)
    for copy in copies:
        copy.wait()


ROWS = RHS * 24 * 8
FIELD = [((ROWS, 128), BF16)]
SUM = [((ROWS, 128), F32)]
T_HALOS = [((RHS * 3 * 16, 128), BF16)] * 2
HALOS = T_HALOS + [((RHS * 3 * 8, 128), BF16)] * 2


def call(kernel, args, outs, flops, scratch=(), in_space=pltpu.VMEM, out_space=pltpu.VMEM):
    return pl.pallas_call(
        kernel,
        out_shape=tuple(jax.ShapeDtypeStruct(shape, dtype) for shape, dtype in outs),
        in_specs=[pl.BlockSpec(memory_space=in_space)] * len(args),
        out_specs=tuple([pl.BlockSpec(memory_space=out_space)] * len(outs)),
        scratch_shapes=list(scratch),
        compiler_params=pltpu.CompilerParams(vmem_limit_bytes=24 * 1024 * 1024),
        cost_estimate=pl.CostEstimate(flops=flops, bytes_accessed=2 * 1024 * 1024, transcendentals=0),
    )(*args)


def swap(value, axis, far):
    count = lax.axis_size(axis)
    assert count % 2 == 0
    pairs = [(i, (i + (1 if (i % 2 == 0) != far else -1)) % count) for i in range(count)]
    return lax.ppermute(value, axis, pairs)


def swap_t(value, ahead):
    count, across = lax.axis_size("ta"), lax.axis_size("gx")
    assert count % 2 == 0 and across % 2 == 0
    pairs = []
    for i in range(count):
        for j in range(across):
            step = 1 if ((i + j) % 2 == 0) == ahead else -1
            pairs.append((i * across + j, (i + step) % count * across + j))
    return lax.ppermute(value, ("ta", "gx"), pairs)


def per_device(source, gauge_links, clover_even, clover_odd_inv):
    shape = source.shape
    f = source.reshape(-1, 128)
    links = gauge_links.reshape(-1, 128)
    even = clover_even.reshape(-1, 128)
    odd = clover_odd_inv.reshape(-1, 128)
    held = [pltpu.with_memory_space_constraint(v, pltpu.HBM) for v in (f, links)]
    start_scratch = [
        pltpu.VMEM((ROWS, 128), BF16),
        pltpu.VMEM((links.shape[0] // 2, 128), BF16),
        pltpu.SemaphoreType.DMA((RHS + 1,)),
    ]
    t_one, t_two, x_far, x_near = call(start_kernel, held, HALOS, 1_500_000, start_scratch, in_space=pltpu.HBM)
    for hop in range(4):
        parity = hop % 2
        t_one, t_two = swap_t(t_one, True), swap_t(t_two, False)
        x_far, x_near = swap(x_far, "gx", True), swap(x_near, "gx", False)
        base = (before, even) if parity else ()
        acc, = call(
            functools.partial(interior_kernel, parity, bool(parity)),
            (f, links, *base), SUM, 8_000_000 if parity else 5_000_000,
        )
        acc, = call(functools.partial(join_x_kernel, parity), (links, acc, x_far, x_near), SUM, 1_000_000)
        before = f
        if parity == 0:
            f, t_one, t_two, x_far, x_near = call(
                odd_kernel, (links, odd, acc, t_one, t_two), FIELD + HALOS, 4_000_000,
                [pltpu.VMEM((ROWS, 128), BF16)],
            )
        elif hop == 1:
            f, t_one, t_two, x_far, x_near = call(
                even_kernel, (links, acc, t_one, t_two), FIELD + HALOS, 2_000_000
            )
        else:
            out, = call(
                last_kernel, (links, acc, t_one, t_two), FIELD, 1_000_000,
                [pltpu.VMEM((ROWS, 128), BF16), pltpu.SemaphoreType.DMA((RHS,))], out_space=pltpu.HBM,
            )
    return out.reshape(shape)


def solution(mesh):
    field_spec = P(None, None, None, None, ("groups", "ta"), "gx", None)
    link_spec = P(None, None, None, None, None, ("groups", "ta"), "gx", None)
    return jax.shard_map(
        per_device,
        mesh=mesh,
        in_specs=(field_spec, link_spec, field_spec, field_spec),
        out_specs=field_spec,
        check_vma=False,
    )
```

```python
import functools

import jax
import jax.numpy as jnp
from jax import lax
from jax.experimental import pallas as pl
from jax.experimental.pallas import tpu as pltpu
from jax.sharding import PartitionSpec as P

HALF_DEPTH = 8
KAPPA2 = 0.14 * 0.14
RHS = 4
F32 = jnp.float32
BF16 = jnp.bfloat16

SPIN = (((0, 0), (1, 0)), ((1, 3), (0, 3)), ((1, 2), (0, 0)), ((0, 3), (1, 1)))
SPIN_INV = (((0, 0), (1, 0)), ((1, 1), (0, 1)), ((1, 0), (0, 2)), ((0, 1), (1, 3)))


def add_power(base, value, power):
    (br, bi), (vr, vi) = base, value
    if power == 0:
        return br + vr, bi + vi
    if power == 1:
        return br - vi, bi + vr
    if power == 2:
        return br - vr, bi - vi
    return br + vi, bi - vr


def project(field, mu, sign):
    shift = 0 if sign > 0 else 2
    half = []
    for row in range(2):
        col, power = SPIN[mu][row]
        for c in range(3):
            half.append(add_power(field[row * 3 + c], field[(2 + col) * 3 + c], (power + shift) % 4))
    return half


def rebuild(acc, half, mu, sign):
    shift = 0 if sign > 0 else 2
    out = list(acc)
    for j in range(6):
        out[j] = add_power(out[j], half[j], 0)
    for row in range(2):
        col, power = SPIN_INV[mu][row]
        for c in range(3):
            j = (2 + row) * 3 + c
            out[j] = add_power(out[j], half[col * 3 + c], (power + shift) % 4)
    return out


def color(links, half, adjoint):
    out = []
    for s in range(2):
        for a in range(3):
            re = im = None
            for b in range(3):
                lr, li = links[b][a] if adjoint else links[a][b]
                vr, vi = half[s * 3 + b]
                if adjoint:
                    tr, ti = lr * vr + li * vi, lr * vi - li * vr
                else:
                    tr, ti = lr * vr - li * vi, lr * vi + li * vr
                re = tr if re is None else re + tr
                im = ti if im is None else im + ti
            out.append((re, im))
    return out


def each(function, half):
    return [(function(re), function(im)) for re, im in half]


def load_pair(ref, index):
    block = ref[index * 16:(index + 1) * 16, :].astype(F32)
    return block[0:8], block[8:16]


def rounded(half):
    out = []
    for pair in half:
        block = jnp.concatenate(pair, axis=0).astype(BF16).astype(F32)
        out.append((block[0:8], block[8:16]))
    return out


def load_links(ref, mu, parity):
    links = []
    for a in range(3):
        row = []
        for b in range(3):
            k = ((mu * 3 + a) * 3 + b) * 2
            row.append((load_pair(ref, k)[parity], load_pair(ref, k + 1)[parity]))
        links.append(row)
    return links


def load_field(ref, r):
    return [load_pair(ref, r * 12 + j) for j in range(12)]


def store_pair(ref, index, pair):
    ref[index * 16:(index + 1) * 16, :] = jnp.concatenate(pair, axis=0).astype(ref.dtype)


def store_field(ref, r, field):
    for j in range(12):
        store_pair(ref, r * 12 + j, field[j])


def site_masks():
    rows = lax.broadcasted_iota(jnp.int32, (8, 128), 0)
    return rows // 4, rows % 4


def even_device(*axes):
    place = sum(lax.axis_index(axis) for axis in axes)
    return lax.broadcast(place % 2, (8, 128)) == 0


def either(even, a, b):
    return [select(even, a[i], b[i]) for i in range(2)]


def roll_rows(value, shift):
    shift %= 8
    return pltpu.roll(value, shift, 0) if shift else value


def select(mask, a, b):
    return jnp.where(mask, a, b)


def t_edges(links):
    t_idx, _ = site_masks()
    return [each(lambda v: select(t_idx == 0, roll_rows(v, 4), v), row) for row in links]


def x_edges(links):
    _, x_idx = site_masks()

    def edge(value):
        out = value
        for k in range(3):
            out = select(x_idx == k, roll_rows(value, k - 3), out)
        return out

    return [each(edge, row) for row in links]


def send_t(f_ref, links_ref, parity, t_one, t_two, ready=lambda r: None):
    even = even_device("ta", "gx")
    t_idx, _ = site_masks()
    first = t_idx == 0
    links = t_edges(load_links(links_ref, 0, parity))
    for r in range(RHS):
        ready(r)
        field = load_field(f_ref, r)
        ahead, behind = project(field, 0, -1), project(field, 0, 1)
        rears = [
            tuple(select(first, roll_rows(behind[c][i], 4), behind[c + 3][i]) for i in range(2)) for c in range(3)
        ]
        rears = matvec(links, rounded(rears), True)
        for c in range(3):
            front = [select(first, ahead[c + 3][i], roll_rows(ahead[c][i], 4)) for i in range(2)]
            store_pair(t_one, r * 3 + c, either(even, rears[c], front))
            store_pair(t_two, r * 3 + c, either(even, front, rears[c]))


def send_x(f_ref, links_ref, parity, x_far, x_near):
    even = even_device("gx")
    _, x_idx = site_masks()
    links = x_edges(load_links(links_ref, 1, parity))

    def packed(values, row, step):
        out = values[0]
        for k in range(1, 4):
            out = select(x_idx == row + step * k, roll_rows(values[k], step * k), out)
        return out

    for q in range(RHS // 2):
        fields = [load_field(f_ref, r) for r in (2 * q, 2 * q + 1)]
        ahead = [project(field, 1, -1) for field in fields]
        behind = [project(field, 1, 1) for field in fields]
        fronts, rears = [], []
        for c in range(3):
            fronts.append([packed([h[j][i] for h in ahead for j in (c, c + 3)], 0, 1) for i in range(2)])
            rears.append([packed([h[j][i] for h in behind for j in (c, c + 3)], 3, -1) for i in range(2)])
        rears = matvec(links, rounded(rears), True)
        for c in range(3):
            store_pair(x_near, q * 3 + c, either(even, rears[c], fronts[c]))
            store_pair(x_far, q * 3 + c, either(even, fronts[c], rears[c]))


def start_kernel(f_hbm, links_hbm, *refs):
    outs, (f_ref, links_ref, sems) = refs[:4], refs[4:]
    part = f_ref.shape[0] // RHS
    copies = [pltpu.make_async_copy(links_hbm.at[pl.ds(0, links_ref.shape[0])], links_ref, sems.at[RHS])]
    for r in range(RHS):
        rows = pl.ds(r * part, part)
        copies.append(pltpu.make_async_copy(f_hbm.at[rows], f_ref.at[rows], sems.at[r]))
    for copy in copies:
        copy.start()
    copies[0].wait()
    send_t(f_ref, links_ref, 0, *outs[:2], ready=lambda r: copies[1 + r].wait())
    send_x(f_ref, links_ref, 0, *outs[2:])


def interior_kernel(parity, with_base, *refs):
    if with_base:
        f_ref, links_ref, base_ref, clover_ref, acc_ref = refs
        clover_to(clover_ref, lambda r: load_field(base_ref, r), acc_ref, -1.0 / KAPPA2)
    else:
        f_ref, links_ref, acc_ref = refs
    out_parity = 1 - parity
    t_idx, x_idx = site_masks()
    lane = lax.broadcasted_iota(jnp.int32, (8, 128), 1)
    odd = (t_idx + x_idx + lane // HALF_DEPTH + out_parity) % 2
    start = lane - lane % HALF_DEPTH
    up = jnp.where(odd == 1, start + (lane + 1) % HALF_DEPTH, lane)
    down = jnp.where(odd == 0, start + (lane + HALF_DEPTH - 1) % HALF_DEPTH, lane)
    zero = jnp.zeros((8, 128), F32)

    def take(value, index):
        return jnp.take_along_axis(value, index, axis=1, mode="promise_in_bounds")

    for mu in (2, 3, 0, 1):
        if mu == 2:
            ahead_of = lambda v: pltpu.roll(v, 128 - HALF_DEPTH, 1)
            behind_of = lambda v: pltpu.roll(v, HALF_DEPTH, 1)
        elif mu == 3:
            ahead_of = lambda v: take(v, up)
            behind_of = lambda v: take(v, down)
        elif mu == 0:
            ahead_of = lambda v: select(t_idx == 0, roll_rows(v, 4), 0.0)
            behind_of = lambda v: select(t_idx == 1, roll_rows(v, 4), 0.0)
        else:
            ahead_of = lambda v: select(x_idx < 3, roll_rows(v, 7), 0.0)
            behind_of = lambda v: select(x_idx > 0, roll_rows(v, 1), 0.0)
        links_out = load_links(links_ref, mu, out_parity)
        links_in = load_links(links_ref, mu, parity)
        for r in range(RHS):
            field = load_field(f_ref, r)
            if mu == 2 and not with_base:
                acc = [(zero, zero)] * 12
            else:
                acc = load_field(acc_ref, r)
            half = color(links_out, each(ahead_of, rounded(project(field, mu, -1))), False)
            acc = rebuild(acc, half, mu, -1)
            half = rounded(color(links_in, rounded(project(field, mu, 1)), True))
            acc = rebuild(acc, each(behind_of, half), mu, 1)
            store_field(acc_ref, r, acc)


def clover_to(clover_ref, get_field, out_ref, scale):
    for chi in range(2):
        matrix = {}
        for i in range(6):
            for j in range(i, 6):
                k = (chi * 6 + i) * 6 + j
                block = clover_ref[k * 16:(k + 1) * 16, :].astype(F32)
                re, im = block[0:8], block[8:16]
                if scale != 1.0:
                    re, im = re * scale, im * scale
                matrix[i, j] = (re, re + im, im - re)
        for r in range(RHS):
            field = get_field(r)[chi * 6:chi * 6 + 6]
            both = [vr + vi for vr, vi in field]
            for i in range(6):
                one = two = three = None
                for j in range(6):
                    vr, vi = field[j]
                    m, plus, minus = matrix[min(i, j), max(i, j)]
                    t_one = m * both[j]
                    if i <= j:
                        t_two, t_three = -(vi * plus), vr * minus
                    else:
                        t_two, t_three = vi * minus, -(vr * plus)
                    one = t_one if one is None else one + t_one
                    two = t_two if two is None else two + t_two
                    three = t_three if three is None else three + t_three
                store_pair(out_ref, r * 12 + chi * 6 + i, (one + two, one + three))


def matvec(links, vector, adjoint):
    out = []
    for a in range(3):
        re = im = None
        for b in range(3):
            lr, li = links[b][a] if adjoint else links[a][b]
            vr, vi = vector[b]
            if adjoint:
                tr, ti = lr * vr + li * vi, lr * vi - li * vr
            else:
                tr, ti = lr * vr - li * vi, lr * vi + li * vr
            re = tr if re is None else re + tr
            im = ti if im is None else im + ti
        out.append((re, im))
    return out


def rebuild_signed(acc, half, mu, sign):
    out = list(acc)
    for j in range(6):
        out[j] = add_power(out[j], half[j], 0)
    half = each(lambda v: v * sign, half)
    for row in range(2):
        col, power = SPIN_INV[mu][row]
        for c in range(3):
            j = (2 + row) * 3 + c
            out[j] = add_power(out[j], half[col * 3 + c], power)
    return out


def join_x(links_ref, acc_ref, x_far, x_near, parity, out_ref, scale=None, done=lambda r: None):
    even = even_device("gx")
    _, x_idx = site_masks()
    sign = jnp.where(x_idx == 3, -1.0, 1.0).astype(F32)
    links = x_edges(load_links(links_ref, 1, 1 - parity))
    for q in range(RHS // 2):
        nxt, last = [], []
        for c in range(3):
            near, far = load_pair(x_near, q * 3 + c), load_pair(x_far, q * 3 + c)
            nxt.append(either(even, near, far))
            last.append(either(even, far, near))
        ahead = matvec(links, nxt, False)
        for r in (2 * q, 2 * q + 1):
            half = [None] * 6
            for s in range(2):
                k = (r % 2) * 2 + s
                for c in range(3):
                    half[s * 3 + c] = tuple(
                        select(
                            x_idx == 3,
                            roll_rows(ahead[c][i], 3 - k),
                            select(x_idx == 0, roll_rows(last[c][i], 5 + k), 0.0),
                        )
                        for i in range(2)
                    )
            field = rebuild_signed(load_field(acc_ref, r), half, 1, sign)
            if scale is not None:
                field = each(lambda v: v * scale, field)
            store_field(out_ref, r, field)
            done(r)


def join_t_kernel(parity, links_ref, acc_ref, t_one, t_two, out_ref):
    even = even_device("ta", "gx")
    t_idx, _ = site_masks()
    first = t_idx == 0
    sign = jnp.where(first, 1.0, -1.0).astype(F32)
    links = t_edges(load_links(links_ref, 0, 1 - parity))
    for r in range(RHS):
        nxt, last = [], []
        for c in range(3):
            one, two = load_pair(t_one, r * 3 + c), load_pair(t_two, r * 3 + c)
            nxt.append(either(even, one, two))
            last.append(either(even, two, one))
        ahead = matvec(links, nxt, False)
        half = [tuple(select(first, last[c][i], ahead[c][i]) for i in range(2)) for c in range(3)]
        half += [
            tuple(roll_rows(select(first, ahead[c][i], last[c][i]), 4) for i in range(2)) for c in range(3)
        ]
        store_field(out_ref, r, rebuild_signed(load_field(acc_ref, r), half, 0, sign))


def odd_kernel(links_ref, clover_ref, acc_ref, x_far, x_near, out_ref, *refs):
    outs, summed = refs[:4], refs[4]
    join_x(links_ref, acc_ref, x_far, x_near, 0, summed)
    clover_to(clover_ref, lambda r: load_field(summed, r), out_ref, 1.0)
    send_t(out_ref, links_ref, 1, *outs[:2])
    send_x(out_ref, links_ref, 1, *outs[2:])


def even_kernel(links_ref, acc_ref, x_far, x_near, out_ref, *outs):
    join_x(links_ref, acc_ref, x_far, x_near, 1, out_ref, -KAPPA2)
    send_t(out_ref, links_ref, 0, *outs[:2])
    send_x(out_ref, links_ref, 0, *outs[2:])


def last_kernel(links_ref, acc_ref, x_far, x_near, out_hbm, held, sems):
    part = held.shape[0] // RHS
    copies = []

    def done(r):
        rows = pl.ds(r * part, part)
        copies.append(pltpu.make_async_copy(held.at[rows], out_hbm.at[rows], sems.at[r]))
        copies[-1].start()

    join_x(links_ref, acc_ref, x_far, x_near, 1, held, -KAPPA2, done)
    for copy in copies:
        copy.wait()


ROWS = RHS * 24 * 8
FIELD = [((ROWS, 128), BF16)]
SUM = [((ROWS, 128), F32)]
T_HALOS = [((RHS * 3 * 16, 128), BF16)] * 2
HALOS = T_HALOS + [((RHS * 3 * 8, 128), BF16)] * 2


def call(kernel, args, outs, flops, scratch=(), in_space=pltpu.VMEM, out_space=pltpu.VMEM):
    return pl.pallas_call(
        kernel,
        out_shape=tuple(jax.ShapeDtypeStruct(shape, dtype) for shape, dtype in outs),
        in_specs=[pl.BlockSpec(memory_space=in_space)] * len(args),
        out_specs=tuple([pl.BlockSpec(memory_space=out_space)] * len(outs)),
        scratch_shapes=list(scratch),
        compiler_params=pltpu.CompilerParams(vmem_limit_bytes=24 * 1024 * 1024),
        cost_estimate=pl.CostEstimate(flops=flops, bytes_accessed=2 * 1024 * 1024, transcendentals=0),
    )(*args)


def swap(value, axis, far):
    count = lax.axis_size(axis)
    assert count % 2 == 0
    pairs = [(i, (i + (1 if (i % 2 == 0) != far else -1)) % count) for i in range(count)]
    return lax.ppermute(value, axis, pairs)


def swap_t(value, ahead):
    count, across = lax.axis_size("ta"), lax.axis_size("gx")
    assert count % 2 == 0 and across % 2 == 0
    pairs = []
    for i in range(count):
        for j in range(across):
            step = 1 if ((i + j) % 2 == 0) == ahead else -1
            pairs.append((i * across + j, (i + step) % count * across + j))
    return lax.ppermute(value, ("ta", "gx"), pairs)


def per_device(source, gauge_links, clover_even, clover_odd_inv):
    shape = source.shape
    f = source.reshape(-1, 128)
    links = gauge_links.reshape(-1, 128)
    even = clover_even.reshape(-1, 128)
    odd = clover_odd_inv.reshape(-1, 128)
    held = [pltpu.with_memory_space_constraint(v, pltpu.HBM) for v in (f, links)]
    start_scratch = [
        pltpu.VMEM((ROWS, 128), BF16),
        pltpu.VMEM((links.shape[0] // 2, 128), BF16),
        pltpu.SemaphoreType.DMA((RHS + 1,)),
    ]
    t_one, t_two, x_far, x_near = call(start_kernel, held, HALOS, 1_500_000, start_scratch, in_space=pltpu.HBM)
    for hop in range(4):
        parity = hop % 2
        t_one, t_two = swap_t(t_one, True), swap_t(t_two, False)
        x_far, x_near = swap(x_far, "gx", True), swap(x_near, "gx", False)
        base = (before, even) if parity else ()
        acc, = call(
            functools.partial(interior_kernel, parity, bool(parity)),
            (f, links, *base), SUM, 8_000_000 if parity else 5_000_000,
        )
        acc, = call(functools.partial(join_t_kernel, parity), (links, acc, t_one, t_two), SUM, 1_000_000)
        before = f
        if parity == 0:
            f, t_one, t_two, x_far, x_near = call(
                odd_kernel, (links, odd, acc, x_far, x_near), FIELD + HALOS, 4_000_000,
                [pltpu.VMEM((ROWS, 128), BF16)],
            )
        elif hop == 1:
            f, t_one, t_two, x_far, x_near = call(
                even_kernel, (links, acc, x_far, x_near), FIELD + HALOS, 2_000_000
            )
        else:
            out, = call(
                last_kernel, (links, acc, x_far, x_near), FIELD, 1_000_000,
                [pltpu.VMEM((ROWS, 128), BF16), pltpu.SemaphoreType.DMA((RHS,))], out_space=pltpu.HBM,
            )
    return out.reshape(shape)


def solution(mesh):
    field_spec = P(None, None, None, None, ("groups", "ta"), "gx", None)
    link_spec = P(None, None, None, None, None, ("groups", "ta"), "gx", None)
    return jax.shard_map(
        per_device,
        mesh=mesh,
        in_specs=(field_spec, link_spec, field_spec, field_spec),
        out_specs=field_spec,
        check_vma=False,
    )
```

```python
import functools

import jax
import jax.numpy as jnp
from jax import lax
from jax.experimental import pallas as pl
from jax.experimental.pallas import tpu as pltpu
from jax.sharding import PartitionSpec as P

HALF_DEPTH = 8
KAPPA2 = 0.14 * 0.14
RHS = 4
F32 = jnp.float32
BF16 = jnp.bfloat16

SPIN = (((0, 0), (1, 0)), ((1, 3), (0, 3)), ((1, 2), (0, 0)), ((0, 3), (1, 1)))
SPIN_INV = (((0, 0), (1, 0)), ((1, 1), (0, 1)), ((1, 0), (0, 2)), ((0, 1), (1, 3)))


def add_power(base, value, power):
    (br, bi), (vr, vi) = base, value
    if power == 0:
        return br + vr, bi + vi
    if power == 1:
        return br - vi, bi + vr
    if power == 2:
        return br - vr, bi - vi
    return br + vi, bi - vr


def project(field, mu, sign):
    shift = 0 if sign > 0 else 2
    half = []
    for row in range(2):
        col, power = SPIN[mu][row]
        for c in range(3):
            half.append(add_power(field[row * 3 + c], field[(2 + col) * 3 + c], (power + shift) % 4))
    return half


def rebuild(acc, half, mu, sign):
    shift = 0 if sign > 0 else 2
    out = list(acc)
    for j in range(6):
        out[j] = add_power(out[j], half[j], 0)
    for row in range(2):
        col, power = SPIN_INV[mu][row]
        for c in range(3):
            j = (2 + row) * 3 + c
            out[j] = add_power(out[j], half[col * 3 + c], (power + shift) % 4)
    return out


def color(links, half, adjoint):
    out = []
    for s in range(2):
        for a in range(3):
            re = im = None
            for b in range(3):
                lr, li = links[b][a] if adjoint else links[a][b]
                vr, vi = half[s * 3 + b]
                if adjoint:
                    tr, ti = lr * vr + li * vi, lr * vi - li * vr
                else:
                    tr, ti = lr * vr - li * vi, lr * vi + li * vr
                re = tr if re is None else re + tr
                im = ti if im is None else im + ti
            out.append((re, im))
    return out


def each(function, half):
    return [(function(re), function(im)) for re, im in half]


def load_pair(ref, index):
    block = ref[index * 16:(index + 1) * 16, :].astype(F32)
    return block[0:8], block[8:16]


def rounded(half):
    out = []
    for pair in half:
        block = jnp.concatenate(pair, axis=0).astype(BF16).astype(F32)
        out.append((block[0:8], block[8:16]))
    return out


def load_links(ref, mu, parity):
    links = []
    for a in range(3):
        row = []
        for b in range(3):
            k = ((mu * 3 + a) * 3 + b) * 2
            row.append((load_pair(ref, k)[parity], load_pair(ref, k + 1)[parity]))
        links.append(row)
    return links


def load_field(ref, r):
    return [load_pair(ref, r * 12 + j) for j in range(12)]


def store_pair(ref, index, pair):
    ref[index * 16:(index + 1) * 16, :] = jnp.concatenate(pair, axis=0).astype(ref.dtype)


def store_field(ref, r, field):
    for j in range(12):
        store_pair(ref, r * 12 + j, field[j])


def site_masks():
    rows = lax.broadcasted_iota(jnp.int32, (8, 128), 0)
    return rows // 4, rows % 4


def even_device(*axes):
    place = sum(lax.axis_index(axis) for axis in axes)
    return lax.broadcast(place % 2, (8, 128)) == 0


def either(even, a, b):
    return [select(even, a[i], b[i]) for i in range(2)]


def roll_rows(value, shift):
    shift %= 8
    return pltpu.roll(value, shift, 0) if shift else value


def select(mask, a, b):
    return jnp.where(mask, a, b)


def t_edges(links):
    t_idx, _ = site_masks()
    return [each(lambda v: select(t_idx == 0, roll_rows(v, 4), v), row) for row in links]


def x_edges(links):
    _, x_idx = site_masks()

    def edge(value):
        out = value
        for k in range(3):
            out = select(x_idx == k, roll_rows(value, k - 3), out)
        return out

    return [each(edge, row) for row in links]


def send_t(f_ref, links_ref, parity, t_one, t_two, ready=lambda r: None):
    even = even_device("ta")
    t_idx, _ = site_masks()
    first = t_idx == 0
    links = t_edges(load_links(links_ref, 0, parity))
    for r in range(RHS):
        ready(r)
        field = load_field(f_ref, r)
        ahead, behind = project(field, 0, -1), project(field, 0, 1)
        rears = [
            tuple(select(first, roll_rows(behind[c][i], 4), behind[c + 3][i]) for i in range(2)) for c in range(3)
        ]
        rears = matvec(links, rounded(rears), True)
        for c in range(3):
            front = [select(first, ahead[c + 3][i], roll_rows(ahead[c][i], 4)) for i in range(2)]
            store_pair(t_one, r * 3 + c, either(even, rears[c], front))
            store_pair(t_two, r * 3 + c, either(even, front, rears[c]))


def send_x_kernel(parity, f_ref, links_ref, x_far, x_near):
    even = even_device("gx")
    _, x_idx = site_masks()
    links = x_edges(load_links(links_ref, 1, parity))

    def packed(values, row, step):
        out = values[0]
        for k in range(1, 4):
            out = select(x_idx == row + step * k, roll_rows(values[k], step * k), out)
        return out

    for q in range(RHS // 2):
        fields = [load_field(f_ref, r) for r in (2 * q, 2 * q + 1)]
        ahead = [project(field, 1, -1) for field in fields]
        behind = [project(field, 1, 1) for field in fields]
        fronts, rears = [], []
        for c in range(3):
            fronts.append([packed([h[j][i] for h in ahead for j in (c, c + 3)], 0, 1) for i in range(2)])
            rears.append([packed([h[j][i] for h in behind for j in (c, c + 3)], 3, -1) for i in range(2)])
        rears = matvec(links, rounded(rears), True)
        for c in range(3):
            store_pair(x_near, q * 3 + c, either(even, rears[c], fronts[c]))
            store_pair(x_far, q * 3 + c, either(even, fronts[c], rears[c]))


def start_kernel(f_hbm, links_hbm, *refs):
    outs, (f_ref, links_ref, sems) = refs[:2], refs[2:]
    part = f_ref.shape[0] // RHS
    copies = [pltpu.make_async_copy(links_hbm.at[pl.ds(0, links_ref.shape[0])], links_ref, sems.at[RHS])]
    for r in range(RHS):
        rows = pl.ds(r * part, part)
        copies.append(pltpu.make_async_copy(f_hbm.at[rows], f_ref.at[rows], sems.at[r]))
    for copy in copies:
        copy.start()
    copies[0].wait()
    send_t(f_ref, links_ref, 0, *outs, ready=lambda r: copies[1 + r].wait())


def interior_kernel(parity, with_base, *refs):
    if with_base:
        f_ref, links_ref, base_ref, clover_ref, acc_ref = refs
        clover_to(clover_ref, lambda r: load_field(base_ref, r), acc_ref, -1.0 / KAPPA2)
    else:
        f_ref, links_ref, acc_ref = refs
    out_parity = 1 - parity
    t_idx, x_idx = site_masks()
    lane = lax.broadcasted_iota(jnp.int32, (8, 128), 1)
    odd = (t_idx + x_idx + lane // HALF_DEPTH + out_parity) % 2
    start = lane - lane % HALF_DEPTH
    up = jnp.where(odd == 1, start + (lane + 1) % HALF_DEPTH, lane)
    down = jnp.where(odd == 0, start + (lane + HALF_DEPTH - 1) % HALF_DEPTH, lane)
    zero = jnp.zeros((8, 128), F32)

    def take(value, index):
        return jnp.take_along_axis(value, index, axis=1, mode="promise_in_bounds")

    for mu in (2, 3, 0, 1):
        if mu == 2:
            ahead_of = lambda v: pltpu.roll(v, 128 - HALF_DEPTH, 1)
            behind_of = lambda v: pltpu.roll(v, HALF_DEPTH, 1)
        elif mu == 3:
            ahead_of = lambda v: take(v, up)
            behind_of = lambda v: take(v, down)
        elif mu == 0:
            ahead_of = lambda v: select(t_idx == 0, roll_rows(v, 4), 0.0)
            behind_of = lambda v: select(t_idx == 1, roll_rows(v, 4), 0.0)
        else:
            ahead_of = lambda v: select(x_idx < 3, roll_rows(v, 7), 0.0)
            behind_of = lambda v: select(x_idx > 0, roll_rows(v, 1), 0.0)
        links_out = load_links(links_ref, mu, out_parity)
        links_in = load_links(links_ref, mu, parity)
        for r in range(RHS):
            field = load_field(f_ref, r)
            if mu == 2 and not with_base:
                acc = [(zero, zero)] * 12
            else:
                acc = load_field(acc_ref, r)
            half = color(links_out, each(ahead_of, rounded(project(field, mu, -1))), False)
            acc = rebuild(acc, half, mu, -1)
            half = rounded(color(links_in, rounded(project(field, mu, 1)), True))
            acc = rebuild(acc, each(behind_of, half), mu, 1)
            store_field(acc_ref, r, acc)


def clover_to(clover_ref, get_field, out_ref, scale):
    for chi in range(2):
        matrix = {}
        for i in range(6):
            for j in range(i, 6):
                k = (chi * 6 + i) * 6 + j
                block = clover_ref[k * 16:(k + 1) * 16, :].astype(F32)
                re, im = block[0:8], block[8:16]
                if scale != 1.0:
                    re, im = re * scale, im * scale
                matrix[i, j] = (re, re + im, im - re)
        for r in range(RHS):
            field = get_field(r)[chi * 6:chi * 6 + 6]
            both = [vr + vi for vr, vi in field]
            for i in range(6):
                one = two = three = None
                for j in range(6):
                    vr, vi = field[j]
                    m, plus, minus = matrix[min(i, j), max(i, j)]
                    t_one = m * both[j]
                    if i <= j:
                        t_two, t_three = -(vi * plus), vr * minus
                    else:
                        t_two, t_three = vi * minus, -(vr * plus)
                    one = t_one if one is None else one + t_one
                    two = t_two if two is None else two + t_two
                    three = t_three if three is None else three + t_three
                store_pair(out_ref, r * 12 + chi * 6 + i, (one + two, one + three))


def matvec(links, vector, adjoint):
    out = []
    for a in range(3):
        re = im = None
        for b in range(3):
            lr, li = links[b][a] if adjoint else links[a][b]
            vr, vi = vector[b]
            if adjoint:
                tr, ti = lr * vr + li * vi, lr * vi - li * vr
            else:
                tr, ti = lr * vr - li * vi, lr * vi + li * vr
            re = tr if re is None else re + tr
            im = ti if im is None else im + ti
        out.append((re, im))
    return out


def rebuild_signed(acc, half, mu, sign):
    out = list(acc)
    for j in range(6):
        out[j] = add_power(out[j], half[j], 0)
    half = each(lambda v: v * sign, half)
    for row in range(2):
        col, power = SPIN_INV[mu][row]
        for c in range(3):
            j = (2 + row) * 3 + c
            out[j] = add_power(out[j], half[col * 3 + c], power)
    return out


def join_x_kernel(parity, links_ref, acc_ref, x_far, x_near, out_ref):
    even = even_device("gx")
    _, x_idx = site_masks()
    sign = jnp.where(x_idx == 3, -1.0, 1.0).astype(F32)
    links = x_edges(load_links(links_ref, 1, 1 - parity))
    for q in range(RHS // 2):
        nxt, last = [], []
        for c in range(3):
            near, far = load_pair(x_near, q * 3 + c), load_pair(x_far, q * 3 + c)
            nxt.append(either(even, near, far))
            last.append(either(even, far, near))
        ahead = matvec(links, nxt, False)
        for r in (2 * q, 2 * q + 1):
            half = [None] * 6
            for s in range(2):
                k = (r % 2) * 2 + s
                for c in range(3):
                    half[s * 3 + c] = tuple(
                        select(
                            x_idx == 3,
                            roll_rows(ahead[c][i], 3 - k),
                            select(x_idx == 0, roll_rows(last[c][i], 5 + k), 0.0),
                        )
                        for i in range(2)
                    )
            store_field(out_ref, r, rebuild_signed(load_field(acc_ref, r), half, 1, sign))


def join_t(links_ref, acc_ref, t_one, t_two, parity, out_ref, scale=None, done=lambda r: None):
    even = even_device("ta")
    t_idx, _ = site_masks()
    first = t_idx == 0
    sign = jnp.where(first, 1.0, -1.0).astype(F32)
    links = t_edges(load_links(links_ref, 0, 1 - parity))
    for r in range(RHS):
        nxt, last = [], []
        for c in range(3):
            one, two = load_pair(t_one, r * 3 + c), load_pair(t_two, r * 3 + c)
            nxt.append(either(even, one, two))
            last.append(either(even, two, one))
        ahead = matvec(links, nxt, False)
        half = [tuple(select(first, last[c][i], ahead[c][i]) for i in range(2)) for c in range(3)]
        half += [
            tuple(roll_rows(select(first, ahead[c][i], last[c][i]), 4) for i in range(2)) for c in range(3)
        ]
        field = rebuild_signed(load_field(acc_ref, r), half, 0, sign)
        if scale is not None:
            field = each(lambda v: v * scale, field)
        store_field(out_ref, r, field)
        done(r)


def odd_kernel(links_ref, clover_ref, acc_ref, t_one, t_two, out_ref, *refs):
    outs, summed = refs[:2], refs[2]
    join_t(links_ref, acc_ref, t_one, t_two, 0, summed)
    clover_to(clover_ref, lambda r: load_field(summed, r), out_ref, 1.0)
    send_t(out_ref, links_ref, 1, *outs)


def even_kernel(links_ref, acc_ref, t_one, t_two, out_ref, *outs):
    join_t(links_ref, acc_ref, t_one, t_two, 1, out_ref, -KAPPA2)
    send_t(out_ref, links_ref, 0, *outs)


def last_kernel(links_ref, acc_ref, t_one, t_two, out_hbm, held, sems):
    part = held.shape[0] // RHS
    copies = []

    def done(r):
        rows = pl.ds(r * part, part)
        copies.append(pltpu.make_async_copy(held.at[rows], out_hbm.at[rows], sems.at[r]))
        copies[-1].start()

    join_t(links_ref, acc_ref, t_one, t_two, 1, held, -KAPPA2, done)
    for copy in copies:
        copy.wait()


ROWS = RHS * 24 * 8
FIELD = [((ROWS, 128), BF16)]
SUM = [((ROWS, 128), F32)]
T_HALOS = [((RHS * 3 * 16, 128), BF16)] * 2
X_HALOS = [((RHS * 3 * 8, 128), BF16)] * 2


def call(kernel, args, outs, flops, scratch=(), in_space=pltpu.VMEM, out_space=pltpu.VMEM):
    return pl.pallas_call(
        kernel,
        out_shape=tuple(jax.ShapeDtypeStruct(shape, dtype) for shape, dtype in outs),
        in_specs=[pl.BlockSpec(memory_space=in_space)] * len(args),
        out_specs=tuple([pl.BlockSpec(memory_space=out_space)] * len(outs)),
        scratch_shapes=list(scratch),
        compiler_params=pltpu.CompilerParams(vmem_limit_bytes=24 * 1024 * 1024),
        cost_estimate=pl.CostEstimate(flops=flops, bytes_accessed=2 * 1024 * 1024, transcendentals=0),
    )(*args)


def swap(value, axis, far):
    count = lax.axis_size(axis)
    assert count % 2 == 0
    pairs = [(i, (i + (1 if (i % 2 == 0) != far else -1)) % count) for i in range(count)]
    return lax.ppermute(value, axis, pairs)


def per_device(source, gauge_links, clover_even, clover_odd_inv):
    shape = source.shape
    f = source.reshape(-1, 128)
    links = gauge_links.reshape(-1, 128)
    even = clover_even.reshape(-1, 128)
    odd = clover_odd_inv.reshape(-1, 128)
    held = [pltpu.with_memory_space_constraint(v, pltpu.HBM) for v in (f, links)]
    start_scratch = [
        pltpu.VMEM((ROWS, 128), BF16),
        pltpu.VMEM((links.shape[0] // 4, 128), BF16),
        pltpu.SemaphoreType.DMA((RHS + 1,)),
    ]
    t_one, t_two = call(start_kernel, held, T_HALOS, 1_500_000, start_scratch, in_space=pltpu.HBM)
    for hop in range(4):
        parity = hop % 2
        t_one, t_two = swap(t_one, "ta", False), swap(t_two, "ta", True)
        x_far, x_near = call(
            functools.partial(send_x_kernel, parity), (f, links), X_HALOS, 1_500_000
        )
        here, x_far, x_near = lax.optimization_barrier((f, x_far, x_near))
        x_far, x_near = swap(x_far, "gx", True), swap(x_near, "gx", False)
        base = (before, even) if parity else ()
        acc, = call(
            functools.partial(interior_kernel, parity, bool(parity)),
            (here, links, *base), SUM, 8_000_000 if parity else 5_000_000,
        )
        acc, = call(functools.partial(join_x_kernel, parity), (links, acc, x_far, x_near), SUM, 1_000_000)
        before = f
        if parity == 0:
            f, t_one, t_two = call(
                odd_kernel, (links, odd, acc, t_one, t_two), FIELD + T_HALOS, 4_000_000,
                [pltpu.VMEM((ROWS, 128), BF16)],
            )
        elif hop == 1:
            f, t_one, t_two = call(
                even_kernel, (links, acc, t_one, t_two), FIELD + T_HALOS, 2_000_000
            )
        else:
            out, = call(
                last_kernel, (links, acc, t_one, t_two), FIELD, 1_000_000,
                [pltpu.VMEM((ROWS, 128), BF16), pltpu.SemaphoreType.DMA((RHS,))], out_space=pltpu.HBM,
            )
    return out.reshape(shape)


def solution(mesh):
    field_spec = P(None, None, None, None, ("groups", "ta"), "gx", None)
    link_spec = P(None, None, None, None, None, ("groups", "ta"), "gx", None)
    return jax.shard_map(
        per_device,
        mesh=mesh,
        in_specs=(field_spec, link_spec, field_spec, field_spec),
        out_specs=field_spec,
        check_vma=False,
    )
```

```python
import functools

import jax
import jax.numpy as jnp
from jax import lax
from jax.experimental import pallas as pl
from jax.experimental.pallas import tpu as pltpu
from jax.sharding import PartitionSpec as P

HALF_DEPTH = 8
KAPPA2 = 0.14 * 0.14
RHS = 4
F32 = jnp.float32
BF16 = jnp.bfloat16

SPIN = (((0, 0), (1, 0)), ((1, 3), (0, 3)), ((1, 2), (0, 0)), ((0, 3), (1, 1)))
SPIN_INV = (((0, 0), (1, 0)), ((1, 1), (0, 1)), ((1, 0), (0, 2)), ((0, 1), (1, 3)))


def add_power(base, value, power):
    (br, bi), (vr, vi) = base, value
    if power == 0:
        return br + vr, bi + vi
    if power == 1:
        return br - vi, bi + vr
    if power == 2:
        return br - vr, bi - vi
    return br + vi, bi - vr


def project(field, mu, sign):
    shift = 0 if sign > 0 else 2
    half = []
    for row in range(2):
        col, power = SPIN[mu][row]
        for c in range(3):
            half.append(add_power(field[row * 3 + c], field[(2 + col) * 3 + c], (power + shift) % 4))
    return half


def rebuild(acc, half, mu, sign):
    shift = 0 if sign > 0 else 2
    out = list(acc)
    for j in range(6):
        out[j] = add_power(out[j], half[j], 0)
    for row in range(2):
        col, power = SPIN_INV[mu][row]
        for c in range(3):
            j = (2 + row) * 3 + c
            out[j] = add_power(out[j], half[col * 3 + c], (power + shift) % 4)
    return out


def color(links, half, adjoint):
    out = []
    for s in range(2):
        for a in range(3):
            re = im = None
            for b in range(3):
                lr, li = links[b][a] if adjoint else links[a][b]
                vr, vi = half[s * 3 + b]
                if adjoint:
                    tr, ti = lr * vr + li * vi, lr * vi - li * vr
                else:
                    tr, ti = lr * vr - li * vi, lr * vi + li * vr
                re = tr if re is None else re + tr
                im = ti if im is None else im + ti
            out.append((re, im))
    return out


def each(function, half):
    return [(function(re), function(im)) for re, im in half]


def load_pair(ref, index):
    block = ref[index * 16:(index + 1) * 16, :].astype(F32)
    return block[0:8], block[8:16]


def rounded(half):
    out = []
    for pair in half:
        block = jnp.concatenate(pair, axis=0).astype(BF16).astype(F32)
        out.append((block[0:8], block[8:16]))
    return out


def load_links(ref, mu, parity):
    links = []
    for a in range(3):
        row = []
        for b in range(3):
            k = ((mu * 3 + a) * 3 + b) * 2
            row.append((load_pair(ref, k)[parity], load_pair(ref, k + 1)[parity]))
        links.append(row)
    return links


def load_field(ref, r):
    return [load_pair(ref, r * 12 + j) for j in range(12)]


def store_pair(ref, index, pair):
    ref[index * 16:(index + 1) * 16, :] = jnp.concatenate(pair, axis=0).astype(ref.dtype)


def store_field(ref, r, field):
    for j in range(12):
        store_pair(ref, r * 12 + j, field[j])


def site_masks():
    rows = lax.broadcasted_iota(jnp.int32, (8, 128), 0)
    return rows // 4, rows % 4


def even_device(*axes):
    place = sum(lax.axis_index(axis) for axis in axes)
    return lax.broadcast(place % 2, (8, 128)) == 0


def either(even, a, b):
    return [select(even, a[i], b[i]) for i in range(2)]


def roll_rows(value, shift):
    shift %= 8
    return pltpu.roll(value, shift, 0) if shift else value


def select(mask, a, b):
    return jnp.where(mask, a, b)


def t_edges(links):
    t_idx, _ = site_masks()
    return [each(lambda v: select(t_idx == 0, roll_rows(v, 4), v), row) for row in links]


def x_edges(links):
    _, x_idx = site_masks()

    def edge(value):
        out = value
        for k in range(3):
            out = select(x_idx == k, roll_rows(value, k - 3), out)
        return out

    return [each(edge, row) for row in links]


def send_t(f_ref, links_ref, parity, t_one, t_two, ready=lambda r: None):
    even = even_device("ta", "gx")
    t_idx, _ = site_masks()
    first = t_idx == 0
    links = t_edges(load_links(links_ref, 0, parity))
    for r in range(RHS):
        ready(r)
        field = load_field(f_ref, r)
        ahead, behind = project(field, 0, -1), project(field, 0, 1)
        rears = [
            tuple(select(first, roll_rows(behind[c][i], 4), behind[c + 3][i]) for i in range(2)) for c in range(3)
        ]
        rears = matvec(links, rounded(rears), True)
        for c in range(3):
            front = [select(first, ahead[c + 3][i], roll_rows(ahead[c][i], 4)) for i in range(2)]
            store_pair(t_one, r * 3 + c, either(even, rears[c], front))
            store_pair(t_two, r * 3 + c, either(even, front, rears[c]))


def send_x_kernel(parity, f_ref, links_ref, x_near, x_far):
    even = even_device("gx")
    _, x_idx = site_masks()
    links = x_edges(load_links(links_ref, 1, parity))

    def packed(values, row, step):
        out = values[0]
        for k in range(1, 4):
            out = select(x_idx == row + step * k, roll_rows(values[k], step * k), out)
        return out

    for q in range(RHS // 2):
        fields = [load_field(f_ref, r) for r in (2 * q, 2 * q + 1)]
        ahead = [project(field, 1, -1) for field in fields]
        behind = [project(field, 1, 1) for field in fields]
        fronts, rears = [], []
        for c in range(3):
            fronts.append([packed([h[j][i] for h in ahead for j in (c, c + 3)], 0, 1) for i in range(2)])
            rears.append([packed([h[j][i] for h in behind for j in (c, c + 3)], 3, -1) for i in range(2)])
        rears = matvec(links, rounded(rears), True)
        for c in range(3):
            store_pair(x_near, q * 3 + c, either(even, rears[c], fronts[c]))
            store_pair(x_far, q * 3 + c, either(even, fronts[c], rears[c]))


def start_kernel(f_hbm, links_hbm, *refs):
    outs, (f_ref, links_ref, sems) = refs[:2], refs[2:]
    part = f_ref.shape[0] // RHS
    copies = [pltpu.make_async_copy(links_hbm.at[pl.ds(0, links_ref.shape[0])], links_ref, sems.at[RHS])]
    for r in range(RHS):
        rows = pl.ds(r * part, part)
        copies.append(pltpu.make_async_copy(f_hbm.at[rows], f_ref.at[rows], sems.at[r]))
    for copy in copies:
        copy.start()
    copies[0].wait()
    send_t(f_ref, links_ref, 0, *outs, ready=lambda r: copies[1 + r].wait())


def interior_kernel(parity, with_base, *refs):
    if with_base:
        f_ref, links_ref, base_ref, clover_ref, acc_ref = refs
        clover_to(clover_ref, lambda r: load_field(base_ref, r), acc_ref, -1.0 / KAPPA2)
    else:
        f_ref, links_ref, acc_ref = refs
    out_parity = 1 - parity
    t_idx, x_idx = site_masks()
    lane = lax.broadcasted_iota(jnp.int32, (8, 128), 1)
    odd = (t_idx + x_idx + lane // HALF_DEPTH + out_parity) % 2
    start = lane - lane % HALF_DEPTH
    up = jnp.where(odd == 1, start + (lane + 1) % HALF_DEPTH, lane)
    down = jnp.where(odd == 0, start + (lane + HALF_DEPTH - 1) % HALF_DEPTH, lane)
    zero = jnp.zeros((8, 128), F32)

    def take(value, index):
        return jnp.take_along_axis(value, index, axis=1, mode="promise_in_bounds")

    for mu in (2, 3, 0, 1):
        if mu == 2:
            ahead_of = lambda v: pltpu.roll(v, 128 - HALF_DEPTH, 1)
            behind_of = lambda v: pltpu.roll(v, HALF_DEPTH, 1)
        elif mu == 3:
            ahead_of = lambda v: take(v, up)
            behind_of = lambda v: take(v, down)
        elif mu == 0:
            ahead_of = lambda v: select(t_idx == 0, roll_rows(v, 4), 0.0)
            behind_of = lambda v: select(t_idx == 1, roll_rows(v, 4), 0.0)
        else:
            ahead_of = lambda v: select(x_idx < 3, roll_rows(v, 7), 0.0)
            behind_of = lambda v: select(x_idx > 0, roll_rows(v, 1), 0.0)
        links_out = load_links(links_ref, mu, out_parity)
        links_in = load_links(links_ref, mu, parity)
        for r in range(RHS):
            field = load_field(f_ref, r)
            if mu == 2 and not with_base:
                acc = [(zero, zero)] * 12
            else:
                acc = load_field(acc_ref, r)
            half = color(links_out, each(ahead_of, rounded(project(field, mu, -1))), False)
            acc = rebuild(acc, half, mu, -1)
            half = rounded(color(links_in, rounded(project(field, mu, 1)), True))
            acc = rebuild(acc, each(behind_of, half), mu, 1)
            store_field(acc_ref, r, acc)


def clover_to(clover_ref, get_field, out_ref, scale):
    for chi in range(2):
        matrix = {}
        for i in range(6):
            for j in range(i, 6):
                k = (chi * 6 + i) * 6 + j
                block = clover_ref[k * 16:(k + 1) * 16, :].astype(F32)
                re, im = block[0:8], block[8:16]
                if scale != 1.0:
                    re, im = re * scale, im * scale
                matrix[i, j] = (re, re + im, im - re)
        for r in range(RHS):
            field = get_field(r)[chi * 6:chi * 6 + 6]
            both = [vr + vi for vr, vi in field]
            for i in range(6):
                one = two = three = None
                for j in range(6):
                    vr, vi = field[j]
                    m, plus, minus = matrix[min(i, j), max(i, j)]
                    t_one = m * both[j]
                    if i <= j:
                        t_two, t_three = -(vi * plus), vr * minus
                    else:
                        t_two, t_three = vi * minus, -(vr * plus)
                    one = t_one if one is None else one + t_one
                    two = t_two if two is None else two + t_two
                    three = t_three if three is None else three + t_three
                store_pair(out_ref, r * 12 + chi * 6 + i, (one + two, one + three))


def matvec(links, vector, adjoint):
    out = []
    for a in range(3):
        re = im = None
        for b in range(3):
            lr, li = links[b][a] if adjoint else links[a][b]
            vr, vi = vector[b]
            if adjoint:
                tr, ti = lr * vr + li * vi, lr * vi - li * vr
            else:
                tr, ti = lr * vr - li * vi, lr * vi + li * vr
            re = tr if re is None else re + tr
            im = ti if im is None else im + ti
        out.append((re, im))
    return out


def rebuild_signed(acc, half, mu, sign):
    out = list(acc)
    for j in range(6):
        out[j] = add_power(out[j], half[j], 0)
    half = each(lambda v: v * sign, half)
    for row in range(2):
        col, power = SPIN_INV[mu][row]
        for c in range(3):
            j = (2 + row) * 3 + c
            out[j] = add_power(out[j], half[col * 3 + c], power)
    return out


def join_x_kernel(parity, links_ref, acc_ref, x_near, x_far, out_ref):
    even = even_device("gx")
    _, x_idx = site_masks()
    sign = jnp.where(x_idx == 3, -1.0, 1.0).astype(F32)
    links = x_edges(load_links(links_ref, 1, 1 - parity))
    for q in range(RHS // 2):
        nxt, last = [], []
        for c in range(3):
            near, far = load_pair(x_near, q * 3 + c), load_pair(x_far, q * 3 + c)
            nxt.append(either(even, near, far))
            last.append(either(even, far, near))
        ahead = matvec(links, nxt, False)
        for r in (2 * q, 2 * q + 1):
            half = [None] * 6
            for s in range(2):
                k = (r % 2) * 2 + s
                for c in range(3):
                    half[s * 3 + c] = tuple(
                        select(
                            x_idx == 3,
                            roll_rows(ahead[c][i], 3 - k),
                            select(x_idx == 0, roll_rows(last[c][i], 5 + k), 0.0),
                        )
                        for i in range(2)
                    )
            store_field(out_ref, r, rebuild_signed(load_field(acc_ref, r), half, 1, sign))


def join_t(links_ref, acc_ref, t_one, t_two, parity, out_ref, scale=None, done=lambda r: None):
    even = even_device("ta", "gx")
    t_idx, _ = site_masks()
    first = t_idx == 0
    sign = jnp.where(first, 1.0, -1.0).astype(F32)
    links = t_edges(load_links(links_ref, 0, 1 - parity))
    for r in range(RHS):
        nxt, last = [], []
        for c in range(3):
            one, two = load_pair(t_one, r * 3 + c), load_pair(t_two, r * 3 + c)
            nxt.append(either(even, one, two))
            last.append(either(even, two, one))
        ahead = matvec(links, nxt, False)
        half = [tuple(select(first, last[c][i], ahead[c][i]) for i in range(2)) for c in range(3)]
        half += [
            tuple(roll_rows(select(first, ahead[c][i], last[c][i]), 4) for i in range(2)) for c in range(3)
        ]
        field = rebuild_signed(load_field(acc_ref, r), half, 0, sign)
        if scale is not None:
            field = each(lambda v: v * scale, field)
        store_field(out_ref, r, field)
        done(r)


def odd_kernel(links_ref, clover_ref, acc_ref, t_one, t_two, out_ref, *refs):
    outs, summed = refs[:2], refs[2]
    join_t(links_ref, acc_ref, t_one, t_two, 0, summed)
    clover_to(clover_ref, lambda r: load_field(summed, r), out_ref, 1.0)
    send_t(out_ref, links_ref, 1, *outs)


def even_kernel(links_ref, acc_ref, t_one, t_two, out_ref, *outs):
    join_t(links_ref, acc_ref, t_one, t_two, 1, out_ref, -KAPPA2)
    send_t(out_ref, links_ref, 0, *outs)


def last_kernel(links_ref, acc_ref, t_one, t_two, out_hbm, held, sems):
    part = held.shape[0] // RHS
    copies = []

    def done(r):
        rows = pl.ds(r * part, part)
        copies.append(pltpu.make_async_copy(held.at[rows], out_hbm.at[rows], sems.at[r]))
        copies[-1].start()

    join_t(links_ref, acc_ref, t_one, t_two, 1, held, -KAPPA2, done)
    for copy in copies:
        copy.wait()


ROWS = RHS * 24 * 8
FIELD = [((ROWS, 128), BF16)]
SUM = [((ROWS, 128), F32)]
T_HALOS = [((RHS * 3 * 16, 128), BF16)] * 2
X_HALOS = [((RHS * 3 * 8, 128), BF16)] * 2


def call(kernel, args, outs, flops, scratch=(), in_space=pltpu.VMEM, out_space=pltpu.VMEM):
    return pl.pallas_call(
        kernel,
        out_shape=tuple(jax.ShapeDtypeStruct(shape, dtype) for shape, dtype in outs),
        in_specs=[pl.BlockSpec(memory_space=in_space)] * len(args),
        out_specs=tuple([pl.BlockSpec(memory_space=out_space)] * len(outs)),
        scratch_shapes=list(scratch),
        compiler_params=pltpu.CompilerParams(vmem_limit_bytes=24 * 1024 * 1024),
        cost_estimate=pl.CostEstimate(flops=flops, bytes_accessed=2 * 1024 * 1024, transcendentals=0),
    )(*args)


def swap(value, axis, far):
    count = lax.axis_size(axis)
    assert count % 2 == 0
    pairs = [(i, (i + (1 if (i % 2 == 0) != far else -1)) % count) for i in range(count)]
    return lax.ppermute(value, axis, pairs)


def swap_t(value, ahead):
    count, across = lax.axis_size("ta"), lax.axis_size("gx")
    assert count % 2 == 0 and across % 2 == 0
    pairs = []
    for i in range(count):
        for j in range(across):
            step = 1 if ((i + j) % 2 == 0) == ahead else -1
            pairs.append((i * across + j, (i + step) % count * across + j))
    return lax.ppermute(value, ("ta", "gx"), pairs)


def per_device(source, gauge_links, clover_even, clover_odd_inv):
    shape = source.shape
    f = source.reshape(-1, 128)
    links = gauge_links.reshape(-1, 128)
    even = clover_even.reshape(-1, 128)
    odd = clover_odd_inv.reshape(-1, 128)
    held = [pltpu.with_memory_space_constraint(v, pltpu.HBM) for v in (f, links)]
    start_scratch = [
        pltpu.VMEM((ROWS, 128), BF16),
        pltpu.VMEM((links.shape[0] // 4, 128), BF16),
        pltpu.SemaphoreType.DMA((RHS + 1,)),
    ]
    t_one, t_two = call(start_kernel, held, T_HALOS, 1_500_000, start_scratch, in_space=pltpu.HBM)
    for hop in range(4):
        parity = hop % 2
        t_one, t_two = swap_t(t_one, True), swap_t(t_two, False)
        x_near, x_far = call(
            functools.partial(send_x_kernel, parity), (f, links), X_HALOS, 1_500_000
        )
        here, x_near, x_far = lax.optimization_barrier((f, x_near, x_far))
        x_near, x_far = swap(x_near, "gx", False), swap(x_far, "gx", True)
        base = (before, even) if parity else ()
        acc, = call(
            functools.partial(interior_kernel, parity, bool(parity)),
            (here, links, *base), SUM, 8_000_000 if parity else 5_000_000,
        )
        acc, = call(functools.partial(join_x_kernel, parity), (links, acc, x_near, x_far), SUM, 1_000_000)
        before = f
        if parity == 0:
            f, t_one, t_two = call(
                odd_kernel, (links, odd, acc, t_one, t_two), FIELD + T_HALOS, 4_000_000,
                [pltpu.VMEM((ROWS, 128), BF16)],
            )
        elif hop == 1:
            f, t_one, t_two = call(
                even_kernel, (links, acc, t_one, t_two), FIELD + T_HALOS, 2_000_000
            )
        else:
            out, = call(
                last_kernel, (links, acc, t_one, t_two), FIELD, 1_000_000,
                [pltpu.VMEM((ROWS, 128), BF16), pltpu.SemaphoreType.DMA((RHS,))], out_space=pltpu.HBM,
            )
    return out.reshape(shape)


def solution(mesh):
    field_spec = P(None, None, None, None, ("groups", "ta"), "gx", None)
    link_spec = P(None, None, None, None, None, ("groups", "ta"), "gx", None)
    return jax.shard_map(
        per_device,
        mesh=mesh,
        in_specs=(field_spec, link_spec, field_spec, field_spec),
        out_specs=field_spec,
        check_vma=False,
    )
```

```python
import functools

import jax
import jax.numpy as jnp
from jax import lax
from jax.experimental import pallas as pl
from jax.experimental.pallas import tpu as pltpu
from jax.sharding import PartitionSpec as P

HALF_DEPTH = 8
KAPPA2 = 0.14 * 0.14
RHS = 4
F32 = jnp.float32
BF16 = jnp.bfloat16

SPIN = (((0, 0), (1, 0)), ((1, 3), (0, 3)), ((1, 2), (0, 0)), ((0, 3), (1, 1)))
SPIN_INV = (((0, 0), (1, 0)), ((1, 1), (0, 1)), ((1, 0), (0, 2)), ((0, 1), (1, 3)))


def add_power(base, value, power):
    (br, bi), (vr, vi) = base, value
    if power == 0:
        return br + vr, bi + vi
    if power == 1:
        return br - vi, bi + vr
    if power == 2:
        return br - vr, bi - vi
    return br + vi, bi - vr


def project(field, mu, sign):
    shift = 0 if sign > 0 else 2
    half = []
    for row in range(2):
        col, power = SPIN[mu][row]
        for c in range(3):
            half.append(add_power(field[row * 3 + c], field[(2 + col) * 3 + c], (power + shift) % 4))
    return half


def rebuild(acc, half, mu, sign):
    shift = 0 if sign > 0 else 2
    out = list(acc)
    for j in range(6):
        out[j] = add_power(out[j], half[j], 0)
    for row in range(2):
        col, power = SPIN_INV[mu][row]
        for c in range(3):
            j = (2 + row) * 3 + c
            out[j] = add_power(out[j], half[col * 3 + c], (power + shift) % 4)
    return out


def color(links, half, adjoint):
    out = []
    for s in range(2):
        for a in range(3):
            re = im = None
            for b in range(3):
                lr, li = links[b][a] if adjoint else links[a][b]
                vr, vi = half[s * 3 + b]
                if adjoint:
                    tr, ti = lr * vr + li * vi, lr * vi - li * vr
                else:
                    tr, ti = lr * vr - li * vi, lr * vi + li * vr
                re = tr if re is None else re + tr
                im = ti if im is None else im + ti
            out.append((re, im))
    return out


def each(function, half):
    return [(function(re), function(im)) for re, im in half]


def load_pair(ref, index):
    block = ref[index * 16:(index + 1) * 16, :].astype(F32)
    return block[0:8], block[8:16]


def rounded(half):
    out = []
    for pair in half:
        block = jnp.concatenate(pair, axis=0).astype(BF16).astype(F32)
        out.append((block[0:8], block[8:16]))
    return out


def load_links(ref, mu, parity):
    links = []
    for a in range(3):
        row = []
        for b in range(3):
            k = ((mu * 3 + a) * 3 + b) * 2
            row.append((load_pair(ref, k)[parity], load_pair(ref, k + 1)[parity]))
        links.append(row)
    return links


def load_field(ref, r):
    return [load_pair(ref, r * 12 + j) for j in range(12)]


def store_pair(ref, index, pair):
    ref[index * 16:(index + 1) * 16, :] = jnp.concatenate(pair, axis=0).astype(ref.dtype)


def store_field(ref, r, field):
    for j in range(12):
        store_pair(ref, r * 12 + j, field[j])


def site_masks():
    rows = lax.broadcasted_iota(jnp.int32, (8, 128), 0)
    return rows // 4, rows % 4


def even_device(*axes):
    place = sum(lax.axis_index(axis) for axis in axes)
    return lax.broadcast(place % 2, (8, 128)) == 0


def either(even, a, b):
    return [select(even, a[i], b[i]) for i in range(2)]


def roll_rows(value, shift):
    shift %= 8
    return pltpu.roll(value, shift, 0) if shift else value


def select(mask, a, b):
    return jnp.where(mask, a, b)


def t_edges(links):
    t_idx, _ = site_masks()
    return [each(lambda v: select(t_idx == 0, roll_rows(v, 4), v), row) for row in links]


def x_edges(links):
    _, x_idx = site_masks()

    def edge(value):
        out = value
        for k in range(3):
            out = select(x_idx == k, roll_rows(value, k - 3), out)
        return out

    return [each(edge, row) for row in links]


def send_t(f_ref, links_ref, parity, t_one, t_two, ready=lambda r: None):
    even = even_device("ta", "gx")
    t_idx, _ = site_masks()
    first = t_idx == 0
    links = t_edges(load_links(links_ref, 0, parity))
    for r in range(RHS):
        ready(r)
        field = load_field(f_ref, r)
        ahead, behind = project(field, 0, -1), project(field, 0, 1)
        rears = [
            tuple(select(first, roll_rows(behind[c][i], 4), behind[c + 3][i]) for i in range(2)) for c in range(3)
        ]
        rears = matvec(links, rounded(rears), True)
        for c in range(3):
            front = [select(first, ahead[c + 3][i], roll_rows(ahead[c][i], 4)) for i in range(2)]
            store_pair(t_one, r * 3 + c, either(even, rears[c], front))
            store_pair(t_two, r * 3 + c, either(even, front, rears[c]))


def send_x_kernel(parity, f_ref, links_ref, x_back, x_ahead):
    _, x_idx = site_masks()
    links = x_edges(load_links(links_ref, 1, parity))

    def packed(values, row, step):
        out = values[0]
        for k in range(1, 4):
            out = select(x_idx == row + step * k, roll_rows(values[k], step * k), out)
        return out

    for q in range(RHS // 2):
        fields = [load_field(f_ref, r) for r in (2 * q, 2 * q + 1)]
        ahead = [project(field, 1, -1) for field in fields]
        behind = [project(field, 1, 1) for field in fields]
        fronts, rears = [], []
        for c in range(3):
            fronts.append([packed([h[j][i] for h in ahead for j in (c, c + 3)], 0, 1) for i in range(2)])
            rears.append([packed([h[j][i] for h in behind for j in (c, c + 3)], 3, -1) for i in range(2)])
        rears = matvec(links, rounded(rears), True)
        for c in range(3):
            store_pair(x_back, q * 3 + c, fronts[c])
            store_pair(x_ahead, q * 3 + c, rears[c])


def start_kernel(f_hbm, links_hbm, *refs):
    outs, (f_ref, links_ref, sems) = refs[:2], refs[2:]
    part = f_ref.shape[0] // RHS
    copies = [pltpu.make_async_copy(links_hbm.at[pl.ds(0, links_ref.shape[0])], links_ref, sems.at[RHS])]
    for r in range(RHS):
        rows = pl.ds(r * part, part)
        copies.append(pltpu.make_async_copy(f_hbm.at[rows], f_ref.at[rows], sems.at[r]))
    for copy in copies:
        copy.start()
    copies[0].wait()
    send_t(f_ref, links_ref, 0, *outs, ready=lambda r: copies[1 + r].wait())


def interior_kernel(parity, with_base, *refs):
    if with_base:
        f_ref, links_ref, base_ref, clover_ref, acc_ref = refs
        clover_to(clover_ref, lambda r: load_field(base_ref, r), acc_ref, -1.0 / KAPPA2)
    else:
        f_ref, links_ref, acc_ref = refs
    out_parity = 1 - parity
    t_idx, x_idx = site_masks()
    lane = lax.broadcasted_iota(jnp.int32, (8, 128), 1)
    odd = (t_idx + x_idx + lane // HALF_DEPTH + out_parity) % 2
    start = lane - lane % HALF_DEPTH
    up = jnp.where(odd == 1, start + (lane + 1) % HALF_DEPTH, lane)
    down = jnp.where(odd == 0, start + (lane + HALF_DEPTH - 1) % HALF_DEPTH, lane)
    zero = jnp.zeros((8, 128), F32)

    def take(value, index):
        return jnp.take_along_axis(value, index, axis=1, mode="promise_in_bounds")

    for mu in (2, 3, 0, 1):
        if mu == 2:
            ahead_of = lambda v: pltpu.roll(v, 128 - HALF_DEPTH, 1)
            behind_of = lambda v: pltpu.roll(v, HALF_DEPTH, 1)
        elif mu == 3:
            ahead_of = lambda v: take(v, up)
            behind_of = lambda v: take(v, down)
        elif mu == 0:
            ahead_of = lambda v: select(t_idx == 0, roll_rows(v, 4), 0.0)
            behind_of = lambda v: select(t_idx == 1, roll_rows(v, 4), 0.0)
        else:
            ahead_of = lambda v: select(x_idx < 3, roll_rows(v, 7), 0.0)
            behind_of = lambda v: select(x_idx > 0, roll_rows(v, 1), 0.0)
        links_out = load_links(links_ref, mu, out_parity)
        links_in = load_links(links_ref, mu, parity)
        for r in range(RHS):
            field = load_field(f_ref, r)
            if mu == 2 and not with_base:
                acc = [(zero, zero)] * 12
            else:
                acc = load_field(acc_ref, r)
            half = color(links_out, each(ahead_of, rounded(project(field, mu, -1))), False)
            acc = rebuild(acc, half, mu, -1)
            half = rounded(color(links_in, rounded(project(field, mu, 1)), True))
            acc = rebuild(acc, each(behind_of, half), mu, 1)
            store_field(acc_ref, r, acc)


def clover_to(clover_ref, get_field, out_ref, scale):
    for chi in range(2):
        matrix = {}
        for i in range(6):
            for j in range(i, 6):
                k = (chi * 6 + i) * 6 + j
                block = clover_ref[k * 16:(k + 1) * 16, :].astype(F32)
                re, im = block[0:8], block[8:16]
                if scale != 1.0:
                    re, im = re * scale, im * scale
                matrix[i, j] = (re, re + im, im - re)
        for r in range(RHS):
            field = get_field(r)[chi * 6:chi * 6 + 6]
            both = [vr + vi for vr, vi in field]
            for i in range(6):
                one = two = three = None
                for j in range(6):
                    vr, vi = field[j]
                    m, plus, minus = matrix[min(i, j), max(i, j)]
                    t_one = m * both[j]
                    if i <= j:
                        t_two, t_three = -(vi * plus), vr * minus
                    else:
                        t_two, t_three = vi * minus, -(vr * plus)
                    one = t_one if one is None else one + t_one
                    two = t_two if two is None else two + t_two
                    three = t_three if three is None else three + t_three
                store_pair(out_ref, r * 12 + chi * 6 + i, (one + two, one + three))


def matvec(links, vector, adjoint):
    out = []
    for a in range(3):
        re = im = None
        for b in range(3):
            lr, li = links[b][a] if adjoint else links[a][b]
            vr, vi = vector[b]
            if adjoint:
                tr, ti = lr * vr + li * vi, lr * vi - li * vr
            else:
                tr, ti = lr * vr - li * vi, lr * vi + li * vr
            re = tr if re is None else re + tr
            im = ti if im is None else im + ti
        out.append((re, im))
    return out


def rebuild_signed(acc, half, mu, sign):
    out = list(acc)
    for j in range(6):
        out[j] = add_power(out[j], half[j], 0)
    half = each(lambda v: v * sign, half)
    for row in range(2):
        col, power = SPIN_INV[mu][row]
        for c in range(3):
            j = (2 + row) * 3 + c
            out[j] = add_power(out[j], half[col * 3 + c], power)
    return out


def join_x_kernel(parity, links_ref, acc_ref, from_next, from_last, out_ref):
    _, x_idx = site_masks()
    sign = jnp.where(x_idx == 3, -1.0, 1.0).astype(F32)
    links = x_edges(load_links(links_ref, 1, 1 - parity))
    for q in range(RHS // 2):
        nxt, last = [], []
        for c in range(3):
            nxt.append(load_pair(from_next, q * 3 + c))
            last.append(load_pair(from_last, q * 3 + c))
        ahead = matvec(links, nxt, False)
        for r in (2 * q, 2 * q + 1):
            half = [None] * 6
            for s in range(2):
                k = (r % 2) * 2 + s
                for c in range(3):
                    half[s * 3 + c] = tuple(
                        select(
                            x_idx == 3,
                            roll_rows(ahead[c][i], 3 - k),
                            select(x_idx == 0, roll_rows(last[c][i], 5 + k), 0.0),
                        )
                        for i in range(2)
                    )
            store_field(out_ref, r, rebuild_signed(load_field(acc_ref, r), half, 1, sign))


def join_t(links_ref, acc_ref, t_one, t_two, parity, out_ref, scale=None, done=lambda r: None):
    even = even_device("ta", "gx")
    t_idx, _ = site_masks()
    first = t_idx == 0
    sign = jnp.where(first, 1.0, -1.0).astype(F32)
    links = t_edges(load_links(links_ref, 0, 1 - parity))
    for r in range(RHS):
        nxt, last = [], []
        for c in range(3):
            one, two = load_pair(t_one, r * 3 + c), load_pair(t_two, r * 3 + c)
            nxt.append(either(even, one, two))
            last.append(either(even, two, one))
        ahead = matvec(links, nxt, False)
        half = [tuple(select(first, last[c][i], ahead[c][i]) for i in range(2)) for c in range(3)]
        half += [
            tuple(roll_rows(select(first, ahead[c][i], last[c][i]), 4) for i in range(2)) for c in range(3)
        ]
        field = rebuild_signed(load_field(acc_ref, r), half, 0, sign)
        if scale is not None:
            field = each(lambda v: v * scale, field)
        store_field(out_ref, r, field)
        done(r)


def odd_kernel(links_ref, clover_ref, acc_ref, t_one, t_two, out_ref, *refs):
    outs, summed = refs[:2], refs[2]
    join_t(links_ref, acc_ref, t_one, t_two, 0, summed)
    clover_to(clover_ref, lambda r: load_field(summed, r), out_ref, 1.0)
    send_t(out_ref, links_ref, 1, *outs)


def even_kernel(links_ref, acc_ref, t_one, t_two, out_ref, *outs):
    join_t(links_ref, acc_ref, t_one, t_two, 1, out_ref, -KAPPA2)
    send_t(out_ref, links_ref, 0, *outs)


def last_kernel(links_ref, acc_ref, t_one, t_two, out_hbm, held, sems):
    part = held.shape[0] // RHS
    copies = []

    def done(r):
        rows = pl.ds(r * part, part)
        copies.append(pltpu.make_async_copy(held.at[rows], out_hbm.at[rows], sems.at[r]))
        copies[-1].start()

    join_t(links_ref, acc_ref, t_one, t_two, 1, held, -KAPPA2, done)
    for copy in copies:
        copy.wait()


ROWS = RHS * 24 * 8
FIELD = [((ROWS, 128), BF16)]
SUM = [((ROWS, 128), F32)]
T_HALOS = [((RHS * 3 * 16, 128), BF16)] * 2
X_HALOS = [((RHS * 3 * 8, 128), BF16)] * 2


def call(kernel, args, outs, flops, scratch=(), in_space=pltpu.VMEM, out_space=pltpu.VMEM):
    return pl.pallas_call(
        kernel,
        out_shape=tuple(jax.ShapeDtypeStruct(shape, dtype) for shape, dtype in outs),
        in_specs=[pl.BlockSpec(memory_space=in_space)] * len(args),
        out_specs=tuple([pl.BlockSpec(memory_space=out_space)] * len(outs)),
        scratch_shapes=list(scratch),
        compiler_params=pltpu.CompilerParams(vmem_limit_bytes=24 * 1024 * 1024),
        cost_estimate=pl.CostEstimate(flops=flops, bytes_accessed=2 * 1024 * 1024, transcendentals=0),
    )(*args)


def shift(value, axis, step):
    count = lax.axis_size(axis)
    return lax.ppermute(value, axis, [(i, (i + step) % count) for i in range(count)])


def swap_t(value, ahead):
    count, across = lax.axis_size("ta"), lax.axis_size("gx")
    assert count % 2 == 0 and across % 2 == 0
    pairs = []
    for i in range(count):
        for j in range(across):
            step = 1 if ((i + j) % 2 == 0) == ahead else -1
            pairs.append((i * across + j, (i + step) % count * across + j))
    return lax.ppermute(value, ("ta", "gx"), pairs)


def per_device(source, gauge_links, clover_even, clover_odd_inv):
    shape = source.shape
    f = source.reshape(-1, 128)
    links = gauge_links.reshape(-1, 128)
    even = clover_even.reshape(-1, 128)
    odd = clover_odd_inv.reshape(-1, 128)
    held = [pltpu.with_memory_space_constraint(v, pltpu.HBM) for v in (f, links)]
    start_scratch = [
        pltpu.VMEM((ROWS, 128), BF16),
        pltpu.VMEM((links.shape[0] // 4, 128), BF16),
        pltpu.SemaphoreType.DMA((RHS + 1,)),
    ]
    t_one, t_two = call(start_kernel, held, T_HALOS, 1_500_000, start_scratch, in_space=pltpu.HBM)
    for hop in range(4):
        parity = hop % 2
        t_one, t_two = swap_t(t_one, True), swap_t(t_two, False)
        x_back, x_ahead = call(
            functools.partial(send_x_kernel, parity), (f, links), X_HALOS, 1_500_000
        )
        here, x_back, x_ahead = lax.optimization_barrier((f, x_back, x_ahead))
        x_back, x_ahead = shift(x_back, "gx", -1), shift(x_ahead, "gx", 1)
        base = (before, even) if parity else ()
        acc, = call(
            functools.partial(interior_kernel, parity, bool(parity)),
            (here, links, *base), SUM, 8_000_000 if parity else 5_000_000,
        )
        acc, = call(functools.partial(join_x_kernel, parity), (links, acc, x_back, x_ahead), SUM, 1_000_000)
        before = f
        if parity == 0:
            f, t_one, t_two = call(
                odd_kernel, (links, odd, acc, t_one, t_two), FIELD + T_HALOS, 4_000_000,
                [pltpu.VMEM((ROWS, 128), BF16)],
            )
        elif hop == 1:
            f, t_one, t_two = call(
                even_kernel, (links, acc, t_one, t_two), FIELD + T_HALOS, 2_000_000
            )
        else:
            out, = call(
                last_kernel, (links, acc, t_one, t_two), FIELD, 1_000_000,
                [pltpu.VMEM((ROWS, 128), BF16), pltpu.SemaphoreType.DMA((RHS,))], out_space=pltpu.HBM,
            )
    return out.reshape(shape)


def solution(mesh):
    field_spec = P(None, None, None, None, ("groups", "ta"), "gx", None)
    link_spec = P(None, None, None, None, None, ("groups", "ta"), "gx", None)
    return jax.shard_map(
        per_device,
        mesh=mesh,
        in_specs=(field_spec, link_spec, field_spec, field_spec),
        out_specs=field_spec,
        check_vma=False,
    )
```

```python
import functools

import jax
import jax.numpy as jnp
from jax import lax
from jax.experimental import pallas as pl
from jax.experimental.pallas import tpu as pltpu
from jax.sharding import PartitionSpec as P

HALF_DEPTH = 8
KAPPA2 = 0.14 * 0.14
RHS = 4
F32 = jnp.float32
BF16 = jnp.bfloat16

SPIN = (((0, 0), (1, 0)), ((1, 3), (0, 3)), ((1, 2), (0, 0)), ((0, 3), (1, 1)))
SPIN_INV = (((0, 0), (1, 0)), ((1, 1), (0, 1)), ((1, 0), (0, 2)), ((0, 1), (1, 3)))


def add_power(base, value, power):
    (br, bi), (vr, vi) = base, value
    if power == 0:
        return br + vr, bi + vi
    if power == 1:
        return br - vi, bi + vr
    if power == 2:
        return br - vr, bi - vi
    return br + vi, bi - vr


def project(field, mu, sign):
    shift = 0 if sign > 0 else 2
    half = []
    for row in range(2):
        col, power = SPIN[mu][row]
        for c in range(3):
            half.append(add_power(field[row * 3 + c], field[(2 + col) * 3 + c], (power + shift) % 4))
    return half


def rebuild(acc, half, mu, sign):
    shift = 0 if sign > 0 else 2
    out = list(acc)
    for j in range(6):
        out[j] = add_power(out[j], half[j], 0)
    for row in range(2):
        col, power = SPIN_INV[mu][row]
        for c in range(3):
            j = (2 + row) * 3 + c
            out[j] = add_power(out[j], half[col * 3 + c], (power + shift) % 4)
    return out


def color(links, half, adjoint):
    out = []
    for s in range(2):
        for a in range(3):
            re = im = None
            for b in range(3):
                lr, li = links[b][a] if adjoint else links[a][b]
                vr, vi = half[s * 3 + b]
                if adjoint:
                    tr, ti = lr * vr + li * vi, lr * vi - li * vr
                else:
                    tr, ti = lr * vr - li * vi, lr * vi + li * vr
                re = tr if re is None else re + tr
                im = ti if im is None else im + ti
            out.append((re, im))
    return out


def each(function, half):
    return [(function(re), function(im)) for re, im in half]


def load_pair(ref, index):
    block = ref[index * 16:(index + 1) * 16, :].astype(F32)
    return block[0:8], block[8:16]


def rounded(half):
    out = []
    for pair in half:
        block = jnp.concatenate(pair, axis=0).astype(BF16).astype(F32)
        out.append((block[0:8], block[8:16]))
    return out


def load_links(ref, mu, parity):
    links = []
    for a in range(3):
        row = []
        for b in range(3):
            k = ((mu * 3 + a) * 3 + b) * 2
            row.append((load_pair(ref, k)[parity], load_pair(ref, k + 1)[parity]))
        links.append(row)
    return links


def load_field(ref, r):
    return [load_pair(ref, r * 12 + j) for j in range(12)]


def store_pair(ref, index, pair):
    ref[index * 16:(index + 1) * 16, :] = jnp.concatenate(pair, axis=0).astype(ref.dtype)


def store_field(ref, r, field):
    for j in range(12):
        store_pair(ref, r * 12 + j, field[j])


def site_masks():
    rows = lax.broadcasted_iota(jnp.int32, (8, 128), 0)
    return rows // 4, rows % 4


def even_device(*axes):
    place = sum(lax.axis_index(axis) for axis in axes)
    return lax.broadcast(place % 2, (8, 128)) == 0


def either(even, a, b):
    return [select(even, a[i], b[i]) for i in range(2)]


def roll_rows(value, shift):
    shift %= 8
    return pltpu.roll(value, shift, 0) if shift else value


def select(mask, a, b):
    return jnp.where(mask, a, b)


def t_edges(links):
    t_idx, _ = site_masks()
    return [each(lambda v: select(t_idx == 0, roll_rows(v, 4), v), row) for row in links]


def x_edges(links):
    _, x_idx = site_masks()

    def edge(value):
        out = value
        for k in range(3):
            out = select(x_idx == k, roll_rows(value, k - 3), out)
        return out

    return [each(edge, row) for row in links]


def send_t(f_ref, links_ref, parity, t_one, t_two, ready=lambda r: None):
    even = even_device("ta", "gx")
    t_idx, _ = site_masks()
    first = t_idx == 0
    links = t_edges(load_links(links_ref, 0, parity))
    for r in range(RHS):
        ready(r)
        field = load_field(f_ref, r)
        ahead, behind = project(field, 0, -1), project(field, 0, 1)
        rears = [
            tuple(select(first, roll_rows(behind[c][i], 4), behind[c + 3][i]) for i in range(2)) for c in range(3)
        ]
        rears = matvec(links, rounded(rears), True)
        for c in range(3):
            front = [select(first, ahead[c + 3][i], roll_rows(ahead[c][i], 4)) for i in range(2)]
            store_pair(t_one, r * 3 + c, either(even, rears[c], front))
            store_pair(t_two, r * 3 + c, either(even, front, rears[c]))


def send_x(f_ref, links_ref, parity, x_far, x_near):
    even = even_device("gx")
    pad = x_far.shape[0] - x_near.shape[0]
    x_far[x_near.shape[0]:, :] = jnp.zeros((pad, 128), BF16)
    _, x_idx = site_masks()
    links = x_edges(load_links(links_ref, 1, parity))

    def packed(values, row, step):
        out = values[0]
        for k in range(1, 4):
            out = select(x_idx == row + step * k, roll_rows(values[k], step * k), out)
        return out

    for q in range(RHS // 2):
        fields = [load_field(f_ref, r) for r in (2 * q, 2 * q + 1)]
        ahead = [project(field, 1, -1) for field in fields]
        behind = [project(field, 1, 1) for field in fields]
        fronts, rears = [], []
        for c in range(3):
            fronts.append([packed([h[j][i] for h in ahead for j in (c, c + 3)], 0, 1) for i in range(2)])
            rears.append([packed([h[j][i] for h in behind for j in (c, c + 3)], 3, -1) for i in range(2)])
        rears = matvec(links, rounded(rears), True)
        for c in range(3):
            store_pair(x_near, q * 3 + c, either(even, rears[c], fronts[c]))
            store_pair(x_far, q * 3 + c, either(even, fronts[c], rears[c]))


def start_kernel(f_hbm, links_hbm, *refs):
    outs, (f_ref, links_ref, sems) = refs[:4], refs[4:]
    part = f_ref.shape[0] // RHS
    copies = [pltpu.make_async_copy(links_hbm.at[pl.ds(0, links_ref.shape[0])], links_ref, sems.at[RHS])]
    for r in range(RHS):
        rows = pl.ds(r * part, part)
        copies.append(pltpu.make_async_copy(f_hbm.at[rows], f_ref.at[rows], sems.at[r]))
    for copy in copies:
        copy.start()
    copies[0].wait()
    send_t(f_ref, links_ref, 0, *outs[:2], ready=lambda r: copies[1 + r].wait())
    send_x(f_ref, links_ref, 0, *outs[2:])


def interior_kernel(parity, with_base, *refs):
    if with_base:
        f_ref, links_ref, base_ref, clover_ref, acc_ref = refs
        clover_to(clover_ref, lambda r: load_field(base_ref, r), acc_ref, -1.0 / KAPPA2)
    else:
        f_ref, links_ref, acc_ref = refs
    out_parity = 1 - parity
    t_idx, x_idx = site_masks()
    lane = lax.broadcasted_iota(jnp.int32, (8, 128), 1)
    odd = (t_idx + x_idx + lane // HALF_DEPTH + out_parity) % 2
    start = lane - lane % HALF_DEPTH
    up = jnp.where(odd == 1, start + (lane + 1) % HALF_DEPTH, lane)
    down = jnp.where(odd == 0, start + (lane + HALF_DEPTH - 1) % HALF_DEPTH, lane)
    zero = jnp.zeros((8, 128), F32)

    def take(value, index):
        return jnp.take_along_axis(value, index, axis=1, mode="promise_in_bounds")

    for mu in (2, 3, 0, 1):
        if mu == 2:
            ahead_of = lambda v: pltpu.roll(v, 128 - HALF_DEPTH, 1)
            behind_of = lambda v: pltpu.roll(v, HALF_DEPTH, 1)
        elif mu == 3:
            ahead_of = lambda v: take(v, up)
            behind_of = lambda v: take(v, down)
        elif mu == 0:
            ahead_of = lambda v: select(t_idx == 0, roll_rows(v, 4), 0.0)
            behind_of = lambda v: select(t_idx == 1, roll_rows(v, 4), 0.0)
        else:
            ahead_of = lambda v: select(x_idx < 3, roll_rows(v, 7), 0.0)
            behind_of = lambda v: select(x_idx > 0, roll_rows(v, 1), 0.0)
        links_out = load_links(links_ref, mu, out_parity)
        links_in = load_links(links_ref, mu, parity)
        for r in range(RHS):
            field = load_field(f_ref, r)
            if mu == 2 and not with_base:
                acc = [(zero, zero)] * 12
            else:
                acc = load_field(acc_ref, r)
            half = color(links_out, each(ahead_of, rounded(project(field, mu, -1))), False)
            acc = rebuild(acc, half, mu, -1)
            half = rounded(color(links_in, rounded(project(field, mu, 1)), True))
            acc = rebuild(acc, each(behind_of, half), mu, 1)
            store_field(acc_ref, r, acc)


def clover_to(clover_ref, get_field, out_ref, scale):
    for chi in range(2):
        matrix = {}
        for i in range(6):
            for j in range(i, 6):
                k = (chi * 6 + i) * 6 + j
                block = clover_ref[k * 16:(k + 1) * 16, :].astype(F32)
                re, im = block[0:8], block[8:16]
                if scale != 1.0:
                    re, im = re * scale, im * scale
                matrix[i, j] = (re, re + im, im - re)
        for r in range(RHS):
            field = get_field(r)[chi * 6:chi * 6 + 6]
            both = [vr + vi for vr, vi in field]
            for i in range(6):
                one = two = three = None
                for j in range(6):
                    vr, vi = field[j]
                    m, plus, minus = matrix[min(i, j), max(i, j)]
                    t_one = m * both[j]
                    if i <= j:
                        t_two, t_three = -(vi * plus), vr * minus
                    else:
                        t_two, t_three = vi * minus, -(vr * plus)
                    one = t_one if one is None else one + t_one
                    two = t_two if two is None else two + t_two
                    three = t_three if three is None else three + t_three
                store_pair(out_ref, r * 12 + chi * 6 + i, (one + two, one + three))


def matvec(links, vector, adjoint):
    out = []
    for a in range(3):
        re = im = None
        for b in range(3):
            lr, li = links[b][a] if adjoint else links[a][b]
            vr, vi = vector[b]
            if adjoint:
                tr, ti = lr * vr + li * vi, lr * vi - li * vr
            else:
                tr, ti = lr * vr - li * vi, lr * vi + li * vr
            re = tr if re is None else re + tr
            im = ti if im is None else im + ti
        out.append((re, im))
    return out


def rebuild_signed(acc, half, mu, sign):
    out = list(acc)
    for j in range(6):
        out[j] = add_power(out[j], half[j], 0)
    half = each(lambda v: v * sign, half)
    for row in range(2):
        col, power = SPIN_INV[mu][row]
        for c in range(3):
            j = (2 + row) * 3 + c
            out[j] = add_power(out[j], half[col * 3 + c], power)
    return out


def join_x_kernel(parity, links_ref, acc_ref, x_far, x_near, out_ref):
    even = even_device("gx")
    _, x_idx = site_masks()
    sign = jnp.where(x_idx == 3, -1.0, 1.0).astype(F32)
    links = x_edges(load_links(links_ref, 1, 1 - parity))
    for q in range(RHS // 2):
        nxt, last = [], []
        for c in range(3):
            near, far = load_pair(x_near, q * 3 + c), load_pair(x_far, q * 3 + c)
            nxt.append(either(even, near, far))
            last.append(either(even, far, near))
        ahead = matvec(links, nxt, False)
        for r in (2 * q, 2 * q + 1):
            half = [None] * 6
            for s in range(2):
                k = (r % 2) * 2 + s
                for c in range(3):
                    half[s * 3 + c] = tuple(
                        select(
                            x_idx == 3,
                            roll_rows(ahead[c][i], 3 - k),
                            select(x_idx == 0, roll_rows(last[c][i], 5 + k), 0.0),
                        )
                        for i in range(2)
                    )
            store_field(out_ref, r, rebuild_signed(load_field(acc_ref, r), half, 1, sign))


def join_t(links_ref, acc_ref, t_one, t_two, parity, out_ref, scale=None, done=lambda r: None):
    even = even_device("ta", "gx")
    t_idx, _ = site_masks()
    first = t_idx == 0
    sign = jnp.where(first, 1.0, -1.0).astype(F32)
    links = t_edges(load_links(links_ref, 0, 1 - parity))
    for r in range(RHS):
        nxt, last = [], []
        for c in range(3):
            one, two = load_pair(t_one, r * 3 + c), load_pair(t_two, r * 3 + c)
            nxt.append(either(even, one, two))
            last.append(either(even, two, one))
        ahead = matvec(links, nxt, False)
        half = [tuple(select(first, last[c][i], ahead[c][i]) for i in range(2)) for c in range(3)]
        half += [
            tuple(roll_rows(select(first, ahead[c][i], last[c][i]), 4) for i in range(2)) for c in range(3)
        ]
        field = rebuild_signed(load_field(acc_ref, r), half, 0, sign)
        if scale is not None:
            field = each(lambda v: v * scale, field)
        store_field(out_ref, r, field)
        done(r)


def odd_kernel(links_ref, clover_ref, acc_ref, t_one, t_two, out_ref, *refs):
    outs, summed = refs[:4], refs[4]
    join_t(links_ref, acc_ref, t_one, t_two, 0, summed)
    clover_to(clover_ref, lambda r: load_field(summed, r), out_ref, 1.0)
    send_t(out_ref, links_ref, 1, *outs[:2])
    send_x(out_ref, links_ref, 1, *outs[2:])


def even_kernel(links_ref, acc_ref, t_one, t_two, out_ref, *outs):
    join_t(links_ref, acc_ref, t_one, t_two, 1, out_ref, -KAPPA2)
    send_t(out_ref, links_ref, 0, *outs[:2])
    send_x(out_ref, links_ref, 0, *outs[2:])


def last_kernel(links_ref, acc_ref, t_one, t_two, out_hbm, held, sems):
    part = held.shape[0] // RHS
    copies = []

    def done(r):
        rows = pl.ds(r * part, part)
        copies.append(pltpu.make_async_copy(held.at[rows], out_hbm.at[rows], sems.at[r]))
        copies[-1].start()

    join_t(links_ref, acc_ref, t_one, t_two, 1, held, -KAPPA2, done)
    for copy in copies:
        copy.wait()


ROWS = RHS * 24 * 8
FIELD = [((ROWS, 128), BF16)]
SUM = [((ROWS, 128), F32)]
T_HALOS = [((RHS * 3 * 16, 128), BF16)] * 2
X_ROWS = RHS * 3 * 8
HALOS = T_HALOS + [((RHS * 3 * 16 + 16, 128), BF16), ((X_ROWS, 128), BF16)]


def call(kernel, args, outs, flops, scratch=(), in_space=pltpu.VMEM, out_space=pltpu.VMEM):
    return pl.pallas_call(
        kernel,
        out_shape=tuple(jax.ShapeDtypeStruct(shape, dtype) for shape, dtype in outs),
        in_specs=[pl.BlockSpec(memory_space=in_space)] * len(args),
        out_specs=tuple([pl.BlockSpec(memory_space=out_space)] * len(outs)),
        scratch_shapes=list(scratch),
        compiler_params=pltpu.CompilerParams(vmem_limit_bytes=24 * 1024 * 1024),
        cost_estimate=pl.CostEstimate(flops=flops, bytes_accessed=2 * 1024 * 1024, transcendentals=0),
    )(*args)


def swap(value, axis, far):
    count = lax.axis_size(axis)
    assert count % 2 == 0
    pairs = [(i, (i + (1 if (i % 2 == 0) != far else -1)) % count) for i in range(count)]
    return lax.ppermute(value, axis, pairs)


def swap_t(value, ahead):
    count, across = lax.axis_size("ta"), lax.axis_size("gx")
    assert count % 2 == 0 and across % 2 == 0
    pairs = []
    for i in range(count):
        for j in range(across):
            step = 1 if ((i + j) % 2 == 0) == ahead else -1
            pairs.append((i * across + j, (i + step) % count * across + j))
    return lax.ppermute(value, ("ta", "gx"), pairs)


def per_device(source, gauge_links, clover_even, clover_odd_inv):
    shape = source.shape
    f = source.reshape(-1, 128)
    links = gauge_links.reshape(-1, 128)
    even = clover_even.reshape(-1, 128)
    odd = clover_odd_inv.reshape(-1, 128)
    held = [pltpu.with_memory_space_constraint(v, pltpu.HBM) for v in (f, links)]
    start_scratch = [
        pltpu.VMEM((ROWS, 128), BF16),
        pltpu.VMEM((links.shape[0] // 2, 128), BF16),
        pltpu.SemaphoreType.DMA((RHS + 1,)),
    ]
    t_one, t_two, x_far, x_near = call(start_kernel, held, HALOS, 1_500_000, start_scratch, in_space=pltpu.HBM)
    for hop in range(4):
        parity = hop % 2
        t_one, t_two = swap_t(t_one, True), swap_t(t_two, False)
        x_far, x_near = swap(x_far, "gx", True), swap(x_near, "gx", False)
        base = (before, even) if parity else ()
        acc, = call(
            functools.partial(interior_kernel, parity, bool(parity)),
            (f, links, *base), SUM, 8_000_000 if parity else 5_000_000,
        )
        acc, = call(functools.partial(join_x_kernel, parity), (links, acc, x_far, x_near), SUM, 1_000_000)
        before = f
        if parity == 0:
            f, t_one, t_two, x_far, x_near = call(
                odd_kernel, (links, odd, acc, t_one, t_two), FIELD + HALOS, 4_000_000,
                [pltpu.VMEM((ROWS, 128), BF16)],
            )
        elif hop == 1:
            f, t_one, t_two, x_far, x_near = call(
                even_kernel, (links, acc, t_one, t_two), FIELD + HALOS, 2_000_000
            )
        else:
            out, = call(
                last_kernel, (links, acc, t_one, t_two), FIELD, 1_000_000,
                [pltpu.VMEM((ROWS, 128), BF16), pltpu.SemaphoreType.DMA((RHS,))], out_space=pltpu.HBM,
            )
    return out.reshape(shape)


def solution(mesh):
    field_spec = P(None, None, None, None, ("groups", "ta"), "gx", None)
    link_spec = P(None, None, None, None, None, ("groups", "ta"), "gx", None)
    return jax.shard_map(
        per_device,
        mesh=mesh,
        in_specs=(field_spec, link_spec, field_spec, field_spec),
        out_specs=field_spec,
        check_vma=False,
    )
```

```python
import functools

import jax
import jax.numpy as jnp
from jax import lax
from jax.experimental import pallas as pl
from jax.experimental.pallas import tpu as pltpu
from jax.sharding import PartitionSpec as P

HALF_DEPTH = 8
KAPPA2 = 0.14 * 0.14
RHS = 4
F32 = jnp.float32
BF16 = jnp.bfloat16

SPIN = (((0, 0), (1, 0)), ((1, 3), (0, 3)), ((1, 2), (0, 0)), ((0, 3), (1, 1)))
SPIN_INV = (((0, 0), (1, 0)), ((1, 1), (0, 1)), ((1, 0), (0, 2)), ((0, 1), (1, 3)))


def add_power(base, value, power):
    (br, bi), (vr, vi) = base, value
    if power == 0:
        return br + vr, bi + vi
    if power == 1:
        return br - vi, bi + vr
    if power == 2:
        return br - vr, bi - vi
    return br + vi, bi - vr


def project(field, mu, sign):
    shift = 0 if sign > 0 else 2
    half = []
    for row in range(2):
        col, power = SPIN[mu][row]
        for c in range(3):
            half.append(add_power(field[row * 3 + c], field[(2 + col) * 3 + c], (power + shift) % 4))
    return half


def rebuild(acc, half, mu, sign):
    shift = 0 if sign > 0 else 2
    out = list(acc)
    for j in range(6):
        out[j] = add_power(out[j], half[j], 0)
    for row in range(2):
        col, power = SPIN_INV[mu][row]
        for c in range(3):
            j = (2 + row) * 3 + c
            out[j] = add_power(out[j], half[col * 3 + c], (power + shift) % 4)
    return out


def color(links, half, adjoint):
    out = []
    for s in range(2):
        for a in range(3):
            re = im = None
            for b in range(3):
                lr, li = links[b][a] if adjoint else links[a][b]
                vr, vi = half[s * 3 + b]
                if adjoint:
                    tr, ti = lr * vr + li * vi, lr * vi - li * vr
                else:
                    tr, ti = lr * vr - li * vi, lr * vi + li * vr
                re = tr if re is None else re + tr
                im = ti if im is None else im + ti
            out.append((re, im))
    return out


def each(function, half):
    return [(function(re), function(im)) for re, im in half]


def load_pair(ref, index):
    block = ref[index * 16:(index + 1) * 16, :].astype(F32)
    return block[0:8], block[8:16]


def rounded(half):
    out = []
    for pair in half:
        block = jnp.concatenate(pair, axis=0).astype(BF16).astype(F32)
        out.append((block[0:8], block[8:16]))
    return out


def load_links(ref, mu, parity):
    links = []
    for a in range(3):
        row = []
        for b in range(3):
            k = ((mu * 3 + a) * 3 + b) * 2
            row.append((load_pair(ref, k)[parity], load_pair(ref, k + 1)[parity]))
        links.append(row)
    return links


def load_field(ref, r):
    return [load_pair(ref, r * 12 + j) for j in range(12)]


def store_pair(ref, index, pair):
    ref[index * 16:(index + 1) * 16, :] = jnp.concatenate(pair, axis=0).astype(ref.dtype)


def store_field(ref, r, field):
    for j in range(12):
        store_pair(ref, r * 12 + j, field[j])


def site_masks():
    rows = lax.broadcasted_iota(jnp.int32, (8, 128), 0)
    return rows // 4, rows % 4


def even_device(*axes):
    place = sum(lax.axis_index(axis) for axis in axes)
    return lax.broadcast(place % 2, (8, 128)) == 0


def either(even, a, b):
    return [select(even, a[i], b[i]) for i in range(2)]


def roll_rows(value, shift):
    shift %= 8
    return pltpu.roll(value, shift, 0) if shift else value


def select(mask, a, b):
    return jnp.where(mask, a, b)


def t_edges(links):
    t_idx, _ = site_masks()
    return [each(lambda v: select(t_idx == 0, roll_rows(v, 4), v), row) for row in links]


def x_edges(links):
    _, x_idx = site_masks()

    def edge(value):
        out = value
        for k in range(3):
            out = select(x_idx == k, roll_rows(value, k - 3), out)
        return out

    return [each(edge, row) for row in links]


def send_t(f_ref, links_ref, parity, t_one, t_two, ready=lambda r: None):
    even = even_device("ta", "gx")
    t_idx, _ = site_masks()
    first = t_idx == 0
    links = t_edges(load_links(links_ref, 0, parity))
    for r in range(RHS):
        ready(r)
        field = load_field(f_ref, r)
        ahead, behind = project(field, 0, -1), project(field, 0, 1)
        rears = [
            tuple(select(first, roll_rows(behind[c][i], 4), behind[c + 3][i]) for i in range(2)) for c in range(3)
        ]
        rears = matvec(links, rounded(rears), True)
        for c in range(3):
            front = [select(first, ahead[c + 3][i], roll_rows(ahead[c][i], 4)) for i in range(2)]
            store_pair(t_one, r * 3 + c, either(even, rears[c], front))
            store_pair(t_two, r * 3 + c, either(even, front, rears[c]))


def send_x_kernel(parity, f_ref, links_ref, x_far, x_near):
    even = even_device("gx")
    _, x_idx = site_masks()
    links = x_edges(load_links(links_ref, 1, parity))

    def packed(values, row, step):
        out = values[0]
        for k in range(1, 4):
            out = select(x_idx == row + step * k, roll_rows(values[k], step * k), out)
        return out

    for q in range(RHS // 2):
        fields = [load_field(f_ref, r) for r in (2 * q, 2 * q + 1)]
        ahead = [project(field, 1, -1) for field in fields]
        behind = [project(field, 1, 1) for field in fields]
        fronts, rears = [], []
        for c in range(3):
            fronts.append([packed([h[j][i] for h in ahead for j in (c, c + 3)], 0, 1) for i in range(2)])
            rears.append([packed([h[j][i] for h in behind for j in (c, c + 3)], 3, -1) for i in range(2)])
        rears = matvec(links, rounded(rears), True)
        for c in range(3):
            store_pair(x_near, q * 3 + c, either(even, rears[c], fronts[c]))
            store_pair(x_far, q * 3 + c, either(even, fronts[c], rears[c]))


def start_kernel(f_hbm, links_hbm, *refs):
    outs, (f_ref, links_ref, sems) = refs[:2], refs[2:]
    part = f_ref.shape[0] // RHS
    copies = [pltpu.make_async_copy(links_hbm.at[pl.ds(0, links_ref.shape[0])], links_ref, sems.at[RHS])]
    for r in range(RHS):
        rows = pl.ds(r * part, part)
        copies.append(pltpu.make_async_copy(f_hbm.at[rows], f_ref.at[rows], sems.at[r]))
    for copy in copies:
        copy.start()
    copies[0].wait()
    send_t(f_ref, links_ref, 0, *outs, ready=lambda r: copies[1 + r].wait())


def interior_kernel(parity, with_base, turn, count, *refs):
    here = True if turn is None else lax.axis_index("gx") % 2 == turn
    pl.when(here)(lambda: interior(parity, with_base, *refs[:count], refs[-1]))


def interior(parity, with_base, *refs):
    if with_base:
        f_ref, links_ref, base_ref, clover_ref, acc_ref = refs
        clover_to(clover_ref, lambda r: load_field(base_ref, r), acc_ref, -1.0 / KAPPA2)
    else:
        f_ref, links_ref, acc_ref = refs
    out_parity = 1 - parity
    t_idx, x_idx = site_masks()
    lane = lax.broadcasted_iota(jnp.int32, (8, 128), 1)
    odd = (t_idx + x_idx + lane // HALF_DEPTH + out_parity) % 2
    start = lane - lane % HALF_DEPTH
    up = jnp.where(odd == 1, start + (lane + 1) % HALF_DEPTH, lane)
    down = jnp.where(odd == 0, start + (lane + HALF_DEPTH - 1) % HALF_DEPTH, lane)
    zero = jnp.zeros((8, 128), F32)

    def take(value, index):
        return jnp.take_along_axis(value, index, axis=1, mode="promise_in_bounds")

    for mu in (2, 3, 0, 1):
        if mu == 2:
            ahead_of = lambda v: pltpu.roll(v, 128 - HALF_DEPTH, 1)
            behind_of = lambda v: pltpu.roll(v, HALF_DEPTH, 1)
        elif mu == 3:
            ahead_of = lambda v: take(v, up)
            behind_of = lambda v: take(v, down)
        elif mu == 0:
            ahead_of = lambda v: select(t_idx == 0, roll_rows(v, 4), 0.0)
            behind_of = lambda v: select(t_idx == 1, roll_rows(v, 4), 0.0)
        else:
            ahead_of = lambda v: select(x_idx < 3, roll_rows(v, 7), 0.0)
            behind_of = lambda v: select(x_idx > 0, roll_rows(v, 1), 0.0)
        links_out = load_links(links_ref, mu, out_parity)
        links_in = load_links(links_ref, mu, parity)
        for r in range(RHS):
            field = load_field(f_ref, r)
            if mu == 2 and not with_base:
                acc = [(zero, zero)] * 12
            else:
                acc = load_field(acc_ref, r)
            half = color(links_out, each(ahead_of, rounded(project(field, mu, -1))), False)
            acc = rebuild(acc, half, mu, -1)
            half = rounded(color(links_in, rounded(project(field, mu, 1)), True))
            acc = rebuild(acc, each(behind_of, half), mu, 1)
            store_field(acc_ref, r, acc)


def clover_to(clover_ref, get_field, out_ref, scale):
    for chi in range(2):
        matrix = {}
        for i in range(6):
            for j in range(i, 6):
                k = (chi * 6 + i) * 6 + j
                block = clover_ref[k * 16:(k + 1) * 16, :].astype(F32)
                re, im = block[0:8], block[8:16]
                if scale != 1.0:
                    re, im = re * scale, im * scale
                matrix[i, j] = (re, re + im, im - re)
        for r in range(RHS):
            field = get_field(r)[chi * 6:chi * 6 + 6]
            both = [vr + vi for vr, vi in field]
            for i in range(6):
                one = two = three = None
                for j in range(6):
                    vr, vi = field[j]
                    m, plus, minus = matrix[min(i, j), max(i, j)]
                    t_one = m * both[j]
                    if i <= j:
                        t_two, t_three = -(vi * plus), vr * minus
                    else:
                        t_two, t_three = vi * minus, -(vr * plus)
                    one = t_one if one is None else one + t_one
                    two = t_two if two is None else two + t_two
                    three = t_three if three is None else three + t_three
                store_pair(out_ref, r * 12 + chi * 6 + i, (one + two, one + three))


def matvec(links, vector, adjoint):
    out = []
    for a in range(3):
        re = im = None
        for b in range(3):
            lr, li = links[b][a] if adjoint else links[a][b]
            vr, vi = vector[b]
            if adjoint:
                tr, ti = lr * vr + li * vi, lr * vi - li * vr
            else:
                tr, ti = lr * vr - li * vi, lr * vi + li * vr
            re = tr if re is None else re + tr
            im = ti if im is None else im + ti
        out.append((re, im))
    return out


def rebuild_signed(acc, half, mu, sign):
    out = list(acc)
    for j in range(6):
        out[j] = add_power(out[j], half[j], 0)
    half = each(lambda v: v * sign, half)
    for row in range(2):
        col, power = SPIN_INV[mu][row]
        for c in range(3):
            j = (2 + row) * 3 + c
            out[j] = add_power(out[j], half[col * 3 + c], power)
    return out


def join_x_kernel(parity, links_ref, acc_ref, x_far, x_near, out_ref):
    even = even_device("gx")
    _, x_idx = site_masks()
    sign = jnp.where(x_idx == 3, -1.0, 1.0).astype(F32)
    links = x_edges(load_links(links_ref, 1, 1 - parity))
    for q in range(RHS // 2):
        nxt, last = [], []
        for c in range(3):
            near, far = load_pair(x_near, q * 3 + c), load_pair(x_far, q * 3 + c)
            nxt.append(either(even, near, far))
            last.append(either(even, far, near))
        ahead = matvec(links, nxt, False)
        for r in (2 * q, 2 * q + 1):
            half = [None] * 6
            for s in range(2):
                k = (r % 2) * 2 + s
                for c in range(3):
                    half[s * 3 + c] = tuple(
                        select(
                            x_idx == 3,
                            roll_rows(ahead[c][i], 3 - k),
                            select(x_idx == 0, roll_rows(last[c][i], 5 + k), 0.0),
                        )
                        for i in range(2)
                    )
            store_field(out_ref, r, rebuild_signed(load_field(acc_ref, r), half, 1, sign))


def join_t(links_ref, acc_ref, t_one, t_two, parity, out_ref, scale=None, done=lambda r: None):
    even = even_device("ta", "gx")
    t_idx, _ = site_masks()
    first = t_idx == 0
    sign = jnp.where(first, 1.0, -1.0).astype(F32)
    links = t_edges(load_links(links_ref, 0, 1 - parity))
    for r in range(RHS):
        nxt, last = [], []
        for c in range(3):
            one, two = load_pair(t_one, r * 3 + c), load_pair(t_two, r * 3 + c)
            nxt.append(either(even, one, two))
            last.append(either(even, two, one))
        ahead = matvec(links, nxt, False)
        half = [tuple(select(first, last[c][i], ahead[c][i]) for i in range(2)) for c in range(3)]
        half += [
            tuple(roll_rows(select(first, ahead[c][i], last[c][i]), 4) for i in range(2)) for c in range(3)
        ]
        field = rebuild_signed(load_field(acc_ref, r), half, 0, sign)
        if scale is not None:
            field = each(lambda v: v * scale, field)
        store_field(out_ref, r, field)
        done(r)


def odd_kernel(links_ref, clover_ref, acc_ref, t_one, t_two, out_ref, *refs):
    outs, summed = refs[:2], refs[2]
    join_t(links_ref, acc_ref, t_one, t_two, 0, summed)
    clover_to(clover_ref, lambda r: load_field(summed, r), out_ref, 1.0)
    send_t(out_ref, links_ref, 1, *outs)


def even_kernel(links_ref, acc_ref, t_one, t_two, out_ref, *outs):
    join_t(links_ref, acc_ref, t_one, t_two, 1, out_ref, -KAPPA2)
    send_t(out_ref, links_ref, 0, *outs)


def last_kernel(links_ref, acc_ref, t_one, t_two, out_hbm, held, sems):
    part = held.shape[0] // RHS
    copies = []

    def done(r):
        rows = pl.ds(r * part, part)
        copies.append(pltpu.make_async_copy(held.at[rows], out_hbm.at[rows], sems.at[r]))
        copies[-1].start()

    join_t(links_ref, acc_ref, t_one, t_two, 1, held, -KAPPA2, done)
    for copy in copies:
        copy.wait()


ROWS = RHS * 24 * 8
FIELD = [((ROWS, 128), BF16)]
SUM = [((ROWS, 128), F32)]
T_HALOS = [((RHS * 3 * 16, 128), BF16)] * 2
X_HALOS = [((RHS * 3 * 8, 128), BF16)] * 2


def call(kernel, args, outs, flops, scratch=(), in_space=pltpu.VMEM, out_space=pltpu.VMEM, kept=()):
    return pl.pallas_call(
        kernel,
        out_shape=tuple(jax.ShapeDtypeStruct(shape, dtype) for shape, dtype in outs),
        in_specs=[pl.BlockSpec(memory_space=in_space)] * len(args) + [pl.BlockSpec(memory_space=pl.ANY)] * len(kept),
        out_specs=tuple([pl.BlockSpec(memory_space=out_space)] * len(outs)),
        scratch_shapes=list(scratch),
        input_output_aliases={len(args) + i: i for i in range(len(kept))},
        compiler_params=pltpu.CompilerParams(vmem_limit_bytes=24 * 1024 * 1024),
        cost_estimate=pl.CostEstimate(flops=flops, bytes_accessed=2 * 1024 * 1024, transcendentals=0),
    )(*args, *kept)


def swap(value, axis, far):
    count = lax.axis_size(axis)
    assert count % 2 == 0
    pairs = [(i, (i + (1 if (i % 2 == 0) != far else -1)) % count) for i in range(count)]
    return lax.ppermute(value, axis, pairs)


def swap_t(value, ahead):
    count, across = lax.axis_size("ta"), lax.axis_size("gx")
    assert count % 2 == 0 and across % 2 == 0
    pairs = []
    for i in range(count):
        for j in range(across):
            step = 1 if ((i + j) % 2 == 0) == ahead else -1
            pairs.append((i * across + j, (i + step) % count * across + j))
    return lax.ppermute(value, ("ta", "gx"), pairs)


def per_device(source, gauge_links, clover_even, clover_odd_inv):
    shape = source.shape
    f = source.reshape(-1, 128)
    links = gauge_links.reshape(-1, 128)
    even = clover_even.reshape(-1, 128)
    odd = clover_odd_inv.reshape(-1, 128)
    held = [pltpu.with_memory_space_constraint(v, pltpu.HBM) for v in (f, links)]
    start_scratch = [
        pltpu.VMEM((ROWS, 128), BF16),
        pltpu.VMEM((links.shape[0] // 4, 128), BF16),
        pltpu.SemaphoreType.DMA((RHS + 1,)),
    ]
    t_one, t_two = call(start_kernel, held, T_HALOS, 1_500_000, start_scratch, in_space=pltpu.HBM)
    for hop in range(4):
        parity = hop % 2
        base = (before, even) if parity else ()
        part = functools.partial(interior_kernel, parity, bool(parity))
        cost = 8_000_000 if parity else 5_000_000
        count = 2 + len(base)
        early = ()
        if hop >= 2:
            early = call(functools.partial(part, 1, count), (f, links, *base), SUM, cost)
            t_one, t_two, *early = lax.optimization_barrier((t_one, t_two, *early))
        t_one, t_two = swap_t(t_one, True), swap_t(t_two, False)
        x_far, x_near = call(
            functools.partial(send_x_kernel, parity), (f, links), X_HALOS, 1_500_000
        )
        here, x_far, x_near = lax.optimization_barrier((f, x_far, x_near))
        x_far, x_near = swap(x_far, "gx", True), swap(x_near, "gx", False)
        acc, = call(functools.partial(part, 0 if early else None, count), (here, links, *base), SUM, cost, kept=early)
        acc, = call(functools.partial(join_x_kernel, parity), (links, acc, x_far, x_near), SUM, 1_000_000)
        before = f
        if parity == 0:
            f, t_one, t_two = call(
                odd_kernel, (links, odd, acc, t_one, t_two), FIELD + T_HALOS, 4_000_000,
                [pltpu.VMEM((ROWS, 128), BF16)],
            )
        elif hop == 1:
            f, t_one, t_two = call(
                even_kernel, (links, acc, t_one, t_two), FIELD + T_HALOS, 2_000_000
            )
        else:
            out, = call(
                last_kernel, (links, acc, t_one, t_two), FIELD, 1_000_000,
                [pltpu.VMEM((ROWS, 128), BF16), pltpu.SemaphoreType.DMA((RHS,))], out_space=pltpu.HBM,
            )
    return out.reshape(shape)


def solution(mesh):
    field_spec = P(None, None, None, None, ("groups", "ta"), "gx", None)
    link_spec = P(None, None, None, None, None, ("groups", "ta"), "gx", None)
    return jax.shard_map(
        per_device,
        mesh=mesh,
        in_specs=(field_spec, link_spec, field_spec, field_spec),
        out_specs=field_spec,
        check_vma=False,
    )
```

```python
import functools

import jax
import jax.numpy as jnp
from jax import lax
from jax.experimental import pallas as pl
from jax.experimental.pallas import tpu as pltpu
from jax.sharding import PartitionSpec as P

HALF_DEPTH = 8
KAPPA2 = 0.14 * 0.14
RHS = 4
F32 = jnp.float32
BF16 = jnp.bfloat16

SPIN = (((0, 0), (1, 0)), ((1, 3), (0, 3)), ((1, 2), (0, 0)), ((0, 3), (1, 1)))
SPIN_INV = (((0, 0), (1, 0)), ((1, 1), (0, 1)), ((1, 0), (0, 2)), ((0, 1), (1, 3)))


def add_power(base, value, power):
    (br, bi), (vr, vi) = base, value
    if power == 0:
        return br + vr, bi + vi
    if power == 1:
        return br - vi, bi + vr
    if power == 2:
        return br - vr, bi - vi
    return br + vi, bi - vr


def project(field, mu, sign):
    shift = 0 if sign > 0 else 2
    half = []
    for row in range(2):
        col, power = SPIN[mu][row]
        for c in range(3):
            half.append(add_power(field[row * 3 + c], field[(2 + col) * 3 + c], (power + shift) % 4))
    return half


def rebuild(acc, half, mu, sign):
    shift = 0 if sign > 0 else 2
    out = list(acc)
    for j in range(6):
        out[j] = add_power(out[j], half[j], 0)
    for row in range(2):
        col, power = SPIN_INV[mu][row]
        for c in range(3):
            j = (2 + row) * 3 + c
            out[j] = add_power(out[j], half[col * 3 + c], (power + shift) % 4)
    return out


def color(links, half, adjoint):
    out = []
    for s in range(2):
        for a in range(3):
            re = im = None
            for b in range(3):
                lr, li = links[b][a] if adjoint else links[a][b]
                vr, vi = half[s * 3 + b]
                if adjoint:
                    tr, ti = lr * vr + li * vi, lr * vi - li * vr
                else:
                    tr, ti = lr * vr - li * vi, lr * vi + li * vr
                re = tr if re is None else re + tr
                im = ti if im is None else im + ti
            out.append((re, im))
    return out


def each(function, half):
    return [(function(re), function(im)) for re, im in half]


def load_pair(ref, index):
    block = ref[index * 16:(index + 1) * 16, :].astype(F32)
    return block[0:8], block[8:16]


def rounded(half):
    out = []
    for pair in half:
        block = jnp.concatenate(pair, axis=0).astype(BF16).astype(F32)
        out.append((block[0:8], block[8:16]))
    return out


def load_links(ref, mu, parity):
    links = []
    for a in range(3):
        row = []
        for b in range(3):
            k = ((mu * 3 + a) * 3 + b) * 2
            row.append((load_pair(ref, k)[parity], load_pair(ref, k + 1)[parity]))
        links.append(row)
    return links


def load_field(ref, r):
    return [load_pair(ref, r * 12 + j) for j in range(12)]


def store_pair(ref, index, pair):
    ref[index * 16:(index + 1) * 16, :] = jnp.concatenate(pair, axis=0).astype(ref.dtype)


def store_field(ref, r, field):
    for j in range(12):
        store_pair(ref, r * 12 + j, field[j])


def site_masks():
    rows = lax.broadcasted_iota(jnp.int32, (8, 128), 0)
    return rows // 4, rows % 4


def even_device(*axes, extra=0):
    place = sum(lax.axis_index(axis) for axis in axes) + extra
    return lax.broadcast(place % 2, (8, 128)) == 0


def either(even, a, b):
    return [select(even, a[i], b[i]) for i in range(2)]


def roll_rows(value, shift):
    shift %= 8
    return pltpu.roll(value, shift, 0) if shift else value


def select(mask, a, b):
    return jnp.where(mask, a, b)


def t_edges(links):
    t_idx, _ = site_masks()
    return [each(lambda v: select(t_idx == 0, roll_rows(v, 4), v), row) for row in links]


def x_edges(links):
    _, x_idx = site_masks()

    def edge(value):
        out = value
        for k in range(3):
            out = select(x_idx == k, roll_rows(value, k - 3), out)
        return out

    return [each(edge, row) for row in links]


def send_t(f_ref, links_ref, parity, t_one, t_two, ready=lambda r: None):
    even = even_device("ta", "gx", extra=parity)
    t_idx, _ = site_masks()
    first = t_idx == 0
    links = t_edges(load_links(links_ref, 0, parity))
    for r in range(RHS):
        ready(r)
        field = load_field(f_ref, r)
        ahead, behind = project(field, 0, -1), project(field, 0, 1)
        rears = [
            tuple(select(first, roll_rows(behind[c][i], 4), behind[c + 3][i]) for i in range(2)) for c in range(3)
        ]
        rears = matvec(links, rounded(rears), True)
        for c in range(3):
            front = [select(first, ahead[c + 3][i], roll_rows(ahead[c][i], 4)) for i in range(2)]
            store_pair(t_one, r * 3 + c, either(even, rears[c], front))
            store_pair(t_two, r * 3 + c, either(even, front, rears[c]))


def send_x_kernel(parity, f_ref, links_ref, x_far, x_near):
    even = even_device("gx")
    _, x_idx = site_masks()
    links = x_edges(load_links(links_ref, 1, parity))

    def packed(values, row, step):
        out = values[0]
        for k in range(1, 4):
            out = select(x_idx == row + step * k, roll_rows(values[k], step * k), out)
        return out

    for q in range(RHS // 2):
        fields = [load_field(f_ref, r) for r in (2 * q, 2 * q + 1)]
        ahead = [project(field, 1, -1) for field in fields]
        behind = [project(field, 1, 1) for field in fields]
        fronts, rears = [], []
        for c in range(3):
            fronts.append([packed([h[j][i] for h in ahead for j in (c, c + 3)], 0, 1) for i in range(2)])
            rears.append([packed([h[j][i] for h in behind for j in (c, c + 3)], 3, -1) for i in range(2)])
        rears = matvec(links, rounded(rears), True)
        for c in range(3):
            store_pair(x_near, q * 3 + c, either(even, rears[c], fronts[c]))
            store_pair(x_far, q * 3 + c, either(even, fronts[c], rears[c]))


def start_kernel(f_hbm, links_hbm, *refs):
    outs, (f_ref, links_ref, sems) = refs[:2], refs[2:]
    part = f_ref.shape[0] // RHS
    copies = [pltpu.make_async_copy(links_hbm.at[pl.ds(0, links_ref.shape[0])], links_ref, sems.at[RHS])]
    for r in range(RHS):
        rows = pl.ds(r * part, part)
        copies.append(pltpu.make_async_copy(f_hbm.at[rows], f_ref.at[rows], sems.at[r]))
    for copy in copies:
        copy.start()
    copies[0].wait()
    send_t(f_ref, links_ref, 0, *outs, ready=lambda r: copies[1 + r].wait())


def interior_kernel(parity, with_base, *refs):
    if with_base:
        f_ref, links_ref, base_ref, clover_ref, acc_ref = refs
        clover_to(clover_ref, lambda r: load_field(base_ref, r), acc_ref, -1.0 / KAPPA2)
    else:
        f_ref, links_ref, acc_ref = refs
    out_parity = 1 - parity
    t_idx, x_idx = site_masks()
    lane = lax.broadcasted_iota(jnp.int32, (8, 128), 1)
    odd = (t_idx + x_idx + lane // HALF_DEPTH + out_parity) % 2
    start = lane - lane % HALF_DEPTH
    up = jnp.where(odd == 1, start + (lane + 1) % HALF_DEPTH, lane)
    down = jnp.where(odd == 0, start + (lane + HALF_DEPTH - 1) % HALF_DEPTH, lane)
    zero = jnp.zeros((8, 128), F32)

    def take(value, index):
        return jnp.take_along_axis(value, index, axis=1, mode="promise_in_bounds")

    for mu in (2, 3, 0, 1):
        if mu == 2:
            ahead_of = lambda v: pltpu.roll(v, 128 - HALF_DEPTH, 1)
            behind_of = lambda v: pltpu.roll(v, HALF_DEPTH, 1)
        elif mu == 3:
            ahead_of = lambda v: take(v, up)
            behind_of = lambda v: take(v, down)
        elif mu == 0:
            ahead_of = lambda v: select(t_idx == 0, roll_rows(v, 4), 0.0)
            behind_of = lambda v: select(t_idx == 1, roll_rows(v, 4), 0.0)
        else:
            ahead_of = lambda v: select(x_idx < 3, roll_rows(v, 7), 0.0)
            behind_of = lambda v: select(x_idx > 0, roll_rows(v, 1), 0.0)
        links_out = load_links(links_ref, mu, out_parity)
        links_in = load_links(links_ref, mu, parity)
        for r in range(RHS):
            field = load_field(f_ref, r)
            if mu == 2 and not with_base:
                acc = [(zero, zero)] * 12
            else:
                acc = load_field(acc_ref, r)
            half = color(links_out, each(ahead_of, rounded(project(field, mu, -1))), False)
            acc = rebuild(acc, half, mu, -1)
            half = rounded(color(links_in, rounded(project(field, mu, 1)), True))
            acc = rebuild(acc, each(behind_of, half), mu, 1)
            store_field(acc_ref, r, acc)


def clover_to(clover_ref, get_field, out_ref, scale):
    for chi in range(2):
        matrix = {}
        for i in range(6):
            for j in range(i, 6):
                k = (chi * 6 + i) * 6 + j
                block = clover_ref[k * 16:(k + 1) * 16, :].astype(F32)
                re, im = block[0:8], block[8:16]
                if scale != 1.0:
                    re, im = re * scale, im * scale
                matrix[i, j] = (re, re + im, im - re)
        for r in range(RHS):
            field = get_field(r)[chi * 6:chi * 6 + 6]
            both = [vr + vi for vr, vi in field]
            for i in range(6):
                one = two = three = None
                for j in range(6):
                    vr, vi = field[j]
                    m, plus, minus = matrix[min(i, j), max(i, j)]
                    t_one = m * both[j]
                    if i <= j:
                        t_two, t_three = -(vi * plus), vr * minus
                    else:
                        t_two, t_three = vi * minus, -(vr * plus)
                    one = t_one if one is None else one + t_one
                    two = t_two if two is None else two + t_two
                    three = t_three if three is None else three + t_three
                store_pair(out_ref, r * 12 + chi * 6 + i, (one + two, one + three))


def matvec(links, vector, adjoint):
    out = []
    for a in range(3):
        re = im = None
        for b in range(3):
            lr, li = links[b][a] if adjoint else links[a][b]
            vr, vi = vector[b]
            if adjoint:
                tr, ti = lr * vr + li * vi, lr * vi - li * vr
            else:
                tr, ti = lr * vr - li * vi, lr * vi + li * vr
            re = tr if re is None else re + tr
            im = ti if im is None else im + ti
        out.append((re, im))
    return out


def rebuild_signed(acc, half, mu, sign):
    out = list(acc)
    for j in range(6):
        out[j] = add_power(out[j], half[j], 0)
    half = each(lambda v: v * sign, half)
    for row in range(2):
        col, power = SPIN_INV[mu][row]
        for c in range(3):
            j = (2 + row) * 3 + c
            out[j] = add_power(out[j], half[col * 3 + c], power)
    return out


def join_x_kernel(parity, links_ref, acc_ref, x_far, x_near, out_ref):
    even = even_device("gx")
    _, x_idx = site_masks()
    sign = jnp.where(x_idx == 3, -1.0, 1.0).astype(F32)
    links = x_edges(load_links(links_ref, 1, 1 - parity))
    for q in range(RHS // 2):
        nxt, last = [], []
        for c in range(3):
            near, far = load_pair(x_near, q * 3 + c), load_pair(x_far, q * 3 + c)
            nxt.append(either(even, near, far))
            last.append(either(even, far, near))
        ahead = matvec(links, nxt, False)
        for r in (2 * q, 2 * q + 1):
            half = [None] * 6
            for s in range(2):
                k = (r % 2) * 2 + s
                for c in range(3):
                    half[s * 3 + c] = tuple(
                        select(
                            x_idx == 3,
                            roll_rows(ahead[c][i], 3 - k),
                            select(x_idx == 0, roll_rows(last[c][i], 5 + k), 0.0),
                        )
                        for i in range(2)
                    )
            store_field(out_ref, r, rebuild_signed(load_field(acc_ref, r), half, 1, sign))


def join_t(links_ref, acc_ref, t_one, t_two, parity, out_ref, scale=None, done=lambda r: None):
    even = even_device("ta", "gx", extra=parity)
    t_idx, _ = site_masks()
    first = t_idx == 0
    sign = jnp.where(first, 1.0, -1.0).astype(F32)
    links = t_edges(load_links(links_ref, 0, 1 - parity))
    for r in range(RHS):
        nxt, last = [], []
        for c in range(3):
            one, two = load_pair(t_one, r * 3 + c), load_pair(t_two, r * 3 + c)
            nxt.append(either(even, one, two))
            last.append(either(even, two, one))
        ahead = matvec(links, nxt, False)
        half = [tuple(select(first, last[c][i], ahead[c][i]) for i in range(2)) for c in range(3)]
        half += [
            tuple(roll_rows(select(first, ahead[c][i], last[c][i]), 4) for i in range(2)) for c in range(3)
        ]
        field = rebuild_signed(load_field(acc_ref, r), half, 0, sign)
        if scale is not None:
            field = each(lambda v: v * scale, field)
        store_field(out_ref, r, field)
        done(r)


def odd_kernel(links_ref, clover_ref, acc_ref, t_one, t_two, out_ref, *refs):
    outs, summed = refs[:2], refs[2]
    join_t(links_ref, acc_ref, t_one, t_two, 0, summed)
    clover_to(clover_ref, lambda r: load_field(summed, r), out_ref, 1.0)
    send_t(out_ref, links_ref, 1, *outs)


def even_kernel(links_ref, acc_ref, t_one, t_two, out_ref, *outs):
    join_t(links_ref, acc_ref, t_one, t_two, 1, out_ref, -KAPPA2)
    send_t(out_ref, links_ref, 0, *outs)


def last_kernel(links_ref, acc_ref, t_one, t_two, out_hbm, held, sems):
    part = held.shape[0] // RHS
    copies = []

    def done(r):
        rows = pl.ds(r * part, part)
        copies.append(pltpu.make_async_copy(held.at[rows], out_hbm.at[rows], sems.at[r]))
        copies[-1].start()

    join_t(links_ref, acc_ref, t_one, t_two, 1, held, -KAPPA2, done)
    for copy in copies:
        copy.wait()


ROWS = RHS * 24 * 8
FIELD = [((ROWS, 128), BF16)]
SUM = [((ROWS, 128), F32)]
T_HALOS = [((RHS * 3 * 16, 128), BF16)] * 2
X_HALOS = [((RHS * 3 * 8, 128), BF16)] * 2


def call(kernel, args, outs, flops, scratch=(), in_space=pltpu.VMEM, out_space=pltpu.VMEM):
    return pl.pallas_call(
        kernel,
        out_shape=tuple(jax.ShapeDtypeStruct(shape, dtype) for shape, dtype in outs),
        in_specs=[pl.BlockSpec(memory_space=in_space)] * len(args),
        out_specs=tuple([pl.BlockSpec(memory_space=out_space)] * len(outs)),
        scratch_shapes=list(scratch),
        compiler_params=pltpu.CompilerParams(vmem_limit_bytes=24 * 1024 * 1024),
        cost_estimate=pl.CostEstimate(flops=flops, bytes_accessed=2 * 1024 * 1024, transcendentals=0),
    )(*args)


def swap(value, axis, far):
    count = lax.axis_size(axis)
    assert count % 2 == 0
    pairs = [(i, (i + (1 if (i % 2 == 0) != far else -1)) % count) for i in range(count)]
    return lax.ppermute(value, axis, pairs)


def swap_t(value, ahead):
    count, across = lax.axis_size("ta"), lax.axis_size("gx")
    assert count % 2 == 0 and across % 2 == 0
    pairs = []
    for i in range(count):
        for j in range(across):
            step = 1 if ((i + j) % 2 == 0) == ahead else -1
            pairs.append((i * across + j, (i + step) % count * across + j))
    return lax.ppermute(value, ("ta", "gx"), pairs)


def per_device(source, gauge_links, clover_even, clover_odd_inv):
    shape = source.shape
    f = source.reshape(-1, 128)
    links = gauge_links.reshape(-1, 128)
    even = clover_even.reshape(-1, 128)
    odd = clover_odd_inv.reshape(-1, 128)
    held = [pltpu.with_memory_space_constraint(v, pltpu.HBM) for v in (f, links)]
    start_scratch = [
        pltpu.VMEM((ROWS, 128), BF16),
        pltpu.VMEM((links.shape[0] // 4, 128), BF16),
        pltpu.SemaphoreType.DMA((RHS + 1,)),
    ]
    t_one, t_two = call(start_kernel, held, T_HALOS, 1_500_000, start_scratch, in_space=pltpu.HBM)
    for hop in range(4):
        parity = hop % 2
        t_one, t_two = swap_t(t_one, parity == 0), swap_t(t_two, parity == 1)
        x_far, x_near = call(
            functools.partial(send_x_kernel, parity), (f, links), X_HALOS, 1_500_000
        )
        here, x_far, x_near = lax.optimization_barrier((f, x_far, x_near))
        x_far, x_near = swap(x_far, "gx", True), swap(x_near, "gx", False)
        base = (before, even) if parity else ()
        acc, = call(
            functools.partial(interior_kernel, parity, bool(parity)),
            (here, links, *base), SUM, 8_000_000 if parity else 5_000_000,
        )
        acc, = call(functools.partial(join_x_kernel, parity), (links, acc, x_far, x_near), SUM, 1_000_000)
        before = f
        if parity == 0:
            f, t_one, t_two = call(
                odd_kernel, (links, odd, acc, t_one, t_two), FIELD + T_HALOS, 4_000_000,
                [pltpu.VMEM((ROWS, 128), BF16)],
            )
        elif hop == 1:
            f, t_one, t_two = call(
                even_kernel, (links, acc, t_one, t_two), FIELD + T_HALOS, 2_000_000
            )
        else:
            out, = call(
                last_kernel, (links, acc, t_one, t_two), FIELD, 1_000_000,
                [pltpu.VMEM((ROWS, 128), BF16), pltpu.SemaphoreType.DMA((RHS,))], out_space=pltpu.HBM,
            )
    return out.reshape(shape)


def solution(mesh):
    field_spec = P(None, None, None, None, ("groups", "ta"), "gx", None)
    link_spec = P(None, None, None, None, None, ("groups", "ta"), "gx", None)
    return jax.shard_map(
        per_device,
        mesh=mesh,
        in_specs=(field_spec, link_spec, field_spec, field_spec),
        out_specs=field_spec,
        check_vma=False,
    )
```

```python
import functools

import jax
import jax.numpy as jnp
from jax import lax
from jax.experimental import pallas as pl
from jax.experimental.pallas import tpu as pltpu
from jax.sharding import PartitionSpec as P

HALF_DEPTH = 8
KAPPA2 = 0.14 * 0.14
RHS = 4
F32 = jnp.float32
BF16 = jnp.bfloat16

SPIN = (((0, 0), (1, 0)), ((1, 3), (0, 3)), ((1, 2), (0, 0)), ((0, 3), (1, 1)))
SPIN_INV = (((0, 0), (1, 0)), ((1, 1), (0, 1)), ((1, 0), (0, 2)), ((0, 1), (1, 3)))


def add_power(base, value, power):
    (br, bi), (vr, vi) = base, value
    if power == 0:
        return br + vr, bi + vi
    if power == 1:
        return br - vi, bi + vr
    if power == 2:
        return br - vr, bi - vi
    return br + vi, bi - vr


def project(field, mu, sign):
    shift = 0 if sign > 0 else 2
    half = []
    for row in range(2):
        col, power = SPIN[mu][row]
        for c in range(3):
            half.append(add_power(field[row * 3 + c], field[(2 + col) * 3 + c], (power + shift) % 4))
    return half


def rebuild(acc, half, mu, sign):
    shift = 0 if sign > 0 else 2
    out = list(acc)
    for j in range(6):
        out[j] = add_power(out[j], half[j], 0)
    for row in range(2):
        col, power = SPIN_INV[mu][row]
        for c in range(3):
            j = (2 + row) * 3 + c
            out[j] = add_power(out[j], half[col * 3 + c], (power + shift) % 4)
    return out


def color(links, half, adjoint):
    out = []
    for s in range(2):
        for a in range(3):
            re = im = None
            for b in range(3):
                lr, li = links[b][a] if adjoint else links[a][b]
                vr, vi = half[s * 3 + b]
                if adjoint:
                    tr, ti = lr * vr + li * vi, lr * vi - li * vr
                else:
                    tr, ti = lr * vr - li * vi, lr * vi + li * vr
                re = tr if re is None else re + tr
                im = ti if im is None else im + ti
            out.append((re, im))
    return out


def each(function, half):
    return [(function(re), function(im)) for re, im in half]


def load_pair(ref, index):
    block = ref[index * 16:(index + 1) * 16, :].astype(F32)
    return block[0:8], block[8:16]


def rounded(half):
    out = []
    for pair in half:
        block = jnp.concatenate(pair, axis=0).astype(BF16).astype(F32)
        out.append((block[0:8], block[8:16]))
    return out


def load_links(ref, mu, parity):
    links = []
    for a in range(3):
        row = []
        for b in range(3):
            k = ((mu * 3 + a) * 3 + b) * 2
            row.append((load_pair(ref, k)[parity], load_pair(ref, k + 1)[parity]))
        links.append(row)
    return links


def load_field(ref, r):
    return [load_pair(ref, r * 12 + j) for j in range(12)]


def store_pair(ref, index, pair):
    ref[index * 16:(index + 1) * 16, :] = jnp.concatenate(pair, axis=0).astype(ref.dtype)


def store_field(ref, r, field):
    for j in range(12):
        store_pair(ref, r * 12 + j, field[j])


def site_masks():
    rows = lax.broadcasted_iota(jnp.int32, (8, 128), 0)
    return rows // 4, rows % 4


def even_device(*axes):
    place = sum(lax.axis_index(axis) for axis in axes)
    return lax.broadcast(place % 2, (8, 128)) == 0


def either(even, a, b):
    return [select(even, a[i], b[i]) for i in range(2)]


def roll_rows(value, shift):
    shift %= 8
    return pltpu.roll(value, shift, 0) if shift else value


def select(mask, a, b):
    return jnp.where(mask, a, b)


def t_edges(links):
    t_idx, _ = site_masks()
    return [each(lambda v: select(t_idx == 0, roll_rows(v, 4), v), row) for row in links]


def x_edges(links):
    _, x_idx = site_masks()

    def edge(value):
        out = value
        for k in range(3):
            out = select(x_idx == k, roll_rows(value, k - 3), out)
        return out

    return [each(edge, row) for row in links]


def send_t(f_ref, links_ref, parity, t_one, t_two, ready=lambda r: None):
    even = even_device("ta", "gx")
    t_idx, _ = site_masks()
    first = t_idx == 0
    links = t_edges(load_links(links_ref, 0, parity))
    for r in range(RHS):
        ready(r)
        field = load_field(f_ref, r)
        ahead, behind = project(field, 0, -1), project(field, 0, 1)
        rears = [
            tuple(select(first, roll_rows(behind[c][i], 4), behind[c + 3][i]) for i in range(2)) for c in range(3)
        ]
        rears = matvec(links, rounded(rears), True)
        for c in range(3):
            front = [select(first, ahead[c + 3][i], roll_rows(ahead[c][i], 4)) for i in range(2)]
            store_pair(t_one, r * 3 + c, either(even, rears[c], front))
            store_pair(t_two, r * 3 + c, either(even, front, rears[c]))


def send_x_kernel(parity, f_ref, links_ref, x_far, x_near):
    even = even_device("gx")
    _, x_idx = site_masks()
    links = x_edges(load_links(links_ref, 1, parity))

    def packed(values, row, step):
        out = values[0]
        for k in range(1, 4):
            out = select(x_idx == row + step * k, roll_rows(values[k], step * k), out)
        return out

    for q in range(RHS // 2):
        fields = [load_field(f_ref, r) for r in (2 * q, 2 * q + 1)]
        ahead = [project(field, 1, -1) for field in fields]
        behind = [project(field, 1, 1) for field in fields]
        fronts, rears = [], []
        for c in range(3):
            fronts.append([packed([h[j][i] for h in ahead for j in (c, c + 3)], 0, 1) for i in range(2)])
            rears.append([packed([h[j][i] for h in behind for j in (c, c + 3)], 3, -1) for i in range(2)])
        rears = matvec(links, rounded(rears), True)
        for c in range(3):
            store_pair(x_near, q * 3 + c, either(even, rears[c], fronts[c]))
            store_pair(x_far, q * 3 + c, either(even, fronts[c], rears[c]))


def start_kernel(f_hbm, links_hbm, *refs):
    outs, (f_ref, links_ref, sems) = refs[:2], refs[2:]
    part = f_ref.shape[0] // RHS
    copies = [pltpu.make_async_copy(links_hbm.at[pl.ds(0, links_ref.shape[0])], links_ref, sems.at[RHS])]
    for r in range(RHS):
        rows = pl.ds(r * part, part)
        copies.append(pltpu.make_async_copy(f_hbm.at[rows], f_ref.at[rows], sems.at[r]))
    for copy in copies:
        copy.start()
    copies[0].wait()
    send_t(f_ref, links_ref, 0, *outs, ready=lambda r: copies[1 + r].wait())


def interior_kernel(parity, with_base, *refs):
    if with_base:
        f_ref, links_ref, base_ref, clover_ref, acc_ref = refs
        clover_to(clover_ref, lambda r: load_field(base_ref, r), acc_ref, -1.0 / KAPPA2)
    else:
        f_ref, links_ref, acc_ref = refs
    out_parity = 1 - parity
    t_idx, x_idx = site_masks()
    lane = lax.broadcasted_iota(jnp.int32, (8, 128), 1)
    odd = (t_idx + x_idx + lane // HALF_DEPTH + out_parity) % 2
    start = lane - lane % HALF_DEPTH
    up = jnp.where(odd == 1, start + (lane + 1) % HALF_DEPTH, lane)
    down = jnp.where(odd == 0, start + (lane + HALF_DEPTH - 1) % HALF_DEPTH, lane)
    zero = jnp.zeros((8, 128), F32)

    def take(value, index):
        return jnp.take_along_axis(value, index, axis=1, mode="promise_in_bounds")

    for mu in (2, 3, 0, 1):
        if mu == 2:
            ahead_of = lambda v: pltpu.roll(v, 128 - HALF_DEPTH, 1)
            behind_of = lambda v: pltpu.roll(v, HALF_DEPTH, 1)
        elif mu == 3:
            ahead_of = lambda v: take(v, up)
            behind_of = lambda v: take(v, down)
        elif mu == 0:
            ahead_of = lambda v: select(t_idx == 0, roll_rows(v, 4), 0.0)
            behind_of = lambda v: select(t_idx == 1, roll_rows(v, 4), 0.0)
        else:
            ahead_of = lambda v: select(x_idx < 3, roll_rows(v, 7), 0.0)
            behind_of = lambda v: select(x_idx > 0, roll_rows(v, 1), 0.0)
        links_out = load_links(links_ref, mu, out_parity)
        links_in = load_links(links_ref, mu, parity)
        for r in range(RHS):
            field = load_field(f_ref, r)
            if mu == 2 and not with_base:
                acc = [(zero, zero)] * 12
            else:
                acc = load_field(acc_ref, r)
            half = color(links_out, each(ahead_of, rounded(project(field, mu, -1))), False)
            acc = rebuild(acc, half, mu, -1)
            half = rounded(color(links_in, rounded(project(field, mu, 1)), True))
            acc = rebuild(acc, each(behind_of, half), mu, 1)
            store_field(acc_ref, r, acc)


def clover_to(clover_ref, get_field, out_ref, scale):
    for chi in range(2):
        matrix = {}
        for i in range(6):
            for j in range(i, 6):
                k = (chi * 6 + i) * 6 + j
                block = clover_ref[k * 16:(k + 1) * 16, :].astype(F32)
                re, im = block[0:8], block[8:16]
                if scale != 1.0:
                    re, im = re * scale, im * scale
                matrix[i, j] = (re, re + im, im - re)
        for r in range(RHS):
            field = get_field(r)[chi * 6:chi * 6 + 6]
            both = [vr + vi for vr, vi in field]
            for i in range(6):
                one = two = three = None
                for j in range(6):
                    vr, vi = field[j]
                    m, plus, minus = matrix[min(i, j), max(i, j)]
                    t_one = m * both[j]
                    if i <= j:
                        t_two, t_three = -(vi * plus), vr * minus
                    else:
                        t_two, t_three = vi * minus, -(vr * plus)
                    one = t_one if one is None else one + t_one
                    two = t_two if two is None else two + t_two
                    three = t_three if three is None else three + t_three
                store_pair(out_ref, r * 12 + chi * 6 + i, (one + two, one + three))


def matvec(links, vector, adjoint):
    out = []
    for a in range(3):
        re = im = None
        for b in range(3):
            lr, li = links[b][a] if adjoint else links[a][b]
            vr, vi = vector[b]
            if adjoint:
                tr, ti = lr * vr + li * vi, lr * vi - li * vr
            else:
                tr, ti = lr * vr - li * vi, lr * vi + li * vr
            re = tr if re is None else re + tr
            im = ti if im is None else im + ti
        out.append((re, im))
    return out


def rebuild_signed(acc, half, mu, sign):
    out = list(acc)
    for j in range(6):
        out[j] = add_power(out[j], half[j], 0)
    half = each(lambda v: v * sign, half)
    for row in range(2):
        col, power = SPIN_INV[mu][row]
        for c in range(3):
            j = (2 + row) * 3 + c
            out[j] = add_power(out[j], half[col * 3 + c], power)
    return out


def join_x(links_ref, acc_ref, x_far, x_near, parity, out_ref):
    even = even_device("gx")
    _, x_idx = site_masks()
    sign = jnp.where(x_idx == 3, -1.0, 1.0).astype(F32)
    links = x_edges(load_links(links_ref, 1, 1 - parity))
    for q in range(RHS // 2):
        nxt, last = [], []
        for c in range(3):
            near, far = load_pair(x_near, q * 3 + c), load_pair(x_far, q * 3 + c)
            nxt.append(either(even, near, far))
            last.append(either(even, far, near))
        ahead = matvec(links, nxt, False)
        for r in (2 * q, 2 * q + 1):
            half = [None] * 6
            for s in range(2):
                k = (r % 2) * 2 + s
                for c in range(3):
                    half[s * 3 + c] = tuple(
                        select(
                            x_idx == 3,
                            roll_rows(ahead[c][i], 3 - k),
                            select(x_idx == 0, roll_rows(last[c][i], 5 + k), 0.0),
                        )
                        for i in range(2)
                    )
            store_field(out_ref, r, rebuild_signed(load_field(acc_ref, r), half, 1, sign))


def join_t(links_ref, acc_ref, t_one, t_two, parity, out_ref, scale=None, done=lambda r: None):
    even = even_device("ta", "gx")
    t_idx, _ = site_masks()
    first = t_idx == 0
    sign = jnp.where(first, 1.0, -1.0).astype(F32)
    links = t_edges(load_links(links_ref, 0, 1 - parity))
    for r in range(RHS):
        nxt, last = [], []
        for c in range(3):
            one, two = load_pair(t_one, r * 3 + c), load_pair(t_two, r * 3 + c)
            nxt.append(either(even, one, two))
            last.append(either(even, two, one))
        ahead = matvec(links, nxt, False)
        half = [tuple(select(first, last[c][i], ahead[c][i]) for i in range(2)) for c in range(3)]
        half += [
            tuple(roll_rows(select(first, ahead[c][i], last[c][i]), 4) for i in range(2)) for c in range(3)
        ]
        field = rebuild_signed(load_field(acc_ref, r), half, 0, sign)
        if scale is not None:
            field = each(lambda v: v * scale, field)
        store_field(out_ref, r, field)
        done(r)


def odd_kernel(links_ref, clover_ref, acc_ref, t_one, t_two, x_far, x_near, out_ref, *refs):
    outs, summed, both = refs[:2], refs[2], refs[3]
    join_x(links_ref, acc_ref, x_far, x_near, 0, both)
    join_t(links_ref, both, t_one, t_two, 0, summed)
    clover_to(clover_ref, lambda r: load_field(summed, r), out_ref, 1.0)
    send_t(out_ref, links_ref, 1, *outs)


def even_kernel(links_ref, acc_ref, t_one, t_two, x_far, x_near, out_ref, *refs):
    outs, both = refs[:2], refs[2]
    join_x(links_ref, acc_ref, x_far, x_near, 1, both)
    join_t(links_ref, both, t_one, t_two, 1, out_ref, -KAPPA2)
    send_t(out_ref, links_ref, 0, *outs)


def last_kernel(links_ref, acc_ref, t_one, t_two, x_far, x_near, out_hbm, held, sems, both):
    part = held.shape[0] // RHS
    copies = []

    def done(r):
        rows = pl.ds(r * part, part)
        copies.append(pltpu.make_async_copy(held.at[rows], out_hbm.at[rows], sems.at[r]))
        copies[-1].start()

    join_x(links_ref, acc_ref, x_far, x_near, 1, both)
    join_t(links_ref, both, t_one, t_two, 1, held, -KAPPA2, done)
    for copy in copies:
        copy.wait()


ROWS = RHS * 24 * 8
FIELD = [((ROWS, 128), BF16)]
SUM = [((ROWS, 128), F32)]
T_HALOS = [((RHS * 3 * 16, 128), BF16)] * 2
X_HALOS = [((RHS * 3 * 8, 128), BF16)] * 2


def call(kernel, args, outs, flops, scratch=(), in_space=pltpu.VMEM, out_space=pltpu.VMEM):
    return pl.pallas_call(
        kernel,
        out_shape=tuple(jax.ShapeDtypeStruct(shape, dtype) for shape, dtype in outs),
        in_specs=[pl.BlockSpec(memory_space=in_space)] * len(args),
        out_specs=tuple([pl.BlockSpec(memory_space=out_space)] * len(outs)),
        scratch_shapes=list(scratch),
        compiler_params=pltpu.CompilerParams(vmem_limit_bytes=24 * 1024 * 1024),
        cost_estimate=pl.CostEstimate(flops=flops, bytes_accessed=2 * 1024 * 1024, transcendentals=0),
    )(*args)


def swap(value, axis, far):
    count = lax.axis_size(axis)
    assert count % 2 == 0
    pairs = [(i, (i + (1 if (i % 2 == 0) != far else -1)) % count) for i in range(count)]
    return lax.ppermute(value, axis, pairs)


def swap_t(value, ahead):
    count, across = lax.axis_size("ta"), lax.axis_size("gx")
    assert count % 2 == 0 and across % 2 == 0
    pairs = []
    for i in range(count):
        for j in range(across):
            step = 1 if ((i + j) % 2 == 0) == ahead else -1
            pairs.append((i * across + j, (i + step) % count * across + j))
    return lax.ppermute(value, ("ta", "gx"), pairs)


def per_device(source, gauge_links, clover_even, clover_odd_inv):
    shape = source.shape
    f = source.reshape(-1, 128)
    links = gauge_links.reshape(-1, 128)
    even = clover_even.reshape(-1, 128)
    odd = clover_odd_inv.reshape(-1, 128)
    held = [pltpu.with_memory_space_constraint(v, pltpu.HBM) for v in (f, links)]
    start_scratch = [
        pltpu.VMEM((ROWS, 128), BF16),
        pltpu.VMEM((links.shape[0] // 4, 128), BF16),
        pltpu.SemaphoreType.DMA((RHS + 1,)),
    ]
    t_one, t_two = call(start_kernel, held, T_HALOS, 1_500_000, start_scratch, in_space=pltpu.HBM)
    for hop in range(4):
        parity = hop % 2
        t_one, t_two = swap_t(t_one, True), swap_t(t_two, False)
        x_far, x_near = call(
            functools.partial(send_x_kernel, parity), (f, links), X_HALOS, 1_500_000
        )
        here, x_far, x_near = lax.optimization_barrier((f, x_far, x_near))
        x_far, x_near = swap(x_far, "gx", True), swap(x_near, "gx", False)
        base = (before, even) if parity else ()
        acc, = call(
            functools.partial(interior_kernel, parity, bool(parity)),
            (here, links, *base), SUM, 8_000_000 if parity else 5_000_000,
        )
        before = f
        if parity == 0:
            f, t_one, t_two = call(
                odd_kernel, (links, odd, acc, t_one, t_two, x_far, x_near), FIELD + T_HALOS, 4_000_000,
                [pltpu.VMEM((ROWS, 128), BF16), pltpu.VMEM((ROWS, 128), F32)],
            )
        elif hop == 1:
            f, t_one, t_two = call(
                even_kernel, (links, acc, t_one, t_two, x_far, x_near), FIELD + T_HALOS, 2_000_000, [pltpu.VMEM((ROWS, 128), F32)]
            )
        else:
            out, = call(
                last_kernel, (links, acc, t_one, t_two, x_far, x_near), FIELD, 1_000_000,
                [pltpu.VMEM((ROWS, 128), BF16), pltpu.SemaphoreType.DMA((RHS,)), pltpu.VMEM((ROWS, 128), F32)], out_space=pltpu.HBM,
            )
    return out.reshape(shape)


def solution(mesh):
    field_spec = P(None, None, None, None, ("groups", "ta"), "gx", None)
    link_spec = P(None, None, None, None, None, ("groups", "ta"), "gx", None)
    return jax.shard_map(
        per_device,
        mesh=mesh,
        in_specs=(field_spec, link_spec, field_spec, field_spec),
        out_specs=field_spec,
        check_vma=False,
    )
```

```python
import functools

import jax
import jax.numpy as jnp
from jax import lax
from jax.experimental import pallas as pl
from jax.experimental.pallas import tpu as pltpu
from jax.sharding import PartitionSpec as P

HALF_DEPTH = 8
KAPPA2 = 0.14 * 0.14
RHS = 4
F32 = jnp.float32
BF16 = jnp.bfloat16

SPIN = (((0, 0), (1, 0)), ((1, 3), (0, 3)), ((1, 2), (0, 0)), ((0, 3), (1, 1)))
SPIN_INV = (((0, 0), (1, 0)), ((1, 1), (0, 1)), ((1, 0), (0, 2)), ((0, 1), (1, 3)))


def add_power(base, value, power):
    (br, bi), (vr, vi) = base, value
    if power == 0:
        return br + vr, bi + vi
    if power == 1:
        return br - vi, bi + vr
    if power == 2:
        return br - vr, bi - vi
    return br + vi, bi - vr


def project(field, mu, sign):
    shift = 0 if sign > 0 else 2
    half = []
    for row in range(2):
        col, power = SPIN[mu][row]
        for c in range(3):
            half.append(add_power(field[row * 3 + c], field[(2 + col) * 3 + c], (power + shift) % 4))
    return half


def rebuild(acc, half, mu, sign):
    shift = 0 if sign > 0 else 2
    out = list(acc)
    for j in range(6):
        out[j] = add_power(out[j], half[j], 0)
    for row in range(2):
        col, power = SPIN_INV[mu][row]
        for c in range(3):
            j = (2 + row) * 3 + c
            out[j] = add_power(out[j], half[col * 3 + c], (power + shift) % 4)
    return out


def color(links, half, adjoint):
    out = []
    for s in range(2):
        for a in range(3):
            re = im = None
            for b in range(3):
                lr, li = links[b][a] if adjoint else links[a][b]
                vr, vi = half[s * 3 + b]
                if adjoint:
                    tr, ti = lr * vr + li * vi, lr * vi - li * vr
                else:
                    tr, ti = lr * vr - li * vi, lr * vi + li * vr
                re = tr if re is None else re + tr
                im = ti if im is None else im + ti
            out.append((re, im))
    return out


def each(function, half):
    return [(function(re), function(im)) for re, im in half]


def load_pair(ref, index):
    block = ref[index * 16:(index + 1) * 16, :].astype(F32)
    return block[0:8], block[8:16]


def rounded(half):
    out = []
    for pair in half:
        block = jnp.concatenate(pair, axis=0).astype(BF16).astype(F32)
        out.append((block[0:8], block[8:16]))
    return out


def load_links(ref, mu, parity):
    links = []
    for a in range(3):
        row = []
        for b in range(3):
            k = ((mu * 3 + a) * 3 + b) * 2
            row.append((load_pair(ref, k)[parity], load_pair(ref, k + 1)[parity]))
        links.append(row)
    return links


def load_field(ref, r):
    return [load_pair(ref, r * 12 + j) for j in range(12)]


def store_pair(ref, index, pair):
    ref[index * 16:(index + 1) * 16, :] = jnp.concatenate(pair, axis=0).astype(ref.dtype)


def store_field(ref, r, field):
    for j in range(12):
        store_pair(ref, r * 12 + j, field[j])


def site_masks():
    rows = lax.broadcasted_iota(jnp.int32, (8, 128), 0)
    return rows // 4, rows % 4


def even_device(*axes):
    place = sum(lax.axis_index(axis) for axis in axes)
    return lax.broadcast(place % 2, (8, 128)) == 0


def either(even, a, b):
    return [select(even, a[i], b[i]) for i in range(2)]


def roll_rows(value, shift):
    shift %= 8
    return pltpu.roll(value, shift, 0) if shift else value


def select(mask, a, b):
    return jnp.where(mask, a, b)


def t_edges(links):
    t_idx, _ = site_masks()
    return [each(lambda v: select(t_idx == 0, roll_rows(v, 4), v), row) for row in links]


def x_edges(links):
    _, x_idx = site_masks()

    def edge(value):
        out = value
        for k in range(3):
            out = select(x_idx == k, roll_rows(value, k - 3), out)
        return out

    return [each(edge, row) for row in links]


def send_t(f_ref, links_ref, parity, t_one, t_two, ready=lambda r: None):
    even = even_device("ta", "gx")
    t_idx, _ = site_masks()
    first = t_idx == 0
    links = t_edges(load_links(links_ref, 0, parity))
    for r in range(RHS):
        ready(r)
        field = load_field(f_ref, r)
        ahead, behind = project(field, 0, -1), project(field, 0, 1)
        rears = [
            tuple(select(first, roll_rows(behind[c][i], 4), behind[c + 3][i]) for i in range(2)) for c in range(3)
        ]
        rears = matvec(links, rounded(rears), True)
        for c in range(3):
            front = [select(first, ahead[c + 3][i], roll_rows(ahead[c][i], 4)) for i in range(2)]
            store_pair(t_one, r * 3 + c, either(even, rears[c], front))
            store_pair(t_two, r * 3 + c, either(even, front, rears[c]))


def send_x_kernel(parity, f_ref, links_ref, x_far, x_near):
    even = even_device("gx")
    _, x_idx = site_masks()
    links = x_edges(load_links(links_ref, 1, parity))

    def packed(values, row, step):
        out = values[0]
        for k in range(1, 4):
            out = select(x_idx == row + step * k, roll_rows(values[k], step * k), out)
        return out

    for q in range(RHS // 2):
        fields = [load_field(f_ref, r) for r in (2 * q, 2 * q + 1)]
        ahead = [project(field, 1, -1) for field in fields]
        behind = [project(field, 1, 1) for field in fields]
        fronts, rears = [], []
        for c in range(3):
            fronts.append([packed([h[j][i] for h in ahead for j in (c, c + 3)], 0, 1) for i in range(2)])
            rears.append([packed([h[j][i] for h in behind for j in (c, c + 3)], 3, -1) for i in range(2)])
        rears = matvec(links, rounded(rears), True)
        for c in range(3):
            store_pair(x_near, q * 3 + c, either(even, rears[c], fronts[c]))
            store_pair(x_far, q * 3 + c, either(even, fronts[c], rears[c]))


def start_kernel(f_hbm, links_hbm, *refs):
    outs, (f_ref, links_ref, sems) = refs[:2], refs[2:]
    part = f_ref.shape[0] // RHS
    copies = [pltpu.make_async_copy(links_hbm.at[pl.ds(0, links_ref.shape[0])], links_ref, sems.at[RHS])]
    for r in range(RHS):
        rows = pl.ds(r * part, part)
        copies.append(pltpu.make_async_copy(f_hbm.at[rows], f_ref.at[rows], sems.at[r]))
    for copy in copies:
        copy.start()
    copies[0].wait()
    send_t(f_ref, links_ref, 0, *outs, ready=lambda r: copies[1 + r].wait())


def interior_kernel(parity, with_base, *refs):
    if with_base:
        f_ref, links_ref, base_ref, clover_ref, acc_ref = refs
        clover_to(clover_ref, lambda r: load_field(base_ref, r), acc_ref, -1.0 / KAPPA2)
    else:
        f_ref, links_ref, acc_ref = refs
    out_parity = 1 - parity
    t_idx, x_idx = site_masks()
    lane = lax.broadcasted_iota(jnp.int32, (8, 128), 1)
    odd = (t_idx + x_idx + lane // HALF_DEPTH + out_parity) % 2
    start = lane - lane % HALF_DEPTH
    up = jnp.where(odd == 1, start + (lane + 1) % HALF_DEPTH, lane)
    down = jnp.where(odd == 0, start + (lane + HALF_DEPTH - 1) % HALF_DEPTH, lane)
    zero = jnp.zeros((8, 128), F32)

    def take(value, index):
        return jnp.take_along_axis(value, index, axis=1, mode="promise_in_bounds")

    for mu in (2, 3, 0, 1):
        if mu == 2:
            ahead_of = lambda v: pltpu.roll(v, 128 - HALF_DEPTH, 1)
            behind_of = lambda v: pltpu.roll(v, HALF_DEPTH, 1)
        elif mu == 3:
            ahead_of = lambda v: take(v, up)
            behind_of = lambda v: take(v, down)
        elif mu == 0:
            ahead_of = lambda v: select(t_idx == 0, roll_rows(v, 4), 0.0)
            behind_of = lambda v: select(t_idx == 1, roll_rows(v, 4), 0.0)
        else:
            ahead_of = lambda v: select(x_idx < 3, roll_rows(v, 7), 0.0)
            behind_of = lambda v: select(x_idx > 0, roll_rows(v, 1), 0.0)
        links_out = load_links(links_ref, mu, out_parity)
        links_in = load_links(links_ref, mu, parity)
        for r in range(RHS):
            field = load_field(f_ref, r)
            if mu == 2 and not with_base:
                acc = [(zero, zero)] * 12
            else:
                acc = load_field(acc_ref, r)
            half = color(links_out, each(ahead_of, rounded(project(field, mu, -1))), False)
            acc = rebuild(acc, half, mu, -1)
            half = rounded(color(links_in, rounded(project(field, mu, 1)), True))
            acc = rebuild(acc, each(behind_of, half), mu, 1)
            store_field(acc_ref, r, acc)


def clover_to(clover_ref, get_field, out_ref, scale):
    for chi in range(2):
        matrix = {}
        for i in range(6):
            for j in range(i, 6):
                k = (chi * 6 + i) * 6 + j
                block = clover_ref[k * 16:(k + 1) * 16, :].astype(F32)
                re, im = block[0:8], block[8:16]
                if scale != 1.0:
                    re, im = re * scale, im * scale
                matrix[i, j] = (re, re + im, im - re)
        for r in range(RHS):
            field = get_field(r)[chi * 6:chi * 6 + 6]
            both = [vr + vi for vr, vi in field]
            for i in range(6):
                re, im = matrix[i, i][0] * field[i][0], matrix[i, i][0] * field[i][1]
                one = None
                for j in range(6):
                    if j == i:
                        continue
                    vr, vi = field[j]
                    m, plus, minus = matrix[min(i, j), max(i, j)]
                    t_one = m * both[j]
                    one = t_one if one is None else one + t_one
                    if i < j:
                        re, im = re - vi * plus, im + vr * minus
                    else:
                        re, im = re + vi * minus, im - vr * plus
                store_pair(out_ref, r * 12 + chi * 6 + i, (re + one, im + one))


def matvec(links, vector, adjoint):
    out = []
    for a in range(3):
        re = im = None
        for b in range(3):
            lr, li = links[b][a] if adjoint else links[a][b]
            vr, vi = vector[b]
            if adjoint:
                tr, ti = lr * vr + li * vi, lr * vi - li * vr
            else:
                tr, ti = lr * vr - li * vi, lr * vi + li * vr
            re = tr if re is None else re + tr
            im = ti if im is None else im + ti
        out.append((re, im))
    return out


def rebuild_signed(acc, half, mu, sign):
    out = list(acc)
    for j in range(6):
        out[j] = add_power(out[j], half[j], 0)
    half = each(lambda v: v * sign, half)
    for row in range(2):
        col, power = SPIN_INV[mu][row]
        for c in range(3):
            j = (2 + row) * 3 + c
            out[j] = add_power(out[j], half[col * 3 + c], power)
    return out


def join_x_kernel(parity, links_ref, acc_ref, x_far, x_near, out_ref):
    even = even_device("gx")
    _, x_idx = site_masks()
    sign = jnp.where(x_idx == 3, -1.0, 1.0).astype(F32)
    links = x_edges(load_links(links_ref, 1, 1 - parity))
    for q in range(RHS // 2):
        nxt, last = [], []
        for c in range(3):
            near, far = load_pair(x_near, q * 3 + c), load_pair(x_far, q * 3 + c)
            nxt.append(either(even, near, far))
            last.append(either(even, far, near))
        ahead = matvec(links, nxt, False)
        for r in (2 * q, 2 * q + 1):
            half = [None] * 6
            for s in range(2):
                k = (r % 2) * 2 + s
                for c in range(3):
                    half[s * 3 + c] = tuple(
                        select(
                            x_idx == 3,
                            roll_rows(ahead[c][i], 3 - k),
                            select(x_idx == 0, roll_rows(last[c][i], 5 + k), 0.0),
                        )
                        for i in range(2)
                    )
            store_field(out_ref, r, rebuild_signed(load_field(acc_ref, r), half, 1, sign))


def join_t(links_ref, acc_ref, t_one, t_two, parity, out_ref, scale=None, done=lambda r: None):
    even = even_device("ta", "gx")
    t_idx, _ = site_masks()
    first = t_idx == 0
    sign = jnp.where(first, 1.0, -1.0).astype(F32)
    links = t_edges(load_links(links_ref, 0, 1 - parity))
    for r in range(RHS):
        nxt, last = [], []
        for c in range(3):
            one, two = load_pair(t_one, r * 3 + c), load_pair(t_two, r * 3 + c)
            nxt.append(either(even, one, two))
            last.append(either(even, two, one))
        ahead = matvec(links, nxt, False)
        half = [tuple(select(first, last[c][i], ahead[c][i]) for i in range(2)) for c in range(3)]
        half += [
            tuple(roll_rows(select(first, ahead[c][i], last[c][i]), 4) for i in range(2)) for c in range(3)
        ]
        field = rebuild_signed(load_field(acc_ref, r), half, 0, sign)
        if scale is not None:
            field = each(lambda v: v * scale, field)
        store_field(out_ref, r, field)
        done(r)


def odd_kernel(links_ref, clover_ref, acc_ref, t_one, t_two, out_ref, *refs):
    outs, summed = refs[:2], refs[2]
    join_t(links_ref, acc_ref, t_one, t_two, 0, summed)
    clover_to(clover_ref, lambda r: load_field(summed, r), out_ref, 1.0)
    send_t(out_ref, links_ref, 1, *outs)


def even_kernel(links_ref, acc_ref, t_one, t_two, out_ref, *outs):
    join_t(links_ref, acc_ref, t_one, t_two, 1, out_ref, -KAPPA2)
    send_t(out_ref, links_ref, 0, *outs)


def last_kernel(links_ref, acc_ref, t_one, t_two, out_hbm, held, sems):
    part = held.shape[0] // RHS
    copies = []

    def done(r):
        rows = pl.ds(r * part, part)
        copies.append(pltpu.make_async_copy(held.at[rows], out_hbm.at[rows], sems.at[r]))
        copies[-1].start()

    join_t(links_ref, acc_ref, t_one, t_two, 1, held, -KAPPA2, done)
    for copy in copies:
        copy.wait()


ROWS = RHS * 24 * 8
FIELD = [((ROWS, 128), BF16)]
SUM = [((ROWS, 128), F32)]
T_HALOS = [((RHS * 3 * 16, 128), BF16)] * 2
X_HALOS = [((RHS * 3 * 8, 128), BF16)] * 2


def call(kernel, args, outs, flops, scratch=(), in_space=pltpu.VMEM, out_space=pltpu.VMEM):
    return pl.pallas_call(
        kernel,
        out_shape=tuple(jax.ShapeDtypeStruct(shape, dtype) for shape, dtype in outs),
        in_specs=[pl.BlockSpec(memory_space=in_space)] * len(args),
        out_specs=tuple([pl.BlockSpec(memory_space=out_space)] * len(outs)),
        scratch_shapes=list(scratch),
        compiler_params=pltpu.CompilerParams(vmem_limit_bytes=24 * 1024 * 1024),
        cost_estimate=pl.CostEstimate(flops=flops, bytes_accessed=2 * 1024 * 1024, transcendentals=0),
    )(*args)


def swap(value, axis, far):
    count = lax.axis_size(axis)
    assert count % 2 == 0
    pairs = [(i, (i + (1 if (i % 2 == 0) != far else -1)) % count) for i in range(count)]
    return lax.ppermute(value, axis, pairs)


def swap_t(value, ahead):
    count, across = lax.axis_size("ta"), lax.axis_size("gx")
    assert count % 2 == 0 and across % 2 == 0
    pairs = []
    for i in range(count):
        for j in range(across):
            step = 1 if ((i + j) % 2 == 0) == ahead else -1
            pairs.append((i * across + j, (i + step) % count * across + j))
    return lax.ppermute(value, ("ta", "gx"), pairs)


def per_device(source, gauge_links, clover_even, clover_odd_inv):
    shape = source.shape
    f = source.reshape(-1, 128)
    links = gauge_links.reshape(-1, 128)
    even = clover_even.reshape(-1, 128)
    odd = clover_odd_inv.reshape(-1, 128)
    held = [pltpu.with_memory_space_constraint(v, pltpu.HBM) for v in (f, links)]
    start_scratch = [
        pltpu.VMEM((ROWS, 128), BF16),
        pltpu.VMEM((links.shape[0] // 4, 128), BF16),
        pltpu.SemaphoreType.DMA((RHS + 1,)),
    ]
    t_one, t_two = call(start_kernel, held, T_HALOS, 1_500_000, start_scratch, in_space=pltpu.HBM)
    for hop in range(4):
        parity = hop % 2
        t_one, t_two = swap_t(t_one, True), swap_t(t_two, False)
        x_far, x_near = call(
            functools.partial(send_x_kernel, parity), (f, links), X_HALOS, 1_500_000
        )
        here, x_far, x_near = lax.optimization_barrier((f, x_far, x_near))
        x_far, x_near = swap(x_far, "gx", True), swap(x_near, "gx", False)
        base = (before, even) if parity else ()
        acc, = call(
            functools.partial(interior_kernel, parity, bool(parity)),
            (here, links, *base), SUM, 8_000_000 if parity else 5_000_000,
        )
        acc, = call(functools.partial(join_x_kernel, parity), (links, acc, x_far, x_near), SUM, 1_000_000)
        before = f
        if parity == 0:
            f, t_one, t_two = call(
                odd_kernel, (links, odd, acc, t_one, t_two), FIELD + T_HALOS, 4_000_000,
                [pltpu.VMEM((ROWS, 128), BF16)],
            )
        elif hop == 1:
            f, t_one, t_two = call(
                even_kernel, (links, acc, t_one, t_two), FIELD + T_HALOS, 2_000_000
            )
        else:
            out, = call(
                last_kernel, (links, acc, t_one, t_two), FIELD, 1_000_000,
                [pltpu.VMEM((ROWS, 128), BF16), pltpu.SemaphoreType.DMA((RHS,))], out_space=pltpu.HBM,
            )
    return out.reshape(shape)


def solution(mesh):
    field_spec = P(None, None, None, None, ("groups", "ta"), "gx", None)
    link_spec = P(None, None, None, None, None, ("groups", "ta"), "gx", None)
    return jax.shard_map(
        per_device,
        mesh=mesh,
        in_specs=(field_spec, link_spec, field_spec, field_spec),
        out_specs=field_spec,
        check_vma=False,
    )
```

```python
import functools

import jax
import jax.numpy as jnp
from jax import lax
from jax.experimental import pallas as pl
from jax.experimental.pallas import tpu as pltpu
from jax.sharding import PartitionSpec as P

HALF_DEPTH = 8
KAPPA2 = 0.14 * 0.14
RHS = 4
F32 = jnp.float32
BF16 = jnp.bfloat16

SPIN = (((0, 0), (1, 0)), ((1, 3), (0, 3)), ((1, 2), (0, 0)), ((0, 3), (1, 1)))
SPIN_INV = (((0, 0), (1, 0)), ((1, 1), (0, 1)), ((1, 0), (0, 2)), ((0, 1), (1, 3)))


def add_power(base, value, power):
    (br, bi), (vr, vi) = base, value
    if power == 0:
        return br + vr, bi + vi
    if power == 1:
        return br - vi, bi + vr
    if power == 2:
        return br - vr, bi - vi
    return br + vi, bi - vr


def project(field, mu, sign):
    shift = 0 if sign > 0 else 2
    half = []
    for row in range(2):
        col, power = SPIN[mu][row]
        for c in range(3):
            half.append(add_power(field[row * 3 + c], field[(2 + col) * 3 + c], (power + shift) % 4))
    return half


def rebuild(acc, half, mu, sign):
    shift = 0 if sign > 0 else 2
    out = list(acc)
    for j in range(6):
        out[j] = add_power(out[j], half[j], 0)
    for row in range(2):
        col, power = SPIN_INV[mu][row]
        for c in range(3):
            j = (2 + row) * 3 + c
            out[j] = add_power(out[j], half[col * 3 + c], (power + shift) % 4)
    return out


def color(links, half, adjoint):
    out = []
    for s in range(2):
        for a in range(3):
            re = im = None
            for b in range(3):
                lr, li = links[b][a] if adjoint else links[a][b]
                vr, vi = half[s * 3 + b]
                if adjoint:
                    tr, ti = lr * vr + li * vi, lr * vi - li * vr
                else:
                    tr, ti = lr * vr - li * vi, lr * vi + li * vr
                re = tr if re is None else re + tr
                im = ti if im is None else im + ti
            out.append((re, im))
    return out


def each(function, half):
    return [(function(re), function(im)) for re, im in half]


def load_pair(ref, index):
    block = ref[index * 16:(index + 1) * 16, :].astype(F32)
    return block[0:8], block[8:16]


def rounded(half):
    out = []
    for pair in half:
        block = jnp.concatenate(pair, axis=0).astype(BF16).astype(F32)
        out.append((block[0:8], block[8:16]))
    return out


def load_links(ref, mu, parity):
    links = []
    for a in range(3):
        row = []
        for b in range(3):
            k = ((mu * 3 + a) * 3 + b) * 2
            row.append((load_pair(ref, k)[parity], load_pair(ref, k + 1)[parity]))
        links.append(row)
    return links


def load_field(ref, r):
    return [load_pair(ref, r * 12 + j) for j in range(12)]


def store_pair(ref, index, pair):
    ref[index * 16:(index + 1) * 16, :] = jnp.concatenate(pair, axis=0).astype(ref.dtype)


def store_field(ref, r, field):
    for j in range(12):
        store_pair(ref, r * 12 + j, field[j])


def site_masks():
    rows = lax.broadcasted_iota(jnp.int32, (8, 128), 0)
    return rows // 4, rows % 4


def even_device(*axes):
    place = sum(lax.axis_index(axis) for axis in axes)
    return lax.broadcast(place % 2, (8, 128)) == 0


def either(even, a, b):
    return [select(even, a[i], b[i]) for i in range(2)]


def roll_rows(value, shift):
    shift %= 8
    return pltpu.roll(value, shift, 0) if shift else value


def select(mask, a, b):
    return jnp.where(mask, a, b)


def t_edges(links):
    t_idx, _ = site_masks()
    return [each(lambda v: select(t_idx == 0, roll_rows(v, 4), v), row) for row in links]


def x_edges(links):
    _, x_idx = site_masks()

    def edge(value):
        out = value
        for k in range(3):
            out = select(x_idx == k, roll_rows(value, k - 3), out)
        return out

    return [each(edge, row) for row in links]


def send_t(f_ref, links_ref, parity, t_one, t_two, ready=lambda r: None):
    even = even_device("ta", "gx")
    t_idx, _ = site_masks()
    first = t_idx == 0
    links = t_edges(load_links(links_ref, 0, parity))
    for r in range(RHS):
        ready(r)
        field = load_field(f_ref, r)
        ahead, behind = project(field, 0, -1), project(field, 0, 1)
        rears = [
            tuple(select(first, roll_rows(behind[c][i], 4), behind[c + 3][i]) for i in range(2)) for c in range(3)
        ]
        rears = matvec(links, rounded(rears), True)
        for c in range(3):
            front = [select(first, ahead[c + 3][i], roll_rows(ahead[c][i], 4)) for i in range(2)]
            store_pair(t_one, r * 3 + c, either(even, rears[c], front))
            store_pair(t_two, r * 3 + c, either(even, front, rears[c]))


def send_x_kernel(parity, f_ref, links_ref, x_far, x_near):
    even = even_device("gx")
    _, x_idx = site_masks()
    links = x_edges(load_links(links_ref, 1, parity))

    def packed(values, row, step):
        out = values[0]
        for k in range(1, 4):
            out = select(x_idx == row + step * k, roll_rows(values[k], step * k), out)
        return out

    for q in range(RHS // 2):
        fields = [load_field(f_ref, r) for r in (2 * q, 2 * q + 1)]
        ahead = [project(field, 1, -1) for field in fields]
        behind = [project(field, 1, 1) for field in fields]
        fronts, rears = [], []
        for c in range(3):
            fronts.append([packed([h[j][i] for h in ahead for j in (c, c + 3)], 0, 1) for i in range(2)])
            rears.append([packed([h[j][i] for h in behind for j in (c, c + 3)], 3, -1) for i in range(2)])
        rears = matvec(links, rounded(rears), True)
        for c in range(3):
            store_pair(x_near, q * 3 + c, either(even, rears[c], fronts[c]))
            store_pair(x_far, q * 3 + c, either(even, fronts[c], rears[c]))


def start_kernel(f_hbm, links_hbm, *refs):
    outs, (f_ref, links_ref, sems) = refs[:2], refs[2:]
    part = f_ref.shape[0] // RHS
    copies = [pltpu.make_async_copy(links_hbm.at[pl.ds(0, links_ref.shape[0])], links_ref, sems.at[RHS])]
    for r in range(RHS):
        rows = pl.ds(r * part, part)
        copies.append(pltpu.make_async_copy(f_hbm.at[rows], f_ref.at[rows], sems.at[r]))
    for copy in copies:
        copy.start()
    copies[0].wait()
    send_t(f_ref, links_ref, 0, *outs, ready=lambda r: copies[1 + r].wait())


def interior_kernel(parity, with_base, *refs):
    if with_base:
        f_ref, links_ref, base_ref, clover_ref, acc_ref = refs
        clover_to(clover_ref, lambda r: load_field(base_ref, r), acc_ref, -1.0 / KAPPA2)
    else:
        f_ref, links_ref, acc_ref = refs
    out_parity = 1 - parity
    t_idx, x_idx = site_masks()
    lane = lax.broadcasted_iota(jnp.int32, (8, 128), 1)
    odd = (t_idx + x_idx + lane // HALF_DEPTH + out_parity) % 2
    start = lane - lane % HALF_DEPTH
    up = jnp.where(odd == 1, start + (lane + 1) % HALF_DEPTH, lane)
    down = jnp.where(odd == 0, start + (lane + HALF_DEPTH - 1) % HALF_DEPTH, lane)
    zero = jnp.zeros((8, 128), F32)

    def take(value, index):
        return jnp.take_along_axis(value, index, axis=1, mode="promise_in_bounds")

    for mu in (2, 3, 0, 1):
        if mu == 2:
            ahead_of = lambda v: pltpu.roll(v, 128 - HALF_DEPTH, 1)
            behind_of = lambda v: pltpu.roll(v, HALF_DEPTH, 1)
        elif mu == 3:
            ahead_of = lambda v: take(v, up)
            behind_of = lambda v: take(v, down)
        elif mu == 0:
            ahead_of = lambda v: select(t_idx == 0, roll_rows(v, 4), 0.0)
            behind_of = lambda v: select(t_idx == 1, roll_rows(v, 4), 0.0)
        else:
            ahead_of = lambda v: select(x_idx < 3, roll_rows(v, 7), 0.0)
            behind_of = lambda v: select(x_idx > 0, roll_rows(v, 1), 0.0)
        links_out = load_links(links_ref, mu, out_parity)
        links_in = load_links(links_ref, mu, parity)
        for r in range(RHS):
            field = load_field(f_ref, r)
            if mu == 2 and not with_base:
                acc = [(zero, zero)] * 12
            else:
                acc = load_field(acc_ref, r)
            half = color(links_out, each(ahead_of, rounded(project(field, mu, -1))), False)
            acc = rebuild(acc, half, mu, -1)
            half = rounded(color(links_in, rounded(project(field, mu, 1)), True))
            acc = rebuild(acc, each(behind_of, half), mu, 1)
            store_field(acc_ref, r, acc)


def clover_to(clover_ref, get_field, out_ref, scale):
    for chi in range(2):
        matrix = {}
        for i in range(6):
            for j in range(i, 6):
                k = (chi * 6 + i) * 6 + j
                block = clover_ref[k * 16:(k + 1) * 16, :].astype(F32)
                re, im = block[0:8], block[8:16]
                if scale != 1.0:
                    re, im = re * scale, im * scale
                matrix[i, j] = (re, re + im, im - re)
        for r in range(RHS):
            field = get_field(r)[chi * 6:chi * 6 + 6]
            both = [vr + vi for vr, vi in field]
            for i in range(6):
                re, im = matrix[i, i][0] * field[i][0], matrix[i, i][0] * field[i][1]
                one = None
                for j in range(6):
                    if j == i:
                        continue
                    vr, vi = field[j]
                    m, plus, minus = matrix[min(i, j), max(i, j)]
                    t_one = m * both[j]
                    one = t_one if one is None else one + t_one
                    if i < j:
                        re, im = re - vi * plus, im + vr * minus
                    else:
                        re, im = re + vi * minus, im - vr * plus
                store_pair(out_ref, r * 12 + chi * 6 + i, (re + one, im + one))


def matvec(links, vector, adjoint):
    both = [vr + vi for vr, vi in vector]
    out = []
    for a in range(3):
        one = re = im = None
        for b in range(3):
            lr, li = links[b][a] if adjoint else links[a][b]
            vr, vi = vector[b]
            plus, minus = lr + li, li - lr
            t_one = lr * both[b]
            t_re, t_im = (vi * minus, vr * plus) if adjoint else (vi * plus, vr * minus)
            one = t_one if one is None else one + t_one
            re = t_re if re is None else re + t_re
            im = t_im if im is None else im + t_im
        out.append((one + re, one - im) if adjoint else (one - re, one + im))
    return out


def rebuild_signed(acc, half, mu, sign):
    out = list(acc)
    for j in range(6):
        out[j] = add_power(out[j], half[j], 0)
    half = each(lambda v: v * sign, half)
    for row in range(2):
        col, power = SPIN_INV[mu][row]
        for c in range(3):
            j = (2 + row) * 3 + c
            out[j] = add_power(out[j], half[col * 3 + c], power)
    return out


def join_x_kernel(parity, links_ref, acc_ref, x_far, x_near, out_ref):
    even = even_device("gx")
    _, x_idx = site_masks()
    sign = jnp.where(x_idx == 3, -1.0, 1.0).astype(F32)
    links = x_edges(load_links(links_ref, 1, 1 - parity))
    for q in range(RHS // 2):
        nxt, last = [], []
        for c in range(3):
            near, far = load_pair(x_near, q * 3 + c), load_pair(x_far, q * 3 + c)
            nxt.append(either(even, near, far))
            last.append(either(even, far, near))
        ahead = matvec(links, nxt, False)
        for r in (2 * q, 2 * q + 1):
            half = [None] * 6
            for s in range(2):
                k = (r % 2) * 2 + s
                for c in range(3):
                    half[s * 3 + c] = tuple(
                        select(
                            x_idx == 3,
                            roll_rows(ahead[c][i], 3 - k),
                            select(x_idx == 0, roll_rows(last[c][i], 5 + k), 0.0),
                        )
                        for i in range(2)
                    )
            store_field(out_ref, r, rebuild_signed(load_field(acc_ref, r), half, 1, sign))


def join_t(links_ref, acc_ref, t_one, t_two, parity, out_ref, scale=None, done=lambda r: None):
    even = even_device("ta", "gx")
    t_idx, _ = site_masks()
    first = t_idx == 0
    sign = jnp.where(first, 1.0, -1.0).astype(F32)
    links = t_edges(load_links(links_ref, 0, 1 - parity))
    for r in range(RHS):
        nxt, last = [], []
        for c in range(3):
            one, two = load_pair(t_one, r * 3 + c), load_pair(t_two, r * 3 + c)
            nxt.append(either(even, one, two))
            last.append(either(even, two, one))
        ahead = matvec(links, nxt, False)
        half = [tuple(select(first, last[c][i], ahead[c][i]) for i in range(2)) for c in range(3)]
        half += [
            tuple(roll_rows(select(first, ahead[c][i], last[c][i]), 4) for i in range(2)) for c in range(3)
        ]
        field = rebuild_signed(load_field(acc_ref, r), half, 0, sign)
        if scale is not None:
            field = each(lambda v: v * scale, field)
        store_field(out_ref, r, field)
        done(r)


def odd_kernel(links_ref, clover_ref, acc_ref, t_one, t_two, out_ref, *refs):
    outs, summed = refs[:2], refs[2]
    join_t(links_ref, acc_ref, t_one, t_two, 0, summed)
    clover_to(clover_ref, lambda r: load_field(summed, r), out_ref, 1.0)
    send_t(out_ref, links_ref, 1, *outs)


def even_kernel(links_ref, acc_ref, t_one, t_two, out_ref, *outs):
    join_t(links_ref, acc_ref, t_one, t_two, 1, out_ref, -KAPPA2)
    send_t(out_ref, links_ref, 0, *outs)


def last_kernel(links_ref, acc_ref, t_one, t_two, out_hbm, held, sems):
    part = held.shape[0] // RHS
    copies = []

    def done(r):
        rows = pl.ds(r * part, part)
        copies.append(pltpu.make_async_copy(held.at[rows], out_hbm.at[rows], sems.at[r]))
        copies[-1].start()

    join_t(links_ref, acc_ref, t_one, t_two, 1, held, -KAPPA2, done)
    for copy in copies:
        copy.wait()


ROWS = RHS * 24 * 8
FIELD = [((ROWS, 128), BF16)]
SUM = [((ROWS, 128), F32)]
T_HALOS = [((RHS * 3 * 16, 128), BF16)] * 2
X_HALOS = [((RHS * 3 * 8, 128), BF16)] * 2


def call(kernel, args, outs, flops, scratch=(), in_space=pltpu.VMEM, out_space=pltpu.VMEM):
    return pl.pallas_call(
        kernel,
        out_shape=tuple(jax.ShapeDtypeStruct(shape, dtype) for shape, dtype in outs),
        in_specs=[pl.BlockSpec(memory_space=in_space)] * len(args),
        out_specs=tuple([pl.BlockSpec(memory_space=out_space)] * len(outs)),
        scratch_shapes=list(scratch),
        compiler_params=pltpu.CompilerParams(vmem_limit_bytes=24 * 1024 * 1024),
        cost_estimate=pl.CostEstimate(flops=flops, bytes_accessed=2 * 1024 * 1024, transcendentals=0),
    )(*args)


def swap(value, axis, far):
    count = lax.axis_size(axis)
    assert count % 2 == 0
    pairs = [(i, (i + (1 if (i % 2 == 0) != far else -1)) % count) for i in range(count)]
    return lax.ppermute(value, axis, pairs)


def swap_t(value, ahead):
    count, across = lax.axis_size("ta"), lax.axis_size("gx")
    assert count % 2 == 0 and across % 2 == 0
    pairs = []
    for i in range(count):
        for j in range(across):
            step = 1 if ((i + j) % 2 == 0) == ahead else -1
            pairs.append((i * across + j, (i + step) % count * across + j))
    return lax.ppermute(value, ("ta", "gx"), pairs)


def per_device(source, gauge_links, clover_even, clover_odd_inv):
    shape = source.shape
    f = source.reshape(-1, 128)
    links = gauge_links.reshape(-1, 128)
    even = clover_even.reshape(-1, 128)
    odd = clover_odd_inv.reshape(-1, 128)
    held = [pltpu.with_memory_space_constraint(v, pltpu.HBM) for v in (f, links)]
    start_scratch = [
        pltpu.VMEM((ROWS, 128), BF16),
        pltpu.VMEM((links.shape[0] // 4, 128), BF16),
        pltpu.SemaphoreType.DMA((RHS + 1,)),
    ]
    t_one, t_two = call(start_kernel, held, T_HALOS, 1_500_000, start_scratch, in_space=pltpu.HBM)
    for hop in range(4):
        parity = hop % 2
        t_one, t_two = swap_t(t_one, True), swap_t(t_two, False)
        x_far, x_near = call(
            functools.partial(send_x_kernel, parity), (f, links), X_HALOS, 1_500_000
        )
        here, x_far, x_near = lax.optimization_barrier((f, x_far, x_near))
        x_far, x_near = swap(x_far, "gx", True), swap(x_near, "gx", False)
        base = (before, even) if parity else ()
        acc, = call(
            functools.partial(interior_kernel, parity, bool(parity)),
            (here, links, *base), SUM, 8_000_000 if parity else 5_000_000,
        )
        acc, = call(functools.partial(join_x_kernel, parity), (links, acc, x_far, x_near), SUM, 1_000_000)
        before = f
        if parity == 0:
            f, t_one, t_two = call(
                odd_kernel, (links, odd, acc, t_one, t_two), FIELD + T_HALOS, 4_000_000,
                [pltpu.VMEM((ROWS, 128), BF16)],
            )
        elif hop == 1:
            f, t_one, t_two = call(
                even_kernel, (links, acc, t_one, t_two), FIELD + T_HALOS, 2_000_000
            )
        else:
            out, = call(
                last_kernel, (links, acc, t_one, t_two), FIELD, 1_000_000,
                [pltpu.VMEM((ROWS, 128), BF16), pltpu.SemaphoreType.DMA((RHS,))], out_space=pltpu.HBM,
            )
    return out.reshape(shape)


def solution(mesh):
    field_spec = P(None, None, None, None, ("groups", "ta"), "gx", None)
    link_spec = P(None, None, None, None, None, ("groups", "ta"), "gx", None)
    return jax.shard_map(
        per_device,
        mesh=mesh,
        in_specs=(field_spec, link_spec, field_spec, field_spec),
        out_specs=field_spec,
        check_vma=False,
    )
```
